32 devices in a mesh: gx: 8 (over z, x), gy: 4 (over y, core).
Axes of the slice: x: 2, y: 2, z: 4, core: 2. Of those that a mesh axis runs over, the one named last changes fastest.
Arguments:
- features: bfloat16 [8, 4, 16, 48, 512], P('gx', 'gy'), may hold values from -6 to 6
- block_slots: int32 [8, 4, 16], P('gx', 'gy'), may hold values from 0 to 15, as said below
- block_count: int32 [8, 4], P('gx', 'gy'), may hold values from 2 to 16
- cotangent: bfloat16 [8, 4, 16, 48, 512], P('gx', 'gy'), may hold values from -6 to 6
- fine_weight: bfloat16 [48, 27, 48], replicated, may hold values from -0.15625 to 0.15625
- down_weight: bfloat16 [48, 8, 48], replicated, may hold values from -0.3125 to 0.3125
- coarse_weight: bfloat16 [48, 27, 48], replicated, may hold values from -0.15625 to 0.15625
- up_weight: bfloat16 [8, 48, 48], replicated, may hold values from -0.875 to 0.875
Outputs:
- output: bfloat16 [8, 4, 16, 48, 512], P('gx', 'gy')
- input_grad: bfloat16 [8, 4, 16, 48, 512], P('gx', 'gy')
- fine_weight_grad: float32 [48, 27, 48], replicated
- down_weight_grad: float32 [48, 8, 48], replicated
- coarse_weight_grad: float32 [48, 27, 48], replicated
- up_weight_grad: float32 [8, 48, 48], replicated
The draws below stay inside these ranges and needn't reach their ends.
Inputs may be any that keep to these rules, and one draw needn't show every extreme that they name: `block_slots`: on each device the 16 entries are distinct, so every block position of the region appears once.
All inputs are finite; a program needn't handle non-finite values.
Results may differ from the reference program's by a relative error of at most 0.008.
Values may be sent and summed in bfloat16 or wider, within the bound.
No kernel may reach another device: no remote copies, remote signals or barrier semaphores. Data moves between devices by JAX's collectives and lax.ppermute only.
A program may use at most 192 MiB of HBM per device.

```python
import math
import jax
import jax.numpy as jnp
from jax import lax

C = 48
BLOCK = 8
VOX = 512
KVOL = 27
SUB = 8
BX = 1
SLOTS = 16
BY = 16
N_GX = 8
N_GY = 4


def draw_block_slots(key, part):
    count_dev = N_GX * N_GY
    keys = jax.random.split(jax.random.fold_in(key, 5), count_dev)
    orders = jax.vmap(lambda single: jax.random.permutation(single, SLOTS))(keys)
    return orders.reshape(N_GX, N_GY, SLOTS).astype(jnp.int32)


def draw_block_count(key, part):
    count_dev = N_GX * N_GY
    least = max(1, SLOTS // 8)
    counts = jax.random.randint(jax.random.fold_in(key, 11), (count_dev,), least, SLOTS + 1)
    busiest = jax.random.randint(jax.random.fold_in(key, 12), (), 0, count_dev)
    counts = jnp.where(jnp.arange(count_dev) == busiest, SLOTS, counts)
    return counts.reshape(N_GX, N_GY).astype(jnp.int32)


def steps_of(own_key, extent, shards, low, top_value):
    gain = 1.0
    for dim, shards_of in shards:
        heights = jax.random.uniform(jax.random.fold_in(jax.random.fold_in(own_key, 6), dim), (shards_of,), jnp.float32, low / len(shards), top_value / len(shards))
        gain = gain * jnp.repeat(jnp.exp(heights), extent[dim] // shards_of).reshape((-1,) + (1,) * (len(extent) - 1 - dim))
    return gain


def scatter_about(rng, extent, spread, most, cuts=(), kind=jnp.bfloat16):
    gain = steps_of(rng, extent, cuts, -0.22, 0.18) if cuts else 1.0
    values = jax.random.normal(rng, extent, jnp.float32) * spread * gain
    return jnp.minimum(jnp.maximum(values, -most), most).astype(kind)


def setup_inputs(seed: int = 0) -> dict:
    seeds = jax.random.split(jax.random.key(seed), 9)
    features = scatter_about(seeds[0], (N_GX, N_GY, SLOTS, C, VOX), 1.0, 6.0, ((0, 8), (1, 4)))
    block_slots = draw_block_slots(jax.random.fold_in(seeds[8], 71), 0)
    block_count = draw_block_count(jax.random.fold_in(seeds[8], 71), 0)
    cotangent = scatter_about(seeds[3], (N_GX, N_GY, SLOTS, C, VOX), 1.0, 6.0, ((0, 8), (1, 4)))
    fine_weight = scatter_about(seeds[4], (C, KVOL, C), (KVOL * C) ** -0.5, 0.15625)
    down_weight = scatter_about(seeds[5], (C, SUB, C), (SUB * C) ** -0.5, 0.3125)
    coarse_weight = scatter_about(seeds[6], (C, KVOL, C), (KVOL * C) ** -0.5, 0.15625)
    up_weight = scatter_about(seeds[7], (SUB, C, C), C ** -0.5, 0.875)
    return dict(features=features, block_slots=block_slots, block_count=block_count, cotangent=cotangent, fine_weight=fine_weight, down_weight=down_weight, coarse_weight=coarse_weight, up_weight=up_weight)


def offset_columns(window, edge, flipped):
    pieces = []
    for depth in range(3):
        for across in range(3):
            for along in range(3):
                if flipped:
                    first = (2 - depth, 2 - across, 2 - along)
                else:
                    first = (depth, across, along)
                piece = window[..., first[0]:first[0] + edge, first[1]:first[1] + edge, first[2]:first[2] + edge]
                pieces.append(piece.reshape(piece.shape[:-3] + (edge ** 3,)))
    return jnp.stack(pieces, axis=-3)

def split_parity(fine):
    lead = fine.shape[:-2]
    chans = fine.shape[-2]
    count = len(lead)
    shaped = fine.reshape(lead + (chans, 4, 2, 4, 2, 4, 2))
    order = tuple(range(count)) + (count + 2, count + 4, count + 6, count, count + 1, count + 3, count + 5)
    return shaped.transpose(order).reshape(lead + (8, chans, 64))

def join_parity(parts):
    lead = parts.shape[:-3]
    chans = parts.shape[-2]
    count = len(lead)
    shaped = parts.reshape(lead + (2, 2, 2, chans, 4, 4, 4))
    order = tuple(range(count)) + (count + 3, count + 4, count, count + 5, count + 1, count + 6, count + 2)
    return shaped.transpose(order).reshape(lead + (chans, 512))

def smooth_gate(value):
    return value * jax.nn.sigmoid(value)

def gate_slope(value):
    sigma = jax.nn.sigmoid(value)
    return sigma * (1.0 + value * (1.0 - sigma))

def global_grid(blocks, places, edge):
    count_dev = blocks.shape[0]
    chans = blocks.shape[2]
    owner = jnp.arange(count_dev, dtype=jnp.int32)[:, None]
    dense = jnp.zeros((count_dev, BX * BY, chans, edge ** 3), blocks.dtype).at[owner, places].set(blocks)
    dense = dense.reshape(N_GX, N_GY, BX, BY, chans, edge, edge, edge)
    dense = dense.transpose(4, 5, 0, 2, 6, 1, 3, 7)
    dense = dense.reshape(chans, edge, N_GX * BX * edge, N_GY * BY * edge)
    return jnp.pad(dense, ((0, 0), (1, 1), (1, 1), (1, 1)))

def device_windows(padded, device, places, edge):
    row = places[device]
    start_x = ((device // N_GY * BX + row // BY) * edge).astype(jnp.int32)
    start_y = ((device % N_GY * BY + row % BY) * edge).astype(jnp.int32)
    zero = jnp.zeros((), jnp.int32)

    def single(first_x, first_y):
        return lax.dynamic_slice(padded, (zero, zero, first_x, first_y), (padded.shape[0], edge + 2, edge + 2, edge + 2))
    return jax.vmap(single)(start_x, start_y)

def reference(features, block_slots, block_count, cotangent, fine_weight, down_weight, coarse_weight, up_weight):
    count_dev = N_GX * N_GY
    half = BLOCK // 2
    places = block_slots.reshape(count_dev, SLOTS).astype(jnp.int32)
    live = jnp.arange(SLOTS, dtype=jnp.int32)[None, :] < block_count.reshape(count_dev, 1)
    live_blocks = live[:, :, None, None]
    zero_half = jnp.zeros((), jnp.bfloat16)
    inputs = jnp.where(live_blocks, features.reshape(count_dev, SLOTS, C, VOX), zero_half)
    grad_out = jnp.where(live_blocks, cotangent.reshape(count_dev, SLOTS, C, VOX), zero_half)
    fine_w = fine_weight.astype(jnp.float32)
    down_w = down_weight.astype(jnp.float32)
    coarse_w = coarse_weight.astype(jnp.float32)
    up_w = up_weight.astype(jnp.float32)
    devices = jnp.arange(count_dev, dtype=jnp.int32)
    fine_pad = global_grid(inputs, places, BLOCK)

    def forward_fine(device):
        columns = offset_columns(device_windows(fine_pad, device, places, BLOCK), BLOCK, False).astype(jnp.float32)
        hidden = jnp.einsum('okc,skcv->sov', fine_w, columns)
        hidden = jnp.where(live_blocks[device], hidden, 0.0)
        active = smooth_gate(hidden).astype(jnp.bfloat16)
        lowered = jnp.einsum('oqc,sqcv->sov', down_w, split_parity(active).astype(jnp.float32))
        lowered = jnp.where(live_blocks[device], lowered, 0.0).astype(jnp.bfloat16)
        return (hidden, active, lowered)
    hidden, active, lowered = lax.map(forward_fine, devices)
    coarse_pad = global_grid(lowered, places, half)

    def coarse_section(device):
        columns = offset_columns(device_windows(coarse_pad, device, places, half), half, False).astype(jnp.float32)
        coarse = jnp.einsum('okc,skcv->sov', coarse_w, columns)
        rect = smooth_gate(coarse).astype(jnp.bfloat16)
        rect_wide = rect.astype(jnp.float32)
        upward = join_parity(jnp.einsum('qoc,scv->sqov', up_w, rect_wide))
        output = jnp.where(live_blocks[device], hidden[device] + upward, 0.0).astype(jnp.bfloat16)
        parts = split_parity(grad_out[device]).astype(jnp.float32)
        grad_rect = jnp.einsum('qoc,sqov->scv', up_w, parts)
        grad_coarse = jnp.where(live_blocks[device], grad_rect * gate_slope(coarse), 0.0).astype(jnp.bfloat16)
        up_term = jnp.einsum('sqov,scv->qoc', parts, rect_wide)
        coarse_term = jnp.einsum('sov,skcv->okc', grad_coarse.astype(jnp.float32), columns)
        return (output, grad_coarse, up_term, coarse_term)
    output, grad_coarse, up_terms, coarse_terms = lax.map(coarse_section, devices)
    grad_coarse_pad = global_grid(grad_coarse, places, half)

    def down_section(device):
        back = offset_columns(device_windows(grad_coarse_pad, device, places, half), half, True).astype(jnp.float32)
        grad_down = jnp.einsum('okc,skov->scv', coarse_w, back)
        grad_down = jnp.where(live_blocks[device], grad_down, 0.0).astype(jnp.bfloat16)
        grad_wide = grad_down.astype(jnp.float32)
        down_term = jnp.einsum('sov,sqcv->oqc', grad_wide, split_parity(active[device]).astype(jnp.float32))
        grad_act = join_parity(jnp.einsum('oqc,sov->sqcv', down_w, grad_wide))
        grad_hidden = grad_out[device].astype(jnp.float32) + grad_act * gate_slope(hidden[device])
        grad_hidden = jnp.where(live_blocks[device], grad_hidden, 0.0).astype(jnp.bfloat16)
        return (grad_hidden, down_term)
    grad_hidden, down_terms = lax.map(down_section, devices)
    grad_hidden_pad = global_grid(grad_hidden, places, BLOCK)

    def fine_section(device):
        fore = offset_columns(device_windows(fine_pad, device, places, BLOCK), BLOCK, False).astype(jnp.float32)
        back = offset_columns(device_windows(grad_hidden_pad, device, places, BLOCK), BLOCK, True).astype(jnp.float32)
        fine_term = jnp.einsum('sov,skcv->okc', grad_hidden[device].astype(jnp.float32), fore)
        input_grad = jnp.einsum('okc,skov->scv', fine_w, back)
        input_grad = jnp.where(live_blocks[device], input_grad, 0.0).astype(jnp.bfloat16)
        return (input_grad, fine_term)
    input_grad, fine_terms = lax.map(fine_section, devices)
    scale = 1.0 / math.sqrt(SLOTS * VOX * count_dev)
    shape_out = (N_GX, N_GY, SLOTS, C, VOX)
    return (output.reshape(shape_out), input_grad.reshape(shape_out), lax.optimization_barrier(jnp.sum(fine_terms, axis=0)) * scale, lax.optimization_barrier(jnp.sum(down_terms, axis=0)) * scale, lax.optimization_barrier(jnp.sum(coarse_terms, axis=0)) * scale, lax.optimization_barrier(jnp.sum(up_terms, axis=0)) * scale)
```

```python
import math

import jax
import jax.numpy as jnp
import numpy as np
from jax import lax
from jax.experimental import pallas as pl
from jax.experimental.pallas import tpu as pltpu
from jax.sharding import PartitionSpec as P

C = 48
EDGE = 8
VOX = 512
LANES = 128
F32 = jnp.float32
BF16 = jnp.bfloat16
VMEM_LIMIT = 58 * 1024 * 1024
SHIFTS = (0, 1, 16, 17)


def placing_matrix():
    place = np.zeros((1024, 8 * LANES), np.float32)
    for z in range(8):
        for y in range(8):
            for x in range(8):
                place[64 * z + 8 * x + y, LANES * y + 16 * z + x + 4] = 1.0
            for x in range(4):
                place[512 + 32 * z + 8 * x + y, LANES * y + 16 * z + x] = 1.0
                place[768 + 32 * z + 8 * x + y, LANES * y + 16 * z + x + 12] = 1.0
    return place


def edge_matrix():
    pick = np.zeros((512, 512), np.float32)
    for z in range(8):
        for y in range(8):
            for x in range(8):
                pick[64 * z + 8 * x + y, 256 * (x // 4) + 32 * z + 8 * (x % 4) + y] = 1.0
    return pick


def dot(left, right, contract=(1, 0)):
    dims = (((contract[0],), (contract[1],)), ((), ()))
    return lax.dot_general(left, right, dims, preferred_element_type=F32)


def roll(value, shift):
    return pltpu.roll(value, shift % LANES, 1)


def lane_ids(rows):
    return lax.broadcasted_iota(jnp.int32, (rows, LANES), 1)


def silu_parts(value):
    sigma = 1.0 / (1.0 + jnp.exp(-value))
    return value * sigma, sigma * (1.0 + value * (1.0 - sigma))


def columns(tile, low, high, z_step, x_step):
    zero = jnp.zeros_like(tile)
    below = jnp.where(low, zero, roll(tile, z_step))
    above = jnp.where(high, zero, roll(tile, -z_step))
    base = jnp.concatenate([below, tile, above], axis=0)
    return jnp.concatenate([roll(base, x_step), base, roll(base, -x_step)], axis=0)


def z_masks(z_step):
    ids = lane_ids(C)
    return ids < z_step, ids >= LANES - z_step


def gather_sub(parts):
    total = parts[:C]
    for index in range(1, 4):
        total = total + roll(parts[index * C : (index + 1) * C], -SHIFTS[index])
    return total


def spread_sub(anchored):
    return jnp.concatenate([anchored] + [roll(anchored, step) for step in SHIFTS[1:]], axis=0)


def anchor_mask(own):
    ids = lane_ids(C)
    across = ids % 16
    keep = ((ids // 16) % 2 == 0) & (across % 2 == 0)
    if own:
        keep = keep & (across >= 4) & (across < 12)
    return keep.astype(F32)


def loop(low, high, body, unroll=1):
    def step(index, carry):
        body(index)
        return carry

    lax.fori_loop(low, high, step, 0, unroll=unroll)


def prepare_kernel(
    slots, count, feats, cots, pick, own, cot, x_low, x_high, y_low, y_high, d_ll, d_lh, d_hl, d_hh
):
    number = feats.shape[0]
    rows = lax.broadcasted_iota(jnp.int32, (C, VOX), 0)
    flags = jnp.zeros((C, VOX), F32)
    first = jnp.zeros((), F32)
    last = jnp.zeros((), F32)
    zero = jnp.zeros((C, VOX), BF16)
    for slot in range(number):
        live = slot < count[0]
        alive = jnp.where(live, 1.0, 0.0)
        place = slots[slot]
        own[place] = jnp.where(live, feats[slot], zero)
        cot[place] = jnp.where(live, cots[slot], zero)
        flags = jnp.where(rows == place + 1, alive, flags)
        first = first + jnp.where(place == 0, alive, 0.0)
        last = last + jnp.where(place == number - 1, alive, 0.0)
    own[number] = flags.astype(BF16)
    first_flag = jnp.where(rows == number + 1, first, 0.0).astype(BF16)
    last_flag = jnp.where(rows == 0, last, 0.0).astype(BF16)
    packed = dot(own[...].reshape((number + 1) * C, VOX), pick[...]).astype(BF16)
    packed = packed.reshape(number + 1, C, VOX)
    x_low[...] = packed[:, :, :256]
    x_high[...] = packed[:, :, 256:]
    for out, index, flag in ((y_low, 0, first_flag), (y_high, number - 1, last_flag)):
        out[0] = own[index]
        out[1] = cot[index]
        out[2] = flag
    for out, index, flag, at in (
        (d_ll, 0, first_flag, 0),
        (d_lh, number - 1, last_flag, 0),
        (d_hl, 0, first_flag, 256),
        (d_hh, number - 1, last_flag, 256),
    ):
        out[0] = packed[index, :, at : at + 256]
        out[1] = flag[:, :256]


def forward_kernel(
    own, cot, x_left, x_right, y_left, y_right, d_ll, d_lr, d_rl, d_rr, place, fine_w, down_w,
    coarse_w, up_w,
    grid, cot_grid, hidden, lowered, rects, grad_c, live, pack_low, pack_high,
    rows_in, rows_cot, fine_p, coarse_p,
):
    number = cot.shape[0]
    last = number + 1
    for block in range(number):
        at = (block + 1) * C
        rows_in[at : at + C, 0:512] = own[block]
        rows_in[at : at + C, 512:768] = x_left[block]
        rows_in[at : at + C, 768:1024] = x_right[block]
        rows_cot[at : at + C, :] = cot[block]
    for at, middle, left, right in (
        (0, y_left, d_ll, d_rl),
        (last * C, y_right, d_lr, d_rr),
    ):
        rows_in[at : at + C, 0:512] = middle[0]
        rows_in[at : at + C, 512:768] = left[0]
        rows_in[at : at + C, 768:1024] = right[0]
        rows_cot[at : at + C, :] = middle[1]
    at = (last + 1) * C
    rows_in[at : at + C, 0:512] = own[number] + y_left[2] + y_right[2]
    rows_in[at : at + C, 512:768] = x_left[number] + d_ll[1] + d_lr[1]
    rows_in[at : at + C, 768:1024] = x_right[number] + d_rl[1] + d_rr[1]
    for pair in range(4):
        lanes = slice(256 * pair, 256 * pair + 256)
        placed = dot(rows_in[...], place[:, lanes])
        placed_cot = dot(rows_cot[...], place[0:512, lanes])
        for half in range(2):
            span = slice(LANES * half, LANES * (half + 1))
            for block in range(last + 1):
                tile = EDGE * block + 2 * pair + half
                grid[tile] = placed[block * C : (block + 1) * C, span].astype(BF16)
                cot_grid[tile] = placed_cot[block * C : (block + 1) * C, span].astype(BF16)
        if pair == 0:
            live[...] = placed[(last + 1) * C :, 0:LANES]
    tiles = grid.shape[0]
    coarse_tiles = lowered.shape[0]
    low, high = z_masks(16)

    def fine_step(index):
        tile = 1 + 2 * index
        cols = jnp.concatenate(
            [columns(grid[tile], low, high, 16, 1), columns(grid[tile + 1], low, high, 16, 1)],
            axis=1,
        )
        out = dot(fine_w[...], cols)
        fine_p[tile] = out[:, :LANES]
        fine_p[tile + 1] = out[:, LANES:]

    loop(0, (tiles - 2) // 2, fine_step, 2)
    anchors = anchor_mask(False)

    def lower_step(coarse):
        alive = jnp.broadcast_to(live[pl.ds(coarse // 4, 1), :], (C, LANES))
        actives = []
        for half in range(2):
            tile = 2 * coarse + half
            value = fine_p[tile - 1, 0:C] + fine_p[tile, C : 2 * C] + fine_p[tile + 1, 2 * C :]
            value = value * alive
            hidden[tile] = value
            actives.append(silu_parts(value)[0].astype(BF16))
        parts = dot(down_w[...], jnp.concatenate(actives, axis=0))
        lowered[coarse] = (gather_sub(parts) * (alive * anchors)).astype(BF16)

    loop(1, coarse_tiles - 1, lower_step, 2)
    low_c, high_c = z_masks(32)

    def coarse_step(index):
        coarse = 1 + 2 * index
        cols = jnp.concatenate(
            [
                columns(lowered[coarse], low_c, high_c, 32, 2),
                columns(lowered[coarse + 1], low_c, high_c, 32, 2),
            ],
            axis=1,
        )
        out = dot(coarse_w[...], cols)
        coarse_p[coarse] = out[:, :LANES]
        coarse_p[coarse + 1] = out[:, LANES:]

    loop(0, (coarse_tiles - 2) // 2, coarse_step, 2)
    own_anchors = anchor_mask(True)

    def grad_step(coarse):
        alive = jnp.broadcast_to(live[pl.ds(coarse // 4, 1), :], (C, LANES))
        value = (
            coarse_p[coarse - 1, 0:C] + coarse_p[coarse, C : 2 * C] + coarse_p[coarse + 1, 2 * C :]
        )
        smooth, slope = silu_parts(value)
        rects[coarse] = (smooth * own_anchors).astype(BF16)
        pair = jnp.concatenate([cot_grid[2 * coarse], cot_grid[2 * coarse + 1]], axis=0)
        grad_rect = gather_sub(dot(up_w[...], pair, (0, 0)))
        grad_c[coarse] = (grad_rect * slope * (alive * own_anchors)).astype(BF16)

    loop(2, coarse_tiles - 2, grad_step, 2)
    ids = lane_ids(C)
    zero = jnp.zeros((C, LANES), BF16)
    for out, lane in ((pack_low, 4), (pack_high, 10)):
        for group in range(out.shape[0]):
            total = zero
            for coarse in range(max(2, 32 * group), min(coarse_tiles - 2, 32 * group + 32)):
                picked = jnp.where(ids % 32 == lane, grad_c[coarse], zero)
                total = total + roll(picked, coarse % 32 - lane)
            out[group] = total


def to_blocks(slots, rows_out, place, out):
    flat = dot(rows_out[...], place[...], (1, 1)).astype(BF16)
    rows_out[:, 0:512] = flat
    for slot in range(out.shape[0]):
        start = pl.multiple_of(slots[slot] * C, 16)
        out[slot] = rows_out[pl.ds(start, C), 0:512]


def side_kernel(
    slots, hidden, rects, cot_grid, lowered, grad_c, live, place, up_w, out, up_g, coarse_g,
    rows_out, grad_own,
):
    number = out.shape[0]
    coarse_tiles = lowered.shape[0]
    up_g[...] = jnp.zeros_like(up_g)
    coarse_g[...] = jnp.zeros_like(coarse_g)

    def block_step(block):
        alive = jnp.broadcast_to(live[pl.ds(block + 1, 1), :], (C, LANES))
        spreads = []
        pairs = []
        start = pl.multiple_of(block * C, 16)
        for inner in range(4):
            coarse = 4 * (block + 1) + inner
            spread = spread_sub(rects[coarse])
            spreads.append(spread)
            pairs.append(
                jnp.concatenate([cot_grid[2 * coarse], cot_grid[2 * coarse + 1]], axis=0)
            )
            upward = dot(up_w[...], spread)
            for half in range(2):
                value = hidden[2 * coarse + half] + upward[half * C : (half + 1) * C]
                at = LANES * (2 * inner + half)
                rows_out[pl.ds(start, C), at : at + LANES] = (value * alive).astype(BF16)
        up_g[...] += dot(
            jnp.concatenate(pairs, axis=1), jnp.concatenate(spreads, axis=1), (1, 1)
        )

    loop(0, number, block_step)
    to_blocks(slots, rows_out, place, out)
    zero = jnp.zeros((C, LANES), BF16)
    for coarse in (2, 3, coarse_tiles - 4, coarse_tiles - 3):
        grad_own[coarse] = zero

    def copy_step(coarse):
        grad_own[coarse] = grad_c[coarse]

    loop(4, coarse_tiles - 4, copy_step, 4)
    low, high = z_masks(32)

    def weight_step(index):
        lefts = []
        rights = []
        for inner in range(2):
            coarse = 3 + 2 * index + inner
            lefts.append(
                jnp.concatenate(
                    [grad_own[coarse + 1], grad_own[coarse], grad_own[coarse - 1]], axis=0
                )
            )
            rights.append(columns(lowered[coarse], low, high, 32, 2))
        coarse_g[...] += dot(
            jnp.concatenate(lefts, axis=1), jnp.concatenate(rights, axis=1), (1, 1)
        )

    loop(0, (coarse_tiles - 6) // 2, weight_step)


def backward_kernel(
    grad_c, from_left, from_right, hidden, cot_grid, live, coarse_w, down_w,
    grad_h, grad_d, pack_low, pack_high, coarse_p,
):
    coarse_tiles = grad_c.shape[0]
    ids = lane_ids(C)
    even = (ids // 16) % 2 == 0
    at_left = even & (ids % 16 == 2)
    at_right = even & (ids % 16 == 12)
    zero = jnp.zeros((C, LANES), BF16)
    low, high = z_masks(32)
    for index in range((coarse_tiles - 4) // 2):
        cols = []
        for coarse in (2 + 2 * index, 3 + 2 * index):
            group, place = coarse // 32, coarse % 32
            tile = jnp.where(at_left, roll(from_left[group], 2 - place), grad_c[coarse])
            tile = jnp.where(at_right, roll(from_right[group], 12 - place), tile)
            cols.append(columns(tile, low, high, 32, 2))
        out = dot(coarse_w[...], jnp.concatenate(cols, axis=1))
        coarse_p[2 + 2 * index] = out[:, :LANES]
        coarse_p[3 + 2 * index] = out[:, LANES:]
    own_anchors = anchor_mask(True)
    across = lane_ids(C) % 16
    inside = ((across >= 4) & (across < 12)).astype(F32)

    def step(coarse):
        alive = jnp.broadcast_to(live[pl.ds(coarse // 4, 1), :], (C, LANES)) * inside
        value = (
            coarse_p[coarse - 1, 0:C] + coarse_p[coarse, C : 2 * C] + coarse_p[coarse + 1, 2 * C :]
        )
        down = (value * (alive * own_anchors)).astype(BF16)
        grad_d[coarse] = down
        acts = dot(down_w[...], spread_sub(down), (0, 0))
        for half in range(2):
            tile = 2 * coarse + half
            slope = silu_parts(hidden[tile])[1]
            grad = cot_grid[tile].astype(F32) + acts[half * C : (half + 1) * C] * slope
            grad_h[tile] = (grad * alive).astype(BF16)

    loop(3, coarse_tiles - 3, step, 2)
    tiles = grad_h.shape[0]
    for out, lane in ((pack_low, 4), (pack_high, 11)):
        for group in range(out.shape[0]):
            total = zero
            for tile in range(max(6, 16 * group), min(tiles - 6, 16 * group + 16)):
                picked = jnp.where(ids % 16 == lane, grad_h[tile], zero)
                total = total + roll(picked, tile % 16 - lane)
            out[group] = total


def weight_kernel(grid, grad_h, grad_d, hidden, fine_g, down_g, grad_own):
    tiles = grid.shape[0]
    coarse_tiles = grad_d.shape[0]
    fine_g[...] = jnp.zeros_like(fine_g)
    down_g[...] = jnp.zeros_like(down_g)
    zero = jnp.zeros((C, LANES), BF16)
    for tile in (5, 6, 7, tiles - 8, tiles - 7, tiles - 6):
        grad_own[tile] = zero

    def copy_step(tile):
        grad_own[tile] = grad_h[tile]

    loop(8, tiles - 8, copy_step, 8)
    low, high = z_masks(16)

    def fine_step(index):
        lefts = []
        rights = []
        for inner in range(4):
            tile = 6 + 4 * index + inner
            lefts.append(
                jnp.concatenate([grad_own[tile + 1], grad_own[tile], grad_own[tile - 1]], axis=0)
            )
            rights.append(columns(grid[tile], low, high, 16, 1))
        fine_g[...] += dot(
            jnp.concatenate(lefts, axis=1), jnp.concatenate(rights, axis=1), (1, 1)
        )

    loop(0, (tiles - 12) // 4, fine_step)

    def down_step(index):
        lefts = []
        rights = []
        for inner in range(4):
            coarse = 4 + 4 * index + inner
            lefts.append(spread_sub(grad_d[coarse]))
            rights.append(
                jnp.concatenate(
                    [
                        silu_parts(hidden[2 * coarse])[0].astype(BF16),
                        silu_parts(hidden[2 * coarse + 1])[0].astype(BF16),
                    ],
                    axis=0,
                )
            )
        down_g[...] += dot(
            jnp.concatenate(lefts, axis=1), jnp.concatenate(rights, axis=1), (1, 1)
        )

    loop(0, (coarse_tiles - 8) // 4, down_step)


def input_kernel(slots, grad_h, from_left, from_right, live, place, fine_w, out, fine_p, rows_out):
    tiles = grad_h.shape[0]
    number = out.shape[0]
    ids = lane_ids(C)
    at_left = ids % 16 == 3
    at_right = ids % 16 == 12
    low, high = z_masks(16)

    def group_step(group):
        packed_left = from_left[group]
        packed_right = from_right[group]
        for pair in range(8):
            cols = []
            for inner in (2 * pair, 2 * pair + 1):
                tile = grad_h[16 * group + inner]
                tile = jnp.where(at_left, roll(packed_left, 3 - inner), tile)
                tile = jnp.where(at_right, roll(packed_right, 12 - inner), tile)
                cols.append(columns(tile, low, high, 16, 1))
            res = dot(fine_w[...], jnp.concatenate(cols, axis=1))
            fine_p[16 * group + 2 * pair] = res[:, :LANES]
            fine_p[16 * group + 2 * pair + 1] = res[:, LANES:]

    loop(0, tiles // 16, group_step)

    def block_step(block):
        alive = jnp.broadcast_to(live[pl.ds(block + 1, 1), :], (C, LANES))
        start = pl.multiple_of(block * C, 16)
        for inner in range(EDGE):
            tile = EDGE * (block + 1) + inner
            value = fine_p[tile - 1, 0:C] + fine_p[tile, C : 2 * C] + fine_p[tile + 1, 2 * C :]
            rows_out[pl.ds(start, C), LANES * inner : LANES * (inner + 1)] = (
                value * alive
            ).astype(BF16)

    loop(0, number, block_step)
    to_blocks(slots, rows_out, place, out)


def call(kernel, inputs, outs, scratch=(), scalars=0, flops=0):
    vmem = pl.BlockSpec(memory_space=pltpu.VMEM)
    smem = pl.BlockSpec(memory_space=pltpu.SMEM)
    moved = sum(math.prod(s) * jnp.dtype(d).itemsize for s, d in outs)
    moved += sum(math.prod(a.shape) * a.dtype.itemsize for a in inputs)
    return pl.pallas_call(
        kernel,
        out_shape=tuple(jax.ShapeDtypeStruct(s, d) for s, d in outs),
        in_specs=[smem] * scalars + [vmem] * (len(inputs) - scalars),
        out_specs=tuple(vmem for _ in outs),
        scratch_shapes=[pltpu.VMEM(s, d) for s, d in scratch],
        compiler_params=pltpu.CompilerParams(vmem_limit_bytes=VMEM_LIMIT),
        cost_estimate=pl.CostEstimate(flops=flops, bytes_accessed=moved, transcendentals=0),
        name=kernel.__name__,
    )(*inputs)


def send(array, step_x, step_y):
    number_x, number_y = lax.axis_size("gx"), lax.axis_size("gy")
    pairs = []
    for i in range(number_x):
        for j in range(number_y):
            to_x, to_y = i + step_x, j + step_y
            if 0 <= to_x < number_x and 0 <= to_y < number_y:
                pairs.append((i * number_y + j, to_x * number_y + to_y))
    return lax.ppermute(array, ("gx", "gy"), pairs)


def reduce_all(parts):
    axes = ("gx", "gy")
    devices = lax.axis_size("gx") * lax.axis_size("gy")
    sizes = [part.shape[0] for part in parts]
    rows = sum(sizes)
    share = -(-rows // (16 * devices)) * 16
    joined = jnp.concatenate(parts, axis=0).astype(BF16)
    joined = jnp.pad(joined, ((0, share * devices - rows), (0, 0)))
    mine = lax.all_to_all(joined.reshape(devices, share, LANES), axes, 0, 0)
    mine = jnp.sum(mine.astype(F32), axis=0).astype(BF16)
    full = lax.all_gather(mine, axes, axis=0, tiled=True)
    outs = []
    at = 0
    for size in sizes:
        outs.append(full[at : at + size].astype(F32))
        at += size
    return outs


def lane_split(array):
    rows, width = array.shape
    padded = -(-width // LANES) * LANES
    array = jnp.pad(array, ((0, 0), (0, padded - width)))
    return array.reshape(rows, padded // LANES, LANES).transpose(1, 0, 2).reshape(-1, LANES)


def lane_join(flat, rows, width):
    parts = flat.shape[0] // rows
    array = flat.reshape(parts, rows, LANES).transpose(1, 0, 2).reshape(rows, parts * LANES)
    return array[:, :width]


def on_device(
    features, block_slots, block_count, cotangent, fine_weight, down_weight, coarse_weight,
    up_weight,
):
    number = features.shape[2]
    slots = block_slots.reshape(number)
    count = block_count.reshape(1)
    feats = features.reshape(number, C, VOX)
    cots = cotangent.reshape(number, C, VOX)
    place = jnp.asarray(placing_matrix(), BF16)
    place_own = jnp.asarray(placing_matrix()[:512], BF16)
    pick = jnp.asarray(edge_matrix(), BF16)
    tiles = EDGE * (number + 2)
    coarse_tiles = tiles // 2
    groups = -(-coarse_tiles // 32)
    fine_groups = tiles // 16

    fine_5 = fine_weight.reshape(C, 3, 3, 3, C)
    coarse_5 = coarse_weight.reshape(C, 3, 3, 3, C)
    fine_fore = fine_5.transpose(3, 0, 2, 1, 4).reshape(3 * C, 9 * C)
    fine_back = fine_5[:, ::-1, ::-1, ::-1].transpose(3, 4, 2, 1, 0).reshape(3 * C, 9 * C)
    coarse_fore = coarse_5.transpose(3, 0, 2, 1, 4).reshape(3 * C, 9 * C)
    coarse_back = coarse_5[:, ::-1, ::-1, ::-1].transpose(3, 4, 2, 1, 0).reshape(3 * C, 9 * C)
    down_w = down_weight.reshape(C, 2, 2, 2, C).transpose(1, 2, 0, 3, 4).reshape(4 * C, 2 * C)
    up_w = up_weight.reshape(2, 2, 2, C, C).transpose(2, 3, 0, 1, 4).reshape(2 * C, 4 * C)

    own, cot, x_low, x_high, y_low, y_high, d_ll, d_lh, d_hl, d_hh = call(
        prepare_kernel,
        (slots, count, feats, cots, pick),
        [((number + 1, C, VOX), BF16), ((number, C, VOX), BF16)]
        + [((number + 1, C, 256), BF16)] * 2
        + [((3, C, VOX), BF16)] * 2
        + [((2, C, 256), BF16)] * 4,
        scalars=2,
    )
    x_left = send(x_high, 1, 0)
    x_right = send(x_low, -1, 0)
    y_left = send(y_high, 0, 1)
    y_right = send(y_low, 0, -1)
    c_ll = send(d_hh, 1, 1)
    c_lr = send(d_hl, 1, -1)
    c_rl = send(d_lh, -1, 1)
    c_rr = send(d_ll, -1, -1)
    grid, cot_grid, hidden, lowered, rects, grad_c, live, pack_low, pack_high = call(
        forward_kernel,
        (own, cot, x_left, x_right, y_left, y_right, c_ll, c_lr, c_rl, c_rr, place, fine_fore,
         down_w, coarse_fore, up_w),
        [
            ((tiles, C, LANES), BF16),
            ((tiles, C, LANES), BF16),
            ((tiles, C, LANES), F32),
            ((coarse_tiles, C, LANES), BF16),
            ((coarse_tiles, C, LANES), BF16),
            ((coarse_tiles, C, LANES), BF16),
            ((C, LANES), F32),
            ((groups, C, LANES), BF16),
            ((groups, C, LANES), BF16),
        ],
        [
            (((number + 3) * C, 1024), BF16),
            (((number + 2) * C, VOX), BF16),
            ((tiles, 3 * C, LANES), F32),
            ((coarse_tiles, 3 * C, LANES), F32),
        ],
        flops=3 * 10**9,
    )
    grad_left = send(pack_high, 1, 0)
    grad_right = send(pack_low, -1, 0)
    output, up_part, coarse_part = call(
        side_kernel,
        (slots, hidden, rects, cot_grid, lowered, grad_c, live, place_own, up_w),
        [((number, C, VOX), BF16), ((2 * C, 4 * C), F32), ((3 * C, 9 * C), F32)],
        [((number * C, 1024), BF16), ((coarse_tiles, C, LANES), BF16)],
        scalars=1,
        flops=10**9,
    )
    grad_h, grad_d, edge_low, edge_high = call(
        backward_kernel,
        (grad_c, grad_left, grad_right, hidden, cot_grid, live, coarse_back, down_w),
        [
            ((tiles, C, LANES), BF16),
            ((coarse_tiles, C, LANES), BF16),
            ((fine_groups, C, LANES), BF16),
            ((fine_groups, C, LANES), BF16),
        ],
        [((coarse_tiles, 3 * C, LANES), F32)],
        flops=10**9,
    )
    edge_left = send(edge_high, 1, 0)
    edge_right = send(edge_low, -1, 0)
    fine_part, down_part = call(
        weight_kernel,
        (grid, grad_h, grad_d, hidden),
        [((3 * C, 9 * C), F32), ((4 * C, 2 * C), F32)],
        [((tiles, C, LANES), BF16)],
        flops=3 * 10**9,
    )
    (input_grad,) = call(
        input_kernel,
        (slots, grad_h, edge_left, edge_right, live, place_own, fine_back),
        [((number, C, VOX), BF16)],
        [((tiles, 3 * C, LANES), F32), ((number * C, 1024), BF16)],
        scalars=1,
        flops=3 * 10**9,
    )
    fine_sum, down_sum, coarse_sum, up_sum = reduce_all(
        [lane_split(part) for part in (fine_part, down_part, coarse_part, up_part)]
    )
    scale = 1.0 / math.sqrt(number * VOX * lax.axis_size("gx") * lax.axis_size("gy"))
    fine_total = lane_join(fine_sum, 3 * C, 9 * C).reshape(3, C, 3, 3, C) * scale
    coarse_total = lane_join(coarse_sum, 3 * C, 9 * C).reshape(3, C, 3, 3, C) * scale
    down_total = lane_join(down_sum, 4 * C, 2 * C).reshape(2, 2, C, 2, C) * scale
    up_total = lane_join(up_sum, 2 * C, 4 * C).reshape(2, C, 2, 2, C) * scale
    shape_out = (1, 1, number, C, VOX)
    return (
        output.reshape(shape_out),
        input_grad.reshape(shape_out),
        fine_total.transpose(1, 3, 2, 0, 4).reshape(C, 27, C),
        down_total.transpose(2, 0, 1, 3, 4).reshape(C, 8, C),
        coarse_total.transpose(1, 3, 2, 0, 4).reshape(C, 27, C),
        up_total.transpose(2, 3, 0, 1, 4).reshape(8, C, C),
    )


def solution(mesh):
    split = P("gx", "gy", None, None, None)
    return jax.shard_map(
        on_device,
        mesh=mesh,
        in_specs=(split, P("gx", "gy", None), P("gx", "gy"), split, P(), P(), P(), P()),
        out_specs=(split, split, P(), P(), P(), P()),
        check_vma=False,
    )
```

```python
import math

import jax
import jax.numpy as jnp
import numpy as np
from jax import lax
from jax.experimental import pallas as pl
from jax.experimental.pallas import tpu as pltpu
from jax.sharding import PartitionSpec as P

C = 48
EDGE = 8
VOX = 512
LANES = 128
F32 = jnp.float32
BF16 = jnp.bfloat16
VMEM_LIMIT = 58 * 1024 * 1024
SHIFTS = (0, 1, 16, 17)


def placing_matrix():
    place = np.zeros((1024, 8 * LANES), np.float32)
    for z in range(8):
        for y in range(8):
            for x in range(8):
                place[64 * z + 8 * x + y, LANES * y + 16 * z + x + 4] = 1.0
            for x in range(4):
                place[512 + 32 * z + 8 * x + y, LANES * y + 16 * z + x] = 1.0
                place[768 + 32 * z + 8 * x + y, LANES * y + 16 * z + x + 12] = 1.0
    return place


def edge_matrix():
    pick = np.zeros((512, 512), np.float32)
    for z in range(8):
        for y in range(8):
            for x in range(8):
                pick[64 * z + 8 * x + y, 256 * (x // 4) + 32 * z + 8 * (x % 4) + y] = 1.0
    return pick


def dot(left, right, contract=(1, 0)):
    dims = (((contract[0],), (contract[1],)), ((), ()))
    return lax.dot_general(left, right, dims, preferred_element_type=F32)


def roll(value, shift):
    return pltpu.roll(value, shift % LANES, 1)


def lane_ids(rows):
    return lax.broadcasted_iota(jnp.int32, (rows, LANES), 1)


def silu_parts(value):
    sigma = 1.0 / (1.0 + jnp.exp(-value))
    return value * sigma, sigma * (1.0 + value * (1.0 - sigma))


def columns(tile, low, high, z_step, x_step):
    zero = jnp.zeros_like(tile)
    below = jnp.where(low, zero, roll(tile, z_step))
    above = jnp.where(high, zero, roll(tile, -z_step))
    base = jnp.concatenate([below, tile, above], axis=0)
    return jnp.concatenate([roll(base, x_step), base, roll(base, -x_step)], axis=0)


def z_masks(z_step):
    ids = lane_ids(C)
    return ids < z_step, ids >= LANES - z_step


def gather_sub(parts):
    total = parts[:C]
    for index in range(1, 4):
        total = total + roll(parts[index * C : (index + 1) * C], -SHIFTS[index])
    return total


def spread_sub(anchored):
    return jnp.concatenate([anchored] + [roll(anchored, step) for step in SHIFTS[1:]], axis=0)


def anchor_mask(own):
    ids = lane_ids(C)
    across = ids % 16
    keep = ((ids // 16) % 2 == 0) & (across % 2 == 0)
    if own:
        keep = keep & (across >= 4) & (across < 12)
    return keep.astype(F32)


def loop(low, high, body, unroll=1):
    def step(index, carry):
        body(index)
        return carry

    lax.fori_loop(low, high, step, 0, unroll=unroll)


def prepare_kernel(slots, count, feats, cots, pick, own, cot, x_low, x_high, y_low, y_high):
    number = feats.shape[0]
    rows = lax.broadcasted_iota(jnp.int32, (C, VOX), 0)
    flags = jnp.zeros((C, VOX), F32)
    first = jnp.zeros((), F32)
    last = jnp.zeros((), F32)
    zero = jnp.zeros((C, VOX), BF16)
    for slot in range(number):
        live = slot < count[0]
        alive = jnp.where(live, 1.0, 0.0)
        place = slots[slot]
        own[place] = jnp.where(live, feats[slot], zero)
        cot[place] = jnp.where(live, cots[slot], zero)
        flags = jnp.where(rows == place + 1, alive, flags)
        first = first + jnp.where(place == 0, alive, 0.0)
        last = last + jnp.where(place == number - 1, alive, 0.0)
    own[number] = flags.astype(BF16)
    first_flag = jnp.where(rows == number + 1, first, 0.0).astype(BF16)
    last_flag = jnp.where(rows == 0, last, 0.0).astype(BF16)
    packed = dot(own[...].reshape((number + 1) * C, VOX), pick[...]).astype(BF16)
    packed = packed.reshape(number + 1, C, VOX)
    x_low[...] = packed[:, :, :256]
    x_high[...] = packed[:, :, 256:]
    for out, index, flag in ((y_low, 0, first_flag), (y_high, number - 1, last_flag)):
        out[0] = own[index]
        out[1] = cot[index]
        out[2] = flag


def corner_kernel(y_left, y_right, own, pick, low, high, flags):
    extra = y_left[2] + y_right[2]
    rows = jnp.concatenate([y_left[0], y_right[0], extra], axis=0)
    packed = dot(rows, pick[...]).astype(BF16).reshape(3, C, VOX)
    low[...] = packed[:, :, :256]
    high[...] = packed[:, :, 256:]
    flags[...] = own[0] + extra


def place_kernel(
    own, cot, y_left, y_right, flags, place, up_w, grid, cot_grid, grad_r, live, rows_in, rows_cot
):
    number = cot.shape[0]
    last = number + 1
    for block in range(number):
        at = (block + 1) * C
        rows_in[at : at + C, :] = own[block]
        rows_cot[at : at + C, :] = cot[block]
    for at, middle in ((0, y_left), (last * C, y_right)):
        rows_in[at : at + C, :] = middle[0]
        rows_cot[at : at + C, :] = middle[1]
    rows_in[(last + 1) * C :, :] = flags[...]
    for pair in range(4):
        lanes = slice(256 * pair, 256 * pair + 256)
        placed_cot = dot(rows_cot[...], place[:, lanes])
        placed = dot(rows_in[...], place[:, lanes])
        for half in range(2):
            span = slice(LANES * half, LANES * (half + 1))
            for block in range(last + 1):
                tile = EDGE * block + 2 * pair + half
                grid[tile] = placed[block * C : (block + 1) * C, span].astype(BF16)
                cot_grid[tile] = placed_cot[block * C : (block + 1) * C, span].astype(BF16)
        if pair == 0:
            live[...] = placed[(last + 1) * C :, 0:LANES]

    def rect_step(block):
        pairs = []
        for inner in range(4):
            tile = EDGE * block + 2 * inner
            pairs.append(jnp.concatenate([cot_grid[tile], cot_grid[tile + 1]], axis=0))
        parts = dot(up_w[...], jnp.concatenate(pairs, axis=1), (0, 0))
        for inner in range(4):
            grad_r[4 * block + inner] = gather_sub(parts[:, LANES * inner : LANES * (inner + 1)])

    loop(0, number + 2, rect_step, 2)


def conv_sum(parts, tile):
    return parts[tile, 0:C] + parts[tile + 1, C : 2 * C] + parts[tile + 2, 2 * C :]


def conv_steps(parts, weight, load, tiles, z_step, x_step, unroll):
    low, high = z_masks(z_step)
    spare = jnp.zeros((3 * C, LANES), F32)
    parts[0] = spare
    parts[tiles + 1] = spare

    def step(index):
        tile = 4 * index
        for pair in range(2):
            at = tile + 2 * pair
            cols = [columns(load(at + i), low, high, z_step, x_step) for i in range(2)]
            out = dot(weight[...], jnp.concatenate(cols, axis=1))
            parts[at + 1] = out[:, :LANES]
            parts[at + 2] = out[:, LANES:]

    loop(0, tiles // 4, step, unroll)


def forward_kernel(
    grid_own, live_own, grad_r, x_left, x_right, c_left, c_right, place, fine_w, down_w, coarse_w,
    grid, hidden, lowered, rects, grad_c, live, pack_low, pack_high,
    rows_in, fine_p, coarse_p,
):
    number = x_left.shape[0] - 1
    last = number + 1
    for block in range(number):
        at = (block + 1) * C
        rows_in[at : at + C, 0:256] = x_left[block]
        rows_in[at : at + C, 256:512] = x_right[block]
    for at, index in ((0, 0), (last * C, 1)):
        rows_in[at : at + C, 0:256] = c_left[index]
        rows_in[at : at + C, 256:512] = c_right[index]
    at = (last + 1) * C
    rows_in[at : at + C, 0:256] = x_left[number] + c_left[2]
    rows_in[at : at + C, 256:512] = x_right[number] + c_right[2]
    for pair in range(4):
        lanes = slice(256 * pair, 256 * pair + 256)
        placed = dot(rows_in[...], place[:, lanes])
        for half in range(2):
            span = slice(LANES * half, LANES * (half + 1))
            for block in range(last + 1):
                tile = EDGE * block + 2 * pair + half
                halo = placed[block * C : (block + 1) * C, span].astype(BF16)
                grid[tile] = grid_own[tile] + halo
        if pair == 0:
            live[...] = live_own[...] + placed[(last + 1) * C :, 0:LANES]
    tiles = grid.shape[0]
    coarse_tiles = lowered.shape[0]
    conv_steps(fine_p, fine_w, lambda tile: grid[tile], tiles, 16, 1, 2)
    anchors = anchor_mask(False)

    def lower_step(block):
        alive = jnp.broadcast_to(live[pl.ds(block, 1), :], (C, LANES))
        keep = alive * anchors
        pairs = []
        for inner in range(4):
            actives = []
            for half in range(2):
                tile = EDGE * block + 2 * inner + half
                value = conv_sum(fine_p, tile) * alive
                hidden[tile] = value
                actives.append(silu_parts(value)[0].astype(BF16))
            pairs.append(jnp.concatenate(actives, axis=0))
        parts = dot(down_w[...], jnp.concatenate(pairs, axis=1))
        for inner in range(4):
            total = gather_sub(parts[:, LANES * inner : LANES * (inner + 1)])
            lowered[4 * block + inner] = (total * keep).astype(BF16)

    loop(0, last + 1, lower_step, 2)
    conv_steps(coarse_p, coarse_w, lambda tile: lowered[tile], coarse_tiles, 32, 2, 2)
    own_anchors = anchor_mask(True)

    def grad_step(block):
        alive = jnp.broadcast_to(live[pl.ds(block, 1), :], (C, LANES))
        keep = alive * own_anchors
        for inner in range(4):
            coarse = 4 * block + inner
            smooth, slope = silu_parts(conv_sum(coarse_p, coarse))
            rects[coarse] = (smooth * own_anchors).astype(BF16)
            grad_c[coarse] = (grad_r[coarse] * slope * keep).astype(BF16)

    loop(0, last + 1, grad_step, 2)
    ids = lane_ids(C)
    zero = jnp.zeros((C, LANES), BF16)
    for out, lane in ((pack_low, 4), (pack_high, 10)):
        for group in range(out.shape[0]):
            total = zero
            for coarse in range(max(2, 32 * group), min(coarse_tiles - 2, 32 * group + 32)):
                picked = jnp.where(ids % 32 == lane, grad_c[coarse], zero)
                total = total + roll(picked, coarse % 32 - lane)
            out[group] = total


def to_blocks(slots, rows_out, place, out):
    flat = dot(rows_out[...], place[...], (1, 1)).astype(BF16)
    rows_out[:, 0:512] = flat
    for slot in range(out.shape[0]):
        start = pl.multiple_of(slots[slot] * C, 16)
        out[slot] = rows_out[pl.ds(start, C), 0:512]


def stacks(own, tiles):
    parts = [jnp.concatenate([own[t + 1], own[t], own[t - 1]], axis=0) for t in tiles]
    return jnp.concatenate(parts, axis=1)


def flatten_weights(total, out, at):
    turned = total[...].T.astype(BF16)
    for group in range(4):
        out[at + 3 * C * group : at + 3 * C * (group + 1), :] = turned[
            :, LANES * group : LANES * (group + 1)
        ]


def side_kernel(
    slots, hidden, rects, cot_grid, lowered, grad_c, live, place, up_w, out, flat,
    rows_out, grad_own, up_g, coarse_g,
):
    number = out.shape[0]
    coarse_tiles = lowered.shape[0]
    up_g[...] = jnp.zeros_like(up_g)
    coarse_g[...] = jnp.zeros_like(coarse_g)

    def block_step(block):
        alive = jnp.broadcast_to(live[pl.ds(block + 1, 1), :], (C, LANES))
        start = pl.multiple_of(block * C, 16)
        spreads = []
        pairs = []
        for inner in range(4):
            coarse = 4 * (block + 1) + inner
            spreads.append(spread_sub(rects[coarse]))
            pairs.append(
                jnp.concatenate([cot_grid[2 * coarse], cot_grid[2 * coarse + 1]], axis=0)
            )
        spread = jnp.concatenate(spreads, axis=1)
        upward = dot(up_w[...], spread)
        for inner in range(4):
            for half in range(2):
                part = upward[half * C : (half + 1) * C, LANES * inner : LANES * (inner + 1)]
                value = hidden[EDGE * (block + 1) + 2 * inner + half] + part
                at = LANES * (2 * inner + half)
                rows_out[pl.ds(start, C), at : at + LANES] = (value * alive).astype(BF16)
        up_g[:, 0 : 2 * C] += dot(spread, jnp.concatenate(pairs, axis=1), (1, 1))

    loop(0, number, block_step, 2)
    to_blocks(slots, rows_out, place, out)
    zero = jnp.zeros((C, LANES), BF16)
    for coarse in (1, 2, 3, coarse_tiles - 4, coarse_tiles - 3, coarse_tiles - 2):
        grad_own[coarse] = zero

    def copy_step(coarse):
        grad_own[coarse] = grad_c[coarse]

    loop(4, coarse_tiles - 4, copy_step, 8)
    low, high = z_masks(32)

    def weight_step(index):
        tiles = [2 + 4 * index + inner for inner in range(4)]
        rights = [columns(lowered[tile], low, high, 32, 2) for tile in tiles]
        coarse_g[0 : 9 * C, :] += dot(
            jnp.concatenate(rights, axis=1), stacks(grad_own, tiles), (1, 1)
        )

    loop(0, (coarse_tiles - 4) // 4, weight_step)
    flatten_weights(coarse_g, flat, 0)
    flat[12 * C :, :] = up_g[...].astype(BF16)


def backward_kernel(
    grad_c, from_left, from_right, hidden, cot_grid, live, coarse_w, down_w,
    grad_h, grad_d, pack_low, pack_high, coarse_p, grad_x,
):
    coarse_tiles = grad_c.shape[0]
    ids = lane_ids(C)
    even = (ids // 16) % 2 == 0
    at_left = even & (ids % 16 == 2)
    at_right = even & (ids % 16 == 12)
    zero = jnp.zeros((C, LANES), BF16)
    for coarse in range(coarse_tiles):
        group, place = coarse // 32, coarse % 32
        tile = jnp.where(at_left, roll(from_left[group], 2 - place), grad_c[coarse])
        grad_x[coarse] = jnp.where(at_right, roll(from_right[group], 12 - place), tile)
    conv_steps(coarse_p, coarse_w, lambda tile: grad_x[tile], coarse_tiles, 32, 2, 2)
    own_anchors = anchor_mask(True)
    across = lane_ids(C) % 16
    inside = ((across >= 4) & (across < 12)).astype(F32)

    def step(block):
        alive = jnp.broadcast_to(live[pl.ds(block, 1), :], (C, LANES)) * inside
        keep = alive * own_anchors
        spreads = []
        for inner in range(4):
            coarse = 4 * block + inner
            down = (conv_sum(coarse_p, coarse) * keep).astype(BF16)
            grad_d[coarse] = down
            spreads.append(spread_sub(down))
        acts = dot(down_w[...], jnp.concatenate(spreads, axis=1), (0, 0))
        for inner in range(4):
            for half in range(2):
                tile = EDGE * block + 2 * inner + half
                slope = silu_parts(hidden[tile])[1]
                part = acts[half * C : (half + 1) * C, LANES * inner : LANES * (inner + 1)]
                grad = cot_grid[tile].astype(F32) + part * slope
                grad_h[tile] = (grad * alive).astype(BF16)

    loop(0, coarse_tiles // 4, step, 2)
    for out, lane in ((pack_low, 4), (pack_high, 11)):
        def pack_step(group):
            total = zero
            for inner in range(16):
                picked = jnp.where(ids % 16 == lane, grad_h[16 * group + inner], zero)
                total = total + roll(picked, inner - lane)
            out[group] = total

        loop(0, out.shape[0], pack_step)


def weight_kernel(grid, grad_h, grad_d, hidden, early, joined, grad_own, fine_g, down_g):
    tiles = grid.shape[0]
    coarse_tiles = grad_d.shape[0]
    fine_g[...] = jnp.zeros_like(fine_g)
    down_g[...] = jnp.zeros_like(down_g)
    zero = jnp.zeros((C, LANES), BF16)
    for step in range(3, 8):
        grad_own[step] = zero
        grad_own[tiles - 1 - step] = zero

    def copy_step(tile):
        grad_own[tile] = grad_h[tile]

    loop(8, tiles - 8, copy_step, 8)
    low, high = z_masks(16)

    def fine_step(index):
        at = [4 + 8 * index + inner for inner in range(8)]
        rights = [columns(grid[tile], low, high, 16, 1) for tile in at]
        fine_g[0 : 9 * C, :] += dot(
            jnp.concatenate(rights, axis=1), stacks(grad_own, at), (1, 1)
        )

    loop(0, (tiles - 8) // 8, fine_step)

    def down_step(index):
        lefts = []
        rights = []
        for inner in range(4):
            coarse = 4 + 4 * index + inner
            lefts.append(spread_sub(grad_d[coarse]))
            actives = [silu_parts(hidden[2 * coarse + half])[0].astype(BF16) for half in range(2)]
            rights.append(jnp.concatenate(actives, axis=0))
        down_g[:, 0 : 2 * C] += dot(
            jnp.concatenate(lefts, axis=1), jnp.concatenate(rights, axis=1), (1, 1)
        )

    loop(0, (coarse_tiles - 8) // 4, down_step, 2)
    flatten_weights(fine_g, joined, 0)
    joined[12 * C : 16 * C, :] = down_g[...].astype(BF16)
    joined[16 * C :, :] = early[...]


def input_kernel(
    slots, grad_h, from_left, from_right, live, place, fine_w, out, fine_p, rows_out, grad_x
):
    tiles = grad_h.shape[0]
    number = out.shape[0]
    ids = lane_ids(C)
    at_left = ids % 16 == 3
    at_right = ids % 16 == 12

    def fill_step(group):
        packed_left = from_left[group]
        packed_right = from_right[group]
        for inner in range(16):
            tile = jnp.where(at_left, roll(packed_left, 3 - inner), grad_h[16 * group + inner])
            tile = jnp.where(at_right, roll(packed_right, 12 - inner), tile)
            grad_x[16 * group + inner] = tile

    loop(0, tiles // 16, fill_step)
    conv_steps(fine_p, fine_w, lambda tile: grad_x[tile], tiles, 16, 1, 2)

    def block_step(block):
        alive = jnp.broadcast_to(live[pl.ds(block + 1, 1), :], (C, LANES))
        start = pl.multiple_of(block * C, 16)
        for inner in range(EDGE):
            value = conv_sum(fine_p, EDGE * (block + 1) + inner)
            rows_out[pl.ds(start, C), LANES * inner : LANES * (inner + 1)] = (
                value * alive
            ).astype(BF16)

    loop(0, number, block_step, 2)
    to_blocks(slots, rows_out, place, out)


def call(kernel, inputs, outs, scratch=(), scalars=0, flops=0):
    vmem = pl.BlockSpec(memory_space=pltpu.VMEM)
    smem = pl.BlockSpec(memory_space=pltpu.SMEM)
    moved = sum(math.prod(s) * jnp.dtype(d).itemsize for s, d in outs)
    moved += sum(math.prod(a.shape) * a.dtype.itemsize for a in inputs)
    return pl.pallas_call(
        kernel,
        out_shape=tuple(jax.ShapeDtypeStruct(s, d) for s, d in outs),
        in_specs=[smem] * scalars + [vmem] * (len(inputs) - scalars),
        out_specs=tuple(vmem for _ in outs),
        scratch_shapes=[pltpu.VMEM(s, d) for s, d in scratch],
        compiler_params=pltpu.CompilerParams(vmem_limit_bytes=VMEM_LIMIT),
        cost_estimate=pl.CostEstimate(flops=flops, bytes_accessed=moved, transcendentals=0),
        name=kernel.__name__,
    )(*inputs)


def send(array, step_x, step_y):
    number_x, number_y = lax.axis_size("gx"), lax.axis_size("gy")
    pairs = []
    for i in range(number_x):
        for j in range(number_y):
            to_x, to_y = i + step_x, j + step_y
            if 0 <= to_x < number_x and 0 <= to_y < number_y:
                pairs.append((i * number_y + j, to_x * number_y + to_y))
    return lax.ppermute(array, ("gx", "gy"), pairs)


def reduce_all(joined):
    axes = ("gx", "gy")
    devices = lax.axis_size("gx") * lax.axis_size("gy")
    rows = joined.shape[0]
    share = -(-rows // devices)
    joined = jnp.pad(joined, ((0, share * devices - rows), (0, 0)))
    mine = lax.all_to_all(joined.reshape(devices, share, LANES), axes, 0, 0)
    mine = jnp.sum(mine.astype(F32), axis=0).astype(BF16)
    spread = jnp.broadcast_to(mine[None], (devices, share, LANES))
    full = lax.all_to_all(spread, axes, 0, 0)
    return full.reshape(devices * share, LANES)[:rows]


def lane_join(flat, rows, width):
    parts = flat.shape[0] // rows
    array = flat.reshape(parts, rows, LANES).transpose(1, 0, 2).reshape(rows, parts * LANES)
    return array[:, :width]


def on_device(
    features, block_slots, block_count, cotangent, fine_weight, down_weight, coarse_weight,
    up_weight,
):
    number = features.shape[2]
    slots = block_slots.reshape(number)
    count = block_count.reshape(1)
    feats = features.reshape(number, C, VOX)
    cots = cotangent.reshape(number, C, VOX)
    place_own = jnp.asarray(placing_matrix()[:512], BF16)
    place_halo = jnp.asarray(placing_matrix()[512:], BF16)
    pick = jnp.asarray(edge_matrix(), BF16)
    tiles = EDGE * (number + 2)
    coarse_tiles = tiles // 2
    groups = -(-coarse_tiles // 32)
    fine_groups = tiles // 16

    fine_5 = fine_weight.reshape(C, 3, 3, 3, C)
    coarse_5 = coarse_weight.reshape(C, 3, 3, 3, C)
    fine_fore = fine_5.transpose(3, 0, 2, 1, 4).reshape(3 * C, 9 * C)
    fine_back = fine_5[:, ::-1, ::-1, ::-1].transpose(3, 4, 2, 1, 0).reshape(3 * C, 9 * C)
    coarse_fore = coarse_5.transpose(3, 0, 2, 1, 4).reshape(3 * C, 9 * C)
    coarse_back = coarse_5[:, ::-1, ::-1, ::-1].transpose(3, 4, 2, 1, 0).reshape(3 * C, 9 * C)
    down_w = down_weight.reshape(C, 2, 2, 2, C).transpose(1, 2, 0, 3, 4).reshape(4 * C, 2 * C)
    up_w = up_weight.reshape(2, 2, 2, C, C).transpose(2, 3, 0, 1, 4).reshape(2 * C, 4 * C)

    own, cot, x_low, x_high, y_low, y_high = call(
        prepare_kernel,
        (slots, count, feats, cots, pick),
        [((number + 1, C, VOX), BF16), ((number, C, VOX), BF16)]
        + [((number + 1, C, 256), BF16)] * 2
        + [((3, C, VOX), BF16)] * 2,
        scalars=2,
    )
    x_left = send(x_high, 1, 0)
    x_right = send(x_low, -1, 0)
    y_left = send(y_high, 0, 1)
    y_right = send(y_low, 0, -1)
    corner_low, corner_high, flags = call(
        corner_kernel,
        (y_left, y_right, own[number:], pick),
        [((3, C, 256), BF16), ((3, C, 256), BF16), ((C, VOX), BF16)],
    )
    c_left = send(corner_high, 1, 0)
    c_right = send(corner_low, -1, 0)
    grid_own, cot_grid, grad_r, live_own = call(
        place_kernel,
        (own, cot, y_left, y_right, flags, place_own, up_w),
        [
            ((tiles, C, LANES), BF16),
            ((tiles, C, LANES), BF16),
            ((coarse_tiles, C, LANES), F32),
            ((C, LANES), F32),
        ],
        [(((number + 3) * C, VOX), BF16), (((number + 2) * C, VOX), BF16)],
        flops=8 * 10**9,
    )
    fine_fore, fine_back, coarse_fore, coarse_back, down_w, grid_own = lax.optimization_barrier(
        (fine_fore, fine_back, coarse_fore, coarse_back, down_w, grid_own)
    )
    grid, hidden, lowered, rects, grad_c, live, pack_low, pack_high = call(
        forward_kernel,
        (grid_own, live_own, grad_r, x_left, x_right, c_left, c_right, place_halo, fine_fore,
         down_w, coarse_fore),
        [
            ((tiles, C, LANES), BF16),
            ((tiles, C, LANES), F32),
            ((coarse_tiles, C, LANES), BF16),
            ((coarse_tiles, C, LANES), BF16),
            ((coarse_tiles, C, LANES), BF16),
            ((C, LANES), F32),
            ((groups, C, LANES), BF16),
            ((groups, C, LANES), BF16),
        ],
        [
            (((number + 3) * C, VOX), BF16),
            ((tiles + 2, 3 * C, LANES), F32),
            ((coarse_tiles + 2, 3 * C, LANES), F32),
        ],
        flops=8 * 10**9,
    )
    grad_left = send(pack_high, 1, 0)
    grad_right = send(pack_low, -1, 0)
    output, early = call(
        side_kernel,
        (slots, hidden, rects, cot_grid, lowered, grad_c, live, place_own, up_w),
        [((number, C, VOX), BF16), ((16 * C, LANES), BF16)],
        [
            ((number * C, 1024), BF16),
            ((coarse_tiles, C, LANES), BF16),
            ((4 * C, LANES), F32),
            ((VOX, 3 * C), F32),
        ],
        scalars=1,
        flops=8 * 10**9,
    )
    grad_h, grad_d, edge_low, edge_high = call(
        backward_kernel,
        (grad_c, grad_left, grad_right, hidden, cot_grid, live, coarse_back, down_w),
        [
            ((tiles, C, LANES), BF16),
            ((coarse_tiles, C, LANES), BF16),
            ((fine_groups, C, LANES), BF16),
            ((fine_groups, C, LANES), BF16),
        ],
        [((coarse_tiles + 2, 3 * C, LANES), F32), ((coarse_tiles, C, LANES), BF16)],
        flops=8 * 10**9,
    )
    edge_left = send(edge_high, 1, 0)
    edge_right = send(edge_low, -1, 0)
    (joined,) = call(
        weight_kernel,
        (grid, grad_h, grad_d, hidden, early),
        [((32 * C, LANES), BF16)],
        [((tiles, C, LANES), BF16), ((VOX, 3 * C), F32), ((4 * C, LANES), F32)],
        flops=12 * 10**9,
    )
    joined, edge_left, edge_right = lax.optimization_barrier((joined, edge_left, edge_right))
    total = reduce_all(joined)
    (input_grad,) = call(
        input_kernel,
        (slots, grad_h, edge_left, edge_right, live, place_own, fine_back),
        [((number, C, VOX), BF16)],
        [
            ((tiles + 2, 3 * C, LANES), F32),
            ((number * C, 1024), BF16),
            ((tiles, C, LANES), BF16),
        ],
        scalars=1,
        flops=8 * 10**9,
    )
    total = total.astype(F32)
    fine_sum, down_sum = total[: 12 * C], total[12 * C : 16 * C]
    coarse_sum, up_sum = total[16 * C : 28 * C], total[28 * C :]
    scale = 1.0 / math.sqrt(number * VOX * lax.axis_size("gx") * lax.axis_size("gy"))
    fine_total = lane_join(fine_sum, 3 * C, 9 * C).reshape(3, C, 3, 3, C) * scale
    coarse_total = lane_join(coarse_sum, 3 * C, 9 * C).reshape(3, C, 3, 3, C) * scale
    down_total = down_sum[:, : 2 * C].reshape(2, 2, C, 2, C) * scale
    up_total = up_sum[:, : 2 * C].reshape(2, 2, C, 2, C) * scale
    shape_out = (1, 1, number, C, VOX)
    return (
        output.reshape(shape_out),
        input_grad.reshape(shape_out),
        fine_total.transpose(1, 3, 2, 0, 4).reshape(C, 27, C),
        down_total.transpose(2, 0, 1, 3, 4).reshape(C, 8, C),
        coarse_total.transpose(1, 3, 2, 0, 4).reshape(C, 27, C),
        up_total.transpose(0, 1, 3, 4, 2).reshape(8, C, C),
    )


def solution(mesh):
    split = P("gx", "gy", None, None, None)
    return jax.shard_map(
        on_device,
        mesh=mesh,
        in_specs=(split, P("gx", "gy", None), P("gx", "gy"), split, P(), P(), P(), P()),
        out_specs=(split, split, P(), P(), P(), P()),
        check_vma=False,
    )
```

```python
import functools
import math

import jax
import jax.numpy as jnp
import numpy as np
from jax import lax
from jax.experimental import pallas as pl
from jax.experimental.pallas import tpu as pltpu
from jax.sharding import PartitionSpec as P

C = 48
EDGE = 8
VOX = 512
LANES = 128
F32 = jnp.float32
BF16 = jnp.bfloat16
SLACK = 8 * 1024 * 1024
SHIFTS = (0, 1, 16, 17)


def placing_matrix():
    place = np.zeros((1024, 8 * LANES), np.float32)
    for z in range(8):
        for y in range(8):
            for x in range(8):
                place[64 * z + 8 * x + y, LANES * y + 16 * z + x + 4] = 1.0
            for x in range(4):
                place[512 + 32 * z + 8 * x + y, LANES * y + 16 * z + x] = 1.0
                place[768 + 32 * z + 8 * x + y, LANES * y + 16 * z + x + 12] = 1.0
    return place


def edge_matrix():
    pick = np.zeros((512, 512), np.float32)
    for z in range(8):
        for y in range(8):
            for x in range(8):
                pick[64 * z + 8 * x + y, 256 * (x // 4) + 32 * z + 8 * (x % 4) + y] = 1.0
    return pick


def dot(left, right, contract=(1, 0)):
    dims = (((contract[0],), (contract[1],)), ((), ()))
    return lax.dot_general(left, right, dims, preferred_element_type=F32)


def roll(value, shift):
    return pltpu.roll(value, shift % LANES, 1)


def lane_ids(rows):
    return lax.broadcasted_iota(jnp.int32, (rows, LANES), 1)


def silu_parts(value):
    sigma = 1.0 / (1.0 + jnp.exp(-value))
    return value * sigma, sigma * (1.0 + value * (1.0 - sigma))


def columns(tile, low, high, z_step, x_step):
    zero = jnp.zeros_like(tile)
    below = jnp.where(low, zero, roll(tile, z_step))
    above = jnp.where(high, zero, roll(tile, -z_step))
    base = jnp.concatenate([below, tile, above], axis=0)
    return jnp.concatenate([roll(base, x_step), base, roll(base, -x_step)], axis=0)


def z_masks(z_step):
    ids = lane_ids(C)
    return ids < z_step, ids >= LANES - z_step


def gather_sub(parts):
    total = parts[:C]
    for index in range(1, 4):
        total = total + roll(parts[index * C : (index + 1) * C], -SHIFTS[index])
    return total


def spread_sub(anchored):
    return jnp.concatenate([anchored] + [roll(anchored, step) for step in SHIFTS[1:]], axis=0)


def anchor_mask(own):
    ids = lane_ids(C)
    across = ids % 16
    keep = ((ids // 16) % 2 == 0) & (across % 2 == 0)
    if own:
        keep = keep & (across >= 4) & (across < 12)
    return keep.astype(F32)


def loop(low, high, body, unroll=1):
    def step(index, carry):
        body(index)
        return carry

    lax.fori_loop(low, high, step, 0, unroll=unroll)


def prepare_kernel(
    slots, count, feats, cots, pick, own, cot, flag_rows, x_low, x_high, y_low, y_high, rows_in
):
    number = feats.shape[0]
    rows = lax.broadcasted_iota(jnp.int32, (C, VOX), 0)
    flags = jnp.zeros((C, VOX), F32)
    first = jnp.zeros((), F32)
    last = jnp.zeros((), F32)
    zero = jnp.zeros((C, VOX), BF16)
    for slot in range(number):
        live = slot < count[0]
        alive = jnp.where(live, 1.0, 0.0)
        place = slots[slot]
        block = jnp.where(live, feats[slot], zero)
        own[place] = block
        rows_in[pl.ds(pl.multiple_of(place * C, 16), C), :] = block
        cot[place] = jnp.where(live, cots[slot], zero)
        flags = jnp.where(rows == place + 1, alive, flags)
        first = first + jnp.where(place == 0, alive, 0.0)
        last = last + jnp.where(place == number - 1, alive, 0.0)
    flag_rows[...] = flags.astype(BF16)
    rows_in[number * C :, :] = flags.astype(BF16)
    first_flag = jnp.where(rows == number + 1, first, 0.0).astype(BF16)
    last_flag = jnp.where(rows == 0, last, 0.0).astype(BF16)
    packed = dot(rows_in[...], pick[...]).astype(BF16)
    packed = packed.reshape(number + 1, C, VOX)
    x_low[...] = packed[:, :, :256]
    x_high[...] = packed[:, :, 256:]
    for out, index, flag in ((y_low, 0, first_flag), (y_high, number - 1, last_flag)):
        out[0] = own[index]
        out[1] = cot[index]
        out[2] = flag


def corner_kernel(y_left, y_right, flag_rows, pick, low, high, flags):
    extra = y_left[2] + y_right[2]
    rows = jnp.concatenate([y_left[0], y_right[0], extra], axis=0)
    packed = dot(rows, pick[...]).astype(BF16).reshape(3, C, VOX)
    low[...] = packed[:, :, :256]
    high[...] = packed[:, :, 256:]
    flags[...] = flag_rows[...] + extra


def arrange_weights(fine, down, coarse, up, fine_w, fine_b, coarse_w, coarse_b, down_w, up_w):
    for source, fore, back in ((fine, fine_w, fine_b), (coarse, coarse_w, coarse_b)):
        for along in range(3):
            rows = slice(C * along, C * (along + 1))
            turned_rows = slice(C * (2 - along), C * (3 - along))
            ahead = []
            behind = []
            for across in range(3):
                for depth in range(3):
                    ahead.append(source[9 * depth + 3 * across + along])
                    behind.append(source[9 * (2 - depth) + 3 * (2 - across) + along].T)
            fore[rows, :] = jnp.concatenate(ahead, axis=1)
            back[turned_rows, :] = jnp.concatenate(behind, axis=1)
    for index in range(4):
        pair = [down[2 * index], down[2 * index + 1]]
        down_w[C * index : C * (index + 1), :] = jnp.concatenate(pair, axis=1)
    for along in range(2):
        row = jnp.concatenate([up[2 * index + along] for index in range(4)], axis=1)
        up_w[C * along : C * (along + 1), :] = row


def place_kernel(
    own, cot, y_left, y_right, flags, place, fine, down, coarse, up,
    grid, cot_grid, grad_r, live, fine_w, fine_b, coarse_w, coarse_b, down_w, up_w,
    rows_in, rows_cot,
):
    arrange_weights(fine, down, coarse, up, fine_w, fine_b, coarse_w, coarse_b, down_w, up_w)
    number = cot.shape[0]
    last = number + 1
    for block in range(number):
        at = (block + 1) * C
        rows_in[at : at + C, :] = own[block]
        rows_cot[at : at + C, :] = cot[block]
    for at, middle in ((0, y_left), (last * C, y_right)):
        rows_in[at : at + C, :] = middle[0]
        rows_cot[at : at + C, :] = middle[1]
    rows_in[(last + 1) * C :, :] = flags[...]
    for pair in range(4):
        lanes = slice(256 * pair, 256 * pair + 256)
        placed_cot = dot(rows_cot[...], place[:, lanes])
        placed = dot(rows_in[...], place[:, lanes])
        for half in range(2):
            span = slice(LANES * half, LANES * (half + 1))
            for block in range(last + 1):
                tile = EDGE * block + 2 * pair + half
                grid[tile] = placed[block * C : (block + 1) * C, span].astype(BF16)
                cot_grid[tile] = placed_cot[block * C : (block + 1) * C, span].astype(BF16)
        if pair == 0:
            live[...] = placed[(last + 1) * C :, 0:LANES]

    def rect_step(block):
        pairs = []
        for inner in range(4):
            tile = EDGE * block + 2 * inner
            pairs.append(jnp.concatenate([cot_grid[tile], cot_grid[tile + 1]], axis=0))
        parts = dot(up_w[...], jnp.concatenate(pairs, axis=1), (0, 0))
        for inner in range(4):
            grad_r[4 * block + inner] = gather_sub(parts[:, LANES * inner : LANES * (inner + 1)])

    loop(0, number + 2, rect_step, 2)


def conv_sum(parts, tile):
    return parts[tile, 0:C] + parts[tile + 1, C : 2 * C] + parts[tile + 2, 2 * C :]


def conv_steps(parts, weight, load, tiles, z_step, x_step, unroll):
    low, high = z_masks(z_step)
    spare = jnp.zeros((3 * C, LANES), F32)
    parts[0] = spare
    parts[tiles + 1] = spare

    def step(index):
        tile = 4 * index
        for pair in range(2):
            at = tile + 2 * pair
            cols = [columns(load(at + i), low, high, z_step, x_step) for i in range(2)]
            out = dot(weight[...], jnp.concatenate(cols, axis=1))
            parts[at + 1] = out[:, :LANES]
            parts[at + 2] = out[:, LANES:]

    loop(0, tiles // 4, step, unroll)


def forward_kernel(
    grid_own, live_own, grad_r, x_left, x_right, c_left, c_right, place, fine_w, down_w, coarse_w,
    grid, hidden, lowered, rects, grad_c, live, pack_low, pack_high,
    rows_in, fine_p, coarse_p,
):
    number = x_left.shape[0] - 1
    last = number + 1
    for block in range(number):
        at = (block + 1) * C
        rows_in[at : at + C, 0:256] = x_left[block]
        rows_in[at : at + C, 256:512] = x_right[block]
    for at, index in ((0, 0), (last * C, 1)):
        rows_in[at : at + C, 0:256] = c_left[index]
        rows_in[at : at + C, 256:512] = c_right[index]
    at = (last + 1) * C
    rows_in[at : at + C, 0:256] = x_left[number] + c_left[2]
    rows_in[at : at + C, 256:512] = x_right[number] + c_right[2]
    for pair in range(4):
        lanes = slice(256 * pair, 256 * pair + 256)
        placed = dot(rows_in[...], place[:, lanes])
        for half in range(2):
            span = slice(LANES * half, LANES * (half + 1))
            for block in range(last + 1):
                tile = EDGE * block + 2 * pair + half
                halo = placed[block * C : (block + 1) * C, span].astype(BF16)
                grid[tile] = grid_own[tile] + halo
        if pair == 0:
            live[...] = live_own[...] + placed[(last + 1) * C :, 0:LANES]
    tiles = grid.shape[0]
    coarse_tiles = lowered.shape[0]
    conv_steps(fine_p, fine_w, lambda tile: grid[tile], tiles, 16, 1, 2)
    anchors = anchor_mask(False)

    def lower_step(block):
        alive = jnp.broadcast_to(live[pl.ds(block, 1), :], (C, LANES))
        keep = alive * anchors
        pairs = []
        for inner in range(4):
            actives = []
            for half in range(2):
                tile = EDGE * block + 2 * inner + half
                value = conv_sum(fine_p, tile) * alive
                hidden[tile] = value
                actives.append(silu_parts(value)[0].astype(BF16))
            pairs.append(jnp.concatenate(actives, axis=0))
        parts = dot(down_w[...], jnp.concatenate(pairs, axis=1))
        for inner in range(4):
            total = gather_sub(parts[:, LANES * inner : LANES * (inner + 1)])
            lowered[4 * block + inner] = (total * keep).astype(BF16)

    loop(0, last + 1, lower_step, 2)
    conv_steps(coarse_p, coarse_w, lambda tile: lowered[tile], coarse_tiles, 32, 2, 2)
    own_anchors = anchor_mask(True)

    def grad_step(block):
        alive = jnp.broadcast_to(live[pl.ds(block, 1), :], (C, LANES))
        keep = alive * own_anchors
        for inner in range(4):
            coarse = 4 * block + inner
            smooth, slope = silu_parts(conv_sum(coarse_p, coarse))
            rects[coarse] = (smooth * own_anchors).astype(BF16)
            grad_c[coarse] = (grad_r[coarse] * slope * keep).astype(BF16)

    loop(0, last + 1, grad_step, 2)
    ids = lane_ids(C)
    zero = jnp.zeros((C, LANES), BF16)
    for out, lane in ((pack_low, 4), (pack_high, 10)):
        for group in range(out.shape[0]):
            total = zero
            for coarse in range(max(2, 32 * group), min(coarse_tiles - 2, 32 * group + 32)):
                picked = jnp.where(ids % 32 == lane, grad_c[coarse], zero)
                total = total + roll(picked, coarse % 32 - lane)
            out[group] = total


def to_blocks(slots, rows_out, place, out):
    flat = dot(rows_out[...], place[...]).astype(BF16)
    rows_out[:, 0:512] = flat
    for slot in range(out.shape[0]):
        start = pl.multiple_of(slots[slot] * C, 16)
        out[slot] = rows_out[pl.ds(start, C), 0:512]


def stacks(own, tiles):
    parts = [jnp.concatenate([own[t + 1], own[t], own[t - 1]], axis=0) for t in tiles]
    return jnp.concatenate(parts, axis=1)


def flatten_weights(total, out, at):
    turned = total[...].T.astype(BF16)
    for group in range(4):
        out[at + 3 * C * group : at + 3 * C * (group + 1), :] = turned[
            :, LANES * group : LANES * (group + 1)
        ]


def side_kernel(
    slots, hidden, rects, cot_grid, lowered, grad_c, live, place, up_w, out, flat,
    rows_out, grad_own, up_g, coarse_g,
):
    number = out.shape[0]
    coarse_tiles = lowered.shape[0]
    up_g[...] = jnp.zeros_like(up_g)
    coarse_g[...] = jnp.zeros_like(coarse_g)

    def block_step(block):
        alive = jnp.broadcast_to(live[pl.ds(block + 1, 1), :], (C, LANES))
        start = pl.multiple_of(block * C, 16)
        spreads = []
        pairs = []
        for inner in range(4):
            coarse = 4 * (block + 1) + inner
            spreads.append(spread_sub(rects[coarse]))
            pairs.append(
                jnp.concatenate([cot_grid[2 * coarse], cot_grid[2 * coarse + 1]], axis=0)
            )
        spread = jnp.concatenate(spreads, axis=1)
        upward = dot(up_w[...], spread)
        for inner in range(4):
            for half in range(2):
                part = upward[half * C : (half + 1) * C, LANES * inner : LANES * (inner + 1)]
                value = hidden[EDGE * (block + 1) + 2 * inner + half] + part
                at = LANES * (2 * inner + half)
                rows_out[pl.ds(start, C), at : at + LANES] = (value * alive).astype(BF16)
        up_g[:, 0 : 2 * C] += dot(spread, jnp.concatenate(pairs, axis=1), (1, 1))

    loop(0, number, block_step, 2)
    to_blocks(slots, rows_out, place, out)
    zero = jnp.zeros((C, LANES), BF16)
    for coarse in (1, 2, 3, coarse_tiles - 4, coarse_tiles - 3, coarse_tiles - 2):
        grad_own[coarse] = zero

    def copy_step(coarse):
        grad_own[coarse] = grad_c[coarse]

    loop(4, coarse_tiles - 4, copy_step, 8)
    low, high = z_masks(32)

    def weight_step(index):
        tiles = [2 + 4 * index + inner for inner in range(4)]
        rights = [columns(lowered[tile], low, high, 32, 2) for tile in tiles]
        coarse_g[0 : 9 * C, :] += dot(
            jnp.concatenate(rights, axis=1), stacks(grad_own, tiles), (1, 1)
        )

    loop(0, (coarse_tiles - 4) // 4, weight_step)
    flatten_weights(coarse_g, flat, 0)
    flat[12 * C :, :] = up_g[...].astype(BF16)


def backward_kernel(
    grad_c, from_left, from_right, hidden, cot_grid, live, coarse_w, down_w,
    grad_h, grad_d, pack_low, pack_high, coarse_p, grad_x,
):
    coarse_tiles = grad_c.shape[0]
    ids = lane_ids(C)
    even = (ids // 16) % 2 == 0
    at_left = even & (ids % 16 == 2)
    at_right = even & (ids % 16 == 12)
    zero = jnp.zeros((C, LANES), BF16)
    for coarse in range(coarse_tiles):
        group, place = coarse // 32, coarse % 32
        tile = jnp.where(at_left, roll(from_left[group], 2 - place), grad_c[coarse])
        grad_x[coarse] = jnp.where(at_right, roll(from_right[group], 12 - place), tile)
    conv_steps(coarse_p, coarse_w, lambda tile: grad_x[tile], coarse_tiles, 32, 2, 2)
    own_anchors = anchor_mask(True)
    across = lane_ids(C) % 16
    inside = ((across >= 4) & (across < 12)).astype(F32)

    def step(block):
        alive = jnp.broadcast_to(live[pl.ds(block, 1), :], (C, LANES)) * inside
        keep = alive * own_anchors
        spreads = []
        for inner in range(4):
            coarse = 4 * block + inner
            down = (conv_sum(coarse_p, coarse) * keep).astype(BF16)
            grad_d[coarse] = down
            spreads.append(spread_sub(down))
        acts = dot(down_w[...], jnp.concatenate(spreads, axis=1), (0, 0))
        for inner in range(4):
            for half in range(2):
                tile = EDGE * block + 2 * inner + half
                slope = silu_parts(hidden[tile])[1]
                part = acts[half * C : (half + 1) * C, LANES * inner : LANES * (inner + 1)]
                grad = cot_grid[tile].astype(F32) + part * slope
                grad_h[tile] = (grad * alive).astype(BF16)

    loop(0, coarse_tiles // 4, step, 2)
    for out, lane in ((pack_low, 4), (pack_high, 11)):
        def pack_step(group):
            total = zero
            for inner in range(16):
                picked = jnp.where(ids % 16 == lane, grad_h[16 * group + inner], zero)
                total = total + roll(picked, inner - lane)
            out[group] = total

        loop(0, out.shape[0], pack_step)


def weight_kernel(grid, grad_h, grad_d, hidden, early, joined, grad_own, fine_g, down_g):
    tiles = grid.shape[0]
    coarse_tiles = grad_d.shape[0]
    fine_g[...] = jnp.zeros_like(fine_g)
    down_g[...] = jnp.zeros_like(down_g)
    zero = jnp.zeros((C, LANES), BF16)
    for step in range(3, 8):
        grad_own[step] = zero
        grad_own[tiles - 1 - step] = zero

    def copy_step(tile):
        grad_own[tile] = grad_h[tile]

    loop(8, tiles - 8, copy_step, 8)
    low, high = z_masks(16)

    def fine_step(index):
        at = [4 + 8 * index + inner for inner in range(8)]
        rights = [columns(grid[tile], low, high, 16, 1) for tile in at]
        fine_g[0 : 9 * C, :] += dot(
            jnp.concatenate(rights, axis=1), stacks(grad_own, at), (1, 1)
        )

    loop(0, (tiles - 8) // 8, fine_step)

    def down_step(index):
        lefts = []
        rights = []
        for inner in range(4):
            coarse = 4 + 4 * index + inner
            lefts.append(spread_sub(grad_d[coarse]))
            actives = [silu_parts(hidden[2 * coarse + half])[0].astype(BF16) for half in range(2)]
            rights.append(jnp.concatenate(actives, axis=0))
        down_g[:, 0 : 2 * C] += dot(
            jnp.concatenate(lefts, axis=1), jnp.concatenate(rights, axis=1), (1, 1)
        )

    loop(0, (coarse_tiles - 8) // 4, down_step, 2)
    flatten_weights(fine_g, joined, 0)
    joined[12 * C : 16 * C, :] = down_g[...].astype(BF16)
    joined[16 * C :, :] = early[...]


def input_kernel(
    slots, grad_h, from_left, from_right, live, place, fine_w, out, fine_p, rows_out, grad_x
):
    tiles = grad_h.shape[0]
    number = out.shape[0]
    ids = lane_ids(C)
    at_left = ids % 16 == 3
    at_right = ids % 16 == 12

    def fill_step(group):
        packed_left = from_left[group]
        packed_right = from_right[group]
        for inner in range(16):
            tile = jnp.where(at_left, roll(packed_left, 3 - inner), grad_h[16 * group + inner])
            tile = jnp.where(at_right, roll(packed_right, 12 - inner), tile)
            grad_x[16 * group + inner] = tile

    loop(0, tiles // 16, fill_step)
    conv_steps(fine_p, fine_w, lambda tile: grad_x[tile], tiles, 16, 1, 2)

    def block_step(block):
        alive = jnp.broadcast_to(live[pl.ds(block + 1, 1), :], (C, LANES))
        start = pl.multiple_of(block * C, 16)
        for inner in range(EDGE):
            value = conv_sum(fine_p, EDGE * (block + 1) + inner)
            rows_out[pl.ds(start, C), LANES * inner : LANES * (inner + 1)] = (
                value * alive
            ).astype(BF16)

    loop(0, number, block_step, 2)
    to_blocks(slots, rows_out, place, out)


def finish_kernel(scale, total, fine, down, coarse, up):
    for out, at in ((fine, 0), (coarse, 16 * C)):
        for along in range(3):
            first = at + C * along
            rows = [total[first + 3 * C * g : first + 3 * C * g + C, :] for g in range(4)]
            row = jnp.concatenate(rows, axis=1).astype(F32) * scale
            for index in range(9):
                out[9 * (index % 3) + 3 * (index // 3) + along] = row[:, C * index : C * (index + 1)]
    for out, at, turn in ((down, 12 * C, False), (up, 28 * C, True)):
        for index in range(4):
            rows = total[at + C * index : at + C * (index + 1), :].astype(F32) * scale
            for along in range(2):
                part = rows[:, C * along : C * (along + 1)]
                out[2 * index + along] = part.T if turn else part


def call(kernel, inputs, outs, scratch=(), scalars=0, flops=0):
    vmem = pl.BlockSpec(memory_space=pltpu.VMEM)
    smem = pl.BlockSpec(memory_space=pltpu.SMEM)
    held = SLACK
    for shape, kind in [(a.shape, a.dtype) for a in inputs[scalars:]] + list(outs) + list(scratch):
        rows, lanes = -(-shape[-2] // 16) * 16, -(-shape[-1] // LANES) * LANES
        held += math.prod(shape[:-2]) * rows * lanes * jnp.dtype(kind).itemsize
    moved = sum(math.prod(s) * jnp.dtype(d).itemsize for s, d in outs)
    moved += sum(math.prod(a.shape) * a.dtype.itemsize for a in inputs)
    return pl.pallas_call(
        kernel,
        out_shape=tuple(jax.ShapeDtypeStruct(s, d) for s, d in outs),
        in_specs=[smem] * scalars + [vmem] * (len(inputs) - scalars),
        out_specs=tuple(vmem for _ in outs),
        scratch_shapes=[pltpu.VMEM(s, d) for s, d in scratch],
        compiler_params=pltpu.CompilerParams(vmem_limit_bytes=held),
        cost_estimate=pl.CostEstimate(flops=flops, bytes_accessed=moved, transcendentals=0),
        name=getattr(kernel, "func", kernel).__name__,
    )(*inputs)


def send(array, step_x, step_y):
    number_x, number_y = lax.axis_size("gx"), lax.axis_size("gy")
    pairs = []
    for i in range(number_x):
        for j in range(number_y):
            to_x, to_y = i + step_x, j + step_y
            if 0 <= to_x < number_x and 0 <= to_y < number_y:
                pairs.append((i * number_y + j, to_x * number_y + to_y))
    return lax.ppermute(array, ("gx", "gy"), pairs)


def reduce_all(joined):
    axes = ("gx", "gy")
    devices = lax.axis_size("gx") * lax.axis_size("gy")
    rows = joined.shape[0]
    share = -(-rows // devices)
    joined = jnp.pad(joined, ((0, share * devices - rows), (0, 0)))
    mine = lax.all_to_all(joined.reshape(devices, share, LANES), axes, 0, 0)
    mine = jnp.sum(mine.astype(F32), axis=0).astype(BF16)
    spread = jnp.broadcast_to(mine[None], (devices, share, LANES))
    full = lax.all_to_all(spread, axes, 0, 0)
    return full.reshape(devices * share, LANES)[:rows]


def on_device(
    features, block_slots, block_count, cotangent, fine_weight, down_weight, coarse_weight,
    up_weight,
):
    number = features.shape[2]
    slots = block_slots.reshape(number)
    count = block_count.reshape(1)
    feats = features.reshape(number, C, VOX)
    cots = cotangent.reshape(number, C, VOX)
    place_own = jnp.asarray(placing_matrix()[:512], BF16)
    place_halo = jnp.asarray(placing_matrix()[512:], BF16)
    place_back = jnp.asarray(placing_matrix()[:512].T, BF16)
    pick = jnp.asarray(edge_matrix(), BF16)
    tiles = EDGE * (number + 2)
    coarse_tiles = tiles // 2
    groups = -(-coarse_tiles // 32)
    fine_groups = tiles // 16

    fine_3, down_3, coarse_3 = (
        weight.transpose(1, 0, 2) for weight in (fine_weight, down_weight, coarse_weight)
    )
    own, cot, flag_rows, x_low, x_high, y_low, y_high = call(
        prepare_kernel,
        (slots, count, feats, cots, pick),
        [((number, C, VOX), BF16)] * 2
        + [((C, VOX), BF16)]
        + [((number + 1, C, 256), BF16)] * 2
        + [((3, C, VOX), BF16)] * 2,
        [(((number + 1) * C, VOX), BF16)],
        scalars=2,
    )
    x_left = send(x_high, 1, 0)
    x_right = send(x_low, -1, 0)
    y_left = send(y_high, 0, 1)
    y_right = send(y_low, 0, -1)
    corner_low, corner_high, flags = call(
        corner_kernel,
        (y_left, y_right, flag_rows, pick),
        [((3, C, 256), BF16), ((3, C, 256), BF16), ((C, VOX), BF16)],
    )
    c_left = send(corner_high, 1, 0)
    c_right = send(corner_low, -1, 0)
    (grid_own, cot_grid, grad_r, live_own, fine_fore, fine_back, coarse_fore, coarse_back, down_w,
     up_w) = call(
        place_kernel,
        (own, cot, y_left, y_right, flags, place_own, fine_3, down_3, coarse_3, up_weight),
        [
            ((tiles, C, LANES), BF16),
            ((tiles, C, LANES), BF16),
            ((coarse_tiles, C, LANES), F32),
            ((C, LANES), F32),
        ]
        + [((3 * C, 9 * C), BF16)] * 4
        + [((4 * C, 2 * C), BF16), ((2 * C, 4 * C), BF16)],
        [(((number + 3) * C, VOX), BF16), (((number + 2) * C, VOX), BF16)],
        flops=8 * 10**9,
    )
    grid, hidden, lowered, rects, grad_c, live, pack_low, pack_high = call(
        forward_kernel,
        (grid_own, live_own, grad_r, x_left, x_right, c_left, c_right, place_halo, fine_fore,
         down_w, coarse_fore),
        [
            ((tiles, C, LANES), BF16),
            ((tiles, C, LANES), F32),
            ((coarse_tiles, C, LANES), BF16),
            ((coarse_tiles, C, LANES), BF16),
            ((coarse_tiles, C, LANES), BF16),
            ((C, LANES), F32),
            ((groups, C, LANES), BF16),
            ((groups, C, LANES), BF16),
        ],
        [
            (((number + 3) * C, VOX), BF16),
            ((tiles + 2, 3 * C, LANES), F32),
            ((coarse_tiles + 2, 3 * C, LANES), F32),
        ],
        flops=8 * 10**9,
    )
    grad_left = send(pack_high, 1, 0)
    grad_right = send(pack_low, -1, 0)
    output, early = call(
        side_kernel,
        (slots, hidden, rects, cot_grid, lowered, grad_c, live, place_back, up_w),
        [((number, C, VOX), BF16), ((16 * C, LANES), BF16)],
        [
            ((number * C, 1024), BF16),
            ((coarse_tiles, C, LANES), BF16),
            ((4 * C, LANES), F32),
            ((VOX, 3 * C), F32),
        ],
        scalars=1,
        flops=8 * 10**9,
    )
    grad_h, grad_d, edge_low, edge_high = call(
        backward_kernel,
        (grad_c, grad_left, grad_right, hidden, cot_grid, live, coarse_back, down_w),
        [
            ((tiles, C, LANES), BF16),
            ((coarse_tiles, C, LANES), BF16),
            ((fine_groups, C, LANES), BF16),
            ((fine_groups, C, LANES), BF16),
        ],
        [((coarse_tiles + 2, 3 * C, LANES), F32), ((coarse_tiles, C, LANES), BF16)],
        flops=8 * 10**9,
    )
    edge_left = send(edge_high, 1, 0)
    edge_right = send(edge_low, -1, 0)
    (joined,) = call(
        weight_kernel,
        (grid, grad_h, grad_d, hidden, early),
        [((32 * C, LANES), BF16)],
        [((tiles, C, LANES), BF16), ((VOX, 3 * C), F32), ((4 * C, LANES), F32)],
        flops=12 * 10**9,
    )
    joined, edge_left, edge_right = lax.optimization_barrier((joined, edge_left, edge_right))
    total = reduce_all(joined)
    (input_grad,) = call(
        input_kernel,
        (slots, grad_h, edge_left, edge_right, live, place_back, fine_back),
        [((number, C, VOX), BF16)],
        [
            ((tiles + 2, 3 * C, LANES), F32),
            ((number * C, 1024), BF16),
            ((tiles, C, LANES), BF16),
        ],
        scalars=1,
        flops=8 * 10**9,
    )
    scale = 1.0 / math.sqrt(number * VOX * lax.axis_size("gx") * lax.axis_size("gy"))
    fine_total, down_total, coarse_total, up_total = call(
        functools.partial(finish_kernel, scale),
        (total,),
        [((27, C, C), F32), ((8, C, C), F32), ((27, C, C), F32), ((8, C, C), F32)],
    )
    shape_out = (1, 1, number, C, VOX)
    return (
        output.reshape(shape_out),
        input_grad.reshape(shape_out),
        fine_total.transpose(1, 0, 2),
        down_total.transpose(1, 0, 2),
        coarse_total.transpose(1, 0, 2),
        up_total,
    )


def solution(mesh):
    split = P("gx", "gy", None, None, None)
    return jax.shard_map(
        on_device,
        mesh=mesh,
        in_specs=(split, P("gx", "gy", None), P("gx", "gy"), split, P(), P(), P(), P()),
        out_specs=(split, split, P(), P(), P(), P()),
        check_vma=False,
    )
```

```python
import functools
import math

import jax
import jax.numpy as jnp
import numpy as np
from jax import lax
from jax.experimental import pallas as pl
from jax.experimental.pallas import tpu as pltpu
from jax.sharding import PartitionSpec as P

C = 48
EDGE = 8
VOX = 512
LANES = 128
F32 = jnp.float32
BF16 = jnp.bfloat16
SLACK = 8 * 1024 * 1024
SHIFTS = (0, 1, 16, 17)


def placing_matrix():
    place = np.zeros((1024, 8 * LANES), np.float32)
    for z in range(8):
        for y in range(8):
            for x in range(8):
                place[64 * z + 8 * x + y, LANES * y + 16 * z + x + 4] = 1.0
            for x in range(4):
                place[512 + 32 * z + 8 * x + y, LANES * y + 16 * z + x] = 1.0
                place[768 + 32 * z + 8 * x + y, LANES * y + 16 * z + x + 12] = 1.0
    return place


def edge_matrix():
    pick = np.zeros((512, 512), np.float32)
    for z in range(8):
        for y in range(8):
            for x in range(8):
                pick[64 * z + 8 * x + y, 256 * (x // 4) + 32 * z + 8 * (x % 4) + y] = 1.0
    return pick


def dot(left, right, contract=(1, 0)):
    dims = (((contract[0],), (contract[1],)), ((), ()))
    return lax.dot_general(left, right, dims, preferred_element_type=F32)


def roll(value, shift):
    return pltpu.roll(value, shift % LANES, 1)


def lane_ids(rows):
    return lax.broadcasted_iota(jnp.int32, (rows, LANES), 1)


def silu_parts(value):
    sigma = 1.0 / (1.0 + jnp.exp(-value))
    return value * sigma, sigma * (1.0 + value * (1.0 - sigma))


def columns(tile, low, high, z_step, x_step):
    zero = jnp.zeros_like(tile)
    below = jnp.where(low, zero, roll(tile, z_step))
    above = jnp.where(high, zero, roll(tile, -z_step))
    base = jnp.concatenate([below, tile, above], axis=0)
    return jnp.concatenate([roll(base, x_step), base, roll(base, -x_step)], axis=0)


def z_masks(z_step):
    ids = lane_ids(C)
    return ids < z_step, ids >= LANES - z_step


def gather_sub(parts):
    total = parts[:C]
    for index in range(1, 4):
        total = total + roll(parts[index * C : (index + 1) * C], -SHIFTS[index])
    return total


def spread_sub(anchored):
    return jnp.concatenate([anchored] + [roll(anchored, step) for step in SHIFTS[1:]], axis=0)


def anchor_mask(own):
    ids = lane_ids(C)
    across = ids % 16
    keep = ((ids // 16) % 2 == 0) & (across % 2 == 0)
    if own:
        keep = keep & (across >= 4) & (across < 12)
    return keep.astype(F32)


def loop(low, high, body, unroll=1):
    def step(index, carry):
        body(index)
        return carry

    lax.fori_loop(low, high, step, 0, unroll=unroll)


def prepare_kernel(
    slots, count, pick, feats, cots, own, cot, flag_rows, x_low, x_high, y_low, y_high,
    rows_in, feat_sems, cot_sems,
):
    number = feats.shape[0]
    copies = []
    for source, target, sems in ((feats, own, feat_sems), (cots, cot, cot_sems)):
        group = []
        for slot in range(number):
            copy = pltpu.make_async_copy(source.at[slot], target.at[slots[slot]], sems.at[slot])
            copy.start()
            group.append(copy)
        copies.append(group)
    rows = lax.broadcasted_iota(jnp.int32, (C, VOX), 0)
    flags = jnp.zeros((C, VOX), F32)
    first = jnp.zeros((), F32)
    last = jnp.zeros((), F32)
    zero = jnp.zeros((C, VOX), BF16)
    for slot in range(number):
        alive = jnp.where(slot < count[0], 1.0, 0.0)
        place = slots[slot]
        flags = jnp.where(rows == place + 1, alive, flags)
        first = first + jnp.where(place == 0, alive, 0.0)
        last = last + jnp.where(place == number - 1, alive, 0.0)
    flag_rows[...] = flags.astype(BF16)
    rows_in[number * C :, :] = flags.astype(BF16)
    first_flag = jnp.where(rows == number + 1, first, 0.0).astype(BF16)
    last_flag = jnp.where(rows == 0, last, 0.0).astype(BF16)
    for target, group in ((own, copies[0]), (cot, copies[1])):
        for slot in range(number):
            group[slot].wait()
        for slot in range(number):

            @pl.when(slot >= count[0])
            def _():
                target[slots[slot]] = zero

    for block in range(number):
        rows_in[block * C : (block + 1) * C, :] = own[block]
    packed = dot(rows_in[...], pick[...]).astype(BF16)
    packed = packed.reshape(number + 1, C, VOX)
    x_low[...] = packed[:, :, :256]
    x_high[...] = packed[:, :, 256:]
    for out, index, flag in ((y_low, 0, first_flag), (y_high, number - 1, last_flag)):
        out[0] = own[index]
        out[1] = cot[index]
        out[2] = flag


def corner_kernel(y_left, y_right, flag_rows, pick, low, high, flags):
    extra = y_left[2] + y_right[2]
    rows = jnp.concatenate([y_left[0], y_right[0], extra], axis=0)
    packed = dot(rows, pick[...]).astype(BF16).reshape(3, C, VOX)
    low[...] = packed[:, :, :256]
    high[...] = packed[:, :, 256:]
    flags[...] = flag_rows[...] + extra


def arrange_weights(fine, down, coarse, up, fine_w, fine_b, coarse_w, coarse_b, down_w, up_w):
    for source, fore, back in ((fine, fine_w, fine_b), (coarse, coarse_w, coarse_b)):
        for along in range(3):
            rows = slice(C * along, C * (along + 1))
            turned_rows = slice(C * (2 - along), C * (3 - along))
            ahead = []
            behind = []
            for across in range(3):
                for depth in range(3):
                    ahead.append(source[9 * depth + 3 * across + along])
                    behind.append(source[9 * (2 - depth) + 3 * (2 - across) + along].T)
            fore[rows, :] = jnp.concatenate(ahead, axis=1)
            back[turned_rows, :] = jnp.concatenate(behind, axis=1)
    for index in range(4):
        pair = [down[2 * index], down[2 * index + 1]]
        down_w[C * index : C * (index + 1), :] = jnp.concatenate(pair, axis=1)
    for along in range(2):
        row = jnp.concatenate([up[2 * index + along] for index in range(4)], axis=1)
        up_w[C * along : C * (along + 1), :] = row


def place_kernel(
    own, cot, y_left, y_right, flags, place, fine, down, coarse, up,
    grid, cot_grid, grad_r, live, fine_w, fine_b, coarse_w, coarse_b, down_w, up_w,
    rows_in, rows_cot,
):
    arrange_weights(fine, down, coarse, up, fine_w, fine_b, coarse_w, coarse_b, down_w, up_w)
    number = cot.shape[0]
    last = number + 1
    for block in range(number):
        at = (block + 1) * C
        rows_in[at : at + C, :] = own[block]
        rows_cot[at : at + C, :] = cot[block]
    for at, middle in ((0, y_left), (last * C, y_right)):
        rows_in[at : at + C, :] = middle[0]
        rows_cot[at : at + C, :] = middle[1]
    rows_in[(last + 1) * C :, :] = flags[...]
    for pair in range(4):
        lanes = slice(256 * pair, 256 * pair + 256)
        placed_cot = dot(rows_cot[...], place[:, lanes])
        placed = dot(rows_in[...], place[:, lanes])
        for half in range(2):
            span = slice(LANES * half, LANES * (half + 1))
            for block in range(last + 1):
                tile = EDGE * block + 2 * pair + half
                grid[tile] = placed[block * C : (block + 1) * C, span].astype(BF16)
                cot_grid[tile] = placed_cot[block * C : (block + 1) * C, span].astype(BF16)
        if pair == 0:
            live[...] = placed[(last + 1) * C :, 0:LANES]

    def rect_step(block):
        pairs = []
        for inner in range(4):
            tile = EDGE * block + 2 * inner
            pairs.append(jnp.concatenate([cot_grid[tile], cot_grid[tile + 1]], axis=0))
        parts = dot(up_w[...], jnp.concatenate(pairs, axis=1), (0, 0))
        for inner in range(4):
            grad_r[4 * block + inner] = gather_sub(parts[:, LANES * inner : LANES * (inner + 1)])

    loop(0, number + 2, rect_step, 2)


def conv_sum(parts, tile):
    return parts[tile, 0:C] + parts[tile + 1, C : 2 * C] + parts[tile + 2, 2 * C :]


def conv_steps(parts, weight, load, tiles, z_step, x_step, unroll):
    low, high = z_masks(z_step)
    spare = jnp.zeros((3 * C, LANES), F32)
    parts[0] = spare
    parts[tiles + 1] = spare

    def step(index):
        tile = 4 * index
        for pair in range(2):
            at = tile + 2 * pair
            cols = [columns(load(at + i), low, high, z_step, x_step) for i in range(2)]
            out = dot(weight[...], jnp.concatenate(cols, axis=1))
            parts[at + 1] = out[:, :LANES]
            parts[at + 2] = out[:, LANES:]

    loop(0, tiles // 4, step, unroll)


def forward_kernel(
    grid_own, live_own, grad_r, x_left, x_right, c_left, c_right, place, fine_w, down_w, coarse_w,
    grid, hidden, lowered, rects, grad_c, live, pack_low, pack_high,
    rows_in, fine_p, coarse_p,
):
    number = x_left.shape[0] - 1
    last = number + 1
    for block in range(number):
        at = (block + 1) * C
        rows_in[at : at + C, 0:256] = x_left[block]
        rows_in[at : at + C, 256:512] = x_right[block]
    for at, index in ((0, 0), (last * C, 1)):
        rows_in[at : at + C, 0:256] = c_left[index]
        rows_in[at : at + C, 256:512] = c_right[index]
    at = (last + 1) * C
    rows_in[at : at + C, 0:256] = x_left[number] + c_left[2]
    rows_in[at : at + C, 256:512] = x_right[number] + c_right[2]
    for pair in range(4):
        lanes = slice(256 * pair, 256 * pair + 256)
        placed = dot(rows_in[...], place[:, lanes])
        for half in range(2):
            span = slice(LANES * half, LANES * (half + 1))
            for block in range(last + 1):
                tile = EDGE * block + 2 * pair + half
                halo = placed[block * C : (block + 1) * C, span].astype(BF16)
                grid[tile] = grid_own[tile] + halo
        if pair == 0:
            live[...] = live_own[...] + placed[(last + 1) * C :, 0:LANES]
    tiles = grid.shape[0]
    coarse_tiles = lowered.shape[0]
    conv_steps(fine_p, fine_w, lambda tile: grid[tile], tiles, 16, 1, 2)
    anchors = anchor_mask(False)

    def lower_step(block):
        alive = jnp.broadcast_to(live[pl.ds(block, 1), :], (C, LANES))
        keep = alive * anchors
        pairs = []
        for inner in range(4):
            actives = []
            for half in range(2):
                tile = EDGE * block + 2 * inner + half
                value = conv_sum(fine_p, tile) * alive
                hidden[tile] = value
                actives.append(silu_parts(value)[0].astype(BF16))
            pairs.append(jnp.concatenate(actives, axis=0))
        parts = dot(down_w[...], jnp.concatenate(pairs, axis=1))
        for inner in range(4):
            total = gather_sub(parts[:, LANES * inner : LANES * (inner + 1)])
            lowered[4 * block + inner] = (total * keep).astype(BF16)

    loop(0, last + 1, lower_step, 2)
    conv_steps(coarse_p, coarse_w, lambda tile: lowered[tile], coarse_tiles, 32, 2, 2)
    own_anchors = anchor_mask(True)

    def grad_step(block):
        alive = jnp.broadcast_to(live[pl.ds(block, 1), :], (C, LANES))
        keep = alive * own_anchors
        for inner in range(4):
            coarse = 4 * block + inner
            smooth, slope = silu_parts(conv_sum(coarse_p, coarse))
            rects[coarse] = (smooth * own_anchors).astype(BF16)
            grad_c[coarse] = (grad_r[coarse] * slope * keep).astype(BF16)

    loop(0, last + 1, grad_step, 2)
    ids = lane_ids(C)
    zero = jnp.zeros((C, LANES), BF16)
    for out, lane in ((pack_low, 4), (pack_high, 10)):
        for group in range(out.shape[0]):
            total = zero
            for coarse in range(max(2, 32 * group), min(coarse_tiles - 2, 32 * group + 32)):
                picked = jnp.where(ids % 32 == lane, grad_c[coarse], zero)
                total = total + roll(picked, coarse % 32 - lane)
            out[group] = total


def to_blocks(slots, rows_out, place, out):
    flat = dot(rows_out[...], place[...]).astype(BF16)
    rows_out[:, 0:512] = flat
    for slot in range(out.shape[0]):
        start = pl.multiple_of(slots[slot] * C, 16)
        out[slot] = rows_out[pl.ds(start, C), 0:512]


def stacks(own, tiles):
    parts = [jnp.concatenate([own[t + 1], own[t], own[t - 1]], axis=0) for t in tiles]
    return jnp.concatenate(parts, axis=1)


def flatten_weights(total, out, at):
    turned = total[...].T
    for group in range(4):
        out[at + 3 * C * group : at + 3 * C * (group + 1), :] = turned[
            :, LANES * group : LANES * (group + 1)
        ]


def side_kernel(
    slots, hidden, rects, cot_grid, lowered, grad_c, live, place, up_w, out, flat,
    rows_out, grad_own, up_g, coarse_g,
):
    number = out.shape[0]
    coarse_tiles = lowered.shape[0]
    up_g[...] = jnp.zeros_like(up_g)
    coarse_g[...] = jnp.zeros_like(coarse_g)

    def block_step(block):
        alive = jnp.broadcast_to(live[pl.ds(block + 1, 1), :], (C, LANES))
        start = pl.multiple_of(block * C, 16)
        spreads = []
        pairs = []
        for inner in range(4):
            coarse = 4 * (block + 1) + inner
            spreads.append(spread_sub(rects[coarse]))
            pairs.append(
                jnp.concatenate([cot_grid[2 * coarse], cot_grid[2 * coarse + 1]], axis=0)
            )
        spread = jnp.concatenate(spreads, axis=1)
        upward = dot(up_w[...], spread)
        for inner in range(4):
            for half in range(2):
                part = upward[half * C : (half + 1) * C, LANES * inner : LANES * (inner + 1)]
                value = hidden[EDGE * (block + 1) + 2 * inner + half] + part
                at = LANES * (2 * inner + half)
                rows_out[pl.ds(start, C), at : at + LANES] = (value * alive).astype(BF16)
        up_g[:, 0 : 2 * C] += dot(spread, jnp.concatenate(pairs, axis=1), (1, 1))

    loop(0, number, block_step, 2)
    to_blocks(slots, rows_out, place, out)
    zero = jnp.zeros((C, LANES), BF16)
    for coarse in (1, 2, 3, coarse_tiles - 4, coarse_tiles - 3, coarse_tiles - 2):
        grad_own[coarse] = zero

    def copy_step(coarse):
        grad_own[coarse] = grad_c[coarse]

    loop(4, coarse_tiles - 4, copy_step, 8)
    low, high = z_masks(32)

    def weight_step(index):
        tiles = [2 + 4 * index + inner for inner in range(4)]
        rights = [columns(lowered[tile], low, high, 32, 2) for tile in tiles]
        coarse_g[0 : 9 * C, :] += dot(
            jnp.concatenate(rights, axis=1), stacks(grad_own, tiles), (1, 1)
        )

    loop(0, (coarse_tiles - 4) // 4, weight_step)
    flatten_weights(coarse_g, flat, 0)
    flat[12 * C :, :] = up_g[...]


def backward_kernel(
    grad_c, from_left, from_right, hidden, cot_grid, live, coarse_w, down_w,
    grad_h, grad_d, pack_low, pack_high, coarse_p, grad_x,
):
    coarse_tiles = grad_c.shape[0]
    ids = lane_ids(C)
    even = (ids // 16) % 2 == 0
    at_left = even & (ids % 16 == 2)
    at_right = even & (ids % 16 == 12)
    zero = jnp.zeros((C, LANES), BF16)
    for coarse in range(coarse_tiles):
        group, place = coarse // 32, coarse % 32
        tile = jnp.where(at_left, roll(from_left[group], 2 - place), grad_c[coarse])
        grad_x[coarse] = jnp.where(at_right, roll(from_right[group], 12 - place), tile)
    conv_steps(coarse_p, coarse_w, lambda tile: grad_x[tile], coarse_tiles, 32, 2, 2)
    own_anchors = anchor_mask(True)
    across = lane_ids(C) % 16
    inside = ((across >= 4) & (across < 12)).astype(F32)

    def step(block):
        alive = jnp.broadcast_to(live[pl.ds(block, 1), :], (C, LANES)) * inside
        keep = alive * own_anchors
        spreads = []
        for inner in range(4):
            coarse = 4 * block + inner
            down = (conv_sum(coarse_p, coarse) * keep).astype(BF16)
            grad_d[coarse] = down
            spreads.append(spread_sub(down))
        acts = dot(down_w[...], jnp.concatenate(spreads, axis=1), (0, 0))
        for inner in range(4):
            for half in range(2):
                tile = EDGE * block + 2 * inner + half
                slope = silu_parts(hidden[tile])[1]
                part = acts[half * C : (half + 1) * C, LANES * inner : LANES * (inner + 1)]
                grad = cot_grid[tile].astype(F32) + part * slope
                grad_h[tile] = (grad * alive).astype(BF16)

    loop(0, coarse_tiles // 4, step, 2)
    for out, lane in ((pack_low, 4), (pack_high, 11)):
        def pack_step(group):
            total = zero
            for inner in range(16):
                picked = jnp.where(ids % 16 == lane, grad_h[16 * group + inner], zero)
                total = total + roll(picked, inner - lane)
            out[group] = total

        loop(0, out.shape[0], pack_step)


def weight_kernel(grid, grad_h, grad_d, hidden, flat, grad_own, fine_g, down_g):
    tiles = grid.shape[0]
    coarse_tiles = grad_d.shape[0]
    fine_g[...] = jnp.zeros_like(fine_g)
    down_g[...] = jnp.zeros_like(down_g)
    zero = jnp.zeros((C, LANES), BF16)
    for step in range(3, 8):
        grad_own[step] = zero
        grad_own[tiles - 1 - step] = zero

    def copy_step(tile):
        grad_own[tile] = grad_h[tile]

    loop(8, tiles - 8, copy_step, 8)
    low, high = z_masks(16)

    def fine_step(index):
        at = [4 + 8 * index + inner for inner in range(8)]
        rights = [columns(grid[tile], low, high, 16, 1) for tile in at]
        fine_g[0 : 9 * C, :] += dot(
            jnp.concatenate(rights, axis=1), stacks(grad_own, at), (1, 1)
        )

    loop(0, (tiles - 8) // 8, fine_step)

    def down_step(index):
        lefts = []
        rights = []
        for inner in range(4):
            coarse = 4 + 4 * index + inner
            lefts.append(spread_sub(grad_d[coarse]))
            actives = [silu_parts(hidden[2 * coarse + half])[0].astype(BF16) for half in range(2)]
            rights.append(jnp.concatenate(actives, axis=0))
        down_g[:, 0 : 2 * C] += dot(
            jnp.concatenate(lefts, axis=1), jnp.concatenate(rights, axis=1), (1, 1)
        )

    loop(0, (coarse_tiles - 8) // 4, down_step, 2)
    flatten_weights(fine_g, flat, 0)
    flat[12 * C :, :] = down_g[...]


def input_kernel(
    slots, grad_h, from_left, from_right, live, place, fine_w, out, fine_p, rows_out, grad_x
):
    tiles = grad_h.shape[0]
    number = out.shape[0]
    ids = lane_ids(C)
    at_left = ids % 16 == 3
    at_right = ids % 16 == 12

    def fill_step(group):
        packed_left = from_left[group]
        packed_right = from_right[group]
        for inner in range(16):
            tile = jnp.where(at_left, roll(packed_left, 3 - inner), grad_h[16 * group + inner])
            tile = jnp.where(at_right, roll(packed_right, 12 - inner), tile)
            grad_x[16 * group + inner] = tile

    loop(0, tiles // 16, fill_step)
    conv_steps(fine_p, fine_w, lambda tile: grad_x[tile], tiles, 16, 1, 2)

    def block_step(block):
        alive = jnp.broadcast_to(live[pl.ds(block + 1, 1), :], (C, LANES))
        start = pl.multiple_of(block * C, 16)
        for inner in range(EDGE):
            value = conv_sum(fine_p, EDGE * (block + 1) + inner)
            rows_out[pl.ds(start, C), LANES * inner : LANES * (inner + 1)] = (
                value * alive
            ).astype(BF16)

    loop(0, number, block_step, 2)
    to_blocks(slots, rows_out, place, out)


def finish_kernel(scale, late, early, fine, down, coarse, up):
    for out, total in ((fine, late), (coarse, early)):
        for along in range(3):
            first = C * along
            rows = [total[first + 3 * C * g : first + 3 * C * g + C, :] for g in range(4)]
            row = jnp.concatenate(rows, axis=1) * scale
            for index in range(9):
                out[9 * (index % 3) + 3 * (index // 3) + along] = row[:, C * index : C * (index + 1)]
    for out, total, turn in ((down, late, False), (up, early, True)):
        for index in range(4):
            rows = total[C * (12 + index) : C * (13 + index), :] * scale
            for along in range(2):
                part = rows[:, C * along : C * (along + 1)]
                out[2 * index + along] = part.T if turn else part


def call(kernel, inputs, outs, scratch=(), scalars=0, flops=0, far=0):
    vmem = pl.BlockSpec(memory_space=pltpu.VMEM)
    smem = pl.BlockSpec(memory_space=pltpu.SMEM)
    far_space = pl.BlockSpec(memory_space=pltpu.HBM)
    near = len(inputs) - scalars - far
    sems = [number for number in scratch if isinstance(number, int)]
    scratch = [entry for entry in scratch if not isinstance(entry, int)]
    held = SLACK
    near_kinds = [(a.shape, a.dtype) for a in inputs[scalars : scalars + near]]
    for shape, kind in near_kinds + list(outs) + scratch:
        rows, lanes = -(-shape[-2] // 16) * 16, -(-shape[-1] // LANES) * LANES
        held += math.prod(shape[:-2]) * rows * lanes * jnp.dtype(kind).itemsize
    moved = sum(math.prod(s) * jnp.dtype(d).itemsize for s, d in outs)
    moved += sum(math.prod(a.shape) * a.dtype.itemsize for a in inputs)
    return pl.pallas_call(
        kernel,
        out_shape=tuple(jax.ShapeDtypeStruct(s, d) for s, d in outs),
        in_specs=[smem] * scalars + [vmem] * near + [far_space] * far,
        out_specs=tuple(vmem for _ in outs),
        scratch_shapes=[pltpu.VMEM(s, d) for s, d in scratch]
        + [pltpu.SemaphoreType.DMA((number,)) for number in sems],
        compiler_params=pltpu.CompilerParams(vmem_limit_bytes=held),
        cost_estimate=pl.CostEstimate(flops=flops, bytes_accessed=moved, transcendentals=0),
        name=getattr(kernel, "func", kernel).__name__,
    )(*inputs)


def send(array, step_x, step_y):
    number_x, number_y = lax.axis_size("gx"), lax.axis_size("gy")
    pairs = []
    for i in range(number_x):
        for j in range(number_y):
            to_x, to_y = i + step_x, j + step_y
            if 0 <= to_x < number_x and 0 <= to_y < number_y:
                pairs.append((i * number_y + j, to_x * number_y + to_y))
    return lax.ppermute(array, ("gx", "gy"), pairs)


def reduce_all(part):
    return lax.psum(lax.psum(part, "gx"), "gy")


def on_device(
    features, block_slots, block_count, cotangent, fine_weight, down_weight, coarse_weight,
    up_weight,
):
    number = features.shape[2]
    slots = block_slots.reshape(number)
    count = block_count.reshape(1)
    feats = features.reshape(number, C, VOX)
    cots = cotangent.reshape(number, C, VOX)
    place_own = jnp.asarray(placing_matrix()[:512], BF16)
    place_halo = jnp.asarray(placing_matrix()[512:], BF16)
    place_back = jnp.asarray(placing_matrix()[:512].T, BF16)
    pick = jnp.asarray(edge_matrix(), BF16)
    tiles = EDGE * (number + 2)
    coarse_tiles = tiles // 2
    groups = -(-coarse_tiles // 32)
    fine_groups = tiles // 16

    fine_3, down_3, coarse_3 = (
        weight.transpose(1, 0, 2) for weight in (fine_weight, down_weight, coarse_weight)
    )
    own, cot, flag_rows, x_low, x_high, y_low, y_high = call(
        prepare_kernel,
        (slots, count, pick, feats, cots),
        [((number, C, VOX), BF16)] * 2
        + [((C, VOX), BF16)]
        + [((number + 1, C, 256), BF16)] * 2
        + [((3, C, VOX), BF16)] * 2,
        [(((number + 1) * C, VOX), BF16), number, number],
        scalars=2,
        far=2,
    )
    x_left = send(x_high, 1, 0)
    x_right = send(x_low, -1, 0)
    y_left = send(y_high, 0, 1)
    y_right = send(y_low, 0, -1)
    corner_low, corner_high, flags = call(
        corner_kernel,
        (y_left, y_right, flag_rows, pick),
        [((3, C, 256), BF16), ((3, C, 256), BF16), ((C, VOX), BF16)],
    )
    c_left = send(corner_high, 1, 0)
    c_right = send(corner_low, -1, 0)
    (grid_own, cot_grid, grad_r, live_own, fine_fore, fine_back, coarse_fore, coarse_back, down_w,
     up_w) = call(
        place_kernel,
        (own, cot, y_left, y_right, flags, place_own, fine_3, down_3, coarse_3, up_weight),
        [
            ((tiles, C, LANES), BF16),
            ((tiles, C, LANES), BF16),
            ((coarse_tiles, C, LANES), F32),
            ((C, LANES), F32),
        ]
        + [((3 * C, 9 * C), BF16)] * 4
        + [((4 * C, 2 * C), BF16), ((2 * C, 4 * C), BF16)],
        [(((number + 3) * C, VOX), BF16), (((number + 2) * C, VOX), BF16)],
        flops=8 * 10**9,
    )
    grid, hidden, lowered, rects, grad_c, live, pack_low, pack_high = call(
        forward_kernel,
        (grid_own, live_own, grad_r, x_left, x_right, c_left, c_right, place_halo, fine_fore,
         down_w, coarse_fore),
        [
            ((tiles, C, LANES), BF16),
            ((tiles, C, LANES), F32),
            ((coarse_tiles, C, LANES), BF16),
            ((coarse_tiles, C, LANES), BF16),
            ((coarse_tiles, C, LANES), BF16),
            ((C, LANES), F32),
            ((groups, C, LANES), BF16),
            ((groups, C, LANES), BF16),
        ],
        [
            (((number + 3) * C, VOX), BF16),
            ((tiles + 2, 3 * C, LANES), F32),
            ((coarse_tiles + 2, 3 * C, LANES), F32),
        ],
        flops=8 * 10**9,
    )
    grad_left = send(pack_high, 1, 0)
    grad_right = send(pack_low, -1, 0)
    output, early = call(
        side_kernel,
        (slots, hidden, rects, cot_grid, lowered, grad_c, live, place_back, up_w),
        [((number, C, VOX), BF16), ((16 * C, LANES), F32)],
        [
            ((number * C, 1024), BF16),
            ((coarse_tiles, C, LANES), BF16),
            ((4 * C, LANES), F32),
            ((VOX, 3 * C), F32),
        ],
        scalars=1,
        flops=8 * 10**9,
    )
    early_sum = reduce_all(early)
    grad_h, grad_d, edge_low, edge_high = call(
        backward_kernel,
        (grad_c, grad_left, grad_right, hidden, cot_grid, live, coarse_back, down_w),
        [
            ((tiles, C, LANES), BF16),
            ((coarse_tiles, C, LANES), BF16),
            ((fine_groups, C, LANES), BF16),
            ((fine_groups, C, LANES), BF16),
        ],
        [((coarse_tiles + 2, 3 * C, LANES), F32), ((coarse_tiles, C, LANES), BF16)],
        flops=8 * 10**9,
    )
    edge_left = send(edge_high, 1, 0)
    edge_right = send(edge_low, -1, 0)
    (late,) = call(
        weight_kernel,
        (grid, grad_h, grad_d, hidden),
        [((16 * C, LANES), F32)],
        [((tiles, C, LANES), BF16), ((VOX, 3 * C), F32), ((4 * C, LANES), F32)],
        flops=12 * 10**9,
    )
    late, edge_left, edge_right = lax.optimization_barrier((late, edge_left, edge_right))
    late_sum = reduce_all(late)
    (input_grad,) = call(
        input_kernel,
        (slots, grad_h, edge_left, edge_right, live, place_back, fine_back),
        [((number, C, VOX), BF16)],
        [
            ((tiles + 2, 3 * C, LANES), F32),
            ((number * C, 1024), BF16),
            ((tiles, C, LANES), BF16),
        ],
        scalars=1,
        flops=8 * 10**9,
    )
    scale = 1.0 / math.sqrt(number * VOX * lax.axis_size("gx") * lax.axis_size("gy"))
    fine_total, down_total, coarse_total, up_total = call(
        functools.partial(finish_kernel, scale),
        (late_sum, early_sum),
        [((27, C, C), F32), ((8, C, C), F32), ((27, C, C), F32), ((8, C, C), F32)],
    )
    shape_out = (1, 1, number, C, VOX)
    return (
        output.reshape(shape_out),
        input_grad.reshape(shape_out),
        fine_total.transpose(1, 0, 2),
        down_total.transpose(1, 0, 2),
        coarse_total.transpose(1, 0, 2),
        up_total,
    )


def solution(mesh):
    split = P("gx", "gy", None, None, None)
    return jax.shard_map(
        on_device,
        mesh=mesh,
        in_specs=(split, P("gx", "gy", None), P("gx", "gy"), split, P(), P(), P(), P()),
        out_specs=(split, split, P(), P(), P(), P()),
        check_vma=False,
    )
```

```python
import functools
import math

import jax
import jax.numpy as jnp
import numpy as np
from jax import lax
from jax.experimental import pallas as pl
from jax.experimental.pallas import tpu as pltpu
from jax.sharding import PartitionSpec as P

C = 48
EDGE = 8
VOX = 512
LANES = 128
F32 = jnp.float32
BF16 = jnp.bfloat16
SLACK = 8 * 1024 * 1024
SHIFTS = (0, 1, 16, 17)


def placing_matrix():
    place = np.zeros((1024, 8 * LANES), np.float32)
    for z in range(8):
        for y in range(8):
            for x in range(8):
                place[64 * z + 8 * x + y, LANES * y + 16 * z + x + 4] = 1.0
            for x in range(4):
                place[512 + 32 * z + 8 * x + y, LANES * y + 16 * z + x] = 1.0
                place[768 + 32 * z + 8 * x + y, LANES * y + 16 * z + x + 12] = 1.0
    return place


def pair_matrix():
    place = np.zeros((1024, 8 * LANES), np.float32)
    for half in range(2):
        for z in range(8):
            for x in range(8):
                for y in range(8):
                    lane = (16 * z + 8 * half + x + 4) % LANES
                    place[512 * half + 64 * z + 8 * x + y, LANES * y + lane] = 1.0
    return place


def edge_matrix():
    pick = np.zeros((512, 512), np.float32)
    for z in range(8):
        for y in range(8):
            for x in range(8):
                pick[64 * z + 8 * x + y, 256 * (x // 4) + 32 * z + 8 * (x % 4) + y] = 1.0
    return pick


def dot(left, right, contract=(1, 0)):
    dims = (((contract[0],), (contract[1],)), ((), ()))
    return lax.dot_general(left, right, dims, preferred_element_type=F32)


def roll(value, shift):
    return pltpu.roll(value, shift % LANES, 1)


def lane_ids(rows):
    return lax.broadcasted_iota(jnp.int32, (rows, LANES), 1)


def silu_parts(value):
    sigma = 1.0 / (1.0 + jnp.exp(-value))
    return value * sigma, sigma * (1.0 + value * (1.0 - sigma))


def depth_columns(base, masks, step):
    zero = jnp.zeros_like(base)
    below = jnp.where(masks[0], zero, roll(base, step))
    above = jnp.where(masks[1], zero, roll(base, -step))
    return jnp.concatenate([below, base, above], axis=0)


def depth_masks(step, first):
    ids = (lane_ids(3 * C) - first) % LANES
    return ids < step, ids >= LANES - step


def across_columns(tile, step):
    return jnp.concatenate([roll(tile, step), tile, roll(tile, -step)], axis=0)


def pair_columns(tile, halo, step):
    ids = lane_ids(C) % 8
    left = jnp.where(ids == 4, roll(halo, step), roll(tile, step))
    right = jnp.where(ids == 4 - step, roll(halo, -step), roll(tile, -step))
    return jnp.concatenate([left, tile, right], axis=0)


def own_lanes(rows):
    across = lane_ids(rows) % 16
    return (across >= 4) & (across < 12)


def join_halves(lower, upper):
    return jnp.where(own_lanes(lower.shape[0]), lower, roll(upper, 8))


def join_halos(lower, upper):
    return jnp.where(own_lanes(lower.shape[0]), roll(upper, 8), lower)


def packed_halo(from_left, from_right, first, second, place, step):
    ids = lane_ids(C) % 16
    zero = jnp.zeros((C, LANES), BF16)
    halo = jnp.where(ids == 4 - step, roll(from_left[first], 4 - step - place), zero)
    halo = jnp.where(ids == 12 - step, roll(from_left[second], 12 - step - place), halo)
    halo = jnp.where(ids == 12, roll(from_right[first], 12 - place), halo)
    return jnp.where(ids == 4, roll(from_right[second], 20 - place), halo)


def gather_sub(parts):
    total = parts[:C]
    for index in range(1, 4):
        total = total + roll(parts[index * C : (index + 1) * C], -SHIFTS[index])
    return total


def spread_sub(anchored):
    return jnp.concatenate([anchored] + [roll(anchored, step) for step in SHIFTS[1:]], axis=0)


def anchor_mask(first):
    ids = (lane_ids(C) - first) % LANES
    return (((ids // 16) % 2 == 0) & (ids % 2 == 0)).astype(F32)


def loop(low, high, body, unroll=1):
    def step(index, carry):
        body(index)
        return carry

    lax.fori_loop(low, high, step, 0, unroll=unroll)


def prepare_kernel(
    slots, count, feats, cots, pick, own, cot, flag_rows, x_low, x_high, y_low, y_high, rows_in
):
    number = feats.shape[0]
    rows = lax.broadcasted_iota(jnp.int32, (C, VOX), 0)
    flags = jnp.zeros((C, VOX), F32)
    first = jnp.zeros((), F32)
    last = jnp.zeros((), F32)
    zero = jnp.zeros((C, VOX), BF16)
    for slot in range(number):
        live = slot < count[0]
        alive = jnp.where(live, 1.0, 0.0)
        place = slots[slot]
        block = jnp.where(live, feats[slot], zero)
        own[place] = block
        rows_in[pl.ds(pl.multiple_of(place * C, 16), C), :] = block
        cot[place] = jnp.where(live, cots[slot], zero)
        flags = jnp.where(rows == place + 1, alive, flags)
        first = first + jnp.where(place == 0, alive, 0.0)
        last = last + jnp.where(place == number - 1, alive, 0.0)
    flag_rows[...] = flags.astype(BF16)
    rows_in[number * C :, :] = flags.astype(BF16)
    first_flag = jnp.where(rows == number + 1, first, 0.0).astype(BF16)
    last_flag = jnp.where(rows == 0, last, 0.0).astype(BF16)
    packed = dot(rows_in[...], pick[...]).astype(BF16)
    packed = packed.reshape(number + 1, C, VOX)
    x_low[...] = packed[:, :, :256]
    x_high[...] = packed[:, :, 256:]
    for out, index, flag in ((y_low, 0, first_flag), (y_high, number - 1, last_flag)):
        out[0] = own[index]
        out[1] = cot[index]
        out[2] = flag


def corner_kernel(y_left, y_right, flag_rows, pick, low, high, flags):
    extra = y_left[2] + y_right[2]
    rows = jnp.concatenate([y_left[0], y_right[0], extra], axis=0)
    packed = dot(rows, pick[...]).astype(BF16).reshape(3, C, VOX)
    low[...] = packed[:, :, :256]
    high[...] = packed[:, :, 256:]
    flags[...] = flag_rows[...] + extra


def arrange_weights(fine, down, coarse, up, fine_w, fine_b, coarse_w, coarse_b, down_w, up_w):
    for source, fore, back in ((fine, fine_w, fine_b), (coarse, coarse_w, coarse_b)):
        for along in range(3):
            rows = slice(C * along, C * (along + 1))
            turned_rows = slice(C * (2 - along), C * (3 - along))
            ahead = []
            behind = []
            for depth in range(3):
                for across in range(3):
                    ahead.append(source[9 * depth + 3 * across + along])
                    behind.append(source[9 * (2 - depth) + 3 * (2 - across) + along].T)
            fore[rows, :] = jnp.concatenate(ahead, axis=1)
            back[turned_rows, :] = jnp.concatenate(behind, axis=1)
    for index in range(4):
        pair = [down[2 * index], down[2 * index + 1]]
        down_w[C * index : C * (index + 1), :] = jnp.concatenate(pair, axis=1)
    for along in range(2):
        row = jnp.concatenate([up[2 * index + along] for index in range(4)], axis=1)
        up_w[C * along : C * (along + 1), :] = row


def place_kernel(
    own, cot, y_left, y_right, flags, place, place_pair, fine, down, coarse, up,
    grid, cot_grid, grad_r, live, fine_w, fine_b, coarse_w, coarse_b, down_w, up_w,
    rows_in, rows_cot,
):
    arrange_weights(fine, down, coarse, up, fine_w, fine_b, coarse_w, coarse_b, down_w, up_w)
    number = cot.shape[0]
    last = number + 1
    rows_in[0:C, :] = y_left[0]
    for block in range(number):
        at = (block + 1) * C
        rows_in[at : at + C, :] = own[block]
    rows_in[last * C : (last + 1) * C, :] = y_right[0]
    rows_in[(last + 1) * C :, :] = flags[...]
    pairs = number // 2 + 2
    for group in range(pairs):
        at = group * C
        lower = y_left[1] if group == 0 else cot[group - 1]
        upper = y_right[1] if group == pairs - 1 else cot[group + number // 2 - 1]
        rows_cot[at : at + C, 0:512] = lower
        rows_cot[at : at + C, 512:1024] = upper
    for pair in range(4):
        lanes = slice(256 * pair, 256 * pair + 256)
        placed_cot = dot(rows_cot[...], place_pair[:, lanes])
        placed = dot(rows_in[...], place[:, lanes])
        for half in range(2):
            span = slice(LANES * half, LANES * (half + 1))
            for block in range(last + 1):
                tile = EDGE * block + 2 * pair + half
                grid[tile] = placed[block * C : (block + 1) * C, span].astype(BF16)
            for block in range(pairs):
                tile = EDGE * block + 2 * pair + half
                cot_grid[tile] = placed_cot[block * C : (block + 1) * C, span].astype(BF16)
        if pair == 0:
            live[...] = placed[(last + 1) * C :, 0:LANES]

    def rect_step(block):
        tiles = []
        for inner in range(4):
            tile = EDGE * block + 2 * inner
            tiles.append(jnp.concatenate([cot_grid[tile], cot_grid[tile + 1]], axis=0))
        parts = dot(up_w[...], jnp.concatenate(tiles, axis=1), (0, 0))
        for inner in range(4):
            grad_r[4 * block + inner] = gather_sub(parts[:, LANES * inner : LANES * (inner + 1)])

    loop(0, pairs, rect_step, 2)


def conv_sum(parts, tile):
    return parts[tile, 0:C] + parts[tile + 1, C : 2 * C] + parts[tile + 2, 2 * C :]


def conv_steps(parts, weight, load, tiles, step, first, unroll):
    masks = depth_masks(step, first)
    spare = jnp.zeros((3 * C, LANES), F32)
    parts[0] = spare
    parts[tiles + 1] = spare

    def body(index):
        tile = 4 * index
        for pair in range(2):
            at = tile + 2 * pair
            cols = [depth_columns(load(at + i), masks, step) for i in range(2)]
            out = dot(weight[...], jnp.concatenate(cols, axis=1))
            parts[at + 1] = out[:, :LANES]
            parts[at + 2] = out[:, LANES:]

    loop(0, tiles // 4, body, unroll)


def forward_kernel(
    grid_own, live_own, grad_r, x_left, x_right, c_left, c_right, place, fine_w, down_w, coarse_w,
    grid, hidden, low_cols, rects, grad_c, live, pack_low, pack_high,
    rows_in, fine_p, coarse_p, hidden_all, lowered, live_all,
):
    number = x_left.shape[0] - 1
    last = number + 1
    for block in range(number):
        at = (block + 1) * C
        rows_in[at : at + C, 0:256] = x_left[block]
        rows_in[at : at + C, 256:512] = x_right[block]
    for at, index in ((0, 0), (last * C, 1)):
        rows_in[at : at + C, 0:256] = c_left[index]
        rows_in[at : at + C, 256:512] = c_right[index]
    at = (last + 1) * C
    rows_in[at : at + C, 0:256] = x_left[number] + c_left[2]
    rows_in[at : at + C, 256:512] = x_right[number] + c_right[2]
    for pair in range(4):
        lanes = slice(256 * pair, 256 * pair + 256)
        placed = dot(rows_in[...], place[:, lanes])
        for half in range(2):
            span = slice(LANES * half, LANES * (half + 1))
            for block in range(last + 1):
                tile = EDGE * block + 2 * pair + half
                halo = placed[block * C : (block + 1) * C, span].astype(BF16)
                grid[tile] = grid_own[tile] + halo
        if pair == 0:
            live_all[...] = live_own[...] + placed[(last + 1) * C :, 0:LANES]
    live[...] = join_halves(live_all[0:16, :], live_all[8:24, :])
    tiles = grid.shape[0]
    conv_steps(fine_p, fine_w, lambda tile: across_columns(grid[tile], 1), tiles, 16, 0, 2)
    anchors = anchor_mask(0)

    def lower_step(block):
        alive = jnp.broadcast_to(live_all[pl.ds(block, 1), :], (C, LANES))
        keep = alive * anchors
        pairs = []
        for inner in range(4):
            actives = []
            for half in range(2):
                tile = EDGE * block + 2 * inner + half
                value = conv_sum(fine_p, tile) * alive
                hidden_all[tile] = value
                actives.append(silu_parts(value)[0].astype(BF16))
            pairs.append(jnp.concatenate(actives, axis=0))
        parts = dot(down_w[...], jnp.concatenate(pairs, axis=1))
        for inner in range(4):
            total = gather_sub(parts[:, LANES * inner : LANES * (inner + 1)])
            lowered[4 * block + inner] = (total * keep).astype(BF16)

    loop(0, last + 1, lower_step, 2)
    pairs = hidden.shape[0] // EDGE
    shift = last - pairs + 1

    def pair_step(block):
        for inner in range(EDGE):
            tile = EDGE * block + inner
            hidden[tile] = join_halves(hidden_all[tile], hidden_all[tile + EDGE * shift])
        for inner in range(4):
            tile = 4 * block + inner
            lower, upper = lowered[tile], lowered[tile + 4 * shift]
            low_cols[tile] = pair_columns(join_halves(lower, upper), join_halos(lower, upper), 2)

    loop(0, pairs, pair_step, 2)
    conv_steps(coarse_p, coarse_w, lambda tile: low_cols[tile], 4 * pairs, 32, 4, 2)
    pair_anchors = anchor_mask(4)

    def grad_step(block):
        alive = jnp.broadcast_to(live[pl.ds(block, 1), :], (C, LANES))
        keep = alive * pair_anchors
        for inner in range(4):
            coarse = 4 * block + inner
            smooth, slope = silu_parts(conv_sum(coarse_p, coarse))
            rects[coarse] = (smooth * pair_anchors).astype(BF16)
            grad_c[coarse] = (grad_r[coarse] * slope * keep).astype(BF16)

    loop(0, pairs, grad_step, 2)
    ids = lane_ids(C)
    zero = jnp.zeros((C, LANES), BF16)
    half = 2 * number
    for out, lane in ((pack_low, 4), (pack_high, 10)):
        for group in range(out.shape[0]):
            total = zero
            for coarse in range(max(2, 32 * group), min(2 * half + 6, 32 * group + 32)):
                upper = coarse >= half + 4
                tile = grad_c[coarse - half] if upper else grad_c[coarse]
                at = lane + 8 if upper else lane
                picked = jnp.where(ids % 32 == at, tile, zero)
                total = total + roll(picked, coarse % 32 - at)
            out[group] = total


def to_blocks(slots, rows_out, place_back, flat, out):
    flat[...] = dot(rows_out[...], place_back[...]).astype(BF16)
    number = out.shape[0]
    for slot in range(number):
        place = slots[slot]
        upper = place >= number // 2
        start = pl.multiple_of(jnp.where(upper, place - number // 2, place) * C, 16)
        rows = flat[pl.ds(start, C), :]
        out[slot] = jnp.where(upper, rows[:, 512:], rows[:, :512])


def stacks(own, tiles):
    parts = [jnp.concatenate([own[t + 1], own[t], own[t - 1]], axis=0) for t in tiles]
    return jnp.concatenate(parts, axis=1)


def flatten_weights(total, out, at):
    turned = total[...].T.astype(BF16)
    for group in range(4):
        out[at + 3 * C * group : at + 3 * C * (group + 1), :] = turned[
            :, LANES * group : LANES * (group + 1)
        ]


def output_kernel(slots, hidden, rects, live, place_back, up_w, out, rows_out, flat):
    pairs = hidden.shape[0] // EDGE

    def block_step(block):
        alive = jnp.broadcast_to(live[pl.ds(block, 1), :], (C, LANES))
        start = pl.multiple_of((block - 1) * C, 16)
        spreads = [spread_sub(rects[4 * block + inner]) for inner in range(4)]
        upward = dot(up_w[...], jnp.concatenate(spreads, axis=1))
        for inner in range(4):
            for half in range(2):
                part = upward[half * C : (half + 1) * C, LANES * inner : LANES * (inner + 1)]
                value = hidden[EDGE * block + 2 * inner + half] + part
                at = LANES * (2 * inner + half)
                rows_out[pl.ds(start, C), at : at + LANES] = (value * alive).astype(BF16)

    loop(1, pairs - 1, block_step, 2)
    to_blocks(slots, rows_out, place_back, flat, out)


def side_kernel(rects, cot_grid, low_cols, grad_c, flat, grad_own, up_g, coarse_g):
    tiles = low_cols.shape[0]
    up_g[...] = jnp.zeros_like(up_g)
    coarse_g[...] = jnp.zeros_like(coarse_g)

    def up_step(block):
        spreads = []
        pairs = []
        for inner in range(4):
            coarse = 4 * block + inner
            spreads.append(spread_sub(rects[coarse]))
            pairs.append(
                jnp.concatenate([cot_grid[2 * coarse], cot_grid[2 * coarse + 1]], axis=0)
            )
        up_g[:, 0 : 2 * C] += dot(
            jnp.concatenate(spreads, axis=1), jnp.concatenate(pairs, axis=1), (1, 1)
        )

    loop(1, tiles // 4 - 1, up_step, 2)
    zero = jnp.zeros((C, LANES), BF16)
    for coarse in range(1, 4):
        grad_own[coarse] = zero
        grad_own[tiles - 1 - coarse] = zero

    def copy_step(coarse):
        grad_own[coarse] = grad_c[coarse]

    loop(4, tiles - 4, copy_step, 8)
    masks = depth_masks(32, 4)

    def weight_step(index):
        at = [2 + 4 * index + inner for inner in range(4)]
        rights = [depth_columns(low_cols[tile], masks, 32) for tile in at]
        coarse_g[0 : 9 * C, :] += dot(
            jnp.concatenate(rights, axis=1), stacks(grad_own, at), (1, 1)
        )

    loop(0, (tiles - 4) // 4, weight_step, 3)
    flatten_weights(coarse_g, flat, 0)
    flat[12 * C :, :] = up_g[...].astype(BF16)


def backward_kernel(
    grad_c, from_left, from_right, hidden, cot_grid, live, coarse_w, down_w,
    grad_h, grad_d, pack_low, pack_high, coarse_p, grad_x,
):
    tiles = grad_c.shape[0]
    half = tiles - 8
    for coarse in range(tiles):
        first, second = coarse // 32, (coarse + half) // 32
        halo = packed_halo(from_left, from_right, first, second, coarse % 32, 2)
        grad_x[coarse] = pair_columns(grad_c[coarse], halo, 2)
    conv_steps(coarse_p, coarse_w, lambda tile: grad_x[tile], tiles, 32, 4, 2)
    anchors = anchor_mask(4)

    def step(block):
        alive = jnp.broadcast_to(live[pl.ds(block, 1), :], (C, LANES))
        keep = alive * anchors
        spreads = []
        for inner in range(4):
            coarse = 4 * block + inner
            down = (conv_sum(coarse_p, coarse) * keep).astype(BF16)
            grad_d[coarse] = down
            spreads.append(spread_sub(down))
        acts = dot(down_w[...], jnp.concatenate(spreads, axis=1), (0, 0))
        for inner in range(4):
            for side in range(2):
                tile = EDGE * block + 2 * inner + side
                slope = silu_parts(hidden[tile])[1]
                part = acts[side * C : (side + 1) * C, LANES * inner : LANES * (inner + 1)]
                grad = cot_grid[tile].astype(F32) + part * slope
                grad_h[tile] = (grad * alive).astype(BF16)

    loop(0, tiles // 4, step, 2)
    fine = 2 * tiles
    shift = fine - 16
    ids = lane_ids(C) % 16
    zero = jnp.zeros((C, LANES), BF16)
    for out, lane in ((pack_low, 4), (pack_high, 11)):
        for group in range(out.shape[0]):
            total = zero
            for tile in range(16 * group, 16 * group + 16):
                upper = tile >= shift + 8
                source = grad_h[tile - shift] if upper else grad_h[tile]
                at = lane + 8 if upper else lane
                picked = jnp.where(ids == at % 16, source, zero)
                total = total + roll(picked, tile % 16 - at)
            out[group] = total


def weight_kernel(grid, grad_h, grad_d, hidden, early, joined, grad_own, fine_g, down_g):
    tiles = grad_h.shape[0]
    shift = tiles - 16
    fine_g[...] = jnp.zeros_like(fine_g)
    down_g[...] = jnp.zeros_like(down_g)
    zero = jnp.zeros((C, LANES), BF16)
    for tile in range(3, 8):
        grad_own[tile] = zero
        grad_own[tiles - 1 - tile] = zero

    def copy_step(tile):
        grad_own[tile] = grad_h[tile]

    loop(8, tiles - 8, copy_step, 8)
    masks = depth_masks(16, 4)

    def fine_step(index):
        at = [4 + 8 * index + inner for inner in range(8)]
        rights = []
        for tile in at:
            lower, upper = grid[tile], grid[tile + shift]
            base = pair_columns(join_halves(lower, upper), join_halos(lower, upper), 1)
            rights.append(depth_columns(base, masks, 16))
        fine_g[0 : 9 * C, :] += dot(
            jnp.concatenate(rights, axis=1), stacks(grad_own, at), (1, 1)
        )

    loop(0, (tiles - 8) // 8, fine_step)

    def down_step(index):
        lefts = []
        rights = []
        for inner in range(4):
            coarse = 4 + 4 * index + inner
            lefts.append(spread_sub(grad_d[coarse]))
            actives = [silu_parts(hidden[2 * coarse + side])[0].astype(BF16) for side in range(2)]
            rights.append(jnp.concatenate(actives, axis=0))
        down_g[:, 0 : 2 * C] += dot(
            jnp.concatenate(lefts, axis=1), jnp.concatenate(rights, axis=1), (1, 1)
        )

    loop(0, (tiles // 2 - 8) // 4, down_step, 2)
    flatten_weights(fine_g, joined, 0)
    joined[12 * C : 16 * C, :] = down_g[...].astype(BF16)
    joined[16 * C :, :] = early[...]


def input_kernel(
    slots, grad_h, from_left, from_right, live, place_back, fine_w, out,
    fine_p, rows_out, flat, grad_x,
):
    tiles = grad_h.shape[0]
    shift = tiles - 16

    def fill_step(group):
        for inner in range(16):
            tile = 16 * group + inner
            second = group + shift // 16
            halo = packed_halo(from_left, from_right, group, second, inner, 1)
            grad_x[tile] = pair_columns(grad_h[tile], halo, 1)

    loop(0, tiles // 16, fill_step)
    conv_steps(fine_p, fine_w, lambda tile: grad_x[tile], tiles, 16, 4, 2)

    def block_step(block):
        alive = jnp.broadcast_to(live[pl.ds(block, 1), :], (C, LANES))
        start = pl.multiple_of((block - 1) * C, 16)
        for inner in range(EDGE):
            value = conv_sum(fine_p, EDGE * block + inner)
            rows_out[pl.ds(start, C), LANES * inner : LANES * (inner + 1)] = (
                value * alive
            ).astype(BF16)

    loop(1, tiles // EDGE - 1, block_step, 2)
    to_blocks(slots, rows_out, place_back, flat, out)


def finish_kernel(scale, total, fine, down, coarse, up):
    for out, at in ((fine, 0), (coarse, 16 * C)):
        for along in range(3):
            first = at + C * along
            rows = [total[first + 3 * C * g : first + 3 * C * g + C, :] for g in range(4)]
            row = jnp.concatenate(rows, axis=1).astype(F32) * scale
            for index in range(9):
                out[3 * index + along] = row[:, C * index : C * (index + 1)]
    for out, at, turn in ((down, 12 * C, False), (up, 28 * C, True)):
        for index in range(4):
            rows = total[at + C * index : at + C * (index + 1), :].astype(F32) * scale
            for along in range(2):
                part = rows[:, C * along : C * (along + 1)]
                out[2 * index + along] = part.T if turn else part


def call(kernel, inputs, outs, scratch=(), scalars=0, flops=0, limit=None):
    vmem = pl.BlockSpec(memory_space=pltpu.VMEM)
    smem = pl.BlockSpec(memory_space=pltpu.SMEM)
    held = SLACK
    for shape, kind in [(a.shape, a.dtype) for a in inputs[scalars:]] + list(outs) + list(scratch):
        rows, lanes = -(-shape[-2] // 16) * 16, -(-shape[-1] // LANES) * LANES
        held += math.prod(shape[:-2]) * rows * lanes * jnp.dtype(kind).itemsize
    moved = sum(math.prod(s) * jnp.dtype(d).itemsize for s, d in outs)
    moved += sum(math.prod(a.shape) * a.dtype.itemsize for a in inputs)
    return pl.pallas_call(
        kernel,
        out_shape=tuple(jax.ShapeDtypeStruct(s, d) for s, d in outs),
        in_specs=[smem] * scalars + [vmem] * (len(inputs) - scalars),
        out_specs=tuple(vmem for _ in outs),
        scratch_shapes=[pltpu.VMEM(s, d) for s, d in scratch],
        compiler_params=pltpu.CompilerParams(vmem_limit_bytes=limit or held),
        cost_estimate=pl.CostEstimate(flops=flops, bytes_accessed=moved, transcendentals=0),
        name=getattr(kernel, "func", kernel).__name__,
    )(*inputs)


def send(array, step_x, step_y):
    number_x, number_y = lax.axis_size("gx"), lax.axis_size("gy")
    pairs = []
    for i in range(number_x):
        for j in range(number_y):
            to_x, to_y = i + step_x, j + step_y
            if 0 <= to_x < number_x and 0 <= to_y < number_y:
                pairs.append((i * number_y + j, to_x * number_y + to_y))
    return lax.ppermute(array, ("gx", "gy"), pairs)


def reduce_all(joined):
    axes = ("gx", "gy")
    devices = lax.axis_size("gx") * lax.axis_size("gy")
    rows = joined.shape[0]
    share = -(-rows // devices)
    joined = jnp.pad(joined, ((0, share * devices - rows), (0, 0)))
    mine = lax.all_to_all(joined.reshape(devices, share, LANES), axes, 0, 0)
    mine = jnp.sum(mine.astype(F32), axis=0).astype(BF16)
    spread = jnp.broadcast_to(mine[None], (devices, share, LANES))
    full = lax.all_to_all(spread, axes, 0, 0)
    return full.reshape(devices * share, LANES)[:rows]


def on_device(
    features, block_slots, block_count, cotangent, fine_weight, down_weight, coarse_weight,
    up_weight,
):
    number = features.shape[2]
    slots = block_slots.reshape(number)
    count = block_count.reshape(1)
    feats = features.reshape(number, C, VOX)
    cots = cotangent.reshape(number, C, VOX)
    place_own = jnp.asarray(placing_matrix()[:512], BF16)
    place_halo = jnp.asarray(placing_matrix()[512:], BF16)
    place_pair = jnp.asarray(pair_matrix(), BF16)
    place_back = jnp.asarray(pair_matrix().T, BF16)
    pick = jnp.asarray(edge_matrix(), BF16)
    tiles = EDGE * (number + 2)
    coarse_tiles = tiles // 2
    pairs = number // 2 + 2
    groups = -(-coarse_tiles // 32)
    fine_groups = tiles // 16

    fine_3, down_3, coarse_3 = (
        weight.transpose(1, 0, 2) for weight in (fine_weight, down_weight, coarse_weight)
    )
    own, cot, flag_rows, x_low, x_high, y_low, y_high = call(
        prepare_kernel,
        (slots, count, feats, cots, pick),
        [((number, C, VOX), BF16)] * 2
        + [((C, VOX), BF16)]
        + [((number + 1, C, 256), BF16)] * 2
        + [((3, C, VOX), BF16)] * 2,
        [(((number + 1) * C, VOX), BF16)],
        scalars=2,
        limit=56 * 1024 * 1024,
    )
    x_left = send(x_high, 1, 0)
    x_right = send(x_low, -1, 0)
    y_left = send(y_high, 0, 1)
    y_right = send(y_low, 0, -1)
    corner_low, corner_high, flags = call(
        corner_kernel,
        (y_left, y_right, flag_rows, pick),
        [((3, C, 256), BF16), ((3, C, 256), BF16), ((C, VOX), BF16)],
    )
    c_left = send(corner_high, 1, 0)
    c_right = send(corner_low, -1, 0)
    (grid_own, cot_grid, grad_r, live_own, fine_fore, fine_back, coarse_fore, coarse_back, down_w,
     up_w) = call(
        place_kernel,
        (own, cot, y_left, y_right, flags, place_own, place_pair, fine_3, down_3, coarse_3,
         up_weight),
        [
            ((tiles, C, LANES), BF16),
            ((EDGE * pairs, C, LANES), BF16),
            ((4 * pairs, C, LANES), F32),
            ((C, LANES), F32),
        ]
        + [((3 * C, 9 * C), BF16)] * 4
        + [((4 * C, 2 * C), BF16), ((2 * C, 4 * C), BF16)],
        [(((number + 3) * C, VOX), BF16), ((pairs * C, 1024), BF16)],
        flops=8 * 10**9,
    )
    grid, hidden, low_cols, rects, grad_c, live, pack_low, pack_high = call(
        forward_kernel,
        (grid_own, live_own, grad_r, x_left, x_right, c_left, c_right, place_halo, fine_fore,
         down_w, coarse_fore),
        [
            ((tiles, C, LANES), BF16),
            ((EDGE * pairs, C, LANES), F32),
            ((4 * pairs, 3 * C, LANES), BF16),
            ((4 * pairs, C, LANES), BF16),
            ((4 * pairs, C, LANES), BF16),
            ((16, LANES), F32),
            ((groups, C, LANES), BF16),
            ((groups, C, LANES), BF16),
        ],
        [
            (((number + 3) * C, VOX), BF16),
            ((tiles + 2, 3 * C, LANES), F32),
            ((4 * pairs + 2, 3 * C, LANES), F32),
            ((tiles, C, LANES), F32),
            ((coarse_tiles, C, LANES), BF16),
            ((C, LANES), F32),
        ],
        flops=8 * 10**9,
    )
    grad_left = send(pack_high, 1, 0)
    grad_right = send(pack_low, -1, 0)
    (early,) = call(
        side_kernel,
        (rects, cot_grid, low_cols, grad_c),
        [((16 * C, LANES), BF16)],
        [((4 * pairs, C, LANES), BF16), ((4 * C, LANES), F32), ((VOX, 3 * C), F32)],
        flops=8 * 10**9,
    )
    grad_h, grad_d, edge_low, edge_high = call(
        backward_kernel,
        (grad_c, grad_left, grad_right, hidden, cot_grid, live, coarse_back, down_w),
        [
            ((EDGE * pairs, C, LANES), BF16),
            ((4 * pairs, C, LANES), BF16),
            ((fine_groups, C, LANES), BF16),
            ((fine_groups, C, LANES), BF16),
        ],
        [((4 * pairs + 2, 3 * C, LANES), F32), ((4 * pairs, 3 * C, LANES), BF16)],
        flops=8 * 10**9,
    )
    edge_left = send(edge_high, 1, 0)
    edge_right = send(edge_low, -1, 0)
    (joined,) = call(
        weight_kernel,
        (grid, grad_h, grad_d, hidden, early),
        [((32 * C, LANES), BF16)],
        [((EDGE * pairs, C, LANES), BF16), ((VOX, 3 * C), F32), ((4 * C, LANES), F32)],
        flops=12 * 10**9,
    )
    (output,) = call(
        output_kernel,
        (slots, hidden, rects, live, place_back, up_w),
        [((number, C, VOX), BF16)],
        [((number // 2 * C, 1024), BF16), ((number // 2 * C, 1024), BF16)],
        scalars=1,
        flops=8 * 10**9,
    )
    joined, edge_left, edge_right = lax.optimization_barrier((joined, edge_left, edge_right))
    total = reduce_all(joined)
    (input_grad,) = call(
        input_kernel,
        (slots, grad_h, edge_left, edge_right, live, place_back, fine_back),
        [((number, C, VOX), BF16)],
        [
            ((EDGE * pairs + 2, 3 * C, LANES), F32),
            ((number // 2 * C, 1024), BF16),
            ((number // 2 * C, 1024), BF16),
            ((EDGE * pairs, 3 * C, LANES), BF16),
        ],
        scalars=1,
        flops=8 * 10**9,
    )
    scale = 1.0 / math.sqrt(number * VOX * lax.axis_size("gx") * lax.axis_size("gy"))
    fine_total, down_total, coarse_total, up_total = call(
        functools.partial(finish_kernel, scale),
        (total,),
        [((27, C, C), F32), ((8, C, C), F32), ((27, C, C), F32), ((8, C, C), F32)],
    )
    shape_out = (1, 1, number, C, VOX)
    return (
        output.reshape(shape_out),
        input_grad.reshape(shape_out),
        fine_total.transpose(1, 0, 2),
        down_total.transpose(1, 0, 2),
        coarse_total.transpose(1, 0, 2),
        up_total,
    )


def solution(mesh):
    split = P("gx", "gy", None, None, None)
    return jax.shard_map(
        on_device,
        mesh=mesh,
        in_specs=(split, P("gx", "gy", None), P("gx", "gy"), split, P(), P(), P(), P()),
        out_specs=(split, split, P(), P(), P(), P()),
        check_vma=False,
    )
```

```python
import functools
import math

import jax
import jax.numpy as jnp
import numpy as np
from jax import lax
from jax.experimental import pallas as pl
from jax.experimental.pallas import tpu as pltpu
from jax.sharding import PartitionSpec as P

C = 48
EDGE = 8
VOX = 512
LANES = 128
F32 = jnp.float32
BF16 = jnp.bfloat16
SLACK = 8 * 1024 * 1024
SHIFTS = (0, 1, 16, 17)


def placing_matrix():
    place = np.zeros((1024, 8 * LANES), np.float32)
    for z in range(8):
        for y in range(8):
            for x in range(8):
                place[64 * z + 8 * x + y, LANES * y + 16 * z + x + 4] = 1.0
            for x in range(4):
                place[512 + 32 * z + 8 * x + y, LANES * y + 16 * z + x] = 1.0
                place[768 + 32 * z + 8 * x + y, LANES * y + 16 * z + x + 12] = 1.0
    return place


def pair_matrix():
    place = np.zeros((1024, 8 * LANES), np.float32)
    for half in range(2):
        for z in range(8):
            for x in range(8):
                for y in range(8):
                    lane = (16 * z + 8 * half + x + 4) % LANES
                    place[512 * half + 64 * z + 8 * x + y, LANES * y + lane] = 1.0
    return place


def edge_matrix():
    pick = np.zeros((512, 512), np.float32)
    for z in range(8):
        for y in range(8):
            for x in range(8):
                pick[64 * z + 8 * x + y, 256 * (x // 4) + 32 * z + 8 * (x % 4) + y] = 1.0
    return pick


def dot(left, right, contract=(1, 0)):
    dims = (((contract[0],), (contract[1],)), ((), ()))
    return lax.dot_general(left, right, dims, preferred_element_type=F32)


def roll(value, shift):
    return pltpu.roll(value, shift % LANES, 1)


def lane_ids(rows):
    return lax.broadcasted_iota(jnp.int32, (rows, LANES), 1)


def silu_parts(value):
    sigma = 1.0 / (1.0 + jnp.exp(-value))
    return value * sigma, sigma * (1.0 + value * (1.0 - sigma))


def lane_matrix(rows, sources):
    ids = lax.broadcasted_iota(jnp.int32, (rows, LANES), 0)
    lanes = lax.broadcasted_iota(jnp.int32, (rows, LANES), 1)
    blocks = [jnp.where(ids == source(lanes), 1.0, 0.0).astype(BF16) for source in sources]
    return jnp.concatenate(blocks, axis=1) if len(blocks) > 1 else blocks[0]


def move(rows, matrix):
    return dot(rows, matrix).astype(BF16)


def is_own(lane):
    return (lane % 16 >= 4) & (lane % 16 < 12)


def depth_matrix(step, first):
    def below(lane):
        return jnp.where((lane - first) % LANES >= step, (lane - step) % LANES, -1)

    def above(lane):
        return jnp.where((lane - first) % LANES < LANES - step, (lane + step) % LANES, -1)

    return lane_matrix(LANES, [below, above])


def gather_matrix():
    return lane_matrix(LANES, [lambda lane, s=s: (lane + s) % LANES for s in SHIFTS[1:]])


def spread_matrix():
    return lane_matrix(LANES, [lambda lane, s=s: (lane - s) % LANES for s in SHIFTS[1:]])


def pair_matrix_across(step):
    def joined(lane):
        return jnp.where(is_own(lane), lane, LANES + (lane - 8) % LANES)

    def halo(lane):
        return jnp.where(is_own(lane), LANES + (lane - 8) % LANES, lane)

    def left(lane):
        at = (lane - step) % LANES
        return jnp.where(lane % 8 == 4, halo(at), joined(at))

    def right(lane):
        at = (lane + step) % LANES
        return jnp.where(lane % 8 == 4 - step, halo(at), joined(at))

    return lane_matrix(2 * LANES, [left, joined, right])


def inner_matrix(step):
    def left(lane):
        return jnp.where(lane % 8 == 4, -1, (lane - step) % LANES)

    def right(lane):
        return jnp.where(lane % 8 == 4 - step, -1, (lane + step) % LANES)

    return lane_matrix(LANES, [left, right])


def pack_matrix(step):
    def low(lane):
        place = (lane - 4) % 8
        return LANES * place + (lane - place) % LANES

    def high(lane):
        place = (lane - 4) % 8
        return LANES * place + (lane - place + 8 - step) % LANES

    return lane_matrix(8 * LANES, [low, high])


def unpack_matrix(step, right):
    def source(place):
        def from_left(lane):
            return jnp.where(lane % 8 == 4, (lane + place) % LANES, -1)

        def from_right(lane):
            return jnp.where(lane % 8 == 4 - step, (lane - 8 + step + place) % LANES, -1)

        return from_right if right else from_left

    return lane_matrix(LANES, [source(place) for place in range(8)])


def lane_block(array, index):
    return array[:, LANES * index : LANES * (index + 1)]


def depth_stack(bases, matrix):
    moved = move(jnp.concatenate(bases, axis=0), matrix)
    out = []
    for index, base in enumerate(bases):
        rows = moved[3 * C * index : 3 * C * (index + 1)]
        out.append(jnp.concatenate([lane_block(rows, 0), base, lane_block(rows, 1)], axis=0))
    return out


def sub_stack(tiles, matrix):
    moved = move(jnp.concatenate(tiles, axis=0), matrix)
    size = tiles[0].shape[0]
    out = []
    for index, tile in enumerate(tiles):
        rows = moved[size * index : size * (index + 1)]
        out.append(jnp.concatenate([tile] + [lane_block(rows, i) for i in range(3)], axis=0))
    return out


def pair_stack(lowers, uppers, matrix):
    rows = jnp.concatenate(
        [jnp.concatenate([a, b], axis=1) for a, b in zip(lowers, uppers)], axis=0
    )
    moved = move(rows, matrix)
    out = []
    for index in range(len(lowers)):
        part = moved[C * index : C * (index + 1)]
        out.append(jnp.concatenate([lane_block(part, i) for i in range(3)], axis=0))
    return out


def halo_stack(tiles, left_halos, right_halos, matrix):
    inner = dot(jnp.concatenate(tiles, axis=0), matrix)
    out = []
    for index, tile in enumerate(tiles):
        part = inner[C * index : C * (index + 1)]
        left = (lane_block(part, 0) + lane_block(left_halos, index)).astype(BF16)
        right = (lane_block(part, 1) + lane_block(right_halos, index)).astype(BF16)
        out.append(jnp.concatenate([left, tile, right], axis=0))
    return out


def across_columns(tile, step):
    return jnp.concatenate([roll(tile, step), tile, roll(tile, -step)], axis=0)


def anchor_mask(first):
    ids = (lane_ids(C) - first) % LANES
    return (((ids // 16) % 2 == 0) & (ids % 2 == 0)).astype(F32)


def loop(low, high, body, unroll=1):
    def step(index, carry):
        body(index)
        return carry

    lax.fori_loop(low, high, step, 0, unroll=unroll)


def prepare_kernel(
    slots, count, feats, cots, pick, own, cot, flag_rows, x_low, x_high, y_low, y_high, rows_in
):
    number = feats.shape[0]
    rows = lax.broadcasted_iota(jnp.int32, (C, VOX), 0)
    flags = jnp.zeros((C, VOX), F32)
    first = jnp.zeros((), F32)
    last = jnp.zeros((), F32)
    zero = jnp.zeros((C, VOX), BF16)
    for slot in range(number):
        live = slot < count[0]
        alive = jnp.where(live, 1.0, 0.0)
        place = slots[slot]
        block = jnp.where(live, feats[slot], zero)
        own[place] = block
        rows_in[pl.ds(pl.multiple_of(place * C, 16), C), :] = block
        cot[place] = jnp.where(live, cots[slot], zero)
        flags = jnp.where(rows == place + 1, alive, flags)
        first = first + jnp.where(place == 0, alive, 0.0)
        last = last + jnp.where(place == number - 1, alive, 0.0)
    flag_rows[...] = flags.astype(BF16)
    rows_in[number * C :, :] = flags.astype(BF16)
    first_flag = jnp.where(rows == number + 1, first, 0.0).astype(BF16)
    last_flag = jnp.where(rows == 0, last, 0.0).astype(BF16)
    packed = dot(rows_in[...], pick[...]).astype(BF16)
    packed = packed.reshape(number + 1, C, VOX)
    x_low[...] = packed[:, :, :256]
    x_high[...] = packed[:, :, 256:]
    for out, index, flag in ((y_low, 0, first_flag), (y_high, number - 1, last_flag)):
        out[0] = own[index]
        out[1] = cot[index]
        out[2] = flag


def corner_kernel(y_left, y_right, flag_rows, pick, low, high, flags):
    extra = y_left[2] + y_right[2]
    rows = jnp.concatenate([y_left[0], y_right[0], extra], axis=0)
    packed = dot(rows, pick[...]).astype(BF16).reshape(3, C, VOX)
    low[...] = packed[:, :, :256]
    high[...] = packed[:, :, 256:]
    flags[...] = flag_rows[...] + extra


def arrange_weights(
    fine, down, coarse, up, fine_w, fine_b, coarse_w, coarse_b, down_w, down_t, up_w, up_t
):
    for source, fore, back in ((fine, fine_w, fine_b), (coarse, coarse_w, coarse_b)):
        for along in range(3):
            rows = slice(C * along, C * (along + 1))
            turned_rows = slice(C * (2 - along), C * (3 - along))
            ahead = []
            behind = []
            for depth in range(3):
                for across in range(3):
                    ahead.append(source[9 * depth + 3 * across + along])
                    behind.append(source[9 * (2 - depth) + 3 * (2 - across) + along].T)
            fore[rows, :] = jnp.concatenate(ahead, axis=1)
            back[turned_rows, :] = jnp.concatenate(behind, axis=1)
    down_w[...] = jnp.concatenate([down[index] for index in range(8)], axis=1)
    up_t[...] = jnp.concatenate([up[index].T for index in range(8)], axis=1)
    for along in range(2):
        rows = slice(C * along, C * (along + 1))
        turned = [down[2 * index + along].T for index in range(4)]
        down_t[rows, :] = jnp.concatenate(turned, axis=1)
        up_w[rows, :] = jnp.concatenate([up[2 * index + along] for index in range(4)], axis=1)


def place_kernel(
    own, cot, y_left, y_right, flags, place, place_pair, fine, down, coarse, up,
    grid, cot_grid, grad_r, live, fine_w, fine_b, coarse_w, coarse_b, down_w, down_t, up_w, up_t,
    rows_in, rows_cot,
):
    arrange_weights(
        fine, down, coarse, up, fine_w, fine_b, coarse_w, coarse_b, down_w, down_t, up_w, up_t
    )
    number = cot.shape[0]
    last = number + 1
    rows_in[0:C, :] = y_left[0]
    for block in range(number):
        at = (block + 1) * C
        rows_in[at : at + C, :] = own[block]
    rows_in[last * C : (last + 1) * C, :] = y_right[0]
    rows_in[(last + 1) * C :, :] = flags[...]
    pairs = number // 2 + 2
    for group in range(pairs):
        at = group * C
        lower = y_left[1] if group == 0 else cot[group - 1]
        upper = y_right[1] if group == pairs - 1 else cot[group + number // 2 - 1]
        rows_cot[at : at + C, 0:512] = lower
        rows_cot[at : at + C, 512:1024] = upper
    for pair in range(4):
        lanes = slice(256 * pair, 256 * pair + 256)
        placed_cot = dot(rows_cot[...], place_pair[:, lanes])
        placed = dot(rows_in[...], place[:, lanes])
        for half in range(2):
            span = slice(LANES * half, LANES * (half + 1))
            for block in range(last + 1):
                tile = EDGE * block + 2 * pair + half
                grid[tile] = placed[block * C : (block + 1) * C, span].astype(BF16)
            for block in range(pairs):
                tile = EDGE * block + 2 * pair + half
                cot_grid[tile] = placed_cot[block * C : (block + 1) * C, span].astype(BF16)
        if pair == 0:
            live[...] = placed[(last + 1) * C :, 0:LANES]

    gather = gather_matrix()

    def rect_step(block):
        tiles = []
        for inner in range(4):
            tile = EDGE * block + 2 * inner
            tiles.append(jnp.concatenate([cot_grid[tile], cot_grid[tile + 1]], axis=0))
        parts = dot(up_t[...], jnp.concatenate(sub_stack(tiles, gather), axis=1))
        for inner in range(4):
            grad_r[4 * block + inner] = lane_block(parts, inner)

    loop(0, pairs, rect_step, 2)


def conv_sum(parts, tile):
    return parts[tile, 0:C] + parts[tile + 1, C : 2 * C] + parts[tile + 2, 2 * C :]


def conv_steps(parts, weight, load, tiles, step, first, unroll):
    matrix = depth_matrix(step, first)
    spare = jnp.zeros((3 * C, LANES), F32)
    parts[0] = spare
    parts[tiles + 1] = spare

    def body(index):
        tile = 4 * index
        cols = depth_stack([load(tile + i) for i in range(4)], matrix)
        for pair in range(2):
            out = dot(weight[...], jnp.concatenate(cols[2 * pair : 2 * pair + 2], axis=1))
            parts[tile + 2 * pair + 1] = lane_block(out, 0)
            parts[tile + 2 * pair + 2] = lane_block(out, 1)

    loop(0, tiles // 4, body, unroll)


def forward_kernel(
    grid_own, live_own, grad_r, x_left, x_right, c_left, c_right, place, fine_w, down_w, coarse_w,
    grid, hidden, low_cols, rects, grad_c, live, pack_low, pack_high,
    rows_in, fine_p, coarse_p, hidden_all, lowered, live_all,
):
    number = x_left.shape[0] - 1
    last = number + 1
    for block in range(number):
        at = (block + 1) * C
        rows_in[at : at + C, 0:256] = x_left[block]
        rows_in[at : at + C, 256:512] = x_right[block]
    for at, index in ((0, 0), (last * C, 1)):
        rows_in[at : at + C, 0:256] = c_left[index]
        rows_in[at : at + C, 256:512] = c_right[index]
    at = (last + 1) * C
    rows_in[at : at + C, 0:256] = x_left[number] + c_left[2]
    rows_in[at : at + C, 256:512] = x_right[number] + c_right[2]
    for pair in range(4):
        lanes = slice(256 * pair, 256 * pair + 256)
        placed = dot(rows_in[...], place[:, lanes])
        for half in range(2):
            span = slice(LANES * half, LANES * (half + 1))
            for block in range(last + 1):
                tile = EDGE * block + 2 * pair + half
                halo = placed[block * C : (block + 1) * C, span].astype(BF16)
                grid[tile] = grid_own[tile] + halo
        if pair == 0:
            live_all[...] = live_own[...] + placed[(last + 1) * C :, 0:LANES]
    own = is_own(lane_ids(16))
    live[...] = jnp.where(own, live_all[0:16, :], roll(live_all[8:24, :], 8))
    tiles = grid.shape[0]
    conv_steps(fine_p, fine_w, lambda tile: across_columns(grid[tile], 1), tiles, 16, 0, 2)
    anchors = anchor_mask(0)
    gather = gather_matrix()

    def lower_step(block):
        alive = jnp.broadcast_to(live_all[pl.ds(block, 1), :], (C, LANES))
        keep = alive * anchors
        pairs = []
        for inner in range(4):
            actives = []
            for half in range(2):
                tile = EDGE * block + 2 * inner + half
                value = conv_sum(fine_p, tile) * alive
                hidden_all[tile] = value
                actives.append(silu_parts(value)[0].astype(BF16))
            pairs.append(jnp.concatenate(actives, axis=0))
        parts = dot(down_w[...], jnp.concatenate(sub_stack(pairs, gather), axis=1))
        for inner in range(4):
            lowered[4 * block + inner] = (lane_block(parts, inner) * keep).astype(BF16)

    loop(0, last + 1, lower_step, 2)
    pairs = hidden.shape[0] // EDGE
    shift = last - pairs + 1

    own_lanes = is_own(lane_ids(C))
    turn = lane_matrix(LANES, [lambda lane: (lane - 8) % LANES])
    across = pair_matrix_across(2)

    def pair_step(block):
        first = EDGE * (block + shift)
        upper = jnp.concatenate([hidden_all[first + inner] for inner in range(EDGE)], axis=0)
        high = upper.astype(BF16)
        low = (upper - high.astype(F32)).astype(BF16)
        turned = dot(high, turn) + dot(low, turn)
        for inner in range(EDGE):
            tile = EDGE * block + inner
            part = turned[C * inner : C * (inner + 1)]
            hidden[tile] = jnp.where(own_lanes, hidden_all[tile], part)
        lowers = [lowered[4 * block + inner] for inner in range(4)]
        uppers = [lowered[4 * (block + shift) + inner] for inner in range(4)]
        for inner, cols in enumerate(pair_stack(lowers, uppers, across)):
            low_cols[4 * block + inner] = cols

    loop(0, pairs, pair_step, 2)
    conv_steps(coarse_p, coarse_w, lambda tile: low_cols[tile], 4 * pairs, 32, 4, 2)
    pair_anchors = anchor_mask(4)

    def grad_step(block):
        alive = jnp.broadcast_to(live[pl.ds(block, 1), :], (C, LANES))
        keep = alive * pair_anchors
        for inner in range(4):
            coarse = 4 * block + inner
            smooth, slope = silu_parts(conv_sum(coarse_p, coarse))
            rects[coarse] = (smooth * pair_anchors).astype(BF16)
            grad_c[coarse] = (grad_r[coarse] * slope * keep).astype(BF16)

    loop(0, pairs, grad_step, 2)
    pack_columns(grad_c, pack_low, pack_high, 2)


def pack_columns(tiles, low, high, step):
    groups = low.shape[0]
    rows = [
        jnp.concatenate([tiles[8 * group + inner] for inner in range(8)], axis=1)
        for group in range(groups)
    ]
    packed = move(jnp.concatenate(rows, axis=0), pack_matrix(step))
    for group in range(groups):
        part = packed[C * group : C * (group + 1)]
        low[group] = lane_block(part, 0)
        high[group] = lane_block(part, 1)


def fill_columns(tiles, from_left, from_right, out, step):
    matrix = inner_matrix(step)
    left_matrix, right_matrix = unpack_matrix(step, False), unpack_matrix(step, True)

    def body(group):
        left = dot(from_left[group], left_matrix)
        right = dot(from_right[group], right_matrix)
        at = [8 * group + inner for inner in range(8)]
        for tile, cols in zip(at, halo_stack([tiles[i] for i in at], left, right, matrix)):
            out[tile] = cols

    loop(0, from_left.shape[0], body)


def to_blocks(slots, rows_out, place_back, flat, out):
    flat[...] = dot(rows_out[...], place_back[...]).astype(BF16)
    number = out.shape[0]
    for slot in range(number):
        place = slots[slot]
        upper = place >= number // 2
        start = pl.multiple_of(jnp.where(upper, place - number // 2, place) * C, 16)
        rows = flat[pl.ds(start, C), :]
        out[slot] = jnp.where(upper, rows[:, 512:], rows[:, :512])


def stacks(own, tiles):
    parts = [jnp.concatenate([own[t + 1], own[t], own[t - 1]], axis=0) for t in tiles]
    return jnp.concatenate(parts, axis=1)


def flatten_weights(total, out, at):
    turned = total[...].T.astype(BF16)
    for group in range(4):
        out[at + 3 * C * group : at + 3 * C * (group + 1), :] = turned[
            :, LANES * group : LANES * (group + 1)
        ]


def output_kernel(slots, hidden, rects, live, place_back, up_w, out, rows_out, flat):
    pairs = hidden.shape[0] // EDGE
    spread = spread_matrix()

    def block_step(block):
        alive = jnp.broadcast_to(live[pl.ds(block, 1), :], (C, LANES))
        start = pl.multiple_of((block - 1) * C, 16)
        spreads = sub_stack([rects[4 * block + inner] for inner in range(4)], spread)
        upward = dot(up_w[...], jnp.concatenate(spreads, axis=1))
        for inner in range(4):
            for half in range(2):
                part = upward[half * C : (half + 1) * C, LANES * inner : LANES * (inner + 1)]
                value = hidden[EDGE * block + 2 * inner + half] + part
                at = LANES * (2 * inner + half)
                rows_out[pl.ds(start, C), at : at + LANES] = (value * alive).astype(BF16)

    loop(1, pairs - 1, block_step, 2)
    to_blocks(slots, rows_out, place_back, flat, out)


def side_kernel(rects, cot_grid, low_cols, grad_c, flat, grad_own, up_g, coarse_g):
    tiles = low_cols.shape[0]
    up_g[...] = jnp.zeros_like(up_g)
    coarse_g[...] = jnp.zeros_like(coarse_g)

    spread = spread_matrix()

    def up_step(block):
        at = [4 * block + inner for inner in range(4)]
        spreads = sub_stack([rects[tile] for tile in at], spread)
        pairs = [jnp.concatenate([cot_grid[2 * i], cot_grid[2 * i + 1]], axis=0) for i in at]
        up_g[:, 0 : 2 * C] += dot(
            jnp.concatenate(spreads, axis=1), jnp.concatenate(pairs, axis=1), (1, 1)
        )

    loop(1, tiles // 4 - 1, up_step, 2)
    zero = jnp.zeros((C, LANES), BF16)
    for coarse in range(1, 4):
        grad_own[coarse] = zero
        grad_own[tiles - 1 - coarse] = zero

    def copy_step(coarse):
        grad_own[coarse] = grad_c[coarse]

    loop(4, tiles - 4, copy_step, 8)
    matrix = depth_matrix(32, 4)

    def weight_step(index):
        at = [2 + 4 * index + inner for inner in range(4)]
        rights = depth_stack([low_cols[tile] for tile in at], matrix)
        coarse_g[0 : 9 * C, :] += dot(
            jnp.concatenate(rights, axis=1), stacks(grad_own, at), (1, 1)
        )

    loop(0, (tiles - 4) // 4, weight_step, 3)
    flatten_weights(coarse_g, flat, 0)
    flat[12 * C :, :] = up_g[...].astype(BF16)


def backward_kernel(
    grad_c, from_left, from_right, hidden, cot_grid, live, coarse_w, down_t,
    grad_h, grad_d, pack_low, pack_high, coarse_p, grad_x,
):
    tiles = grad_c.shape[0]
    fill_columns(grad_c, from_left, from_right, grad_x, 2)
    conv_steps(coarse_p, coarse_w, lambda tile: grad_x[tile], tiles, 32, 4, 2)
    anchors = anchor_mask(4)
    spread = spread_matrix()

    def step(block):
        alive = jnp.broadcast_to(live[pl.ds(block, 1), :], (C, LANES))
        keep = alive * anchors
        downs = []
        for inner in range(4):
            coarse = 4 * block + inner
            down = (conv_sum(coarse_p, coarse) * keep).astype(BF16)
            grad_d[coarse] = down
            downs.append(down)
        acts = dot(down_t[...], jnp.concatenate(sub_stack(downs, spread), axis=1))
        for inner in range(4):
            for side in range(2):
                tile = EDGE * block + 2 * inner + side
                slope = silu_parts(hidden[tile])[1]
                part = acts[side * C : (side + 1) * C, LANES * inner : LANES * (inner + 1)]
                grad = cot_grid[tile].astype(F32) + part * slope
                grad_h[tile] = (grad * alive).astype(BF16)

    loop(0, tiles // 4, step, 2)
    pack_columns(grad_h, pack_low, pack_high, 1)


def weight_kernel(grid, grad_h, grad_d, hidden, early, joined, grad_own, fine_g, down_g):
    tiles = grad_h.shape[0]
    shift = tiles - 16
    fine_g[...] = jnp.zeros_like(fine_g)
    down_g[...] = jnp.zeros_like(down_g)
    zero = jnp.zeros((C, LANES), BF16)
    for tile in range(3, 8):
        grad_own[tile] = zero
        grad_own[tiles - 1 - tile] = zero

    def copy_step(tile):
        grad_own[tile] = grad_h[tile]

    loop(8, tiles - 8, copy_step, 8)
    matrix = depth_matrix(16, 4)
    across = pair_matrix_across(1)
    spread = spread_matrix()

    def fine_step(index):
        at = [4 + 8 * index + inner for inner in range(8)]
        bases = pair_stack([grid[i] for i in at], [grid[i + shift] for i in at], across)
        rights = depth_stack(bases, matrix)
        fine_g[0 : 9 * C, :] += dot(
            jnp.concatenate(rights, axis=1), stacks(grad_own, at), (1, 1)
        )

    loop(0, (tiles - 8) // 8, fine_step)

    def down_step(index):
        at = [4 + 4 * index + inner for inner in range(4)]
        lefts = sub_stack([grad_d[i] for i in at], spread)
        rights = []
        for coarse in at:
            actives = [silu_parts(hidden[2 * coarse + side])[0].astype(BF16) for side in range(2)]
            rights.append(jnp.concatenate(actives, axis=0))
        down_g[:, 0 : 2 * C] += dot(
            jnp.concatenate(lefts, axis=1), jnp.concatenate(rights, axis=1), (1, 1)
        )

    loop(0, (tiles // 2 - 8) // 4, down_step, 2)
    flatten_weights(fine_g, joined, 0)
    joined[12 * C : 16 * C, :] = down_g[...].astype(BF16)
    joined[16 * C :, :] = early[...]


def input_kernel(
    slots, grad_h, from_left, from_right, live, place_back, fine_w, out,
    fine_p, rows_out, flat, grad_x,
):
    tiles = grad_h.shape[0]
    fill_columns(grad_h, from_left, from_right, grad_x, 1)
    conv_steps(fine_p, fine_w, lambda tile: grad_x[tile], tiles, 16, 4, 2)

    def block_step(block):
        alive = jnp.broadcast_to(live[pl.ds(block, 1), :], (C, LANES))
        start = pl.multiple_of((block - 1) * C, 16)
        for inner in range(EDGE):
            value = conv_sum(fine_p, EDGE * block + inner)
            rows_out[pl.ds(start, C), LANES * inner : LANES * (inner + 1)] = (
                value * alive
            ).astype(BF16)

    loop(1, tiles // EDGE - 1, block_step, 2)
    to_blocks(slots, rows_out, place_back, flat, out)


def finish_kernel(scale, total, fine, down, coarse, up):
    for out, at in ((fine, 0), (coarse, 16 * C)):
        for along in range(3):
            first = at + C * along
            rows = [total[first + 3 * C * g : first + 3 * C * g + C, :] for g in range(4)]
            row = jnp.concatenate(rows, axis=1).astype(F32) * scale
            for index in range(9):
                out[3 * index + along] = row[:, C * index : C * (index + 1)]
    for out, at, turn in ((down, 12 * C, False), (up, 28 * C, True)):
        for index in range(4):
            rows = total[at + C * index : at + C * (index + 1), :].astype(F32) * scale
            for along in range(2):
                part = rows[:, C * along : C * (along + 1)]
                out[2 * index + along] = part.T if turn else part


def call(kernel, inputs, outs, scratch=(), scalars=0, flops=0, limit=None):
    vmem = pl.BlockSpec(memory_space=pltpu.VMEM)
    smem = pl.BlockSpec(memory_space=pltpu.SMEM)
    held = SLACK
    for shape, kind in [(a.shape, a.dtype) for a in inputs[scalars:]] + list(outs) + list(scratch):
        rows, lanes = -(-shape[-2] // 16) * 16, -(-shape[-1] // LANES) * LANES
        held += math.prod(shape[:-2]) * rows * lanes * jnp.dtype(kind).itemsize
    moved = sum(math.prod(s) * jnp.dtype(d).itemsize for s, d in outs)
    moved += sum(math.prod(a.shape) * a.dtype.itemsize for a in inputs)
    return pl.pallas_call(
        kernel,
        out_shape=tuple(jax.ShapeDtypeStruct(s, d) for s, d in outs),
        in_specs=[smem] * scalars + [vmem] * (len(inputs) - scalars),
        out_specs=tuple(vmem for _ in outs),
        scratch_shapes=[pltpu.VMEM(s, d) for s, d in scratch],
        compiler_params=pltpu.CompilerParams(vmem_limit_bytes=limit or held),
        cost_estimate=pl.CostEstimate(flops=flops, bytes_accessed=moved, transcendentals=0),
        name=getattr(kernel, "func", kernel).__name__,
    )(*inputs)


def send(array, step_x, step_y):
    number_x, number_y = lax.axis_size("gx"), lax.axis_size("gy")
    pairs = []
    for i in range(number_x):
        for j in range(number_y):
            to_x, to_y = i + step_x, j + step_y
            if 0 <= to_x < number_x and 0 <= to_y < number_y:
                pairs.append((i * number_y + j, to_x * number_y + to_y))
    return lax.ppermute(array, ("gx", "gy"), pairs)


def reduce_all(joined):
    axes = ("gx", "gy")
    devices = lax.axis_size("gx") * lax.axis_size("gy")
    rows = joined.shape[0]
    share = -(-rows // devices)
    joined = jnp.pad(joined, ((0, share * devices - rows), (0, 0)))
    mine = lax.all_to_all(joined.reshape(devices, share, LANES), axes, 0, 0)
    mine = jnp.sum(mine.astype(F32), axis=0).astype(BF16)
    spread = jnp.broadcast_to(mine[None], (devices, share, LANES))
    full = lax.all_to_all(spread, axes, 0, 0)
    return full.reshape(devices * share, LANES)[:rows]


def on_device(
    features, block_slots, block_count, cotangent, fine_weight, down_weight, coarse_weight,
    up_weight,
):
    number = features.shape[2]
    slots = block_slots.reshape(number)
    count = block_count.reshape(1)
    feats = features.reshape(number, C, VOX)
    cots = cotangent.reshape(number, C, VOX)
    place_own = jnp.asarray(placing_matrix()[:512], BF16)
    place_halo = jnp.asarray(placing_matrix()[512:], BF16)
    place_pair = jnp.asarray(pair_matrix(), BF16)
    place_back = jnp.asarray(pair_matrix().T, BF16)
    pick = jnp.asarray(edge_matrix(), BF16)
    tiles = EDGE * (number + 2)
    coarse_tiles = tiles // 2
    pairs = number // 2 + 2
    groups = pairs // 2
    fine_groups = pairs

    fine_3, down_3, coarse_3 = (
        weight.transpose(1, 0, 2) for weight in (fine_weight, down_weight, coarse_weight)
    )
    own, cot, flag_rows, x_low, x_high, y_low, y_high = call(
        prepare_kernel,
        (slots, count, feats, cots, pick),
        [((number, C, VOX), BF16)] * 2
        + [((C, VOX), BF16)]
        + [((number + 1, C, 256), BF16)] * 2
        + [((3, C, VOX), BF16)] * 2,
        [(((number + 1) * C, VOX), BF16)],
        scalars=2,
        limit=56 * 1024 * 1024,
    )
    x_left = send(x_high, 1, 0)
    x_right = send(x_low, -1, 0)
    y_left = send(y_high, 0, 1)
    y_right = send(y_low, 0, -1)
    corner_low, corner_high, flags = call(
        corner_kernel,
        (y_left, y_right, flag_rows, pick),
        [((3, C, 256), BF16), ((3, C, 256), BF16), ((C, VOX), BF16)],
    )
    c_left = send(corner_high, 1, 0)
    c_right = send(corner_low, -1, 0)
    (grid_own, cot_grid, grad_r, live_own, fine_fore, fine_back, coarse_fore, coarse_back, down_w,
     down_t, up_w, up_t) = call(
        place_kernel,
        (own, cot, y_left, y_right, flags, place_own, place_pair, fine_3, down_3, coarse_3,
         up_weight),
        [
            ((tiles, C, LANES), BF16),
            ((EDGE * pairs, C, LANES), BF16),
            ((4 * pairs, C, LANES), F32),
            ((C, LANES), F32),
        ]
        + [((3 * C, 9 * C), BF16)] * 4
        + [((C, 8 * C), BF16)]
        + [((2 * C, 4 * C), BF16)] * 2
        + [((C, 8 * C), BF16)],
        [(((number + 3) * C, VOX), BF16), ((pairs * C, 1024), BF16)],
        flops=8 * 10**9,
    )
    grid, hidden, low_cols, rects, grad_c, live, pack_low, pack_high = call(
        forward_kernel,
        (grid_own, live_own, grad_r, x_left, x_right, c_left, c_right, place_halo, fine_fore,
         down_w, coarse_fore),
        [
            ((tiles, C, LANES), BF16),
            ((EDGE * pairs, C, LANES), F32),
            ((4 * pairs, 3 * C, LANES), BF16),
            ((4 * pairs, C, LANES), BF16),
            ((4 * pairs, C, LANES), BF16),
            ((16, LANES), F32),
            ((groups, C, LANES), BF16),
            ((groups, C, LANES), BF16),
        ],
        [
            (((number + 3) * C, VOX), BF16),
            ((tiles + 2, 3 * C, LANES), F32),
            ((4 * pairs + 2, 3 * C, LANES), F32),
            ((tiles, C, LANES), F32),
            ((coarse_tiles, C, LANES), BF16),
            ((C, LANES), F32),
        ],
        flops=8 * 10**9,
    )
    grad_left = send(pack_high, 1, 0)
    grad_right = send(pack_low, -1, 0)
    (early,) = call(
        side_kernel,
        (rects, cot_grid, low_cols, grad_c),
        [((16 * C, LANES), BF16)],
        [((4 * pairs, C, LANES), BF16), ((4 * C, LANES), F32), ((VOX, 3 * C), F32)],
        flops=8 * 10**9,
    )
    grad_h, grad_d, edge_low, edge_high = call(
        backward_kernel,
        (grad_c, grad_left, grad_right, hidden, cot_grid, live, coarse_back, down_t),
        [
            ((EDGE * pairs, C, LANES), BF16),
            ((4 * pairs, C, LANES), BF16),
            ((fine_groups, C, LANES), BF16),
            ((fine_groups, C, LANES), BF16),
        ],
        [((4 * pairs + 2, 3 * C, LANES), F32), ((4 * pairs, 3 * C, LANES), BF16)],
        flops=8 * 10**9,
    )
    edge_left = send(edge_high, 1, 0)
    edge_right = send(edge_low, -1, 0)
    (joined,) = call(
        weight_kernel,
        (grid, grad_h, grad_d, hidden, early),
        [((32 * C, LANES), BF16)],
        [((EDGE * pairs, C, LANES), BF16), ((VOX, 3 * C), F32), ((4 * C, LANES), F32)],
        flops=12 * 10**9,
    )
    (output,) = call(
        output_kernel,
        (slots, hidden, rects, live, place_back, up_w),
        [((number, C, VOX), BF16)],
        [((number // 2 * C, 1024), BF16), ((number // 2 * C, 1024), BF16)],
        scalars=1,
        flops=8 * 10**9,
    )
    joined, edge_left, edge_right = lax.optimization_barrier((joined, edge_left, edge_right))
    total = reduce_all(joined)
    (input_grad,) = call(
        input_kernel,
        (slots, grad_h, edge_left, edge_right, live, place_back, fine_back),
        [((number, C, VOX), BF16)],
        [
            ((EDGE * pairs + 2, 3 * C, LANES), F32),
            ((number // 2 * C, 1024), BF16),
            ((number // 2 * C, 1024), BF16),
            ((EDGE * pairs, 3 * C, LANES), BF16),
        ],
        scalars=1,
        flops=8 * 10**9,
    )
    scale = 1.0 / math.sqrt(number * VOX * lax.axis_size("gx") * lax.axis_size("gy"))
    fine_total, down_total, coarse_total, up_total = call(
        functools.partial(finish_kernel, scale),
        (total,),
        [((27, C, C), F32), ((8, C, C), F32), ((27, C, C), F32), ((8, C, C), F32)],
    )
    shape_out = (1, 1, number, C, VOX)
    return (
        output.reshape(shape_out),
        input_grad.reshape(shape_out),
        fine_total.transpose(1, 0, 2),
        down_total.transpose(1, 0, 2),
        coarse_total.transpose(1, 0, 2),
        up_total,
    )


def solution(mesh):
    split = P("gx", "gy", None, None, None)
    return jax.shard_map(
        on_device,
        mesh=mesh,
        in_specs=(split, P("gx", "gy", None), P("gx", "gy"), split, P(), P(), P(), P()),
        out_specs=(split, split, P(), P(), P(), P()),
        check_vma=False,
    )
```

```python
import functools
import math

import jax
import jax.numpy as jnp
from jax import lax
from jax.experimental import pallas as pl
from jax.experimental.pallas import tpu as pltpu
from jax.sharding import PartitionSpec as P

C = 48
EDGE = 8
VOX = 512
LANES = 128
F32 = jnp.float32
BF16 = jnp.bfloat16
SLACK = 8 * 1024 * 1024
SHIFTS = (0, 1, 16, 17)


def marks(rows, columns, row_key, column_key):
    across = column_key(lax.broadcasted_iota(jnp.int32, (1, columns), 1))
    down = row_key(lax.broadcasted_iota(jnp.int32, (rows, 1), 0))
    return jnp.where(down == across, 1.0, 0.0).astype(BF16)


def plain(index):
    return index


def own_source(column):
    lane, y = column % LANES, column // LANES
    x = lane % 16 - 4
    return jnp.where((x >= 0) & (x < 8), 64 * (lane // 16) + 8 * x + y, -1)


def halo_source(column):
    lane, y = column % LANES, column // LANES
    x = lane % 16
    at = 24 * (lane // 16) + y
    left = jnp.where((x >= 1) & (x < 4), at + 8 * (x - 1), -1)
    return jnp.where((x >= 12) & (x < 15), at + 8 * (x - 12) + 256, left)


def pair_source(column):
    lane, y = (column - 4) % LANES, column // LANES
    return 512 * (lane % 16 // 8) + 64 * (lane // 16) + 8 * (lane % 8) + y


def edge_source(column):
    at, side = column % 256, column // 256
    x = at % 24 // 8 + 5 * side
    return jnp.where(at < 192, 64 * (at // 24) + 8 * x + at % 8, -1)


def dot(left, right, contract=(1, 0)):
    dims = (((contract[0],), (contract[1],)), ((), ()))
    return lax.dot_general(left, right, dims, preferred_element_type=F32)


def roll(value, shift):
    return pltpu.roll(value, shift % LANES, 1)


def lane_ids(rows):
    return lax.broadcasted_iota(jnp.int32, (rows, LANES), 1)


def silu_parts(value):
    sigma = 1.0 / (1.0 + jnp.exp(-value))
    return value * sigma, sigma * (1.0 + value * (1.0 - sigma))


def depth_columns(base, masks, step):
    zero = jnp.zeros_like(base)
    below = jnp.where(masks[0], zero, roll(base, step))
    above = jnp.where(masks[1], zero, roll(base, -step))
    return jnp.concatenate([below, base, above], axis=0)


def depth_masks(step, first):
    ids = (lane_ids(3 * C) - first) % LANES
    return ids < step, ids >= LANES - step


def across_columns(tile, step):
    return jnp.concatenate([roll(tile, step), tile, roll(tile, -step)], axis=0)


def pair_columns(tile, halo, step):
    ids = lane_ids(C) % 8
    left = jnp.where(ids == 4, roll(halo, step), roll(tile, step))
    right = jnp.where(ids == 4 - step, roll(halo, -step), roll(tile, -step))
    return jnp.concatenate([left, tile, right], axis=0)


def own_lanes(rows):
    across = lane_ids(rows) % 16
    return (across >= 4) & (across < 12)


def join_halves(lower, upper):
    return jnp.where(own_lanes(lower.shape[0]), lower, roll(upper, 8))


def join_halos(lower, upper):
    return jnp.where(own_lanes(lower.shape[0]), roll(upper, 8), lower)


def packed_halo(from_left, from_right, first, second, place, step):
    ids = lane_ids(C) % 16
    zero = jnp.zeros((C, LANES), BF16)
    halo = jnp.where(ids == 4 - step, roll(from_left[first], 4 - step - place), zero)
    halo = jnp.where(ids == 12 - step, roll(from_left[second], 12 - step - place), halo)
    halo = jnp.where(ids == 12, roll(from_right[first], 12 - place), halo)
    return jnp.where(ids == 4, roll(from_right[second], 20 - place), halo)


def gather_sub(parts):
    total = parts[:C]
    for index in range(1, 4):
        total = total + roll(parts[index * C : (index + 1) * C], -SHIFTS[index])
    return total


def spread_sub(anchored):
    return jnp.concatenate([anchored] + [roll(anchored, step) for step in SHIFTS[1:]], axis=0)


def anchor_mask(first):
    ids = (lane_ids(C) - first) % LANES
    return (((ids // 16) % 2 == 0) & (ids % 2 == 0)).astype(F32)


def loop(low, high, body, unroll=1):
    def step(index, carry):
        body(index)
        return carry

    lax.fori_loop(low, high, step, 0, unroll=unroll)


def join_rows(first, second):
    low = lane_ids(C) < 64
    lead = roll(second[:, :LANES], 64)
    parts = [
        first[:, :LANES],
        jnp.where(low, first[:, LANES:], lead),
        jnp.where(low, lead, roll(second[:, LANES:], 64)),
    ]
    return jnp.concatenate(parts, axis=1)


def split_rows(joined):
    low = lane_ids(C) < 64
    middle = roll(joined[:, LANES : 2 * LANES], 64)
    last = roll(joined[:, 2 * LANES :], 64)
    second = jnp.concatenate([jnp.where(low, middle, last), last], axis=1)
    return joined[:, : 2 * LANES], second


def prepare_kernel(
    slots, count, feats, cots, own, cot, flag_rows, x_low, x_high, y_low, y_high, rows_in
):
    number = feats.shape[0]
    rows = lax.broadcasted_iota(jnp.int32, (16, LANES), 0)
    flags = jnp.zeros((16, LANES), F32)
    first = jnp.zeros((), F32)
    last = jnp.zeros((), F32)
    zero = jnp.zeros((C, VOX), BF16)
    for slot in range(number):
        live = slot < count[0]
        alive = jnp.where(live, 1.0, 0.0)
        place = slots[slot]
        block = jnp.where(live, feats[slot], zero)
        own[place] = block
        rows_in[pl.ds(pl.multiple_of(place * C, 16), C), :] = block
        cot[place] = jnp.where(live, cots[slot], zero)
        flags = jnp.where(rows == place, alive, flags)
        first = first + jnp.where(place == 0, alive, 0.0)
        last = last + jnp.where(place == number - 1, alive, 0.0)
    flag_rows[...] = flags
    packed = dot(rows_in[...], marks(VOX, 512, plain, edge_source)).astype(BF16)
    spare = jnp.zeros((16, 2 * LANES), BF16)
    for out, at in ((x_low, 0), (x_high, 256)):
        for pair in range(number // 2):
            edges = [packed[C * i : C * (i + 1), at : at + 256] for i in (2 * pair, 2 * pair + 1)]
            out[C * pair : C * (pair + 1), :] = join_rows(*edges)
        out[C * number // 2 :, :LANES] = flags.astype(BF16)
        out[C * number // 2 :, LANES:] = spare
    for out, index, flag in ((y_low, 0, first), (y_high, number - 1, last)):
        out[0:C, :] = own[index]
        out[C : 2 * C, :] = cot[index]
        out[2 * C :, :] = (jnp.zeros((16, VOX), F32) + flag).astype(BF16)


def corner_kernel(y_left, y_right, low, high):
    rows = jnp.concatenate([y_left[0:C, :], y_right[0:C, :]], axis=0)
    packed = dot(rows, marks(VOX, 512, plain, edge_source)).astype(BF16)
    ids = lax.broadcasted_iota(jnp.int32, (16, LANES), 0)
    flags = jnp.where(ids == 0, y_left[2 * C :, :LANES], y_right[2 * C :, :LANES])
    spare = jnp.zeros((16, 2 * LANES), BF16)
    for out, at in ((low, 0), (high, 256)):
        out[0:C, :] = join_rows(packed[:C, at : at + 256], packed[C:, at : at + 256])
        out[C:, :LANES] = flags
        out[C:, LANES:] = spare


def arrange_weights(fine, down, coarse, up, fine_w, fine_b, coarse_w, coarse_b, down_w, up_w):
    for source, fore, back in ((fine, fine_w, fine_b), (coarse, coarse_w, coarse_b)):
        for along in range(3):
            rows = slice(C * along, C * (along + 1))
            turned_rows = slice(C * (2 - along), C * (3 - along))
            ahead = []
            behind = []
            for depth in range(3):
                for across in range(3):
                    ahead.append(source[9 * depth + 3 * across + along])
                    behind.append(source[9 * (2 - depth) + 3 * (2 - across) + along].T)
            fore[rows, :] = jnp.concatenate(ahead, axis=1)
            back[turned_rows, :] = jnp.concatenate(behind, axis=1)
    for index in range(4):
        pair = [down[2 * index], down[2 * index + 1]]
        down_w[C * index : C * (index + 1), :] = jnp.concatenate(pair, axis=1)
    for along in range(2):
        row = jnp.concatenate([up[2 * index + along] for index in range(4)], axis=1)
        up_w[C * along : C * (along + 1), :] = row


def place_kernel(
    own, cot, y_left, y_right, c_low, fine, down, coarse, up,
    grid, cot_grid, grad_r, fine_w, fine_b, coarse_w, coarse_b, down_w, up_w,
    rows_in, rows_cot,
):
    arrange_weights(fine, down, coarse, up, fine_w, fine_b, coarse_w, coarse_b, down_w, up_w)
    number = cot.shape[0]
    last = number + 1
    rows_in[0:C, :] = y_left[0:C, :]
    for block in range(number):
        at = (block + 1) * C
        rows_in[at : at + C, :] = own[block]
    rows_in[last * C : (last + 1) * C, :] = y_right[0:C, :]
    pairs = number // 2 + 2
    for group in range(pairs):
        at = group * C
        lower = y_left[C : 2 * C, :] if group == 0 else cot[group - 1]
        upper = y_right[C : 2 * C, :] if group == pairs - 1 else cot[group + number // 2 - 1]
        rows_cot[at : at + C, 0:512] = lower
        rows_cot[at : at + C, 512:1024] = upper
    for pair in range(4):
        placed_cot = dot(
            rows_cot[...], marks(1024, 256, plain, lambda j, at=256 * pair: pair_source(j + at))
        )
        placed = dot(
            rows_in[...], marks(VOX, 256, plain, lambda j, at=256 * pair: own_source(j + at))
        )
        for half in range(2):
            span = slice(LANES * half, LANES * (half + 1))
            for block in range(last + 1):
                tile = EDGE * block + 2 * pair + half
                grid[tile] = placed[block * C : (block + 1) * C, span].astype(BF16)
            for block in range(pairs):
                tile = EDGE * block + 2 * pair + half
                cot_grid[tile] = placed_cot[block * C : (block + 1) * C, span].astype(BF16)

    def rect_step(block):
        tiles = []
        for inner in range(4):
            tile = EDGE * block + 2 * inner
            tiles.append(jnp.concatenate([cot_grid[tile], cot_grid[tile + 1]], axis=0))
        parts = dot(up_w[...], jnp.concatenate(tiles, axis=1), (0, 0))
        for inner in range(4):
            grad_r[4 * block + inner] = gather_sub(parts[:, LANES * inner : LANES * (inner + 1)])

    loop(0, pairs, rect_step, 2)


def conv_sum(parts, tile):
    return parts[tile, 0:C] + parts[tile + 1, C : 2 * C] + parts[tile + 2, 2 * C :]


def conv_steps(parts, weight, load, tiles, step, first, unroll):
    masks = depth_masks(step, first)
    spare = jnp.zeros((3 * C, LANES), F32)
    parts[0] = spare
    parts[tiles + 1] = spare

    def body(index):
        tile = 4 * index
        cols = [depth_columns(load(tile + i), masks, step) for i in range(4)]
        out = dot(weight[...], jnp.concatenate(cols, axis=1))
        for i in range(4):
            parts[tile + i + 1] = out[:, LANES * i : LANES * (i + 1)]

    loop(0, tiles // 4, body, unroll)


def forward_kernel(
    grid_own, flags, y_left, y_right, grad_r, x_left, x_right, c_left, c_right, fine_w, down_w,
    coarse_w,
    grid, hidden, low_cols, rects, grad_c, live, pack_low, pack_high,
    rows_in, fine_p, coarse_p, hidden_all, lowered, live_all,
):
    number = 2 * (x_left.shape[0] - 16) // C
    last = number + 1
    for at, left, right in ((0, x_left, x_right), (None, c_left, c_right)):
        for pair in range((left.shape[0] - 16) // C):
            rows = slice(C * pair, C * (pair + 1))
            lefts, rights = split_rows(left[rows, :]), split_rows(right[rows, :])
            for inner in range(2):
                block = last * inner if at is None else 2 * pair + inner + 1
                rows_in[block * C : (block + 1) * C, 0:256] = lefts[inner]
                rows_in[block * C : (block + 1) * C, 256:512] = rights[inner]
    across = lane_ids(16) % 16
    for start, middle, left, right in (
        (1, flags[...], x_left[number // 2 * C :, :LANES], x_right[number // 2 * C :, :LANES]),
        (0, y_left[2 * C :, :LANES], c_left[C:, :LANES], c_right[C:, :LANES]),
        (last, y_right[2 * C :, :LANES], c_left[C:, :LANES], c_right[C:, :LANES]),
    ):
        rows = jnp.where(across < 4, left.astype(F32), middle.astype(F32))
        rows = jnp.where(across >= 12, right.astype(F32), rows)
        if start == 1:
            live_all[1 : number + 1, :] = rows
        else:
            at = 0 if start == 0 else 1
            live_all[start : start + 1, :] = rows[at : at + 1, :]
    for pair in range(4):
        placed = dot(
            rows_in[...], marks(512, 256, plain, lambda j, at=256 * pair: halo_source(j + at))
        )
        for half in range(2):
            span = slice(LANES * half, LANES * (half + 1))
            for block in range(last + 1):
                tile = EDGE * block + 2 * pair + half
                halo = placed[block * C : (block + 1) * C, span].astype(BF16)
                grid[tile] = grid_own[tile] + halo
    live[...] = join_halves(live_all[0:16, :], live_all[8:24, :])
    tiles = grid.shape[0]
    conv_steps(fine_p, fine_w, lambda tile: across_columns(grid[tile], 1), tiles, 16, 0, 2)
    anchors = anchor_mask(0)

    def lower_step(block):
        alive = jnp.broadcast_to(live_all[pl.ds(block, 1), :], (C, LANES))
        keep = alive * anchors
        pairs = []
        for inner in range(4):
            actives = []
            for half in range(2):
                tile = EDGE * block + 2 * inner + half
                value = conv_sum(fine_p, tile) * alive
                hidden_all[tile] = value
                actives.append(silu_parts(value)[0].astype(BF16))
            pairs.append(jnp.concatenate(actives, axis=0))
        parts = dot(down_w[...], jnp.concatenate(pairs, axis=1))
        for inner in range(4):
            total = gather_sub(parts[:, LANES * inner : LANES * (inner + 1)])
            lowered[4 * block + inner] = (total * keep).astype(BF16)

    loop(0, last + 1, lower_step, 2)
    pairs = hidden.shape[0] // EDGE
    shift = last - pairs + 1

    def pair_step(block):
        for inner in range(EDGE):
            tile = EDGE * block + inner
            hidden[tile] = join_halves(hidden_all[tile], hidden_all[tile + EDGE * shift])
        for inner in range(4):
            tile = 4 * block + inner
            lower, upper = lowered[tile], lowered[tile + 4 * shift]
            low_cols[tile] = pair_columns(join_halves(lower, upper), join_halos(lower, upper), 2)

    loop(0, pairs, pair_step, 2)
    conv_steps(coarse_p, coarse_w, lambda tile: low_cols[tile], 4 * pairs, 32, 4, 2)
    pair_anchors = anchor_mask(4)

    def grad_step(block):
        alive = jnp.broadcast_to(live[pl.ds(block, 1), :], (C, LANES))
        keep = alive * pair_anchors
        for inner in range(4):
            coarse = 4 * block + inner
            smooth, slope = silu_parts(conv_sum(coarse_p, coarse))
            rects[coarse] = (smooth * pair_anchors).astype(BF16)
            grad_c[coarse] = (grad_r[coarse] * slope * keep).astype(BF16)

    loop(0, pairs, grad_step, 2)
    ids = lane_ids(C)
    zero = jnp.zeros((C, LANES), BF16)
    half = 2 * number
    for out, lane in ((pack_low, 4), (pack_high, 10)):
        for group in range(out.shape[0]):
            total = zero
            for coarse in range(max(2, 32 * group), min(2 * half + 6, 32 * group + 32)):
                upper = coarse >= half + 4
                tile = grad_c[coarse - half] if upper else grad_c[coarse]
                at = lane + 8 if upper else lane
                picked = jnp.where(ids % 32 == at, tile, zero)
                total = total + roll(picked, coarse % 32 - at)
            out[group] = total


def to_blocks(slots, rows_out, flat, out):
    flat[...] = dot(rows_out[...], marks(1024, 1024, pair_source, plain)).astype(BF16)
    number = out.shape[0]
    for slot in range(number):
        place = slots[slot]
        upper = place >= number // 2
        start = pl.multiple_of(jnp.where(upper, place - number // 2, place) * C, 16)
        rows = flat[pl.ds(start, C), :]
        out[slot] = jnp.where(upper, rows[:, 512:], rows[:, :512])


def stacks(own, tiles):
    parts = [jnp.concatenate([own[t + 1], own[t], own[t - 1]], axis=0) for t in tiles]
    return jnp.concatenate(parts, axis=1)


def flatten_weights(total, out, at):
    turned = total[...].T.astype(BF16)
    for group in range(4):
        out[at + 3 * C * group : at + 3 * C * (group + 1), :] = turned[
            :, LANES * group : LANES * (group + 1)
        ]


def output_kernel(slots, hidden, rects, live, up_w, out, rows_out, flat):
    pairs = hidden.shape[0] // EDGE

    def block_step(block):
        alive = jnp.broadcast_to(live[pl.ds(block, 1), :], (C, LANES))
        start = pl.multiple_of((block - 1) * C, 16)
        spreads = [spread_sub(rects[4 * block + inner]) for inner in range(4)]
        upward = dot(up_w[...], jnp.concatenate(spreads, axis=1))
        for inner in range(4):
            for half in range(2):
                part = upward[half * C : (half + 1) * C, LANES * inner : LANES * (inner + 1)]
                value = hidden[EDGE * block + 2 * inner + half] + part
                at = LANES * (2 * inner + half)
                rows_out[pl.ds(start, C), at : at + LANES] = (value * alive).astype(BF16)

    loop(1, pairs - 1, block_step, 2)
    to_blocks(slots, rows_out, flat, out)


def side_kernel(rects, cot_grid, low_cols, grad_c, flat, grad_own, up_g, coarse_g):
    tiles = low_cols.shape[0]
    up_g[...] = jnp.zeros_like(up_g)
    coarse_g[...] = jnp.zeros_like(coarse_g)

    def up_step(block):
        spreads = []
        pairs = []
        for inner in range(4):
            coarse = 4 * block + inner
            spreads.append(spread_sub(rects[coarse]))
            pairs.append(
                jnp.concatenate([cot_grid[2 * coarse], cot_grid[2 * coarse + 1]], axis=0)
            )
        up_g[:, 0 : 2 * C] += dot(
            jnp.concatenate(spreads, axis=1), jnp.concatenate(pairs, axis=1), (1, 1)
        )

    loop(1, tiles // 4 - 1, up_step, 2)
    zero = jnp.zeros((C, LANES), BF16)
    for coarse in range(1, 4):
        grad_own[coarse] = zero
        grad_own[tiles - 1 - coarse] = zero

    def copy_step(coarse):
        grad_own[coarse] = grad_c[coarse]

    loop(4, tiles - 4, copy_step, 8)
    masks = depth_masks(32, 4)

    def weight_step(index):
        at = [2 + 4 * index + inner for inner in range(4)]
        rights = [depth_columns(low_cols[tile], masks, 32) for tile in at]
        coarse_g[0 : 9 * C, :] += dot(
            jnp.concatenate(rights, axis=1), stacks(grad_own, at), (1, 1)
        )

    loop(0, (tiles - 4) // 4, weight_step, 3)
    flatten_weights(coarse_g, flat, 0)
    flat[12 * C :, :] = up_g[...].astype(BF16)


def backward_kernel(
    grad_c, from_left, from_right, hidden, cot_grid, live, coarse_w, down_w,
    grad_h, grad_d, pack_low, pack_high, coarse_p, grad_x,
):
    tiles = grad_c.shape[0]
    half = tiles - 8
    for coarse in range(tiles):
        first, second = coarse // 32, (coarse + half) // 32
        halo = packed_halo(from_left, from_right, first, second, coarse % 32, 2)
        grad_x[coarse] = pair_columns(grad_c[coarse], halo, 2)
    conv_steps(coarse_p, coarse_w, lambda tile: grad_x[tile], tiles, 32, 4, 2)
    anchors = anchor_mask(4)

    def step(block):
        alive = jnp.broadcast_to(live[pl.ds(block, 1), :], (C, LANES))
        keep = alive * anchors
        spreads = []
        for inner in range(4):
            coarse = 4 * block + inner
            down = (conv_sum(coarse_p, coarse) * keep).astype(BF16)
            grad_d[coarse] = down
            spreads.append(spread_sub(down))
        acts = dot(down_w[...], jnp.concatenate(spreads, axis=1), (0, 0))
        for inner in range(4):
            for side in range(2):
                tile = EDGE * block + 2 * inner + side
                slope = silu_parts(hidden[tile])[1]
                part = acts[side * C : (side + 1) * C, LANES * inner : LANES * (inner + 1)]
                grad = cot_grid[tile].astype(F32) + part * slope
                grad_h[tile] = (grad * alive).astype(BF16)

    loop(0, tiles // 4, step, 2)
    fine = 2 * tiles
    shift = fine - 16
    ids = lane_ids(C) % 16
    zero = jnp.zeros((C, LANES), BF16)
    for out, lane in ((pack_low, 4), (pack_high, 11)):
        for group in range(out.shape[0]):
            total = zero
            for tile in range(16 * group, 16 * group + 16):
                upper = tile >= shift + 8
                source = grad_h[tile - shift] if upper else grad_h[tile]
                at = lane + 8 if upper else lane
                picked = jnp.where(ids == at % 16, source, zero)
                total = total + roll(picked, tile % 16 - at)
            out[group] = total


def weight_kernel(grid, grad_h, grad_d, hidden, early, joined, grad_own, fine_g, down_g):
    tiles = grad_h.shape[0]
    shift = tiles - 16
    fine_g[...] = jnp.zeros_like(fine_g)
    down_g[...] = jnp.zeros_like(down_g)
    zero = jnp.zeros((C, LANES), BF16)
    for tile in range(3, 8):
        grad_own[tile] = zero
        grad_own[tiles - 1 - tile] = zero

    def copy_step(tile):
        grad_own[tile] = grad_h[tile]

    loop(8, tiles - 8, copy_step, 8)
    masks = depth_masks(16, 4)

    def fine_step(index):
        at = [4 + 8 * index + inner for inner in range(8)]
        rights = []
        for tile in at:
            lower, upper = grid[tile], grid[tile + shift]
            base = pair_columns(join_halves(lower, upper), join_halos(lower, upper), 1)
            rights.append(depth_columns(base, masks, 16))
        fine_g[0 : 9 * C, :] += dot(
            jnp.concatenate(rights, axis=1), stacks(grad_own, at), (1, 1)
        )

    loop(0, (tiles - 8) // 8, fine_step)

    def down_step(index):
        lefts = []
        rights = []
        for inner in range(4):
            coarse = 4 + 4 * index + inner
            lefts.append(spread_sub(grad_d[coarse]))
            actives = [silu_parts(hidden[2 * coarse + side])[0].astype(BF16) for side in range(2)]
            rights.append(jnp.concatenate(actives, axis=0))
        down_g[:, 0 : 2 * C] += dot(
            jnp.concatenate(lefts, axis=1), jnp.concatenate(rights, axis=1), (1, 1)
        )

    loop(0, (tiles // 2 - 8) // 4, down_step, 2)
    flatten_weights(fine_g, joined, 0)
    joined[12 * C : 16 * C, :] = down_g[...].astype(BF16)
    joined[16 * C :, :] = early[...]


def input_kernel(
    slots, grad_h, from_left, from_right, live, fine_w, out,
    fine_p, rows_out, flat, grad_x,
):
    tiles = grad_h.shape[0]
    shift = tiles - 16

    def fill_step(group):
        for inner in range(16):
            tile = 16 * group + inner
            second = group + shift // 16
            halo = packed_halo(from_left, from_right, group, second, inner, 1)
            grad_x[tile] = pair_columns(grad_h[tile], halo, 1)

    loop(0, tiles // 16, fill_step)
    conv_steps(fine_p, fine_w, lambda tile: grad_x[tile], tiles, 16, 4, 2)

    def block_step(block):
        alive = jnp.broadcast_to(live[pl.ds(block, 1), :], (C, LANES))
        start = pl.multiple_of((block - 1) * C, 16)
        for inner in range(EDGE):
            value = conv_sum(fine_p, EDGE * block + inner)
            rows_out[pl.ds(start, C), LANES * inner : LANES * (inner + 1)] = (
                value * alive
            ).astype(BF16)

    loop(1, tiles // EDGE - 1, block_step, 2)
    to_blocks(slots, rows_out, flat, out)


def finish_kernel(scale, total, fine, down, coarse, up):
    for out, at in ((fine, 0), (coarse, 16 * C)):
        for along in range(3):
            first = at + C * along
            rows = [total[first + 3 * C * g : first + 3 * C * g + C, :] for g in range(4)]
            row = jnp.concatenate(rows, axis=1).astype(F32) * scale
            for index in range(9):
                out[3 * index + along] = row[:, C * index : C * (index + 1)]
    for out, at, turn in ((down, 12 * C, False), (up, 28 * C, True)):
        for index in range(4):
            rows = total[at + C * index : at + C * (index + 1), :].astype(F32) * scale
            for along in range(2):
                part = rows[:, C * along : C * (along + 1)]
                out[2 * index + along] = part.T if turn else part


def call(kernel, inputs, outs, scratch=(), scalars=0, flops=0, limit=None):
    vmem = pl.BlockSpec(memory_space=pltpu.VMEM)
    smem = pl.BlockSpec(memory_space=pltpu.SMEM)
    held = SLACK
    for shape, kind in [(a.shape, a.dtype) for a in inputs[scalars:]] + list(outs) + list(scratch):
        rows, lanes = -(-shape[-2] // 16) * 16, -(-shape[-1] // LANES) * LANES
        held += math.prod(shape[:-2]) * rows * lanes * jnp.dtype(kind).itemsize
    moved = sum(math.prod(s) * jnp.dtype(d).itemsize for s, d in outs)
    moved += sum(math.prod(a.shape) * a.dtype.itemsize for a in inputs)
    return pl.pallas_call(
        kernel,
        out_shape=tuple(jax.ShapeDtypeStruct(s, d) for s, d in outs),
        in_specs=[smem] * scalars + [vmem] * (len(inputs) - scalars),
        out_specs=tuple(vmem for _ in outs),
        scratch_shapes=[pltpu.VMEM(s, d) for s, d in scratch],
        compiler_params=pltpu.CompilerParams(vmem_limit_bytes=limit or held),
        cost_estimate=pl.CostEstimate(flops=flops, bytes_accessed=moved, transcendentals=0),
        name=getattr(kernel, "func", kernel).__name__,
    )(*inputs)


def send(array, step_x, step_y):
    number_x, number_y = lax.axis_size("gx"), lax.axis_size("gy")
    pairs = []
    for i in range(number_x):
        for j in range(number_y):
            to_x, to_y = i + step_x, j + step_y
            if 0 <= to_x < number_x and 0 <= to_y < number_y:
                pairs.append((i * number_y + j, to_x * number_y + to_y))
    return lax.ppermute(array, ("gx", "gy"), pairs)


def reduce_share(joined):
    devices = lax.axis_size("gx") * lax.axis_size("gy")
    rows = joined.shape[0]
    share = -(-rows // devices)
    joined = jnp.pad(joined, ((0, share * devices - rows), (0, 0)))
    mine = lax.all_to_all(joined.reshape(devices, share, LANES), ("gx", "gy"), 0, 0)
    return jnp.sum(mine.astype(F32), axis=0).astype(BF16)


def spread_share(share):
    devices = lax.axis_size("gx") * lax.axis_size("gy")
    rows = share.shape[0]
    copies = jnp.broadcast_to(share[None], (devices, rows, LANES))
    full = lax.all_to_all(copies, ("gx", "gy"), 0, 0)
    return full.reshape(devices * rows, LANES)


def on_device(
    features, block_slots, block_count, cotangent, fine_weight, down_weight, coarse_weight,
    up_weight,
):
    number = features.shape[2]
    slots = block_slots.reshape(number)
    count = block_count.reshape(1)
    feats = features.reshape(number, C, VOX)
    cots = cotangent.reshape(number, C, VOX)
    tiles = EDGE * (number + 2)
    coarse_tiles = tiles // 2
    pairs = number // 2 + 2
    groups = -(-coarse_tiles // 32)
    fine_groups = tiles // 16

    fine_3, down_3, coarse_3 = (
        weight.transpose(1, 0, 2) for weight in (fine_weight, down_weight, coarse_weight)
    )
    own, cot, flag_rows, x_low, x_high, y_low, y_high = call(
        prepare_kernel,
        (slots, count, feats, cots),
        [((number, C, VOX), BF16)] * 2
        + [((16, LANES), F32)]
        + [((number // 2 * C + 16, 384), BF16)] * 2
        + [((2 * C + 16, VOX), BF16)] * 2,
        [((number * C, VOX), BF16)],
        scalars=2,
        limit=56 * 1024 * 1024,
    )
    x_left = send(x_high, 1, 0)
    x_right = send(x_low, -1, 0)
    y_left = send(y_high, 0, 1)
    y_right = send(y_low, 0, -1)
    corner_low, corner_high = call(
        corner_kernel,
        (y_left, y_right),
        [((C + 16, 384), BF16), ((C + 16, 384), BF16)],
    )
    c_left = send(corner_high, 1, 0)
    c_right = send(corner_low, -1, 0)
    (grid_own, cot_grid, grad_r, fine_fore, fine_back, coarse_fore, coarse_back, down_w,
     up_w) = call(
        place_kernel,
        (own, cot, y_left, y_right, corner_low, fine_3, down_3, coarse_3, up_weight),
        [
            ((tiles, C, LANES), BF16),
            ((EDGE * pairs, C, LANES), BF16),
            ((4 * pairs, C, LANES), F32),
        ]
        + [((3 * C, 9 * C), BF16)] * 4
        + [((4 * C, 2 * C), BF16), ((2 * C, 4 * C), BF16)],
        [(((number + 2) * C, VOX), BF16), ((pairs * C, 1024), BF16)],
        flops=8 * 10**9,
    )
    grid, hidden, low_cols, rects, grad_c, live, pack_low, pack_high = call(
        forward_kernel,
        (grid_own, flag_rows, y_left, y_right, grad_r, x_left, x_right, c_left, c_right,
         fine_fore, down_w, coarse_fore),
        [
            ((tiles, C, LANES), BF16),
            ((EDGE * pairs, C, LANES), F32),
            ((4 * pairs, 3 * C, LANES), BF16),
            ((4 * pairs, C, LANES), BF16),
            ((4 * pairs, C, LANES), BF16),
            ((16, LANES), F32),
            ((groups, C, LANES), BF16),
            ((groups, C, LANES), BF16),
        ],
        [
            (((number + 2) * C, VOX), BF16),
            ((tiles + 2, 3 * C, LANES), F32),
            ((4 * pairs + 2, 3 * C, LANES), F32),
            ((tiles, C, LANES), F32),
            ((coarse_tiles, C, LANES), BF16),
            ((C, LANES), F32),
        ],
        flops=8 * 10**9,
    )
    grad_left = send(pack_high, 1, 0)
    grad_right = send(pack_low, -1, 0)
    (early,) = call(
        side_kernel,
        (rects, cot_grid, low_cols, grad_c),
        [((16 * C, LANES), BF16)],
        [((4 * pairs, C, LANES), BF16), ((4 * C, LANES), F32), ((VOX, 3 * C), F32)],
        flops=8 * 10**9,
    )
    grad_h, grad_d, edge_low, edge_high = call(
        backward_kernel,
        (grad_c, grad_left, grad_right, hidden, cot_grid, live, coarse_back, down_w),
        [
            ((EDGE * pairs, C, LANES), BF16),
            ((4 * pairs, C, LANES), BF16),
            ((fine_groups, C, LANES), BF16),
            ((fine_groups, C, LANES), BF16),
        ],
        [((4 * pairs + 2, 3 * C, LANES), F32), ((4 * pairs, 3 * C, LANES), BF16)],
        flops=8 * 10**9,
    )
    edge_left = send(edge_high, 1, 0)
    edge_right = send(edge_low, -1, 0)
    (joined,) = call(
        weight_kernel,
        (grid, grad_h, grad_d, hidden, early),
        [((32 * C, LANES), BF16)],
        [((EDGE * pairs, C, LANES), BF16), ((VOX, 3 * C), F32), ((4 * C, LANES), F32)],
        flops=12 * 10**9,
    )
    joined, edge_left, edge_right, slots = lax.optimization_barrier(
        (joined, edge_left, edge_right, slots)
    )
    share = reduce_share(joined)
    (output,) = call(
        output_kernel,
        (slots, hidden, rects, live, up_w),
        [((number, C, VOX), BF16)],
        [((number // 2 * C, 1024), BF16), ((number // 2 * C, 1024), BF16)],
        scalars=1,
        flops=8 * 10**9,
    )
    (input_grad,) = call(
        input_kernel,
        (slots, grad_h, edge_left, edge_right, live, fine_back),
        [((number, C, VOX), BF16)],
        [
            ((EDGE * pairs + 2, 3 * C, LANES), F32),
            ((number // 2 * C, 1024), BF16),
            ((number // 2 * C, 1024), BF16),
            ((EDGE * pairs, 3 * C, LANES), BF16),
        ],
        scalars=1,
        flops=8 * 10**9,
    )
    share, output, input_grad = lax.optimization_barrier((share, output, input_grad))
    total = spread_share(share)
    scale = 1.0 / math.sqrt(number * VOX * lax.axis_size("gx") * lax.axis_size("gy"))
    fine_total, down_total, coarse_total, up_total = call(
        functools.partial(finish_kernel, scale),
        (total,),
        [((27, C, C), F32), ((8, C, C), F32), ((27, C, C), F32), ((8, C, C), F32)],
    )
    shape_out = (1, 1, number, C, VOX)
    return (
        output.reshape(shape_out),
        input_grad.reshape(shape_out),
        fine_total.transpose(1, 0, 2),
        down_total.transpose(1, 0, 2),
        coarse_total.transpose(1, 0, 2),
        up_total,
    )


def solution(mesh):
    split = P("gx", "gy", None, None, None)
    return jax.shard_map(
        on_device,
        mesh=mesh,
        in_specs=(split, P("gx", "gy", None), P("gx", "gy"), split, P(), P(), P(), P()),
        out_specs=(split, split, P(), P(), P(), P()),
        check_vma=False,
    )
```

```python
import functools
import math

import jax
import jax.numpy as jnp
from jax import lax
from jax.experimental import pallas as pl
from jax.experimental.pallas import tpu as pltpu
from jax.sharding import PartitionSpec as P

C = 48
EDGE = 8
VOX = 512
LANES = 128
F32 = jnp.float32
BF16 = jnp.bfloat16
SLACK = 8 * 1024 * 1024
SHIFTS = (0, 1, 16, 17)


def marks(rows, columns, row_key, column_key):
    across = column_key(lax.broadcasted_iota(jnp.int32, (1, columns), 1))
    down = row_key(lax.broadcasted_iota(jnp.int32, (rows, 1), 0))
    return jnp.where(down == across, 1.0, 0.0).astype(BF16)


def plain(index):
    return index


def own_source(column):
    lane, y = column % LANES, column // LANES
    x = lane % 16 - 4
    return jnp.where((x >= 0) & (x < 8), 64 * (lane // 16) + 8 * x + y, -1)


def halo_source(column):
    lane, y = column % LANES, column // LANES
    x = lane % 16
    at = 24 * (lane // 16) + y
    left = jnp.where((x >= 1) & (x < 4), at + 8 * (x - 1), -1)
    return jnp.where((x >= 12) & (x < 15), at + 8 * (x - 12) + 256, left)


def pair_source(column):
    lane, y = (column - 4) % LANES, column // LANES
    return 512 * (lane % 16 // 8) + 64 * (lane // 16) + 8 * (lane % 8) + y


def edge_source(column):
    at, side = column % 256, column // 256
    x = at % 24 // 8 + 5 * side
    return jnp.where(at < 192, 64 * (at // 24) + 8 * x + at % 8, -1)


def dot(left, right, contract=(1, 0)):
    dims = (((contract[0],), (contract[1],)), ((), ()))
    return lax.dot_general(left, right, dims, preferred_element_type=F32)


def roll(value, shift):
    return pltpu.roll(value, shift % LANES, 1)


def lane_ids(rows):
    return lax.broadcasted_iota(jnp.int32, (rows, LANES), 1)


def silu_parts(value):
    sigma = 1.0 / (1.0 + jnp.exp(-value))
    return value * sigma, sigma * (1.0 + value * (1.0 - sigma))


def depth_columns(base, masks, step):
    zero = jnp.zeros_like(base)
    below = jnp.where(masks[0], zero, roll(base, step))
    above = jnp.where(masks[1], zero, roll(base, -step))
    return jnp.concatenate([below, base, above], axis=0)


def depth_masks(step, first):
    ids = (lane_ids(3 * C) - first) % LANES
    return ids < step, ids >= LANES - step


def across_columns(tile, step):
    return jnp.concatenate([roll(tile, step), tile, roll(tile, -step)], axis=0)


def pair_columns(tile, halo, step):
    ids = lane_ids(C) % 8
    left = jnp.where(ids == 4, roll(halo, step), roll(tile, step))
    right = jnp.where(ids == 4 - step, roll(halo, -step), roll(tile, -step))
    return jnp.concatenate([left, tile, right], axis=0)


def own_lanes(rows):
    across = lane_ids(rows) % 16
    return (across >= 4) & (across < 12)


def join_halves(lower, upper):
    return jnp.where(own_lanes(lower.shape[0]), lower, roll(upper, 8))


def join_halos(lower, upper):
    return jnp.where(own_lanes(lower.shape[0]), roll(upper, 8), lower)


def packed_halo(from_left, from_right, first, second, place, step):
    ids = lane_ids(C) % 16
    zero = jnp.zeros((C, LANES), BF16)
    halo = jnp.where(ids == 4 - step, roll(from_left[first], 4 - step - place), zero)
    halo = jnp.where(ids == 12 - step, roll(from_left[second], 12 - step - place), halo)
    halo = jnp.where(ids == 12, roll(from_right[first], 12 - place), halo)
    return jnp.where(ids == 4, roll(from_right[second], 20 - place), halo)


def gather_sub(parts):
    total = parts[:C]
    for index in range(1, 4):
        total = total + roll(parts[index * C : (index + 1) * C], -SHIFTS[index])
    return total


def spread_sub(anchored):
    return jnp.concatenate([anchored] + [roll(anchored, step) for step in SHIFTS[1:]], axis=0)


def anchor_mask(first):
    ids = (lane_ids(C) - first) % LANES
    return (((ids // 16) % 2 == 0) & (ids % 2 == 0)).astype(F32)


def loop(low, high, body, unroll=1):
    def step(index, carry):
        body(index)
        return carry

    lax.fori_loop(low, high, step, 0, unroll=unroll)


def join_rows(first, second):
    low = lane_ids(C) < 64
    lead = roll(second[:, :LANES], 64)
    parts = [
        first[:, :LANES],
        jnp.where(low, first[:, LANES:], lead),
        jnp.where(low, lead, roll(second[:, LANES:], 64)),
    ]
    return jnp.concatenate(parts, axis=1)


def split_rows(joined):
    low = lane_ids(C) < 64
    middle = roll(joined[:, LANES : 2 * LANES], 64)
    last = roll(joined[:, 2 * LANES :], 64)
    second = jnp.concatenate([jnp.where(low, middle, last), last], axis=1)
    return joined[:, : 2 * LANES], second


def prepare_kernel(slots, count, feats, cots, flag_rows, x_low, x_high, y_low, y_high, rows_in):
    number = feats.shape[0]
    rows = lax.broadcasted_iota(jnp.int32, (16, LANES), 0)
    flags = jnp.zeros((16, LANES), F32)
    zero = jnp.zeros((C, VOX), BF16)
    first = jnp.zeros((), jnp.int32)
    last = jnp.zeros((), jnp.int32)
    for slot in range(number):
        live = slot < count[0]
        place = slots[slot]
        block = jnp.where(live, feats[slot], zero)
        rows_in[pl.ds(pl.multiple_of(place * C, 16), C), :] = block
        flags = jnp.where(rows == place, jnp.where(live, 1.0, 0.0), flags)
        first = jnp.where(place == 0, slot, first)
        last = jnp.where(place == number - 1, slot, last)
    flag_rows[...] = flags
    packed = dot(rows_in[...], marks(VOX, 512, plain, edge_source)).astype(BF16)
    spare = jnp.zeros((16, 2 * LANES), BF16)
    for out, at in ((x_low, 0), (x_high, 256)):
        for pair in range(number // 2):
            edges = [packed[C * i : C * (i + 1), at : at + 256] for i in (2 * pair, 2 * pair + 1)]
            out[C * pair : C * (pair + 1), :] = join_rows(*edges)
        out[C * number // 2 :, :LANES] = flags.astype(BF16)
        out[C * number // 2 :, LANES:] = spare
    for out, index, slot in ((y_low, 0, first), (y_high, number - 1, last)):
        live = slot < count[0]
        out[0:C, :] = rows_in[C * index : C * (index + 1), :]
        out[C : 2 * C, :] = jnp.where(live, cots[slot], zero)
        out[2 * C :, :] = (jnp.zeros((16, VOX), F32) + jnp.where(live, 1.0, 0.0)).astype(BF16)


def corner_kernel(y_left, y_right, low, high):
    rows = jnp.concatenate([y_left[0:C, :], y_right[0:C, :]], axis=0)
    packed = dot(rows, marks(VOX, 512, plain, edge_source)).astype(BF16)
    ids = lax.broadcasted_iota(jnp.int32, (16, LANES), 0)
    flags = jnp.where(ids == 0, y_left[2 * C :, :LANES], y_right[2 * C :, :LANES])
    spare = jnp.zeros((16, 2 * LANES), BF16)
    for out, at in ((low, 0), (high, 256)):
        out[0:C, :] = join_rows(packed[:C, at : at + 256], packed[C:, at : at + 256])
        out[C:, :LANES] = flags
        out[C:, LANES:] = spare


def arrange_weights(fine, down, coarse, up, fine_w, fine_b, coarse_w, coarse_b, down_w, up_w):
    for source, fore, back in ((fine, fine_w, fine_b), (coarse, coarse_w, coarse_b)):
        for along in range(3):
            rows = slice(C * along, C * (along + 1))
            turned_rows = slice(C * (2 - along), C * (3 - along))
            ahead = []
            behind = []
            for depth in range(3):
                for across in range(3):
                    ahead.append(source[9 * depth + 3 * across + along])
                    behind.append(source[9 * (2 - depth) + 3 * (2 - across) + along].T)
            fore[rows, :] = jnp.concatenate(ahead, axis=1)
            back[turned_rows, :] = jnp.concatenate(behind, axis=1)
    for index in range(4):
        pair = [down[2 * index], down[2 * index + 1]]
        down_w[C * index : C * (index + 1), :] = jnp.concatenate(pair, axis=1)
    for along in range(2):
        row = jnp.concatenate([up[2 * index + along] for index in range(4)], axis=1)
        up_w[C * along : C * (along + 1), :] = row


def place_kernel(
    slots, count, feats, cots, y_left, y_right, c_low, fine, down, coarse, up,
    grid, cot_grid, grad_r, fine_w, fine_b, coarse_w, coarse_b, down_w, up_w,
    rows_in, rows_cot, cot,
):
    arrange_weights(fine, down, coarse, up, fine_w, fine_b, coarse_w, coarse_b, down_w, up_w)
    number = feats.shape[0]
    last = number + 1
    zero = jnp.zeros((C, VOX), BF16)
    rows_in[0:C, :] = y_left[0:C, :]
    rows_in[last * C : (last + 1) * C, :] = y_right[0:C, :]
    for slot in range(number):
        live = slot < count[0]
        place = slots[slot]
        start = pl.multiple_of((place + 1) * C, 16)
        rows_in[pl.ds(start, C), :] = jnp.where(live, feats[slot], zero)
        cot[place] = jnp.where(live, cots[slot], zero)
    pairs = number // 2 + 2
    for group in range(pairs):
        at = group * C
        lower = y_left[C : 2 * C, :] if group == 0 else cot[group - 1]
        upper = y_right[C : 2 * C, :] if group == pairs - 1 else cot[group + number // 2 - 1]
        rows_cot[at : at + C, 0:512] = lower
        rows_cot[at : at + C, 512:1024] = upper
    for pair in range(4):
        placed_cot = dot(
            rows_cot[...], marks(1024, 256, plain, lambda j, at=256 * pair: pair_source(j + at))
        )
        placed = dot(
            rows_in[...], marks(VOX, 256, plain, lambda j, at=256 * pair: own_source(j + at))
        )
        for half in range(2):
            span = slice(LANES * half, LANES * (half + 1))
            for block in range(last + 1):
                tile = EDGE * block + 2 * pair + half
                grid[tile] = placed[block * C : (block + 1) * C, span].astype(BF16)
            for block in range(pairs):
                tile = EDGE * block + 2 * pair + half
                cot_grid[tile] = placed_cot[block * C : (block + 1) * C, span].astype(BF16)

    def rect_step(block):
        tiles = []
        for inner in range(4):
            tile = EDGE * block + 2 * inner
            tiles.append(jnp.concatenate([cot_grid[tile], cot_grid[tile + 1]], axis=0))
        parts = dot(up_w[...], jnp.concatenate(tiles, axis=1), (0, 0))
        for inner in range(4):
            grad_r[4 * block + inner] = gather_sub(parts[:, LANES * inner : LANES * (inner + 1)])

    loop(0, pairs, rect_step, 2)


def conv_sum(parts, tile):
    return parts[tile, 0:C] + parts[tile + 1, C : 2 * C] + parts[tile + 2, 2 * C :]


def conv_steps(parts, weight, load, tiles, step, first, unroll):
    masks = depth_masks(step, first)
    spare = jnp.zeros((3 * C, LANES), F32)
    parts[0] = spare
    parts[tiles + 1] = spare

    def body(index):
        tile = 4 * index
        cols = [depth_columns(load(tile + i), masks, step) for i in range(4)]
        out = dot(weight[...], jnp.concatenate(cols, axis=1))
        for i in range(4):
            parts[tile + i + 1] = out[:, LANES * i : LANES * (i + 1)]

    loop(0, tiles // 4, body, unroll)


def forward_kernel(
    grid_own, flags, y_left, y_right, grad_r, x_left, x_right, c_left, c_right, fine_w, down_w,
    coarse_w,
    grid, hidden, low_cols, rects, grad_c, live, pack_low, pack_high,
    rows_in, fine_p, coarse_p, hidden_all, lowered, live_all, ring,
):
    number = 2 * (x_left.shape[0] - 16) // C
    last = number + 1
    for at, left, right in ((0, x_left, x_right), (None, c_left, c_right)):
        for pair in range((left.shape[0] - 16) // C):
            rows = slice(C * pair, C * (pair + 1))
            lefts, rights = split_rows(left[rows, :]), split_rows(right[rows, :])
            for inner in range(2):
                block = last * inner if at is None else 2 * pair + inner + 1
                rows_in[block * C : (block + 1) * C, 0:256] = lefts[inner]
                rows_in[block * C : (block + 1) * C, 256:512] = rights[inner]
    across = lane_ids(16) % 16
    for start, middle, left, right in (
        (1, flags[...], x_left[number // 2 * C :, :LANES], x_right[number // 2 * C :, :LANES]),
        (0, y_left[2 * C :, :LANES], c_left[C:, :LANES], c_right[C:, :LANES]),
        (last, y_right[2 * C :, :LANES], c_left[C:, :LANES], c_right[C:, :LANES]),
    ):
        rows = jnp.where(across < 4, left.astype(F32), middle.astype(F32))
        rows = jnp.where(across >= 12, right.astype(F32), rows)
        if start == 1:
            live_all[1 : number + 1, :] = rows
        else:
            at = 0 if start == 0 else 1
            live_all[start : start + 1, :] = rows[at : at + 1, :]
    for pair in range(4):
        placed = dot(
            rows_in[...], marks(512, 256, plain, lambda j, at=256 * pair: halo_source(j + at))
        )
        for half in range(2):
            span = slice(LANES * half, LANES * (half + 1))
            for block in range(last + 1):
                tile = EDGE * block + 2 * pair + half
                halo = placed[block * C : (block + 1) * C, span].astype(BF16)
                grid[tile] = grid_own[tile] + halo
    live[...] = join_halves(live_all[0:16, :], live_all[8:24, :])
    tiles = grid.shape[0]
    anchors = anchor_mask(0)
    masks = depth_masks(16, 0)
    blocks = last + 1
    ring[1] = jnp.zeros(ring.shape[1:], BF16)

    def fine_step(index):
        block = jnp.maximum(index - 3, 0)
        alive = jnp.broadcast_to(live_all[pl.ds(block, 1), :], (C, LANES))
        keep = alive * anchors
        pairs = []
        for inner in range(4):
            actives = []
            for half in range(2):
                tile = EDGE * block + 2 * inner + half
                value = conv_sum(fine_p, tile + EDGE - 1) * alive
                hidden_all[tile] = value
                actives.append(silu_parts(value)[0].astype(BF16))
            pairs.append(jnp.concatenate(actives, axis=0))
        parts = dot(down_w[...], jnp.concatenate(pairs, axis=1))
        for inner in range(4):
            total = gather_sub(parts[:, LANES * inner : LANES * (inner + 1)])
            lowered[4 * block + inner] = (total * keep).astype(BF16)
        ready = lax.rem(index + 1, 2)
        for quad in range(2):
            out = dot(fine_w[...], ring[ready, quad])
            for i in range(4):
                fine_p[EDGE * index + 4 * quad + i] = out[:, LANES * i : LANES * (i + 1)]
        first = EDGE * jnp.minimum(index, blocks - 1)
        for inner in range(EDGE):
            cols = depth_columns(across_columns(grid[first + inner], 1), masks, 16)
            ring[lax.rem(index, 2), inner // 4, :, LANES * (inner % 4) : LANES * (inner % 4 + 1)] = cols

    loop(0, blocks + 3, fine_step)
    pairs = hidden.shape[0] // EDGE
    shift = last - pairs + 1

    def pair_step(block):
        for inner in range(EDGE):
            tile = EDGE * block + inner
            hidden[tile] = join_halves(hidden_all[tile], hidden_all[tile + EDGE * shift])
        for inner in range(4):
            tile = 4 * block + inner
            lower, upper = lowered[tile], lowered[tile + 4 * shift]
            low_cols[tile] = pair_columns(join_halves(lower, upper), join_halos(lower, upper), 2)

    loop(0, pairs, pair_step, 2)
    conv_steps(coarse_p, coarse_w, lambda tile: low_cols[tile], 4 * pairs, 32, 4, 2)
    pair_anchors = anchor_mask(4)

    def grad_step(block):
        alive = jnp.broadcast_to(live[pl.ds(block, 1), :], (C, LANES))
        keep = alive * pair_anchors
        for inner in range(4):
            coarse = 4 * block + inner
            smooth, slope = silu_parts(conv_sum(coarse_p, coarse))
            rects[coarse] = (smooth * pair_anchors).astype(BF16)
            grad_c[coarse] = (grad_r[coarse] * slope * keep).astype(BF16)

    loop(0, pairs, grad_step, 2)
    ids = lane_ids(C)
    zero = jnp.zeros((C, LANES), BF16)
    half = 2 * number
    for out, lane in ((pack_low, 4), (pack_high, 10)):
        for group in range(out.shape[0]):
            total = zero
            for coarse in range(max(2, 32 * group), min(2 * half + 6, 32 * group + 32)):
                upper = coarse >= half + 4
                tile = grad_c[coarse - half] if upper else grad_c[coarse]
                at = lane + 8 if upper else lane
                picked = jnp.where(ids % 32 == at, tile, zero)
                total = total + roll(picked, coarse % 32 - at)
            out[group] = total


def to_blocks(slots, rows_out, flat, out):
    flat[...] = dot(rows_out[...], marks(1024, 1024, pair_source, plain)).astype(BF16)
    number = out.shape[0]
    for slot in range(number):
        place = slots[slot]
        upper = place >= number // 2
        start = pl.multiple_of(jnp.where(upper, place - number // 2, place) * C, 16)
        rows = flat[pl.ds(start, C), :]
        out[slot] = jnp.where(upper, rows[:, 512:], rows[:, :512])


def stacks(own, tiles):
    parts = [jnp.concatenate([own[t + 1], own[t], own[t - 1]], axis=0) for t in tiles]
    return jnp.concatenate(parts, axis=1)


def flatten_weights(total, out, at):
    turned = total[...].T.astype(BF16)
    for group in range(4):
        out[at + 3 * C * group : at + 3 * C * (group + 1), :] = turned[
            :, LANES * group : LANES * (group + 1)
        ]


def output_kernel(slots, hidden, rects, live, up_w, out, rows_out, flat):
    pairs = hidden.shape[0] // EDGE

    def block_step(block):
        alive = jnp.broadcast_to(live[pl.ds(block, 1), :], (C, LANES))
        start = pl.multiple_of((block - 1) * C, 16)
        spreads = [spread_sub(rects[4 * block + inner]) for inner in range(4)]
        upward = dot(up_w[...], jnp.concatenate(spreads, axis=1))
        for inner in range(4):
            for half in range(2):
                part = upward[half * C : (half + 1) * C, LANES * inner : LANES * (inner + 1)]
                value = hidden[EDGE * block + 2 * inner + half] + part
                at = LANES * (2 * inner + half)
                rows_out[pl.ds(start, C), at : at + LANES] = (value * alive).astype(BF16)

    loop(1, pairs - 1, block_step, 2)
    to_blocks(slots, rows_out, flat, out)


def side_kernel(rects, cot_grid, low_cols, grad_c, flat, grad_own, up_g, coarse_g):
    tiles = low_cols.shape[0]
    up_g[...] = jnp.zeros_like(up_g)
    coarse_g[...] = jnp.zeros_like(coarse_g)

    def up_step(block):
        spreads = []
        pairs = []
        for inner in range(4):
            coarse = 4 * block + inner
            spreads.append(spread_sub(rects[coarse]))
            pairs.append(
                jnp.concatenate([cot_grid[2 * coarse], cot_grid[2 * coarse + 1]], axis=0)
            )
        up_g[:, 0 : 2 * C] += dot(
            jnp.concatenate(spreads, axis=1), jnp.concatenate(pairs, axis=1), (1, 1)
        )

    loop(1, tiles // 4 - 1, up_step, 2)
    zero = jnp.zeros((C, LANES), BF16)
    for coarse in range(1, 4):
        grad_own[coarse] = zero
        grad_own[tiles - 1 - coarse] = zero

    def copy_step(coarse):
        grad_own[coarse] = grad_c[coarse]

    loop(4, tiles - 4, copy_step, 8)
    masks = depth_masks(32, 4)

    def weight_step(index):
        at = [2 + 4 * index + inner for inner in range(4)]
        rights = [depth_columns(low_cols[tile], masks, 32) for tile in at]
        coarse_g[0 : 9 * C, :] += dot(
            jnp.concatenate(rights, axis=1), stacks(grad_own, at), (1, 1)
        )

    loop(0, (tiles - 4) // 4, weight_step, 3)
    flatten_weights(coarse_g, flat, 0)
    flat[12 * C :, :] = up_g[...].astype(BF16)


def backward_kernel(
    grad_c, from_left, from_right, hidden, cot_grid, live, coarse_w, down_w,
    grad_h, grad_d, pack_low, pack_high, coarse_p, grad_x,
):
    tiles = grad_c.shape[0]
    half = tiles - 8
    for coarse in range(tiles):
        first, second = coarse // 32, (coarse + half) // 32
        halo = packed_halo(from_left, from_right, first, second, coarse % 32, 2)
        grad_x[coarse] = pair_columns(grad_c[coarse], halo, 2)
    conv_steps(coarse_p, coarse_w, lambda tile: grad_x[tile], tiles, 32, 4, 2)
    anchors = anchor_mask(4)

    def step(block):
        alive = jnp.broadcast_to(live[pl.ds(block, 1), :], (C, LANES))
        keep = alive * anchors
        spreads = []
        for inner in range(4):
            coarse = 4 * block + inner
            down = (conv_sum(coarse_p, coarse) * keep).astype(BF16)
            grad_d[coarse] = down
            spreads.append(spread_sub(down))
        acts = dot(down_w[...], jnp.concatenate(spreads, axis=1), (0, 0))
        for inner in range(4):
            for side in range(2):
                tile = EDGE * block + 2 * inner + side
                slope = silu_parts(hidden[tile])[1]
                part = acts[side * C : (side + 1) * C, LANES * inner : LANES * (inner + 1)]
                grad = cot_grid[tile].astype(F32) + part * slope
                grad_h[tile] = (grad * alive).astype(BF16)

    loop(0, tiles // 4, step, 2)
    fine = 2 * tiles
    shift = fine - 16
    ids = lane_ids(C) % 16
    zero = jnp.zeros((C, LANES), BF16)
    for out, lane in ((pack_low, 4), (pack_high, 11)):
        for group in range(out.shape[0]):
            total = zero
            for tile in range(16 * group, 16 * group + 16):
                upper = tile >= shift + 8
                source = grad_h[tile - shift] if upper else grad_h[tile]
                at = lane + 8 if upper else lane
                picked = jnp.where(ids == at % 16, source, zero)
                total = total + roll(picked, tile % 16 - at)
            out[group] = total


def weight_kernel(grid, grad_h, grad_d, hidden, early, joined, grad_own, fine_g, down_g, ring):
    tiles = grad_h.shape[0]
    shift = tiles - 16
    fine_g[...] = jnp.zeros_like(fine_g)
    down_g[...] = jnp.zeros_like(down_g)
    zero = jnp.zeros((C, LANES), BF16)
    for tile in range(3, 8):
        grad_own[tile] = zero
        grad_own[tiles - 1 - tile] = zero

    def copy_step(tile):
        grad_own[tile] = grad_h[tile]

    loop(8, tiles - 8, copy_step, 8)
    masks = depth_masks(16, 4)

    steps = (tiles - 8) // 8
    ring[1] = jnp.zeros(ring.shape[1:], BF16)

    def fine_step(index):
        at = [4 + 8 * jnp.maximum(index - 1, 0) + inner for inner in range(8)]
        fine_g[0 : 9 * C, :] += dot(ring[lax.rem(index + 1, 2)], stacks(grad_own, at), (1, 1))
        first = 4 + 8 * jnp.minimum(index, steps - 1)
        for inner in range(8):
            lower, upper = grid[first + inner], grid[first + inner + shift]
            base = pair_columns(join_halves(lower, upper), join_halos(lower, upper), 1)
            ring[lax.rem(index, 2), :, LANES * inner : LANES * (inner + 1)] = depth_columns(
                base, masks, 16
            )

    loop(0, steps + 1, fine_step)

    def down_step(index):
        lefts = []
        rights = []
        for inner in range(4):
            coarse = 4 + 4 * index + inner
            lefts.append(spread_sub(grad_d[coarse]))
            actives = [silu_parts(hidden[2 * coarse + side])[0].astype(BF16) for side in range(2)]
            rights.append(jnp.concatenate(actives, axis=0))
        down_g[:, 0 : 2 * C] += dot(
            jnp.concatenate(lefts, axis=1), jnp.concatenate(rights, axis=1), (1, 1)
        )

    loop(0, (tiles // 2 - 8) // 4, down_step, 2)
    flatten_weights(fine_g, joined, 0)
    joined[12 * C : 16 * C, :] = down_g[...].astype(BF16)
    joined[16 * C :, :] = early[...]


def input_kernel(
    slots, grad_h, from_left, from_right, live, fine_w, out,
    fine_p, rows_out, flat, grad_x,
):
    tiles = grad_h.shape[0]
    shift = tiles - 16

    def fill_step(group):
        for inner in range(16):
            tile = 16 * group + inner
            second = group + shift // 16
            halo = packed_halo(from_left, from_right, group, second, inner, 1)
            grad_x[tile] = pair_columns(grad_h[tile], halo, 1)

    loop(0, tiles // 16, fill_step)
    conv_steps(fine_p, fine_w, lambda tile: grad_x[tile], tiles, 16, 4, 2)

    def block_step(block):
        alive = jnp.broadcast_to(live[pl.ds(block, 1), :], (C, LANES))
        start = pl.multiple_of((block - 1) * C, 16)
        for inner in range(EDGE):
            value = conv_sum(fine_p, EDGE * block + inner)
            rows_out[pl.ds(start, C), LANES * inner : LANES * (inner + 1)] = (
                value * alive
            ).astype(BF16)

    loop(1, tiles // EDGE - 1, block_step, 2)
    to_blocks(slots, rows_out, flat, out)


def finish_kernel(scale, total, fine, down, coarse, up):
    for out, at in ((fine, 0), (coarse, 16 * C)):
        for along in range(3):
            first = at + C * along
            rows = [total[first + 3 * C * g : first + 3 * C * g + C, :] for g in range(4)]
            row = jnp.concatenate(rows, axis=1).astype(F32) * scale
            for index in range(9):
                out[3 * index + along] = row[:, C * index : C * (index + 1)]
    for out, at, turn in ((down, 12 * C, False), (up, 28 * C, True)):
        for index in range(4):
            rows = total[at + C * index : at + C * (index + 1), :].astype(F32) * scale
            for along in range(2):
                part = rows[:, C * along : C * (along + 1)]
                out[2 * index + along] = part.T if turn else part


def call(kernel, inputs, outs, scratch=(), scalars=0, flops=0, limit=None):
    vmem = pl.BlockSpec(memory_space=pltpu.VMEM)
    smem = pl.BlockSpec(memory_space=pltpu.SMEM)
    held = SLACK
    for shape, kind in [(a.shape, a.dtype) for a in inputs[scalars:]] + list(outs) + list(scratch):
        rows, lanes = -(-shape[-2] // 16) * 16, -(-shape[-1] // LANES) * LANES
        held += math.prod(shape[:-2]) * rows * lanes * jnp.dtype(kind).itemsize
    moved = sum(math.prod(s) * jnp.dtype(d).itemsize for s, d in outs)
    moved += sum(math.prod(a.shape) * a.dtype.itemsize for a in inputs)
    return pl.pallas_call(
        kernel,
        out_shape=tuple(jax.ShapeDtypeStruct(s, d) for s, d in outs),
        in_specs=[smem] * scalars + [vmem] * (len(inputs) - scalars),
        out_specs=tuple(vmem for _ in outs),
        scratch_shapes=[pltpu.VMEM(s, d) for s, d in scratch],
        compiler_params=pltpu.CompilerParams(vmem_limit_bytes=limit or held),
        cost_estimate=pl.CostEstimate(flops=flops, bytes_accessed=moved, transcendentals=0),
        name=getattr(kernel, "func", kernel).__name__,
    )(*inputs)


def send(array, step_x, step_y):
    number_x, number_y = lax.axis_size("gx"), lax.axis_size("gy")
    pairs = []
    for i in range(number_x):
        for j in range(number_y):
            to_x, to_y = i + step_x, j + step_y
            if 0 <= to_x < number_x and 0 <= to_y < number_y:
                pairs.append((i * number_y + j, to_x * number_y + to_y))
    return lax.ppermute(array, ("gx", "gy"), pairs)


def reduce_share(joined):
    devices = lax.axis_size("gx") * lax.axis_size("gy")
    rows = joined.shape[0]
    share = -(-rows // devices)
    joined = jnp.pad(joined, ((0, share * devices - rows), (0, 0)))
    mine = lax.all_to_all(joined.reshape(devices, share, LANES), ("gx", "gy"), 0, 0)
    return jnp.sum(mine.astype(F32), axis=0).astype(BF16)


def spread_share(share):
    devices = lax.axis_size("gx") * lax.axis_size("gy")
    rows = share.shape[0]
    copies = jnp.broadcast_to(share[None], (devices, rows, LANES))
    full = lax.all_to_all(copies, ("gx", "gy"), 0, 0)
    return full.reshape(devices * rows, LANES)


def on_device(
    features, block_slots, block_count, cotangent, fine_weight, down_weight, coarse_weight,
    up_weight,
):
    number = features.shape[2]
    slots = block_slots.reshape(number)
    count = block_count.reshape(1)
    feats = features.reshape(number, C, VOX)
    cots = cotangent.reshape(number, C, VOX)
    tiles = EDGE * (number + 2)
    coarse_tiles = tiles // 2
    pairs = number // 2 + 2
    groups = -(-coarse_tiles // 32)
    fine_groups = tiles // 16

    fine_3, down_3, coarse_3 = (
        weight.transpose(1, 0, 2) for weight in (fine_weight, down_weight, coarse_weight)
    )
    flag_rows, x_low, x_high, y_low, y_high = call(
        prepare_kernel,
        (slots, count, feats, cots),
        [((16, LANES), F32)]
        + [((number // 2 * C + 16, 384), BF16)] * 2
        + [((2 * C + 16, VOX), BF16)] * 2,
        [((number * C, VOX), BF16)],
        scalars=2,
        limit=56 * 1024 * 1024,
    )
    x_left = send(x_high, 1, 0)
    x_right = send(x_low, -1, 0)
    y_left = send(y_high, 0, 1)
    y_right = send(y_low, 0, -1)
    corner_low, corner_high = call(
        corner_kernel,
        (y_left, y_right),
        [((C + 16, 384), BF16), ((C + 16, 384), BF16)],
    )
    c_left = send(corner_high, 1, 0)
    c_right = send(corner_low, -1, 0)
    (grid_own, cot_grid, grad_r, fine_fore, fine_back, coarse_fore, coarse_back, down_w,
     up_w) = call(
        place_kernel,
        (slots, count, feats, cots, y_left, y_right, corner_low, fine_3, down_3, coarse_3,
         up_weight),
        [
            ((tiles, C, LANES), BF16),
            ((EDGE * pairs, C, LANES), BF16),
            ((4 * pairs, C, LANES), F32),
        ]
        + [((3 * C, 9 * C), BF16)] * 4
        + [((4 * C, 2 * C), BF16), ((2 * C, 4 * C), BF16)],
        [
            (((number + 2) * C, VOX), BF16),
            ((pairs * C, 1024), BF16),
            ((number, C, VOX), BF16),
        ],
        scalars=2,
        flops=8 * 10**9,
    )
    grid, hidden, low_cols, rects, grad_c, live, pack_low, pack_high = call(
        forward_kernel,
        (grid_own, flag_rows, y_left, y_right, grad_r, x_left, x_right, c_left, c_right,
         fine_fore, down_w, coarse_fore),
        [
            ((tiles, C, LANES), BF16),
            ((EDGE * pairs, C, LANES), F32),
            ((4 * pairs, 3 * C, LANES), BF16),
            ((4 * pairs, C, LANES), BF16),
            ((4 * pairs, C, LANES), BF16),
            ((16, LANES), F32),
            ((groups, C, LANES), BF16),
            ((groups, C, LANES), BF16),
        ],
        [
            (((number + 2) * C, VOX), BF16),
            ((tiles + 3 * EDGE, 3 * C, LANES), F32),
            ((4 * pairs + 2, 3 * C, LANES), F32),
            ((tiles, C, LANES), F32),
            ((coarse_tiles, C, LANES), BF16),
            ((C, LANES), F32),
            ((2, 2, 9 * C, 4 * LANES), BF16),
        ],
        flops=8 * 10**9,
    )
    grad_left = send(pack_high, 1, 0)
    grad_right = send(pack_low, -1, 0)
    (early,) = call(
        side_kernel,
        (rects, cot_grid, low_cols, grad_c),
        [((16 * C, LANES), BF16)],
        [((4 * pairs, C, LANES), BF16), ((4 * C, LANES), F32), ((VOX, 3 * C), F32)],
        flops=8 * 10**9,
    )
    grad_h, grad_d, edge_low, edge_high = call(
        backward_kernel,
        (grad_c, grad_left, grad_right, hidden, cot_grid, live, coarse_back, down_w),
        [
            ((EDGE * pairs, C, LANES), BF16),
            ((4 * pairs, C, LANES), BF16),
            ((fine_groups, C, LANES), BF16),
            ((fine_groups, C, LANES), BF16),
        ],
        [((4 * pairs + 2, 3 * C, LANES), F32), ((4 * pairs, 3 * C, LANES), BF16)],
        flops=8 * 10**9,
    )
    edge_left = send(edge_high, 1, 0)
    edge_right = send(edge_low, -1, 0)
    (joined,) = call(
        weight_kernel,
        (grid, grad_h, grad_d, hidden, early),
        [((32 * C, LANES), BF16)],
        [
            ((EDGE * pairs, C, LANES), BF16),
            ((VOX, 3 * C), F32),
            ((4 * C, LANES), F32),
            ((2, 9 * C, 8 * LANES), BF16),
        ],
        flops=12 * 10**9,
    )
    joined, edge_left, edge_right, slots = lax.optimization_barrier(
        (joined, edge_left, edge_right, slots)
    )
    share = reduce_share(joined)
    (output,) = call(
        output_kernel,
        (slots, hidden, rects, live, up_w),
        [((number, C, VOX), BF16)],
        [((number // 2 * C, 1024), BF16), ((number // 2 * C, 1024), BF16)],
        scalars=1,
        flops=8 * 10**9,
    )
    share, output, slots = lax.optimization_barrier((share, output, slots))
    (input_grad,) = call(
        input_kernel,
        (slots, grad_h, edge_left, edge_right, live, fine_back),
        [((number, C, VOX), BF16)],
        [
            ((EDGE * pairs + 2, 3 * C, LANES), F32),
            ((number // 2 * C, 1024), BF16),
            ((number // 2 * C, 1024), BF16),
            ((EDGE * pairs, 3 * C, LANES), BF16),
        ],
        scalars=1,
        flops=8 * 10**9,
    )
    total = spread_share(share)
    scale = 1.0 / math.sqrt(number * VOX * lax.axis_size("gx") * lax.axis_size("gy"))
    fine_total, down_total, coarse_total, up_total = call(
        functools.partial(finish_kernel, scale),
        (total,),
        [((27, C, C), F32), ((8, C, C), F32), ((27, C, C), F32), ((8, C, C), F32)],
    )
    shape_out = (1, 1, number, C, VOX)
    return (
        output.reshape(shape_out),
        input_grad.reshape(shape_out),
        fine_total.transpose(1, 0, 2),
        down_total.transpose(1, 0, 2),
        coarse_total.transpose(1, 0, 2),
        up_total,
    )


def solution(mesh):
    split = P("gx", "gy", None, None, None)
    return jax.shard_map(
        on_device,
        mesh=mesh,
        in_specs=(split, P("gx", "gy", None), P("gx", "gy"), split, P(), P(), P(), P()),
        out_specs=(split, split, P(), P(), P(), P()),
        check_vma=False,
    )
```

```python
import functools
import math

import jax
import jax.numpy as jnp
from jax import lax
from jax.experimental import pallas as pl
from jax.experimental.pallas import tpu as pltpu
from jax.sharding import PartitionSpec as P

C = 48
EDGE = 8
VOX = 512
LANES = 128
F32 = jnp.float32
BF16 = jnp.bfloat16
SLACK = 8 * 1024 * 1024
SHIFTS = (0, 1, 16, 17)


def marks(rows, columns, row_key, column_key):
    across = column_key(lax.broadcasted_iota(jnp.int32, (1, columns), 1))
    down = row_key(lax.broadcasted_iota(jnp.int32, (rows, 1), 0))
    return jnp.where(down == across, 1.0, 0.0).astype(BF16)


def plain(index):
    return index


def own_source(column):
    lane, y = column % LANES, column // LANES
    x = lane % 16 - 4
    return jnp.where((x >= 0) & (x < 8), 64 * (lane // 16) + 8 * x + y, -1)


def halo_source(column):
    lane, y = column % LANES, column // LANES
    x = lane % 16
    at = 24 * (lane // 16) + y
    left = jnp.where((x >= 1) & (x < 4), at + 8 * (x - 1), -1)
    return jnp.where((x >= 12) & (x < 15), at + 8 * (x - 12) + 256, left)


def pair_source(column):
    lane, y = (column - 4) % LANES, column // LANES
    return 512 * (lane % 16 // 8) + 64 * (lane // 16) + 8 * (lane % 8) + y


def edge_source(column):
    at, side = column % 256, column // 256
    x = at % 24 // 8 + 5 * side
    return jnp.where(at < 192, 64 * (at // 24) + 8 * x + at % 8, -1)


def dot(left, right, contract=(1, 0)):
    dims = (((contract[0],), (contract[1],)), ((), ()))
    return lax.dot_general(left, right, dims, preferred_element_type=F32)


def roll(value, shift):
    return pltpu.roll(value, shift % LANES, 1)


def lane_ids(rows):
    return lax.broadcasted_iota(jnp.int32, (rows, LANES), 1)


def silu_parts(value):
    sigma = 1.0 / (1.0 + jnp.exp(-value))
    return value * sigma, sigma * (1.0 + value * (1.0 - sigma))


def depth_columns(base, masks, step):
    below = roll(base, step) * masks[0]
    above = roll(base, -step) * masks[1]
    return jnp.concatenate([below, base, above], axis=0)


def depth_masks(step, first):
    ids = (lane_ids(3 * C) - first) % LANES
    return (ids >= step).astype(BF16), (ids < LANES - step).astype(BF16)


def across_columns(tile, step):
    return jnp.concatenate([roll(tile, step), tile, roll(tile, -step)], axis=0)


def edge_masks(step):
    ids = lane_ids(C) % 8
    first, last = (ids == 4).astype(BF16), (ids == 4 - step).astype(BF16)
    return first, (ids != 4).astype(BF16), last, (ids != 4 - step).astype(BF16)


def pair_columns(tile, halo, masks, step):
    left = roll(halo, step) * masks[0] + roll(tile, step) * masks[1]
    right = roll(halo, -step) * masks[2] + roll(tile, -step) * masks[3]
    return jnp.concatenate([left, tile, right], axis=0)


def fill_columns(tiles, from_left, from_right, out, step):
    masks = edge_masks(step)

    def body(group):
        packed_left, packed_right = from_left[group], from_right[group]
        for place in range(8):
            tile = tiles[8 * group + place]
            left = roll(packed_left, -place) * masks[0] + roll(tile, step) * masks[1]
            right = roll(packed_right, 8 - step - place) * masks[2]
            right = right + roll(tile, -step) * masks[3]
            out[8 * group + place] = jnp.concatenate([left, tile, right], axis=0)

    loop(0, from_left.shape[0], body)


def pack_columns(tiles, low, high, step):
    masks = edge_masks(step)

    def body(group):
        lows, highs = [], []
        for place in range(8):
            tile = tiles[8 * group + place]
            lows.append(roll(tile * masks[0], place))
            highs.append(roll(tile * masks[2], place - 8 + step))
        for out, parts in ((low, lows), (high, highs)):
            while len(parts) > 1:
                parts = [a + b for a, b in zip(parts[::2], parts[1::2])]
            out[group] = parts[0]

    loop(0, low.shape[0], body)


def own_masks():
    own = own_lanes(C)
    return own.astype(BF16), jnp.logical_not(own).astype(BF16)


def pair_tiles(lower, upper, masks):
    turned = roll(upper, 8)
    return (
        lower * masks[0] + turned * masks[1],
        lower * masks[1] + turned * masks[0],
    )


def own_lanes(rows):
    across = lane_ids(rows) % 16
    return (across >= 4) & (across < 12)


def join_halves(lower, upper):
    return jnp.where(own_lanes(lower.shape[0]), lower, roll(upper, 8))


def gather_sub(parts):
    total = parts[:C]
    for index in range(1, 4):
        total = total + roll(parts[index * C : (index + 1) * C], -SHIFTS[index])
    return total


def spread_sub(anchored):
    return jnp.concatenate([anchored] + [roll(anchored, step) for step in SHIFTS[1:]], axis=0)


def anchor_mask(first):
    ids = (lane_ids(C) - first) % LANES
    return (((ids // 16) % 2 == 0) & (ids % 2 == 0)).astype(F32)


def loop(low, high, body, unroll=1):
    def step(index, carry):
        body(index)
        return carry

    lax.fori_loop(low, high, step, 0, unroll=unroll)


def join_rows(first, second):
    low = lane_ids(C) < 64
    lead = roll(second[:, :LANES], 64)
    parts = [
        first[:, :LANES],
        jnp.where(low, first[:, LANES:], lead),
        jnp.where(low, lead, roll(second[:, LANES:], 64)),
    ]
    return jnp.concatenate(parts, axis=1)


def split_rows(joined):
    low = lane_ids(C) < 64
    middle = roll(joined[:, LANES : 2 * LANES], 64)
    last = roll(joined[:, 2 * LANES :], 64)
    second = jnp.concatenate([jnp.where(low, middle, last), last], axis=1)
    return joined[:, : 2 * LANES], second


def prepare_kernel(slots, count, feats, cots, flag_rows, x_low, x_high, y_low, y_high, rows_in):
    number = feats.shape[0]
    rows = lax.broadcasted_iota(jnp.int32, (16, LANES), 0)
    flags = jnp.zeros((16, LANES), F32)
    zero = jnp.zeros((C, VOX), BF16)
    first = jnp.zeros((), jnp.int32)
    last = jnp.zeros((), jnp.int32)
    for slot in range(number):
        live = slot < count[0]
        place = slots[slot]
        block = jnp.where(live, feats[slot], zero)
        rows_in[pl.ds(pl.multiple_of(place * C, 16), C), :] = block
        flags = jnp.where(rows == place, jnp.where(live, 1.0, 0.0), flags)
        first = jnp.where(place == 0, slot, first)
        last = jnp.where(place == number - 1, slot, last)
    flag_rows[...] = flags
    packed = dot(rows_in[...], marks(VOX, 512, plain, edge_source)).astype(BF16)
    spare = jnp.zeros((16, 2 * LANES), BF16)
    for out, at in ((x_low, 0), (x_high, 256)):
        for pair in range(number // 2):
            edges = [packed[C * i : C * (i + 1), at : at + 256] for i in (2 * pair, 2 * pair + 1)]
            out[C * pair : C * (pair + 1), :] = join_rows(*edges)
        out[C * number // 2 :, :LANES] = flags.astype(BF16)
        out[C * number // 2 :, LANES:] = spare
    for out, index, slot in ((y_low, 0, first), (y_high, number - 1, last)):
        live = slot < count[0]
        out[0:C, :] = rows_in[C * index : C * (index + 1), :]
        out[C : 2 * C, :] = jnp.where(live, cots[slot], zero)
        out[2 * C :, :] = (jnp.zeros((16, VOX), F32) + jnp.where(live, 1.0, 0.0)).astype(BF16)


def corner_kernel(y_left, y_right, low, high):
    rows = jnp.concatenate([y_left[0:C, :], y_right[0:C, :]], axis=0)
    packed = dot(rows, marks(VOX, 512, plain, edge_source)).astype(BF16)
    ids = lax.broadcasted_iota(jnp.int32, (16, LANES), 0)
    flags = jnp.where(ids == 0, y_left[2 * C :, :LANES], y_right[2 * C :, :LANES])
    spare = jnp.zeros((16, 2 * LANES), BF16)
    for out, at in ((low, 0), (high, 256)):
        out[0:C, :] = join_rows(packed[:C, at : at + 256], packed[C:, at : at + 256])
        out[C:, :LANES] = flags
        out[C:, LANES:] = spare


def arrange_weights(fine, down, coarse, up, fine_w, fine_b, coarse_w, coarse_b, down_w, up_w):
    for source, fore, back in ((fine, fine_w, fine_b), (coarse, coarse_w, coarse_b)):
        for along in range(3):
            rows = slice(C * along, C * (along + 1))
            turned_rows = slice(C * (2 - along), C * (3 - along))
            ahead = []
            behind = []
            for depth in range(3):
                for across in range(3):
                    ahead.append(source[9 * depth + 3 * across + along])
                    behind.append(source[9 * (2 - depth) + 3 * (2 - across) + along].T)
            fore[rows, :] = jnp.concatenate(ahead, axis=1)
            back[turned_rows, :] = jnp.concatenate(behind, axis=1)
    for index in range(4):
        pair = [down[:, 2 * index, :], down[:, 2 * index + 1, :]]
        down_w[C * index : C * (index + 1), :] = jnp.concatenate(pair, axis=1)
    for along in range(2):
        row = jnp.concatenate([up[2 * index + along] for index in range(4)], axis=1)
        up_w[C * along : C * (along + 1), :] = row


def place_kernel(
    slots, count, feats, cots, y_left, y_right, c_low, fine, down, coarse, up,
    grid, cot_grid, grad_r, fine_w, fine_b, coarse_w, coarse_b, down_w, up_w,
    rows_in, rows_cot, cot,
):
    arrange_weights(fine, down, coarse, up, fine_w, fine_b, coarse_w, coarse_b, down_w, up_w)
    number = feats.shape[0]
    last = number + 1
    zero = jnp.zeros((C, VOX), BF16)
    rows_in[0:C, :] = y_left[0:C, :]
    rows_in[last * C : (last + 1) * C, :] = y_right[0:C, :]
    for slot in range(number):
        live = slot < count[0]
        place = slots[slot]
        start = pl.multiple_of((place + 1) * C, 16)
        rows_in[pl.ds(start, C), :] = jnp.where(live, feats[slot], zero)
        cot[place] = jnp.where(live, cots[slot], zero)
    pairs = number // 2 + 2
    for group in range(pairs):
        at = group * C
        lower = y_left[C : 2 * C, :] if group == 0 else cot[group - 1]
        upper = y_right[C : 2 * C, :] if group == pairs - 1 else cot[group + number // 2 - 1]
        rows_cot[at : at + C, 0:512] = lower
        rows_cot[at : at + C, 512:1024] = upper
    for pair in range(4):
        placed_cot = dot(
            rows_cot[...], marks(1024, 256, plain, lambda j, at=256 * pair: pair_source(j + at))
        )
        placed = dot(
            rows_in[...], marks(VOX, 256, plain, lambda j, at=256 * pair: own_source(j + at))
        )
        for half in range(2):
            span = slice(LANES * half, LANES * (half + 1))
            for block in range(last + 1):
                tile = EDGE * block + 2 * pair + half
                grid[tile] = placed[block * C : (block + 1) * C, span].astype(BF16)
            for block in range(pairs):
                tile = EDGE * block + 2 * pair + half
                cot_grid[tile] = placed_cot[block * C : (block + 1) * C, span].astype(BF16)

    def rect_step(block):
        tiles = []
        for inner in range(4):
            tile = EDGE * block + 2 * inner
            tiles.append(jnp.concatenate([cot_grid[tile], cot_grid[tile + 1]], axis=0))
        parts = dot(up_w[...], jnp.concatenate(tiles, axis=1), (0, 0))
        for inner in range(4):
            grad_r[4 * block + inner] = gather_sub(parts[:, LANES * inner : LANES * (inner + 1)])

    loop(0, pairs, rect_step, 2)


def conv_sum(parts, tile):
    return parts[tile, 0:C] + parts[tile + 1, C : 2 * C] + parts[tile + 2, 2 * C :]


def conv_steps(parts, weight, load, tiles, step, first, unroll):
    masks = depth_masks(step, first)
    spare = jnp.zeros((3 * C, LANES), F32)
    parts[0] = spare
    parts[tiles + 1] = spare

    def body(index):
        tile = 4 * index
        cols = [depth_columns(load(tile + i), masks, step) for i in range(4)]
        out = dot(weight[...], jnp.concatenate(cols, axis=1))
        for i in range(4):
            parts[tile + i + 1] = out[:, LANES * i : LANES * (i + 1)]

    loop(0, tiles // 4, body, unroll)


def forward_kernel(
    grid_own, flags, y_left, y_right, grad_r, x_left, x_right, c_left, c_right, fine_w, down_w,
    coarse_w,
    grid, hidden, low_cols, rects, grad_c, live, pack_low, pack_high,
    rows_in, fine_p, coarse_p, hidden_all, lowered, live_all,
):
    number = 2 * (x_left.shape[0] - 16) // C
    last = number + 1
    for at, left, right in ((0, x_left, x_right), (None, c_left, c_right)):
        for pair in range((left.shape[0] - 16) // C):
            rows = slice(C * pair, C * (pair + 1))
            lefts, rights = split_rows(left[rows, :]), split_rows(right[rows, :])
            for inner in range(2):
                block = last * inner if at is None else 2 * pair + inner + 1
                rows_in[block * C : (block + 1) * C, 0:256] = lefts[inner]
                rows_in[block * C : (block + 1) * C, 256:512] = rights[inner]
    across = lane_ids(16) % 16
    for start, middle, left, right in (
        (1, flags[...], x_left[number // 2 * C :, :LANES], x_right[number // 2 * C :, :LANES]),
        (0, y_left[2 * C :, :LANES], c_left[C:, :LANES], c_right[C:, :LANES]),
        (last, y_right[2 * C :, :LANES], c_left[C:, :LANES], c_right[C:, :LANES]),
    ):
        rows = jnp.where(across < 4, left.astype(F32), middle.astype(F32))
        rows = jnp.where(across >= 12, right.astype(F32), rows)
        if start == 1:
            live_all[1 : number + 1, :] = rows
        else:
            at = 0 if start == 0 else 1
            live_all[start : start + 1, :] = rows[at : at + 1, :]
    for pair in range(4):
        placed = dot(
            rows_in[...], marks(512, 256, plain, lambda j, at=256 * pair: halo_source(j + at))
        )
        for half in range(2):
            span = slice(LANES * half, LANES * (half + 1))
            for block in range(last + 1):
                tile = EDGE * block + 2 * pair + half
                halo = placed[block * C : (block + 1) * C, span].astype(BF16)
                grid[tile] = grid_own[tile] + halo
    live[...] = join_halves(live_all[0:16, :], live_all[8:24, :])
    tiles = grid.shape[0]
    conv_steps(fine_p, fine_w, lambda tile: across_columns(grid[tile], 1), tiles, 16, 0, 2)
    anchors = anchor_mask(0)

    def lower_step(block):
        alive = jnp.broadcast_to(live_all[pl.ds(block, 1), :], (C, LANES))
        keep = alive * anchors
        pairs = []
        for inner in range(4):
            actives = []
            for half in range(2):
                tile = EDGE * block + 2 * inner + half
                value = conv_sum(fine_p, tile) * alive
                hidden_all[tile] = value
                actives.append(silu_parts(value)[0].astype(BF16))
            pairs.append(jnp.concatenate(actives, axis=0))
        parts = dot(down_w[...], jnp.concatenate(pairs, axis=1))
        for inner in range(4):
            total = gather_sub(parts[:, LANES * inner : LANES * (inner + 1)])
            lowered[4 * block + inner] = (total * keep).astype(BF16)

    loop(0, last + 1, lower_step, 2)
    pairs = hidden.shape[0] // EDGE
    shift = last - pairs + 1
    edges = edge_masks(2)
    halves = own_masks()

    def pair_step(block):
        for inner in range(EDGE):
            tile = EDGE * block + inner
            hidden[tile] = join_halves(hidden_all[tile], hidden_all[tile + EDGE * shift])
        for inner in range(4):
            tile = 4 * block + inner
            lower, upper = lowered[tile], lowered[tile + 4 * shift]
            low_cols[tile] = pair_columns(*pair_tiles(lower, upper, halves), edges, 2)

    loop(0, pairs, pair_step, 2)
    conv_steps(coarse_p, coarse_w, lambda tile: low_cols[tile], 4 * pairs, 32, 4, 2)
    pair_anchors = anchor_mask(4)

    def grad_step(block):
        alive = jnp.broadcast_to(live[pl.ds(block, 1), :], (C, LANES))
        keep = alive * pair_anchors
        for inner in range(4):
            coarse = 4 * block + inner
            smooth, slope = silu_parts(conv_sum(coarse_p, coarse))
            rects[coarse] = (smooth * pair_anchors).astype(BF16)
            grad_c[coarse] = (grad_r[coarse] * slope * keep).astype(BF16)

    loop(0, pairs, grad_step, 2)
    pack_columns(grad_c, pack_low, pack_high, 2)


def to_blocks(slots, rows_out, flat, out):
    flat[...] = dot(rows_out[...], marks(1024, 1024, pair_source, plain)).astype(BF16)
    number = out.shape[0]
    for slot in range(number):
        place = slots[slot]
        upper = place >= number // 2
        start = pl.multiple_of(jnp.where(upper, place - number // 2, place) * C, 16)
        rows = flat[pl.ds(start, C), :]
        out[slot] = jnp.where(upper, rows[:, 512:], rows[:, :512])


def stacks(own, tiles):
    parts = [jnp.concatenate([own[t + 1], own[t], own[t - 1]], axis=0) for t in tiles]
    return jnp.concatenate(parts, axis=1)


def flatten_weights(total, out, at):
    turned = total[...].T.astype(BF16)
    for group in range(4):
        out[at + 3 * C * group : at + 3 * C * (group + 1), :] = turned[
            :, LANES * group : LANES * (group + 1)
        ]


def output_kernel(slots, hidden, rects, live, up_w, out, rows_out, flat):
    pairs = hidden.shape[0] // EDGE

    def block_step(block):
        alive = jnp.broadcast_to(live[pl.ds(block, 1), :], (C, LANES))
        start = pl.multiple_of((block - 1) * C, 16)
        spreads = [spread_sub(rects[4 * block + inner]) for inner in range(4)]
        upward = dot(up_w[...], jnp.concatenate(spreads, axis=1))
        for inner in range(4):
            for half in range(2):
                part = upward[half * C : (half + 1) * C, LANES * inner : LANES * (inner + 1)]
                value = hidden[EDGE * block + 2 * inner + half] + part
                at = LANES * (2 * inner + half)
                rows_out[pl.ds(start, C), at : at + LANES] = (value * alive).astype(BF16)

    loop(1, pairs - 1, block_step, 2)
    to_blocks(slots, rows_out, flat, out)


def side_kernel(rects, cot_grid, low_cols, grad_c, flat, grad_own, up_g, coarse_g):
    tiles = low_cols.shape[0]
    up_g[...] = jnp.zeros_like(up_g)
    coarse_g[...] = jnp.zeros_like(coarse_g)

    def up_step(block):
        spreads = []
        pairs = []
        for inner in range(4):
            coarse = 4 * block + inner
            spreads.append(spread_sub(rects[coarse]))
            pairs.append(
                jnp.concatenate([cot_grid[2 * coarse], cot_grid[2 * coarse + 1]], axis=0)
            )
        up_g[:, 0 : 2 * C] += dot(
            jnp.concatenate(spreads, axis=1), jnp.concatenate(pairs, axis=1), (1, 1)
        )

    loop(1, tiles // 4 - 1, up_step, 2)
    zero = jnp.zeros((C, LANES), BF16)
    for coarse in range(1, 4):
        grad_own[coarse] = zero
        grad_own[tiles - 1 - coarse] = zero

    def copy_step(coarse):
        grad_own[coarse] = grad_c[coarse]

    loop(4, tiles - 4, copy_step, 8)
    masks = depth_masks(32, 4)

    def weight_step(index):
        at = [2 + 4 * index + inner for inner in range(4)]
        rights = [depth_columns(low_cols[tile], masks, 32) for tile in at]
        coarse_g[0 : 9 * C, :] += dot(
            jnp.concatenate(rights, axis=1), stacks(grad_own, at), (1, 1)
        )

    loop(0, (tiles - 4) // 4, weight_step, 3)
    flatten_weights(coarse_g, flat, 0)
    flat[12 * C :, :] = up_g[...].astype(BF16)


def backward_kernel(
    grad_c, from_left, from_right, hidden, cot_grid, live, coarse_w, down_w,
    grad_h, grad_d, pack_low, pack_high, coarse_p, grad_x,
):
    tiles = grad_c.shape[0]
    fill_columns(grad_c, from_left, from_right, grad_x, 2)
    conv_steps(coarse_p, coarse_w, lambda tile: grad_x[tile], tiles, 32, 4, 2)
    anchors = anchor_mask(4)

    def step(block):
        alive = jnp.broadcast_to(live[pl.ds(block, 1), :], (C, LANES))
        keep = alive * anchors
        spreads = []
        for inner in range(4):
            coarse = 4 * block + inner
            down = (conv_sum(coarse_p, coarse) * keep).astype(BF16)
            grad_d[coarse] = down
            spreads.append(spread_sub(down))
        acts = dot(down_w[...], jnp.concatenate(spreads, axis=1), (0, 0))
        for inner in range(4):
            for side in range(2):
                tile = EDGE * block + 2 * inner + side
                slope = silu_parts(hidden[tile])[1]
                part = acts[side * C : (side + 1) * C, LANES * inner : LANES * (inner + 1)]
                grad = cot_grid[tile].astype(F32) + part * slope
                grad_h[tile] = (grad * alive).astype(BF16)

    loop(0, tiles // 4, step, 2)
    pack_columns(grad_h, pack_low, pack_high, 1)


def weight_kernel(grid, grad_h, grad_d, hidden, early, joined, grad_own, fine_g, down_g):
    tiles = grad_h.shape[0]
    shift = tiles - 16
    fine_g[...] = jnp.zeros_like(fine_g)
    down_g[...] = jnp.zeros_like(down_g)
    zero = jnp.zeros((C, LANES), BF16)
    for tile in range(3, 8):
        grad_own[tile] = zero
        grad_own[tiles - 1 - tile] = zero

    def copy_step(tile):
        grad_own[tile] = grad_h[tile]

    loop(8, tiles - 8, copy_step, 8)
    masks = depth_masks(16, 4)
    edges = edge_masks(1)
    halves = own_masks()

    def fine_step(index):
        at = [4 + 8 * index + inner for inner in range(8)]
        rights = []
        for tile in at:
            lower, upper = grid[tile], grid[tile + shift]
            base = pair_columns(*pair_tiles(lower, upper, halves), edges, 1)
            rights.append(depth_columns(base, masks, 16))
        fine_g[0 : 9 * C, :] += dot(
            jnp.concatenate(rights, axis=1), stacks(grad_own, at), (1, 1)
        )

    loop(0, (tiles - 8) // 8, fine_step)

    def down_step(index):
        lefts = []
        rights = []
        for inner in range(4):
            coarse = 4 + 4 * index + inner
            lefts.append(spread_sub(grad_d[coarse]))
            actives = [silu_parts(hidden[2 * coarse + side])[0].astype(BF16) for side in range(2)]
            rights.append(jnp.concatenate(actives, axis=0))
        down_g[:, 0 : 2 * C] += dot(
            jnp.concatenate(lefts, axis=1), jnp.concatenate(rights, axis=1), (1, 1)
        )

    loop(0, (tiles // 2 - 8) // 4, down_step, 2)
    flatten_weights(fine_g, joined, 0)
    joined[12 * C : 16 * C, :] = down_g[...].astype(BF16)
    joined[16 * C :, :] = early[...]


def input_kernel(
    slots, grad_h, from_left, from_right, live, fine_w, out,
    fine_p, rows_out, flat, grad_x,
):
    tiles = grad_h.shape[0]
    fill_columns(grad_h, from_left, from_right, grad_x, 1)
    conv_steps(fine_p, fine_w, lambda tile: grad_x[tile], tiles, 16, 4, 2)

    def block_step(block):
        alive = jnp.broadcast_to(live[pl.ds(block, 1), :], (C, LANES))
        start = pl.multiple_of((block - 1) * C, 16)
        for inner in range(EDGE):
            value = conv_sum(fine_p, EDGE * block + inner)
            rows_out[pl.ds(start, C), LANES * inner : LANES * (inner + 1)] = (
                value * alive
            ).astype(BF16)

    loop(1, tiles // EDGE - 1, block_step, 2)
    to_blocks(slots, rows_out, flat, out)


def finish_kernel(scale, total, fine, down, coarse, up):
    for out, at in ((fine, 0), (coarse, 16 * C)):
        for along in range(3):
            first = at + C * along
            rows = [total[first + 3 * C * g : first + 3 * C * g + C, :] for g in range(4)]
            row = jnp.concatenate(rows, axis=1).astype(F32) * scale
            for index in range(9):
                out[3 * index + along] = row[:, C * index : C * (index + 1)]
    for out, at, turn in ((down, 12 * C, False), (up, 28 * C, True)):
        for index in range(4):
            rows = total[at + C * index : at + C * (index + 1), :].astype(F32) * scale
            for along in range(2):
                part = rows[:, C * along : C * (along + 1)]
                out[2 * index + along] = part.T if turn else part


def call(kernel, inputs, outs, scratch=(), scalars=0, flops=0, limit=None):
    vmem = pl.BlockSpec(memory_space=pltpu.VMEM)
    smem = pl.BlockSpec(memory_space=pltpu.SMEM)
    held = SLACK
    for shape, kind in [(a.shape, a.dtype) for a in inputs[scalars:]] + list(outs) + list(scratch):
        rows, lanes = -(-shape[-2] // 16) * 16, -(-shape[-1] // LANES) * LANES
        held += math.prod(shape[:-2]) * rows * lanes * jnp.dtype(kind).itemsize
    moved = sum(math.prod(s) * jnp.dtype(d).itemsize for s, d in outs)
    moved += sum(math.prod(a.shape) * a.dtype.itemsize for a in inputs)
    return pl.pallas_call(
        kernel,
        out_shape=tuple(jax.ShapeDtypeStruct(s, d) for s, d in outs),
        in_specs=[smem] * scalars + [vmem] * (len(inputs) - scalars),
        out_specs=tuple(vmem for _ in outs),
        scratch_shapes=[pltpu.VMEM(s, d) for s, d in scratch],
        compiler_params=pltpu.CompilerParams(vmem_limit_bytes=limit or held),
        cost_estimate=pl.CostEstimate(flops=flops, bytes_accessed=moved, transcendentals=0),
        name=getattr(kernel, "func", kernel).__name__,
    )(*inputs)


def send(array, step_x, step_y):
    number_x, number_y = lax.axis_size("gx"), lax.axis_size("gy")
    pairs = []
    for i in range(number_x):
        for j in range(number_y):
            to_x, to_y = i + step_x, j + step_y
            if 0 <= to_x < number_x and 0 <= to_y < number_y:
                pairs.append((i * number_y + j, to_x * number_y + to_y))
    return lax.ppermute(array, ("gx", "gy"), pairs)


def reduce_share(joined):
    devices = lax.axis_size("gx") * lax.axis_size("gy")
    rows = joined.shape[0]
    share = -(-rows // devices)
    joined = jnp.pad(joined, ((0, share * devices - rows), (0, 0)))
    mine = lax.all_to_all(joined.reshape(devices, share, LANES), ("gx", "gy"), 0, 0)
    return jnp.sum(mine.astype(F32), axis=0).astype(BF16)


def spread_share(share):
    devices = lax.axis_size("gx") * lax.axis_size("gy")
    rows = share.shape[0]
    copies = jnp.broadcast_to(share[None], (devices, rows, LANES))
    full = lax.all_to_all(copies, ("gx", "gy"), 0, 0)
    return full.reshape(devices * rows, LANES)


def on_device(
    features, block_slots, block_count, cotangent, fine_weight, down_weight, coarse_weight,
    up_weight,
):
    number = features.shape[2]
    slots = block_slots.reshape(number)
    count = block_count.reshape(1)
    feats = features.reshape(number, C, VOX)
    cots = cotangent.reshape(number, C, VOX)
    tiles = EDGE * (number + 2)
    coarse_tiles = tiles // 2
    pairs = number // 2 + 2
    groups = pairs // 2
    fine_groups = pairs

    fine_3, coarse_3 = (weight.transpose(1, 0, 2) for weight in (fine_weight, coarse_weight))
    flag_rows, x_low, x_high, y_low, y_high = call(
        prepare_kernel,
        (slots, count, feats, cots),
        [((16, LANES), F32)]
        + [((number // 2 * C + 16, 384), BF16)] * 2
        + [((2 * C + 16, VOX), BF16)] * 2,
        [((number * C, VOX), BF16)],
        scalars=2,
        limit=56 * 1024 * 1024,
    )
    x_left = send(x_high, 1, 0)
    x_right = send(x_low, -1, 0)
    y_left = send(y_high, 0, 1)
    y_right = send(y_low, 0, -1)
    corner_low, corner_high = call(
        corner_kernel,
        (y_left, y_right),
        [((C + 16, 384), BF16), ((C + 16, 384), BF16)],
    )
    c_left = send(corner_high, 1, 0)
    c_right = send(corner_low, -1, 0)
    (grid_own, cot_grid, grad_r, fine_fore, fine_back, coarse_fore, coarse_back, down_w,
     up_w) = call(
        place_kernel,
        (slots, count, feats, cots, y_left, y_right, corner_low, fine_3, down_weight, coarse_3,
         up_weight),
        [
            ((tiles, C, LANES), BF16),
            ((EDGE * pairs, C, LANES), BF16),
            ((4 * pairs, C, LANES), F32),
        ]
        + [((3 * C, 9 * C), BF16)] * 4
        + [((4 * C, 2 * C), BF16), ((2 * C, 4 * C), BF16)],
        [
            (((number + 2) * C, VOX), BF16),
            ((pairs * C, 1024), BF16),
            ((number, C, VOX), BF16),
        ],
        scalars=2,
        flops=8 * 10**9,
    )
    grid, hidden, low_cols, rects, grad_c, live, pack_low, pack_high = call(
        forward_kernel,
        (grid_own, flag_rows, y_left, y_right, grad_r, x_left, x_right, c_left, c_right,
         fine_fore, down_w, coarse_fore),
        [
            ((tiles, C, LANES), BF16),
            ((EDGE * pairs, C, LANES), F32),
            ((4 * pairs, 3 * C, LANES), BF16),
            ((4 * pairs, C, LANES), BF16),
            ((4 * pairs, C, LANES), BF16),
            ((16, LANES), F32),
            ((groups, C, LANES), BF16),
            ((groups, C, LANES), BF16),
        ],
        [
            (((number + 2) * C, VOX), BF16),
            ((tiles + 2, 3 * C, LANES), F32),
            ((4 * pairs + 2, 3 * C, LANES), F32),
            ((tiles, C, LANES), F32),
            ((coarse_tiles, C, LANES), BF16),
            ((C, LANES), F32),
        ],
        flops=8 * 10**9,
    )
    grad_left = send(pack_high, 1, 0)
    grad_right = send(pack_low, -1, 0)
    (early,) = call(
        side_kernel,
        (rects, cot_grid, low_cols, grad_c),
        [((16 * C, LANES), BF16)],
        [((4 * pairs, C, LANES), BF16), ((4 * C, LANES), F32), ((VOX, 3 * C), F32)],
        flops=8 * 10**9,
    )
    grad_h, grad_d, edge_low, edge_high = call(
        backward_kernel,
        (grad_c, grad_left, grad_right, hidden, cot_grid, live, coarse_back, down_w),
        [
            ((EDGE * pairs, C, LANES), BF16),
            ((4 * pairs, C, LANES), BF16),
            ((fine_groups, C, LANES), BF16),
            ((fine_groups, C, LANES), BF16),
        ],
        [((4 * pairs + 2, 3 * C, LANES), F32), ((4 * pairs, 3 * C, LANES), BF16)],
        flops=8 * 10**9,
    )
    edge_left = send(edge_high, 1, 0)
    edge_right = send(edge_low, -1, 0)
    (joined,) = call(
        weight_kernel,
        (grid, grad_h, grad_d, hidden, early),
        [((32 * C, LANES), BF16)],
        [((EDGE * pairs, C, LANES), BF16), ((VOX, 3 * C), F32), ((4 * C, LANES), F32)],
        flops=12 * 10**9,
    )
    joined, edge_left, edge_right, slots = lax.optimization_barrier(
        (joined, edge_left, edge_right, slots)
    )
    share = reduce_share(joined)
    (output,) = call(
        output_kernel,
        (slots, hidden, rects, live, up_w),
        [((number, C, VOX), BF16)],
        [((number // 2 * C, 1024), BF16), ((number // 2 * C, 1024), BF16)],
        scalars=1,
        flops=8 * 10**9,
    )
    share, output, slots = lax.optimization_barrier((share, output, slots))
    (input_grad,) = call(
        input_kernel,
        (slots, grad_h, edge_left, edge_right, live, fine_back),
        [((number, C, VOX), BF16)],
        [
            ((EDGE * pairs + 2, 3 * C, LANES), F32),
            ((number // 2 * C, 1024), BF16),
            ((number // 2 * C, 1024), BF16),
            ((EDGE * pairs, 3 * C, LANES), BF16),
        ],
        scalars=1,
        flops=8 * 10**9,
    )
    total = spread_share(share)
    scale = 1.0 / math.sqrt(number * VOX * lax.axis_size("gx") * lax.axis_size("gy"))
    fine_total, down_total, coarse_total, up_total = call(
        functools.partial(finish_kernel, scale),
        (total,),
        [((27, C, C), F32), ((8, C, C), F32), ((27, C, C), F32), ((8, C, C), F32)],
    )
    shape_out = (1, 1, number, C, VOX)
    return (
        output.reshape(shape_out),
        input_grad.reshape(shape_out),
        fine_total.transpose(1, 0, 2),
        down_total.transpose(1, 0, 2),
        coarse_total.transpose(1, 0, 2),
        up_total,
    )


def solution(mesh):
    split = P("gx", "gy", None, None, None)
    return jax.shard_map(
        on_device,
        mesh=mesh,
        in_specs=(split, P("gx", "gy", None), P("gx", "gy"), split, P(), P(), P(), P()),
        out_specs=(split, split, P(), P(), P(), P()),
        check_vma=False,
    )
```

```python
import functools
import math

import jax
import jax.numpy as jnp
from jax import lax
from jax.experimental import pallas as pl
from jax.experimental.pallas import tpu as pltpu
from jax.sharding import PartitionSpec as P

C = 48
EDGE = 8
VOX = 512
LANES = 128
F32 = jnp.float32
BF16 = jnp.bfloat16
SLACK = 8 * 1024 * 1024
SHIFTS = (0, 1, 16, 17)


def marks(rows, columns, row_key, column_key):
    across = column_key(lax.broadcasted_iota(jnp.int32, (1, columns), 1))
    down = row_key(lax.broadcasted_iota(jnp.int32, (rows, 1), 0))
    return jnp.where(down == across, 1.0, 0.0).astype(BF16)


def plain(index):
    return index


def own_source(column):
    lane, y = column % LANES, column // LANES
    x = lane % 16 - 4
    return jnp.where((x >= 0) & (x < 8), 64 * (lane // 16) + 8 * x + y, -1)


def halo_source(column):
    lane, y = column % LANES, column // LANES
    x = lane % 16
    at = 24 * (lane // 16) + y
    left = jnp.where((x >= 1) & (x < 4), at + 8 * (x - 1), -1)
    return jnp.where((x >= 12) & (x < 15), at + 8 * (x - 12) + 256, left)


def pair_source(column):
    lane, y = (column - 4) % LANES, column // LANES
    return 512 * (lane % 16 // 8) + 64 * (lane // 16) + 8 * (lane % 8) + y


def edge_source(column):
    at, side = column % 256, column // 256
    x = at % 24 // 8 + 5 * side
    return jnp.where(at < 192, 64 * (at // 24) + 8 * x + at % 8, -1)


def dot(left, right, contract=(1, 0)):
    dims = (((contract[0],), (contract[1],)), ((), ()))
    return lax.dot_general(left, right, dims, preferred_element_type=F32)


def roll(value, shift):
    return pltpu.roll(value, shift % LANES, 1)


def lane_ids(rows):
    return lax.broadcasted_iota(jnp.int32, (rows, LANES), 1)


def silu_parts(value):
    sigma = 1.0 / (1.0 + jnp.exp(-value))
    return value * sigma, sigma * (1.0 + value * (1.0 - sigma))


def depth_columns(base, masks, step):
    below = roll(base, step) * masks[0]
    above = roll(base, -step) * masks[1]
    return jnp.concatenate([below, base, above], axis=0)


def depth_masks(step, first):
    ids = (lane_ids(3 * C) - first) % LANES
    return (ids >= step).astype(BF16), (ids < LANES - step).astype(BF16)


def across_columns(tile, step):
    return jnp.concatenate([roll(tile, step), tile, roll(tile, -step)], axis=0)


def edge_masks(step):
    ids = lane_ids(C) % 8
    first, last = (ids == 4).astype(BF16), (ids == 4 - step).astype(BF16)
    return first, (ids != 4).astype(BF16), last, (ids != 4 - step).astype(BF16)


def pair_columns(tile, halo, masks, step):
    left = roll(halo, step) * masks[0] + roll(tile, step) * masks[1]
    right = roll(halo, -step) * masks[2] + roll(tile, -step) * masks[3]
    return jnp.concatenate([left, tile, right], axis=0)


def fill_columns(tiles, from_left, from_right, out, step):
    masks = edge_masks(step)

    def body(group):
        packed_left, packed_right = from_left[group], from_right[group]
        for place in range(8):
            tile = tiles[8 * group + place]
            left = roll(packed_left, -place) * masks[0] + roll(tile, step) * masks[1]
            right = roll(packed_right, 8 - step - place) * masks[2]
            right = right + roll(tile, -step) * masks[3]
            out[8 * group + place] = jnp.concatenate([left, tile, right], axis=0)

    loop(0, from_left.shape[0], body)


def pack_columns(tiles, low, high, step):
    masks = edge_masks(step)

    def body(group):
        lows, highs = [], []
        for place in range(8):
            tile = tiles[8 * group + place]
            lows.append(roll(tile * masks[0], place))
            highs.append(roll(tile * masks[2], place - 8 + step))
        for out, parts in ((low, lows), (high, highs)):
            while len(parts) > 1:
                parts = [a + b for a, b in zip(parts[::2], parts[1::2])]
            out[group] = parts[0]

    loop(0, low.shape[0], body)


def own_masks():
    own = own_lanes(C)
    return own.astype(BF16), jnp.logical_not(own).astype(BF16)


def pair_tiles(lower, upper, masks):
    turned = roll(upper, 8)
    return (
        lower * masks[0] + turned * masks[1],
        lower * masks[1] + turned * masks[0],
    )


def own_lanes(rows):
    across = lane_ids(rows) % 16
    return (across >= 4) & (across < 12)


def join_halves(lower, upper):
    return jnp.where(own_lanes(lower.shape[0]), lower, roll(upper, 8))


def gather_sub(parts):
    total = parts[:C]
    for index in range(1, 4):
        total = total + roll(parts[index * C : (index + 1) * C], -SHIFTS[index])
    return total


def spread_sub(anchored):
    return jnp.concatenate([anchored] + [roll(anchored, step) for step in SHIFTS[1:]], axis=0)


def anchor_mask(first):
    ids = (lane_ids(C) - first) % LANES
    return (((ids // 16) % 2 == 0) & (ids % 2 == 0)).astype(F32)


def loop(low, high, body, unroll=1):
    def step(index, carry):
        body(index)
        return carry

    lax.fori_loop(low, high, step, 0, unroll=unroll)


def join_rows(first, second):
    low = lane_ids(C) < 64
    lead = roll(second[:, :LANES], 64)
    parts = [
        first[:, :LANES],
        jnp.where(low, first[:, LANES:], lead),
        jnp.where(low, lead, roll(second[:, LANES:], 64)),
    ]
    return jnp.concatenate(parts, axis=1)


def split_rows(joined):
    low = lane_ids(C) < 64
    middle = roll(joined[:, LANES : 2 * LANES], 64)
    last = roll(joined[:, 2 * LANES :], 64)
    second = jnp.concatenate([jnp.where(low, middle, last), last], axis=1)
    return joined[:, : 2 * LANES], second


def prepare_kernel(slots, count, feats, cots, flag_rows, x_low, x_high, y_low, y_high, rows_in):
    number = feats.shape[0]
    rows = lax.broadcasted_iota(jnp.int32, (16, LANES), 0)
    flags = jnp.zeros((16, LANES), F32)
    zero = jnp.zeros((C, VOX), BF16)
    first = jnp.zeros((), jnp.int32)
    last = jnp.zeros((), jnp.int32)
    for slot in range(number):
        live = slot < count[0]
        place = slots[slot]
        block = jnp.where(live, feats[slot], zero)
        rows_in[pl.ds(pl.multiple_of(place * C, 16), C), :] = block
        flags = jnp.where(rows == place, jnp.where(live, 1.0, 0.0), flags)
        first = jnp.where(place == 0, slot, first)
        last = jnp.where(place == number - 1, slot, last)
    flag_rows[...] = flags
    packed = dot(rows_in[...], marks(VOX, 512, plain, edge_source)).astype(BF16)
    spare = jnp.zeros((16, 2 * LANES), BF16)
    for out, at in ((x_low, 0), (x_high, 256)):
        for pair in range(number // 2):
            edges = [packed[C * i : C * (i + 1), at : at + 256] for i in (2 * pair, 2 * pair + 1)]
            out[C * pair : C * (pair + 1), :] = join_rows(*edges)
        out[C * number // 2 :, :LANES] = flags.astype(BF16)
        out[C * number // 2 :, LANES:] = spare
    for out, index, slot in ((y_low, 0, first), (y_high, number - 1, last)):
        live = slot < count[0]
        out[0:C, :] = rows_in[C * index : C * (index + 1), :]
        out[C : 2 * C, :] = jnp.where(live, cots[slot], zero)
        out[2 * C :, :] = (jnp.zeros((16, VOX), F32) + jnp.where(live, 1.0, 0.0)).astype(BF16)


def corner_kernel(y_left, y_right, low, high):
    rows = jnp.concatenate([y_left[0:C, :], y_right[0:C, :]], axis=0)
    packed = dot(rows, marks(VOX, 512, plain, edge_source)).astype(BF16)
    ids = lax.broadcasted_iota(jnp.int32, (16, LANES), 0)
    flags = jnp.where(ids == 0, y_left[2 * C :, :LANES], y_right[2 * C :, :LANES])
    spare = jnp.zeros((16, 2 * LANES), BF16)
    for out, at in ((low, 0), (high, 256)):
        out[0:C, :] = join_rows(packed[:C, at : at + 256], packed[C:, at : at + 256])
        out[C:, :LANES] = flags
        out[C:, LANES:] = spare


def arrange_weights(fine, down, coarse, up, fine_w, fine_b, coarse_w, coarse_b, down_w, up_w):
    for source, fore, back in ((fine, fine_w, fine_b), (coarse, coarse_w, coarse_b)):
        for along in range(3):
            rows = slice(C * along, C * (along + 1))
            turned_rows = slice(C * (2 - along), C * (3 - along))
            ahead = []
            behind = []
            for depth in range(3):
                for across in range(3):
                    ahead.append(source[9 * depth + 3 * across + along])
                    behind.append(source[9 * (2 - depth) + 3 * (2 - across) + along].T)
            fore[rows, :] = jnp.concatenate(ahead, axis=1)
            back[turned_rows, :] = jnp.concatenate(behind, axis=1)
    for index in range(4):
        pair = [down[:, 2 * index, :], down[:, 2 * index + 1, :]]
        down_w[C * index : C * (index + 1), :] = jnp.concatenate(pair, axis=1)
    for along in range(2):
        row = jnp.concatenate([up[2 * index + along] for index in range(4)], axis=1)
        up_w[C * along : C * (along + 1), :] = row


def place_kernel(
    slots, count, feats, cots, y_left, y_right, c_low, fine, down, coarse, up,
    grid, cot_grid, grad_r, fine_w, fine_b, coarse_w, coarse_b, down_w, up_w,
    rows_in, rows_cot, cot,
):
    arrange_weights(fine, down, coarse, up, fine_w, fine_b, coarse_w, coarse_b, down_w, up_w)
    number = feats.shape[0]
    last = number + 1
    zero = jnp.zeros((C, VOX), BF16)
    rows_in[0:C, :] = y_left[0:C, :]
    rows_in[last * C : (last + 1) * C, :] = y_right[0:C, :]
    for slot in range(number):
        live = slot < count[0]
        place = slots[slot]
        start = pl.multiple_of((place + 1) * C, 16)
        rows_in[pl.ds(start, C), :] = jnp.where(live, feats[slot], zero)
        cot[place] = jnp.where(live, cots[slot], zero)
    pairs = number // 2 + 2
    for group in range(pairs):
        at = group * C
        lower = y_left[C : 2 * C, :] if group == 0 else cot[group - 1]
        upper = y_right[C : 2 * C, :] if group == pairs - 1 else cot[group + number // 2 - 1]
        rows_cot[at : at + C, 0:512] = lower
        rows_cot[at : at + C, 512:1024] = upper
    for pair in range(4):
        placed_cot = dot(
            rows_cot[...], marks(1024, 256, plain, lambda j, at=256 * pair: pair_source(j + at))
        )
        placed = dot(
            rows_in[...], marks(VOX, 256, plain, lambda j, at=256 * pair: own_source(j + at))
        )
        for half in range(2):
            span = slice(LANES * half, LANES * (half + 1))
            for block in range(last + 1):
                tile = EDGE * block + 2 * pair + half
                grid[tile] = placed[block * C : (block + 1) * C, span].astype(BF16)
            for block in range(pairs):
                tile = EDGE * block + 2 * pair + half
                cot_grid[tile] = placed_cot[block * C : (block + 1) * C, span].astype(BF16)

    def rect_step(block):
        tiles = []
        for inner in range(4):
            tile = EDGE * block + 2 * inner
            tiles.append(jnp.concatenate([cot_grid[tile], cot_grid[tile + 1]], axis=0))
        parts = dot(up_w[...], jnp.concatenate(tiles, axis=1), (0, 0))
        for inner in range(4):
            grad_r[4 * block + inner] = gather_sub(parts[:, LANES * inner : LANES * (inner + 1)])

    loop(0, pairs, rect_step, 2)


def conv_sum(parts, tile):
    return parts[tile, 0:C] + parts[tile + 1, C : 2 * C] + parts[tile + 2, 2 * C :]


def conv_steps(parts, weight, load, tiles, step, first, even, odd):
    masks = depth_masks(step, first)
    spare = jnp.zeros((3 * C, LANES), F32)
    parts[0] = spare
    parts[tiles + 1] = spare

    def fill(buffer, tile):
        for i in range(4):
            cols = depth_columns(load(tile + i), masks, step)
            buffer[:, LANES * i : LANES * (i + 1)] = cols

    def multiply(buffer, tile):
        out = dot(weight[...], buffer[...])
        for i in range(4):
            parts[tile + i + 1] = out[:, LANES * i : LANES * (i + 1)]

    fill(even, 0)

    def body(index):
        tile = 8 * index
        fill(odd, tile + 4)
        multiply(even, tile)
        fill(even, jnp.minimum(tile + 8, tiles - 4))
        multiply(odd, tile + 4)

    loop(0, tiles // 8, body)


def forward_kernel(
    grid_own, flags, y_left, y_right, grad_r, x_left, x_right, c_left, c_right, fine_w, down_w,
    coarse_w,
    grid, hidden, low_cols, rects, grad_c, live, pack_low, pack_high,
    rows_in, fine_p, coarse_p, hidden_all, lowered, live_all, even, odd,
):
    number = 2 * (x_left.shape[0] - 16) // C
    last = number + 1
    for at, left, right in ((0, x_left, x_right), (None, c_left, c_right)):
        for pair in range((left.shape[0] - 16) // C):
            rows = slice(C * pair, C * (pair + 1))
            lefts, rights = split_rows(left[rows, :]), split_rows(right[rows, :])
            for inner in range(2):
                block = last * inner if at is None else 2 * pair + inner + 1
                rows_in[block * C : (block + 1) * C, 0:256] = lefts[inner]
                rows_in[block * C : (block + 1) * C, 256:512] = rights[inner]
    across = lane_ids(16) % 16
    for start, middle, left, right in (
        (1, flags[...], x_left[number // 2 * C :, :LANES], x_right[number // 2 * C :, :LANES]),
        (0, y_left[2 * C :, :LANES], c_left[C:, :LANES], c_right[C:, :LANES]),
        (last, y_right[2 * C :, :LANES], c_left[C:, :LANES], c_right[C:, :LANES]),
    ):
        rows = jnp.where(across < 4, left.astype(F32), middle.astype(F32))
        rows = jnp.where(across >= 12, right.astype(F32), rows)
        if start == 1:
            live_all[1 : number + 1, :] = rows
        else:
            at = 0 if start == 0 else 1
            live_all[start : start + 1, :] = rows[at : at + 1, :]
    for pair in range(4):
        placed = dot(
            rows_in[...], marks(512, 256, plain, lambda j, at=256 * pair: halo_source(j + at))
        )
        for half in range(2):
            span = slice(LANES * half, LANES * (half + 1))
            for block in range(last + 1):
                tile = EDGE * block + 2 * pair + half
                halo = placed[block * C : (block + 1) * C, span].astype(BF16)
                grid[tile] = grid_own[tile] + halo
    live[...] = join_halves(live_all[0:16, :], live_all[8:24, :])
    tiles = grid.shape[0]
    conv_steps(fine_p, fine_w, lambda tile: across_columns(grid[tile], 1), tiles, 16, 0, even, odd)
    anchors = anchor_mask(0)

    def lower_step(block):
        alive = jnp.broadcast_to(live_all[pl.ds(block, 1), :], (C, LANES))
        keep = alive * anchors
        pairs = []
        for inner in range(4):
            actives = []
            for half in range(2):
                tile = EDGE * block + 2 * inner + half
                value = conv_sum(fine_p, tile) * alive
                hidden_all[tile] = value
                actives.append(silu_parts(value)[0].astype(BF16))
            pairs.append(jnp.concatenate(actives, axis=0))
        parts = dot(down_w[...], jnp.concatenate(pairs, axis=1))
        for inner in range(4):
            total = gather_sub(parts[:, LANES * inner : LANES * (inner + 1)])
            lowered[4 * block + inner] = (total * keep).astype(BF16)

    loop(0, last + 1, lower_step, 2)
    pairs = hidden.shape[0] // EDGE
    shift = last - pairs + 1
    edges = edge_masks(2)
    halves = own_masks()

    def pair_step(block):
        for inner in range(EDGE):
            tile = EDGE * block + inner
            hidden[tile] = join_halves(hidden_all[tile], hidden_all[tile + EDGE * shift])
        for inner in range(4):
            tile = 4 * block + inner
            lower, upper = lowered[tile], lowered[tile + 4 * shift]
            low_cols[tile] = pair_columns(*pair_tiles(lower, upper, halves), edges, 2)

    loop(0, pairs, pair_step, 2)
    conv_steps(coarse_p, coarse_w, lambda tile: low_cols[tile], 4 * pairs, 32, 4, even, odd)
    pair_anchors = anchor_mask(4)

    def grad_step(block):
        alive = jnp.broadcast_to(live[pl.ds(block, 1), :], (C, LANES))
        keep = alive * pair_anchors
        for inner in range(4):
            coarse = 4 * block + inner
            smooth, slope = silu_parts(conv_sum(coarse_p, coarse))
            rects[coarse] = (smooth * pair_anchors).astype(BF16)
            grad_c[coarse] = (grad_r[coarse] * slope * keep).astype(BF16)

    loop(0, pairs, grad_step, 2)
    pack_columns(grad_c, pack_low, pack_high, 2)


def to_blocks(slots, rows_out, flat, out):
    flat[...] = dot(rows_out[...], marks(1024, 1024, pair_source, plain)).astype(BF16)
    number = out.shape[0]
    for slot in range(number):
        place = slots[slot]
        upper = place >= number // 2
        start = pl.multiple_of(jnp.where(upper, place - number // 2, place) * C, 16)
        rows = flat[pl.ds(start, C), :]
        out[slot] = jnp.where(upper, rows[:, 512:], rows[:, :512])


def stacks(own, tiles):
    parts = [jnp.concatenate([own[t + 1], own[t], own[t - 1]], axis=0) for t in tiles]
    return jnp.concatenate(parts, axis=1)


def flatten_weights(total, out, at):
    turned = total[...].T.astype(BF16)
    for group in range(4):
        out[at + 3 * C * group : at + 3 * C * (group + 1), :] = turned[
            :, LANES * group : LANES * (group + 1)
        ]


def output_kernel(slots, hidden, rects, live, up_w, out, rows_out, flat):
    pairs = hidden.shape[0] // EDGE

    def block_step(block):
        alive = jnp.broadcast_to(live[pl.ds(block, 1), :], (C, LANES))
        start = pl.multiple_of((block - 1) * C, 16)
        spreads = [spread_sub(rects[4 * block + inner]) for inner in range(4)]
        upward = dot(up_w[...], jnp.concatenate(spreads, axis=1))
        for inner in range(4):
            for half in range(2):
                part = upward[half * C : (half + 1) * C, LANES * inner : LANES * (inner + 1)]
                value = hidden[EDGE * block + 2 * inner + half] + part
                at = LANES * (2 * inner + half)
                rows_out[pl.ds(start, C), at : at + LANES] = (value * alive).astype(BF16)

    loop(1, pairs - 1, block_step, 2)
    to_blocks(slots, rows_out, flat, out)


def side_kernel(rects, cot_grid, low_cols, grad_c, flat, grad_own, up_g, coarse_g):
    tiles = low_cols.shape[0]
    up_g[...] = jnp.zeros_like(up_g)
    coarse_g[...] = jnp.zeros_like(coarse_g)

    def up_step(block):
        spreads = []
        pairs = []
        for inner in range(4):
            coarse = 4 * block + inner
            spreads.append(spread_sub(rects[coarse]))
            pairs.append(
                jnp.concatenate([cot_grid[2 * coarse], cot_grid[2 * coarse + 1]], axis=0)
            )
        up_g[:, 0 : 2 * C] += dot(
            jnp.concatenate(spreads, axis=1), jnp.concatenate(pairs, axis=1), (1, 1)
        )

    loop(1, tiles // 4 - 1, up_step, 2)
    zero = jnp.zeros((C, LANES), BF16)
    for coarse in range(1, 4):
        grad_own[coarse] = zero
        grad_own[tiles - 1 - coarse] = zero

    def copy_step(coarse):
        grad_own[coarse] = grad_c[coarse]

    loop(4, tiles - 4, copy_step, 8)
    masks = depth_masks(32, 4)

    def weight_step(index):
        at = [2 + 4 * index + inner for inner in range(4)]
        rights = [depth_columns(low_cols[tile], masks, 32) for tile in at]
        coarse_g[0 : 9 * C, :] += dot(
            jnp.concatenate(rights, axis=1), stacks(grad_own, at), (1, 1)
        )

    loop(0, (tiles - 4) // 4, weight_step, 3)
    flatten_weights(coarse_g, flat, 0)
    flat[12 * C :, :] = up_g[...].astype(BF16)


def backward_kernel(
    grad_c, from_left, from_right, hidden, cot_grid, live, coarse_w, down_w,
    grad_h, grad_d, pack_low, pack_high, coarse_p, grad_x, even, odd,
):
    tiles = grad_c.shape[0]
    fill_columns(grad_c, from_left, from_right, grad_x, 2)
    conv_steps(coarse_p, coarse_w, lambda tile: grad_x[tile], tiles, 32, 4, even, odd)
    anchors = anchor_mask(4)

    def step(block):
        alive = jnp.broadcast_to(live[pl.ds(block, 1), :], (C, LANES))
        keep = alive * anchors
        spreads = []
        for inner in range(4):
            coarse = 4 * block + inner
            down = (conv_sum(coarse_p, coarse) * keep).astype(BF16)
            grad_d[coarse] = down
            spreads.append(spread_sub(down))
        acts = dot(down_w[...], jnp.concatenate(spreads, axis=1), (0, 0))
        for inner in range(4):
            for side in range(2):
                tile = EDGE * block + 2 * inner + side
                slope = silu_parts(hidden[tile])[1]
                part = acts[side * C : (side + 1) * C, LANES * inner : LANES * (inner + 1)]
                grad = cot_grid[tile].astype(F32) + part * slope
                grad_h[tile] = (grad * alive).astype(BF16)

    loop(0, tiles // 4, step, 2)
    pack_columns(grad_h, pack_low, pack_high, 1)


def weight_kernel(grid, grad_h, grad_d, hidden, early, joined, grad_own, fine_g, down_g, even, odd):
    tiles = grad_h.shape[0]
    shift = tiles - 16
    fine_g[...] = jnp.zeros_like(fine_g)
    down_g[...] = jnp.zeros_like(down_g)
    zero = jnp.zeros((C, LANES), BF16)
    for tile in range(3, 8):
        grad_own[tile] = zero
        grad_own[tiles - 1 - tile] = zero

    def copy_step(tile):
        grad_own[tile] = grad_h[tile]

    loop(8, tiles - 8, copy_step, 8)
    masks = depth_masks(16, 4)
    edges = edge_masks(1)
    halves = own_masks()

    groups = (tiles - 8) // 8

    def fill(buffer, group):
        for inner in range(8):
            tile = 4 + 8 * group + inner
            lower, upper = grid[tile], grid[tile + shift]
            base = pair_columns(*pair_tiles(lower, upper, halves), edges, 1)
            buffer[:, LANES * inner : LANES * (inner + 1)] = depth_columns(base, masks, 16)

    def multiply(buffer, group):
        at = [4 + 8 * group + inner for inner in range(8)]
        fine_g[0 : 9 * C, :] += dot(buffer[...], stacks(grad_own, at), (1, 1))

    fill(even, 0)

    def fine_step(index):
        fill(odd, 2 * index + 1)
        multiply(even, 2 * index)
        fill(even, jnp.minimum(2 * index + 2, groups - 1))
        multiply(odd, 2 * index + 1)

    loop(0, groups // 2, fine_step)
    if groups % 2:
        multiply(even, groups - 1)

    def down_step(index):
        lefts = []
        rights = []
        for inner in range(4):
            coarse = 4 + 4 * index + inner
            lefts.append(spread_sub(grad_d[coarse]))
            actives = [silu_parts(hidden[2 * coarse + side])[0].astype(BF16) for side in range(2)]
            rights.append(jnp.concatenate(actives, axis=0))
        down_g[:, 0 : 2 * C] += dot(
            jnp.concatenate(lefts, axis=1), jnp.concatenate(rights, axis=1), (1, 1)
        )

    loop(0, (tiles // 2 - 8) // 4, down_step, 2)
    flatten_weights(fine_g, joined, 0)
    joined[12 * C : 16 * C, :] = down_g[...].astype(BF16)
    joined[16 * C :, :] = early[...]


def input_kernel(
    slots, grad_h, from_left, from_right, live, fine_w, out,
    fine_p, rows_out, flat, grad_x, even, odd,
):
    tiles = grad_h.shape[0]
    fill_columns(grad_h, from_left, from_right, grad_x, 1)
    conv_steps(fine_p, fine_w, lambda tile: grad_x[tile], tiles, 16, 4, even, odd)

    def block_step(block):
        alive = jnp.broadcast_to(live[pl.ds(block, 1), :], (C, LANES))
        start = pl.multiple_of((block - 1) * C, 16)
        for inner in range(EDGE):
            value = conv_sum(fine_p, EDGE * block + inner)
            rows_out[pl.ds(start, C), LANES * inner : LANES * (inner + 1)] = (
                value * alive
            ).astype(BF16)

    loop(1, tiles // EDGE - 1, block_step, 2)
    to_blocks(slots, rows_out, flat, out)


def finish_kernel(scale, total, fine, down, coarse, up):
    for out, at in ((fine, 0), (coarse, 16 * C)):
        for along in range(3):
            first = at + C * along
            rows = [total[first + 3 * C * g : first + 3 * C * g + C, :] for g in range(4)]
            row = jnp.concatenate(rows, axis=1).astype(F32) * scale
            for index in range(9):
                out[3 * index + along] = row[:, C * index : C * (index + 1)]
    for out, at, turn in ((down, 12 * C, False), (up, 28 * C, True)):
        for index in range(4):
            rows = total[at + C * index : at + C * (index + 1), :].astype(F32) * scale
            for along in range(2):
                part = rows[:, C * along : C * (along + 1)]
                if turn:
                    out[2 * index + along] = part.T
                else:
                    out[:, 2 * index + along, :] = part


def call(kernel, inputs, outs, scratch=(), scalars=0, flops=0, limit=None):
    vmem = pl.BlockSpec(memory_space=pltpu.VMEM)
    smem = pl.BlockSpec(memory_space=pltpu.SMEM)
    held = SLACK
    for shape, kind in [(a.shape, a.dtype) for a in inputs[scalars:]] + list(outs) + list(scratch):
        rows, lanes = -(-shape[-2] // 16) * 16, -(-shape[-1] // LANES) * LANES
        held += math.prod(shape[:-2]) * rows * lanes * jnp.dtype(kind).itemsize
    moved = sum(math.prod(s) * jnp.dtype(d).itemsize for s, d in outs)
    moved += sum(math.prod(a.shape) * a.dtype.itemsize for a in inputs)
    return pl.pallas_call(
        kernel,
        out_shape=tuple(jax.ShapeDtypeStruct(s, d) for s, d in outs),
        in_specs=[smem] * scalars + [vmem] * (len(inputs) - scalars),
        out_specs=tuple(vmem for _ in outs),
        scratch_shapes=[pltpu.VMEM(s, d) for s, d in scratch],
        compiler_params=pltpu.CompilerParams(vmem_limit_bytes=limit or held),
        cost_estimate=pl.CostEstimate(flops=flops, bytes_accessed=moved, transcendentals=0),
        name=getattr(kernel, "func", kernel).__name__,
    )(*inputs)


def send(array, step_x, step_y):
    number_x, number_y = lax.axis_size("gx"), lax.axis_size("gy")
    pairs = []
    for i in range(number_x):
        for j in range(number_y):
            to_x, to_y = i + step_x, j + step_y
            if 0 <= to_x < number_x and 0 <= to_y < number_y:
                pairs.append((i * number_y + j, to_x * number_y + to_y))
    return lax.ppermute(array, ("gx", "gy"), pairs)


def reduce_share(joined):
    devices = lax.axis_size("gx") * lax.axis_size("gy")
    rows = joined.shape[0]
    share = -(-rows // devices)
    joined = jnp.pad(joined, ((0, share * devices - rows), (0, 0)))
    mine = lax.all_to_all(joined.reshape(devices, share, LANES), ("gx", "gy"), 0, 0)
    return jnp.sum(mine.astype(F32), axis=0).astype(BF16)


def spread_share(share):
    devices = lax.axis_size("gx") * lax.axis_size("gy")
    rows = share.shape[0]
    copies = jnp.broadcast_to(share[None], (devices, rows, LANES))
    full = lax.all_to_all(copies, ("gx", "gy"), 0, 0)
    return full.reshape(devices * rows, LANES)


def on_device(
    features, block_slots, block_count, cotangent, fine_weight, down_weight, coarse_weight,
    up_weight,
):
    number = features.shape[2]
    slots = block_slots.reshape(number)
    count = block_count.reshape(1)
    feats = features.reshape(number, C, VOX)
    cots = cotangent.reshape(number, C, VOX)
    tiles = EDGE * (number + 2)
    coarse_tiles = tiles // 2
    pairs = number // 2 + 2
    groups = pairs // 2
    fine_groups = pairs

    fine_3, coarse_3 = (weight.transpose(1, 0, 2) for weight in (fine_weight, coarse_weight))
    flag_rows, x_low, x_high, y_low, y_high = call(
        prepare_kernel,
        (slots, count, feats, cots),
        [((16, LANES), F32)]
        + [((number // 2 * C + 16, 384), BF16)] * 2
        + [((2 * C + 16, VOX), BF16)] * 2,
        [((number * C, VOX), BF16)],
        scalars=2,
        limit=56 * 1024 * 1024,
    )
    x_left = send(x_high, 1, 0)
    x_right = send(x_low, -1, 0)
    y_left = send(y_high, 0, 1)
    y_right = send(y_low, 0, -1)
    corner_low, corner_high = call(
        corner_kernel,
        (y_left, y_right),
        [((C + 16, 384), BF16), ((C + 16, 384), BF16)],
    )
    c_left = send(corner_high, 1, 0)
    c_right = send(corner_low, -1, 0)
    (grid_own, cot_grid, grad_r, fine_fore, fine_back, coarse_fore, coarse_back, down_w,
     up_w) = call(
        place_kernel,
        (slots, count, feats, cots, y_left, y_right, corner_low, fine_3, down_weight, coarse_3,
         up_weight),
        [
            ((tiles, C, LANES), BF16),
            ((EDGE * pairs, C, LANES), BF16),
            ((4 * pairs, C, LANES), F32),
        ]
        + [((3 * C, 9 * C), BF16)] * 4
        + [((4 * C, 2 * C), BF16), ((2 * C, 4 * C), BF16)],
        [
            (((number + 2) * C, VOX), BF16),
            ((pairs * C, 1024), BF16),
            ((number, C, VOX), BF16),
        ],
        scalars=2,
        flops=8 * 10**9,
    )
    grid, hidden, low_cols, rects, grad_c, live, pack_low, pack_high = call(
        forward_kernel,
        (grid_own, flag_rows, y_left, y_right, grad_r, x_left, x_right, c_left, c_right,
         fine_fore, down_w, coarse_fore),
        [
            ((tiles, C, LANES), BF16),
            ((EDGE * pairs, C, LANES), F32),
            ((4 * pairs, 3 * C, LANES), BF16),
            ((4 * pairs, C, LANES), BF16),
            ((4 * pairs, C, LANES), BF16),
            ((16, LANES), F32),
            ((groups, C, LANES), BF16),
            ((groups, C, LANES), BF16),
        ],
        [
            (((number + 2) * C, VOX), BF16),
            ((tiles + 2, 3 * C, LANES), F32),
            ((4 * pairs + 2, 3 * C, LANES), F32),
            ((tiles, C, LANES), F32),
            ((coarse_tiles, C, LANES), BF16),
            ((C, LANES), F32),
        ]
        + [((9 * C, 4 * LANES), BF16)] * 2,
        flops=8 * 10**9,
    )
    grad_left = send(pack_high, 1, 0)
    grad_right = send(pack_low, -1, 0)
    (early,) = call(
        side_kernel,
        (rects, cot_grid, low_cols, grad_c),
        [((16 * C, LANES), BF16)],
        [((4 * pairs, C, LANES), BF16), ((4 * C, LANES), F32), ((VOX, 3 * C), F32)],
        flops=8 * 10**9,
    )
    grad_h, grad_d, edge_low, edge_high = call(
        backward_kernel,
        (grad_c, grad_left, grad_right, hidden, cot_grid, live, coarse_back, down_w),
        [
            ((EDGE * pairs, C, LANES), BF16),
            ((4 * pairs, C, LANES), BF16),
            ((fine_groups, C, LANES), BF16),
            ((fine_groups, C, LANES), BF16),
        ],
        [((4 * pairs + 2, 3 * C, LANES), F32), ((4 * pairs, 3 * C, LANES), BF16)]
        + [((9 * C, 4 * LANES), BF16)] * 2,
        flops=8 * 10**9,
    )
    edge_left = send(edge_high, 1, 0)
    edge_right = send(edge_low, -1, 0)
    (joined,) = call(
        weight_kernel,
        (grid, grad_h, grad_d, hidden, early),
        [((32 * C, LANES), BF16)],
        [((EDGE * pairs, C, LANES), BF16), ((VOX, 3 * C), F32), ((4 * C, LANES), F32)]
        + [((9 * C, 8 * LANES), BF16)] * 2,
        flops=12 * 10**9,
    )
    joined, edge_left, edge_right, slots = lax.optimization_barrier(
        (joined, edge_left, edge_right, slots)
    )
    share = reduce_share(joined)
    (output,) = call(
        output_kernel,
        (slots, hidden, rects, live, up_w),
        [((number, C, VOX), BF16)],
        [((number // 2 * C, 1024), BF16), ((number // 2 * C, 1024), BF16)],
        scalars=1,
        flops=8 * 10**9,
    )
    share, output, slots = lax.optimization_barrier((share, output, slots))
    (input_grad,) = call(
        input_kernel,
        (slots, grad_h, edge_left, edge_right, live, fine_back),
        [((number, C, VOX), BF16)],
        [
            ((EDGE * pairs + 2, 3 * C, LANES), F32),
            ((number // 2 * C, 1024), BF16),
            ((number // 2 * C, 1024), BF16),
            ((EDGE * pairs, 3 * C, LANES), BF16),
        ]
        + [((9 * C, 4 * LANES), BF16)] * 2,
        scalars=1,
        flops=8 * 10**9,
    )
    total = spread_share(share)
    scale = 1.0 / math.sqrt(number * VOX * lax.axis_size("gx") * lax.axis_size("gy"))
    fine_total, down_total, coarse_total, up_total = call(
        functools.partial(finish_kernel, scale),
        (total,),
        [((27, C, C), F32), ((C, 8, C), F32), ((27, C, C), F32), ((8, C, C), F32)],
    )
    shape_out = (1, 1, number, C, VOX)
    return (
        output.reshape(shape_out),
        input_grad.reshape(shape_out),
        fine_total.transpose(1, 0, 2),
        down_total,
        coarse_total.transpose(1, 0, 2),
        up_total,
    )


def solution(mesh):
    split = P("gx", "gy", None, None, None)
    return jax.shard_map(
        on_device,
        mesh=mesh,
        in_specs=(split, P("gx", "gy", None), P("gx", "gy"), split, P(), P(), P(), P()),
        out_specs=(split, split, P(), P(), P(), P()),
        check_vma=False,
    )
```

```python
import functools
import math

import jax
import jax.numpy as jnp
from jax import lax
from jax.experimental import pallas as pl
from jax.experimental.pallas import tpu as pltpu
from jax.sharding import PartitionSpec as P

C = 48
EDGE = 8
VOX = 512
LANES = 128
F32 = jnp.float32
BF16 = jnp.bfloat16
SLACK = 8 * 1024 * 1024
SHIFTS = (0, 1, 16, 17)


def marks(rows, columns, row_key, column_key):
    across = column_key(lax.broadcasted_iota(jnp.int32, (1, columns), 1))
    down = row_key(lax.broadcasted_iota(jnp.int32, (rows, 1), 0))
    return jnp.where(down == across, 1.0, 0.0).astype(BF16)


def plain(index):
    return index


def own_source(column):
    lane, y = column % LANES, column // LANES
    x = lane % 16 - 4
    return jnp.where((x >= 0) & (x < 8), 64 * (lane // 16) + 8 * x + y, -1)


def halo_source(column):
    lane, y = column % LANES, column // LANES
    x = lane % 16
    at = 24 * (lane // 16) + y
    left = jnp.where((x >= 1) & (x < 4), at + 8 * (x - 1), -1)
    return jnp.where((x >= 12) & (x < 15), at + 8 * (x - 12) + 256, left)


def pair_source(column):
    lane, y = (column - 4) % LANES, column // LANES
    return 512 * (lane % 16 // 8) + 64 * (lane // 16) + 8 * (lane % 8) + y


def edge_source(column):
    at, side = column % 256, column // 256
    x = at % 24 // 8 + 5 * side
    return jnp.where(at < 192, 64 * (at // 24) + 8 * x + at % 8, -1)


def dot(left, right, contract=(1, 0)):
    dims = (((contract[0],), (contract[1],)), ((), ()))
    return lax.dot_general(left, right, dims, preferred_element_type=F32)


def roll(value, shift):
    return pltpu.roll(value, shift % LANES, 1)


def lane_ids(rows):
    return lax.broadcasted_iota(jnp.int32, (rows, LANES), 1)


def silu_parts(value):
    sigma = 1.0 / (1.0 + jnp.exp(-value))
    return value * sigma, sigma * (1.0 + value * (1.0 - sigma))


def depth_columns(base, masks, step):
    below = roll(base, step) * masks[0]
    above = roll(base, -step) * masks[1]
    return jnp.concatenate([below, base, above], axis=0)


def depth_masks(step, first):
    ids = (lane_ids(3 * C) - first) % LANES
    return (ids >= step).astype(BF16), (ids < LANES - step).astype(BF16)


def across_columns(tile, step):
    return jnp.concatenate([roll(tile, step), tile, roll(tile, -step)], axis=0)


def edge_masks(step):
    ids = lane_ids(C) % 8
    first, last = (ids == 4).astype(BF16), (ids == 4 - step).astype(BF16)
    return first, (ids != 4).astype(BF16), last, (ids != 4 - step).astype(BF16)


def pair_columns(tile, halo, masks, step):
    left = roll(halo, step) * masks[0] + roll(tile, step) * masks[1]
    right = roll(halo, -step) * masks[2] + roll(tile, -step) * masks[3]
    return jnp.concatenate([left, tile, right], axis=0)


def fill_columns(tiles, from_left, from_right, out, step):
    masks = edge_masks(step)

    def body(group):
        packed_left, packed_right = from_left[group], from_right[group]
        for place in range(8):
            tile = tiles[8 * group + place]
            left = roll(packed_left, -place) * masks[0] + roll(tile, step) * masks[1]
            right = roll(packed_right, 8 - step - place) * masks[2]
            right = right + roll(tile, -step) * masks[3]
            out[8 * group + place] = jnp.concatenate([left, tile, right], axis=0)

    loop(0, from_left.shape[0], body)


def pack_columns(tiles, low, high, step):
    masks = edge_masks(step)

    def body(group):
        lows, highs = [], []
        for place in range(8):
            tile = tiles[8 * group + place]
            lows.append(roll(tile * masks[0], place))
            highs.append(roll(tile * masks[2], place - 8 + step))
        for out, parts in ((low, lows), (high, highs)):
            while len(parts) > 1:
                parts = [a + b for a, b in zip(parts[::2], parts[1::2])]
            out[group] = parts[0]

    loop(0, low.shape[0], body)


def own_masks():
    own = own_lanes(C)
    return own.astype(BF16), jnp.logical_not(own).astype(BF16)


def pair_tiles(lower, upper, masks):
    turned = roll(upper, 8)
    return (
        lower * masks[0] + turned * masks[1],
        lower * masks[1] + turned * masks[0],
    )


def own_lanes(rows):
    across = lane_ids(rows) % 16
    return (across >= 4) & (across < 12)


def join_halves(lower, upper):
    return jnp.where(own_lanes(lower.shape[0]), lower, roll(upper, 8))


def gather_sub(parts):
    even = lane_ids(C) % 2 == 0
    above = jnp.where(even, parts[2 * C : 3 * C], parts[3 * C :])
    total = jnp.where(even, parts[:C], parts[C : 2 * C]) + roll(above, -16)
    return total + roll(total, -1)


def spread_sub(anchored):
    return jnp.concatenate([anchored] + [roll(anchored, step) for step in SHIFTS[1:]], axis=0)


def anchor_mask(first):
    ids = (lane_ids(C) - first) % LANES
    return (((ids // 16) % 2 == 0) & (ids % 2 == 0)).astype(F32)


def loop(low, high, body, unroll=1):
    def step(index, carry):
        body(index)
        return carry

    lax.fori_loop(low, high, step, 0, unroll=unroll)


def join_rows(first, second):
    low = lane_ids(C) < 64
    lead = roll(second[:, :LANES], 64)
    parts = [
        first[:, :LANES],
        jnp.where(low, first[:, LANES:], lead),
        jnp.where(low, lead, roll(second[:, LANES:], 64)),
    ]
    return jnp.concatenate(parts, axis=1)


def split_rows(joined):
    low = lane_ids(C) < 64
    middle = roll(joined[:, LANES : 2 * LANES], 64)
    last = roll(joined[:, 2 * LANES :], 64)
    second = jnp.concatenate([jnp.where(low, middle, last), last], axis=1)
    return joined[:, : 2 * LANES], second


def prepare_kernel(slots, count, feats, cots, flag_rows, x_low, x_high, y_low, y_high, rows_in):
    number = feats.shape[0]
    rows = lax.broadcasted_iota(jnp.int32, (16, LANES), 0)
    flags = jnp.zeros((16, LANES), F32)
    zero = jnp.zeros((C, VOX), BF16)
    first = jnp.zeros((), jnp.int32)
    last = jnp.zeros((), jnp.int32)
    for slot in range(number):
        live = slot < count[0]
        place = slots[slot]
        block = jnp.where(live, feats[slot], zero)
        rows_in[pl.ds(pl.multiple_of(place * C, 16), C), :] = block
        flags = jnp.where(rows == place, jnp.where(live, 1.0, 0.0), flags)
        first = jnp.where(place == 0, slot, first)
        last = jnp.where(place == number - 1, slot, last)
    flag_rows[...] = flags
    packed = dot(rows_in[...], marks(VOX, 512, plain, edge_source)).astype(BF16)
    spare = jnp.zeros((16, 2 * LANES), BF16)
    for out, at in ((x_low, 0), (x_high, 256)):
        for pair in range(number // 2):
            edges = [packed[C * i : C * (i + 1), at : at + 256] for i in (2 * pair, 2 * pair + 1)]
            out[C * pair : C * (pair + 1), :] = join_rows(*edges)
        out[C * number // 2 :, :LANES] = flags.astype(BF16)
        out[C * number // 2 :, LANES:] = spare
    for out, index, slot in ((y_low, 0, first), (y_high, number - 1, last)):
        live = slot < count[0]
        out[0:C, :] = rows_in[C * index : C * (index + 1), :]
        out[C : 2 * C, :] = jnp.where(live, cots[slot], zero)
        out[2 * C :, :] = (jnp.zeros((16, VOX), F32) + jnp.where(live, 1.0, 0.0)).astype(BF16)


def corner_kernel(y_left, y_right, low, high):
    rows = jnp.concatenate([y_left[0:C, :], y_right[0:C, :]], axis=0)
    packed = dot(rows, marks(VOX, 512, plain, edge_source)).astype(BF16)
    ids = lax.broadcasted_iota(jnp.int32, (16, LANES), 0)
    flags = jnp.where(ids == 0, y_left[2 * C :, :LANES], y_right[2 * C :, :LANES])
    spare = jnp.zeros((16, 2 * LANES), BF16)
    for out, at in ((low, 0), (high, 256)):
        out[0:C, :] = join_rows(packed[:C, at : at + 256], packed[C:, at : at + 256])
        out[C:, :LANES] = flags
        out[C:, LANES:] = spare


def arrange_weights(fine, down, coarse, up, fine_w, fine_b, coarse_w, coarse_b, down_w, up_w):
    for source, fore, back in ((fine, fine_w, fine_b), (coarse, coarse_w, coarse_b)):
        for along in range(3):
            rows = slice(C * along, C * (along + 1))
            turned_rows = slice(C * (2 - along), C * (3 - along))
            ahead = []
            behind = []
            for depth in range(3):
                for across in range(3):
                    ahead.append(source[9 * depth + 3 * across + along])
                    behind.append(source[9 * (2 - depth) + 3 * (2 - across) + along].T)
            fore[rows, :] = jnp.concatenate(ahead, axis=1)
            back[turned_rows, :] = jnp.concatenate(behind, axis=1)
    for index in range(4):
        pair = [down[:, 2 * index, :], down[:, 2 * index + 1, :]]
        down_w[C * index : C * (index + 1), :] = jnp.concatenate(pair, axis=1)
    for along in range(2):
        row = jnp.concatenate([up[2 * index + along] for index in range(4)], axis=1)
        up_w[C * along : C * (along + 1), :] = row


def place_kernel(
    slots, count, feats, cots, y_left, y_right, c_low, fine, down, coarse, up,
    grid, cot_grid, grad_r, fine_w, fine_b, coarse_w, coarse_b, down_w, up_w,
    rows_in, rows_cot, cot,
):
    arrange_weights(fine, down, coarse, up, fine_w, fine_b, coarse_w, coarse_b, down_w, up_w)
    number = feats.shape[0]
    last = number + 1
    zero = jnp.zeros((C, VOX), BF16)
    rows_in[0:C, :] = y_left[0:C, :]
    rows_in[last * C : (last + 1) * C, :] = y_right[0:C, :]
    for slot in range(number):
        live = slot < count[0]
        place = slots[slot]
        start = pl.multiple_of((place + 1) * C, 16)
        rows_in[pl.ds(start, C), :] = jnp.where(live, feats[slot], zero)
        cot[place] = jnp.where(live, cots[slot], zero)
    pairs = number // 2 + 2
    for group in range(pairs):
        at = group * C
        lower = y_left[C : 2 * C, :] if group == 0 else cot[group - 1]
        upper = y_right[C : 2 * C, :] if group == pairs - 1 else cot[group + number // 2 - 1]
        rows_cot[at : at + C, 0:512] = lower
        rows_cot[at : at + C, 512:1024] = upper
    for pair in range(4):
        placed_cot = dot(
            rows_cot[...], marks(1024, 256, plain, lambda j, at=256 * pair: pair_source(j + at))
        )
        placed = dot(
            rows_in[...], marks(VOX, 256, plain, lambda j, at=256 * pair: own_source(j + at))
        )
        for half in range(2):
            span = slice(LANES * half, LANES * (half + 1))
            for block in range(last + 1):
                tile = EDGE * block + 2 * pair + half
                grid[tile] = placed[block * C : (block + 1) * C, span].astype(BF16)
            for block in range(pairs):
                tile = EDGE * block + 2 * pair + half
                cot_grid[tile] = placed_cot[block * C : (block + 1) * C, span].astype(BF16)

    def rect_step(block):
        tiles = []
        for inner in range(4):
            tile = EDGE * block + 2 * inner
            tiles.append(jnp.concatenate([cot_grid[tile], cot_grid[tile + 1]], axis=0))
        parts = dot(up_w[...], jnp.concatenate(tiles, axis=1), (0, 0))
        for inner in range(4):
            grad_r[4 * block + inner] = gather_sub(parts[:, LANES * inner : LANES * (inner + 1)])

    loop(0, pairs, rect_step, 2)


def conv_steps(sums, weight, load, tiles, step, first, even, odd):
    masks = depth_masks(step, first)

    def fill(buffer, tile):
        for i in range(4):
            cols = depth_columns(load(tile + i), masks, step)
            buffer[:, LANES * i : LANES * (i + 1)] = cols

    def multiply(buffer, tile, carry):
        out = dot(weight[...], buffer[...])

        def part(along, i):
            return out[C * along : C * (along + 1), LANES * i : LANES * (i + 1)]

        sums[tile] += part(2, 0)
        sums[tile + 1] = carry + part(1, 0) + part(2, 1)
        sums[tile + 2] = part(0, 0) + part(1, 1) + part(2, 2)
        sums[tile + 3] = part(0, 1) + part(1, 2) + part(2, 3)
        sums[tile + 4] = part(0, 2) + part(1, 3)
        return part(0, 3)

    fill(even, 0)
    sums[0] = jnp.zeros((C, LANES), F32)

    def body(index, carry):
        tile = 8 * index
        fill(odd, tile + 4)
        carry = multiply(even, tile, carry)
        fill(even, jnp.minimum(tile + 8, tiles - 4))
        return multiply(odd, tile + 4, carry)

    lax.fori_loop(0, tiles // 8, body, jnp.zeros((C, LANES), F32))


def forward_kernel(
    grid_own, flags, y_left, y_right, grad_r, x_left, x_right, c_left, c_right, fine_w, down_w,
    coarse_w,
    grid, hidden, low_cols, rects, grad_c, live, pack_low, pack_high,
    rows_in, fine_p, coarse_p, hidden_all, lowered, live_all, even, odd,
):
    number = 2 * (x_left.shape[0] - 16) // C
    last = number + 1
    for at, left, right in ((0, x_left, x_right), (None, c_left, c_right)):
        for pair in range((left.shape[0] - 16) // C):
            rows = slice(C * pair, C * (pair + 1))
            lefts, rights = split_rows(left[rows, :]), split_rows(right[rows, :])
            for inner in range(2):
                block = last * inner if at is None else 2 * pair + inner + 1
                rows_in[block * C : (block + 1) * C, 0:256] = lefts[inner]
                rows_in[block * C : (block + 1) * C, 256:512] = rights[inner]
    across = lane_ids(16) % 16
    for start, middle, left, right in (
        (1, flags[...], x_left[number // 2 * C :, :LANES], x_right[number // 2 * C :, :LANES]),
        (0, y_left[2 * C :, :LANES], c_left[C:, :LANES], c_right[C:, :LANES]),
        (last, y_right[2 * C :, :LANES], c_left[C:, :LANES], c_right[C:, :LANES]),
    ):
        rows = jnp.where(across < 4, left.astype(F32), middle.astype(F32))
        rows = jnp.where(across >= 12, right.astype(F32), rows)
        if start == 1:
            live_all[1 : number + 1, :] = rows
        else:
            at = 0 if start == 0 else 1
            live_all[start : start + 1, :] = rows[at : at + 1, :]
    for pair in range(4):
        placed = dot(
            rows_in[...], marks(512, 256, plain, lambda j, at=256 * pair: halo_source(j + at))
        )
        for half in range(2):
            span = slice(LANES * half, LANES * (half + 1))
            for block in range(last + 1):
                tile = EDGE * block + 2 * pair + half
                halo = placed[block * C : (block + 1) * C, span].astype(BF16)
                grid[tile] = grid_own[tile] + halo
    live[...] = join_halves(live_all[0:16, :], live_all[8:24, :])
    tiles = grid.shape[0]
    conv_steps(fine_p, fine_w, lambda tile: across_columns(grid[tile], 1), tiles, 16, 0, even, odd)
    anchors = anchor_mask(0)

    def lower_step(block):
        alive = jnp.broadcast_to(live_all[pl.ds(block, 1), :], (C, LANES))
        keep = alive * anchors
        pairs = []
        for inner in range(4):
            actives = []
            for half in range(2):
                tile = EDGE * block + 2 * inner + half
                value = fine_p[tile + 1] * alive
                hidden_all[tile] = value
                actives.append(silu_parts(value)[0].astype(BF16))
            pairs.append(jnp.concatenate(actives, axis=0))
        parts = dot(down_w[...], jnp.concatenate(pairs, axis=1))
        for inner in range(4):
            total = gather_sub(parts[:, LANES * inner : LANES * (inner + 1)])
            lowered[4 * block + inner] = (total * keep).astype(BF16)

    loop(0, last + 1, lower_step, 2)
    pairs = hidden.shape[0] // EDGE
    shift = last - pairs + 1
    edges = edge_masks(2)
    halves = own_masks()

    def pair_step(block):
        for inner in range(EDGE):
            tile = EDGE * block + inner
            hidden[tile] = join_halves(hidden_all[tile], hidden_all[tile + EDGE * shift])
        for inner in range(4):
            tile = 4 * block + inner
            lower, upper = lowered[tile], lowered[tile + 4 * shift]
            low_cols[tile] = pair_columns(*pair_tiles(lower, upper, halves), edges, 2)

    loop(0, pairs, pair_step, 2)
    conv_steps(coarse_p, coarse_w, lambda tile: low_cols[tile], 4 * pairs, 32, 4, even, odd)
    pair_anchors = anchor_mask(4)

    def grad_step(block):
        alive = jnp.broadcast_to(live[pl.ds(block, 1), :], (C, LANES))
        keep = alive * pair_anchors
        for inner in range(4):
            coarse = 4 * block + inner
            smooth, slope = silu_parts(coarse_p[coarse + 1])
            rects[coarse] = (smooth * pair_anchors).astype(BF16)
            grad_c[coarse] = (grad_r[coarse] * slope * keep).astype(BF16)

    loop(0, pairs, grad_step, 2)
    pack_columns(grad_c, pack_low, pack_high, 2)


def to_blocks(slots, rows_out, flat, out):
    flat[...] = dot(rows_out[...], marks(1024, 1024, pair_source, plain)).astype(BF16)
    number = out.shape[0]
    for slot in range(number):
        place = slots[slot]
        upper = place >= number // 2
        start = pl.multiple_of(jnp.where(upper, place - number // 2, place) * C, 16)
        rows = flat[pl.ds(start, C), :]
        out[slot] = jnp.where(upper, rows[:, 512:], rows[:, :512])


def stacks(own, tiles):
    parts = [jnp.concatenate([own[t + 1], own[t], own[t - 1]], axis=0) for t in tiles]
    return jnp.concatenate(parts, axis=1)


def flatten_weights(total, out, at):
    turned = total[...].T.astype(BF16)
    for group in range(4):
        out[at + 3 * C * group : at + 3 * C * (group + 1), :] = turned[
            :, LANES * group : LANES * (group + 1)
        ]


def output_kernel(slots, hidden, rects, live, up_w, out, rows_out, flat):
    pairs = hidden.shape[0] // EDGE

    def block_step(block):
        alive = jnp.broadcast_to(live[pl.ds(block, 1), :], (C, LANES))
        start = pl.multiple_of((block - 1) * C, 16)
        spreads = [spread_sub(rects[4 * block + inner]) for inner in range(4)]
        upward = dot(up_w[...], jnp.concatenate(spreads, axis=1))
        for inner in range(4):
            for half in range(2):
                part = upward[half * C : (half + 1) * C, LANES * inner : LANES * (inner + 1)]
                value = hidden[EDGE * block + 2 * inner + half] + part
                at = LANES * (2 * inner + half)
                rows_out[pl.ds(start, C), at : at + LANES] = (value * alive).astype(BF16)

    loop(1, pairs - 1, block_step, 2)
    to_blocks(slots, rows_out, flat, out)


def side_kernel(rects, cot_grid, low_cols, grad_c, flat, grad_own, up_g, coarse_g):
    tiles = low_cols.shape[0]
    up_g[...] = jnp.zeros_like(up_g)
    coarse_g[...] = jnp.zeros_like(coarse_g)

    def up_step(block):
        spreads = []
        pairs = []
        for inner in range(4):
            coarse = 4 * block + inner
            spreads.append(spread_sub(rects[coarse]))
            pairs.append(
                jnp.concatenate([cot_grid[2 * coarse], cot_grid[2 * coarse + 1]], axis=0)
            )
        up_g[:, 0 : 2 * C] += dot(
            jnp.concatenate(spreads, axis=1), jnp.concatenate(pairs, axis=1), (1, 1)
        )

    loop(1, tiles // 4 - 1, up_step, 2)
    zero = jnp.zeros((C, LANES), BF16)
    for coarse in range(1, 4):
        grad_own[coarse] = zero
        grad_own[tiles - 1 - coarse] = zero

    def copy_step(coarse):
        grad_own[coarse] = grad_c[coarse]

    loop(4, tiles - 4, copy_step, 8)
    masks = depth_masks(32, 4)

    def weight_step(index):
        at = [2 + 4 * index + inner for inner in range(4)]
        rights = [depth_columns(low_cols[tile], masks, 32) for tile in at]
        coarse_g[0 : 9 * C, :] += dot(
            jnp.concatenate(rights, axis=1), stacks(grad_own, at), (1, 1)
        )

    loop(0, (tiles - 4) // 4, weight_step, 3)
    flatten_weights(coarse_g, flat, 0)
    flat[12 * C :, :] = up_g[...].astype(BF16)


def backward_kernel(
    grad_c, from_left, from_right, hidden, cot_grid, live, coarse_w, down_w,
    grad_h, grad_d, pack_low, pack_high, coarse_p, grad_x, even, odd,
):
    tiles = grad_c.shape[0]
    fill_columns(grad_c, from_left, from_right, grad_x, 2)
    conv_steps(coarse_p, coarse_w, lambda tile: grad_x[tile], tiles, 32, 4, even, odd)
    anchors = anchor_mask(4)

    def step(block):
        alive = jnp.broadcast_to(live[pl.ds(block, 1), :], (C, LANES))
        keep = alive * anchors
        spreads = []
        for inner in range(4):
            coarse = 4 * block + inner
            down = (coarse_p[coarse + 1] * keep).astype(BF16)
            grad_d[coarse] = down
            spreads.append(spread_sub(down))
        acts = dot(down_w[...], jnp.concatenate(spreads, axis=1), (0, 0))
        for inner in range(4):
            for side in range(2):
                tile = EDGE * block + 2 * inner + side
                slope = silu_parts(hidden[tile])[1]
                part = acts[side * C : (side + 1) * C, LANES * inner : LANES * (inner + 1)]
                grad = cot_grid[tile].astype(F32) + part * slope
                grad_h[tile] = (grad * alive).astype(BF16)

    loop(0, tiles // 4, step, 2)
    pack_columns(grad_h, pack_low, pack_high, 1)


def weight_kernel(grid, grad_h, grad_d, hidden, early, joined, grad_own, fine_g, down_g):
    tiles = grad_h.shape[0]
    shift = tiles - 16
    fine_g[...] = jnp.zeros_like(fine_g)
    down_g[...] = jnp.zeros_like(down_g)
    zero = jnp.zeros((C, LANES), BF16)
    for tile in range(3, 8):
        grad_own[tile] = zero
        grad_own[tiles - 1 - tile] = zero

    def copy_step(tile):
        grad_own[tile] = grad_h[tile]

    loop(8, tiles - 8, copy_step, 8)
    masks = depth_masks(16, 4)
    edges = edge_masks(1)
    halves = own_masks()

    def fine_step(index):
        at = [4 + 8 * index + inner for inner in range(8)]
        rights = []
        for tile in at:
            lower, upper = grid[tile], grid[tile + shift]
            base = pair_columns(*pair_tiles(lower, upper, halves), edges, 1)
            rights.append(depth_columns(base, masks, 16))
        fine_g[0 : 9 * C, :] += dot(
            jnp.concatenate(rights, axis=1), stacks(grad_own, at), (1, 1)
        )

    loop(0, (tiles - 8) // 8, fine_step)

    def down_step(index):
        lefts = []
        rights = []
        for inner in range(4):
            coarse = 4 + 4 * index + inner
            lefts.append(spread_sub(grad_d[coarse]))
            actives = [silu_parts(hidden[2 * coarse + side])[0].astype(BF16) for side in range(2)]
            rights.append(jnp.concatenate(actives, axis=0))
        down_g[:, 0 : 2 * C] += dot(
            jnp.concatenate(lefts, axis=1), jnp.concatenate(rights, axis=1), (1, 1)
        )

    loop(0, (tiles // 2 - 8) // 4, down_step, 2)
    flatten_weights(fine_g, joined, 0)
    joined[12 * C : 16 * C, :] = down_g[...].astype(BF16)
    joined[16 * C :, :] = early[...]


def input_kernel(
    slots, grad_h, from_left, from_right, live, fine_w, out,
    fine_p, rows_out, flat, grad_x, even, odd,
):
    tiles = grad_h.shape[0]
    fill_columns(grad_h, from_left, from_right, grad_x, 1)
    conv_steps(fine_p, fine_w, lambda tile: grad_x[tile], tiles, 16, 4, even, odd)

    def block_step(block):
        alive = jnp.broadcast_to(live[pl.ds(block, 1), :], (C, LANES))
        start = pl.multiple_of((block - 1) * C, 16)
        for inner in range(EDGE):
            value = fine_p[EDGE * block + inner + 1]
            rows_out[pl.ds(start, C), LANES * inner : LANES * (inner + 1)] = (
                value * alive
            ).astype(BF16)

    loop(1, tiles // EDGE - 1, block_step, 2)
    to_blocks(slots, rows_out, flat, out)


def finish_kernel(scale, total, fine, down, coarse, up):
    for out, at in ((fine, 0), (coarse, 16 * C)):
        for along in range(3):
            first = at + C * along
            rows = [total[first + 3 * C * g : first + 3 * C * g + C, :] for g in range(4)]
            row = jnp.concatenate(rows, axis=1).astype(F32) * scale
            for index in range(9):
                out[3 * index + along] = row[:, C * index : C * (index + 1)]
    for out, at, turn in ((down, 12 * C, False), (up, 28 * C, True)):
        for index in range(4):
            rows = total[at + C * index : at + C * (index + 1), :].astype(F32) * scale
            for along in range(2):
                part = rows[:, C * along : C * (along + 1)]
                if turn:
                    out[2 * index + along] = part.T
                else:
                    out[:, 2 * index + along, :] = part


def call(kernel, inputs, outs, scratch=(), scalars=0, flops=0, limit=None):
    vmem = pl.BlockSpec(memory_space=pltpu.VMEM)
    smem = pl.BlockSpec(memory_space=pltpu.SMEM)
    held = SLACK
    for shape, kind in [(a.shape, a.dtype) for a in inputs[scalars:]] + list(outs) + list(scratch):
        rows, lanes = -(-shape[-2] // 16) * 16, -(-shape[-1] // LANES) * LANES
        held += math.prod(shape[:-2]) * rows * lanes * jnp.dtype(kind).itemsize
    moved = sum(math.prod(s) * jnp.dtype(d).itemsize for s, d in outs)
    moved += sum(math.prod(a.shape) * a.dtype.itemsize for a in inputs)
    return pl.pallas_call(
        kernel,
        out_shape=tuple(jax.ShapeDtypeStruct(s, d) for s, d in outs),
        in_specs=[smem] * scalars + [vmem] * (len(inputs) - scalars),
        out_specs=tuple(vmem for _ in outs),
        scratch_shapes=[pltpu.VMEM(s, d) for s, d in scratch],
        compiler_params=pltpu.CompilerParams(vmem_limit_bytes=limit or held),
        cost_estimate=pl.CostEstimate(flops=flops, bytes_accessed=moved, transcendentals=0),
        name=getattr(kernel, "func", kernel).__name__,
    )(*inputs)


def send(array, step_x, step_y):
    number_x, number_y = lax.axis_size("gx"), lax.axis_size("gy")
    pairs = []
    for i in range(number_x):
        for j in range(number_y):
            to_x, to_y = i + step_x, j + step_y
            if 0 <= to_x < number_x and 0 <= to_y < number_y:
                pairs.append((i * number_y + j, to_x * number_y + to_y))
    return lax.ppermute(array, ("gx", "gy"), pairs)


def reduce_share(joined):
    devices = lax.axis_size("gx") * lax.axis_size("gy")
    rows = joined.shape[0]
    share = -(-rows // devices)
    joined = jnp.pad(joined, ((0, share * devices - rows), (0, 0)))
    mine = lax.all_to_all(joined.reshape(devices, share, LANES), ("gx", "gy"), 0, 0)
    return jnp.sum(mine.astype(F32), axis=0).astype(BF16)


def spread_share(share):
    devices = lax.axis_size("gx") * lax.axis_size("gy")
    rows = share.shape[0]
    copies = jnp.broadcast_to(share[None], (devices, rows, LANES))
    full = lax.all_to_all(copies, ("gx", "gy"), 0, 0)
    return full.reshape(devices * rows, LANES)


def on_device(
    features, block_slots, block_count, cotangent, fine_weight, down_weight, coarse_weight,
    up_weight,
):
    number = features.shape[2]
    slots = block_slots.reshape(number)
    count = block_count.reshape(1)
    feats = features.reshape(number, C, VOX)
    cots = cotangent.reshape(number, C, VOX)
    tiles = EDGE * (number + 2)
    coarse_tiles = tiles // 2
    pairs = number // 2 + 2
    groups = pairs // 2
    fine_groups = pairs

    fine_3, coarse_3 = (weight.transpose(1, 0, 2) for weight in (fine_weight, coarse_weight))
    flag_rows, x_low, x_high, y_low, y_high = call(
        prepare_kernel,
        (slots, count, feats, cots),
        [((16, LANES), F32)]
        + [((number // 2 * C + 16, 384), BF16)] * 2
        + [((2 * C + 16, VOX), BF16)] * 2,
        [((number * C, VOX), BF16)],
        scalars=2,
        limit=56 * 1024 * 1024,
    )
    x_left = send(x_high, 1, 0)
    x_right = send(x_low, -1, 0)
    y_left = send(y_high, 0, 1)
    y_right = send(y_low, 0, -1)
    corner_low, corner_high = call(
        corner_kernel,
        (y_left, y_right),
        [((C + 16, 384), BF16), ((C + 16, 384), BF16)],
    )
    c_left = send(corner_high, 1, 0)
    c_right = send(corner_low, -1, 0)
    (grid_own, cot_grid, grad_r, fine_fore, fine_back, coarse_fore, coarse_back, down_w,
     up_w) = call(
        place_kernel,
        (slots, count, feats, cots, y_left, y_right, corner_low, fine_3, down_weight, coarse_3,
         up_weight),
        [
            ((tiles, C, LANES), BF16),
            ((EDGE * pairs, C, LANES), BF16),
            ((4 * pairs, C, LANES), F32),
        ]
        + [((3 * C, 9 * C), BF16)] * 4
        + [((4 * C, 2 * C), BF16), ((2 * C, 4 * C), BF16)],
        [
            (((number + 2) * C, VOX), BF16),
            ((pairs * C, 1024), BF16),
            ((number, C, VOX), BF16),
        ],
        scalars=2,
        flops=8 * 10**9,
    )
    grid, hidden, low_cols, rects, grad_c, live, pack_low, pack_high = call(
        forward_kernel,
        (grid_own, flag_rows, y_left, y_right, grad_r, x_left, x_right, c_left, c_right,
         fine_fore, down_w, coarse_fore),
        [
            ((tiles, C, LANES), BF16),
            ((EDGE * pairs, C, LANES), F32),
            ((4 * pairs, 3 * C, LANES), BF16),
            ((4 * pairs, C, LANES), BF16),
            ((4 * pairs, C, LANES), BF16),
            ((16, LANES), F32),
            ((groups, C, LANES), BF16),
            ((groups, C, LANES), BF16),
        ],
        [
            (((number + 2) * C, VOX), BF16),
            ((tiles + 1, C, LANES), F32),
            ((4 * pairs + 1, C, LANES), F32),
            ((tiles, C, LANES), F32),
            ((coarse_tiles, C, LANES), BF16),
            ((C, LANES), F32),
        ]
        + [((9 * C, 4 * LANES), BF16)] * 2,
        flops=8 * 10**9,
    )
    grad_left = send(pack_high, 1, 0)
    grad_right = send(pack_low, -1, 0)
    (early,) = call(
        side_kernel,
        (rects, cot_grid, low_cols, grad_c),
        [((16 * C, LANES), BF16)],
        [((4 * pairs, C, LANES), BF16), ((4 * C, LANES), F32), ((VOX, 3 * C), F32)],
        flops=8 * 10**9,
    )
    grad_h, grad_d, edge_low, edge_high = call(
        backward_kernel,
        (grad_c, grad_left, grad_right, hidden, cot_grid, live, coarse_back, down_w),
        [
            ((EDGE * pairs, C, LANES), BF16),
            ((4 * pairs, C, LANES), BF16),
            ((fine_groups, C, LANES), BF16),
            ((fine_groups, C, LANES), BF16),
        ],
        [((4 * pairs + 1, C, LANES), F32), ((4 * pairs, 3 * C, LANES), BF16)]
        + [((9 * C, 4 * LANES), BF16)] * 2,
        flops=8 * 10**9,
    )
    edge_left = send(edge_high, 1, 0)
    edge_right = send(edge_low, -1, 0)
    (joined,) = call(
        weight_kernel,
        (grid, grad_h, grad_d, hidden, early),
        [((32 * C, LANES), BF16)],
        [((EDGE * pairs, C, LANES), BF16), ((VOX, 3 * C), F32), ((4 * C, LANES), F32)],
        flops=12 * 10**9,
    )
    joined, edge_left, edge_right, slots = lax.optimization_barrier(
        (joined, edge_left, edge_right, slots)
    )
    share = reduce_share(joined)
    (output,) = call(
        output_kernel,
        (slots, hidden, rects, live, up_w),
        [((number, C, VOX), BF16)],
        [((number // 2 * C, 1024), BF16), ((number // 2 * C, 1024), BF16)],
        scalars=1,
        flops=8 * 10**9,
    )
    share, output, slots = lax.optimization_barrier((share, output, slots))
    (input_grad,) = call(
        input_kernel,
        (slots, grad_h, edge_left, edge_right, live, fine_back),
        [((number, C, VOX), BF16)],
        [
            ((EDGE * pairs + 1, C, LANES), F32),
            ((number // 2 * C, 1024), BF16),
            ((number // 2 * C, 1024), BF16),
            ((EDGE * pairs, 3 * C, LANES), BF16),
        ]
        + [((9 * C, 4 * LANES), BF16)] * 2,
        scalars=1,
        flops=8 * 10**9,
    )
    total = spread_share(share)
    scale = 1.0 / math.sqrt(number * VOX * lax.axis_size("gx") * lax.axis_size("gy"))
    fine_total, down_total, coarse_total, up_total = call(
        functools.partial(finish_kernel, scale),
        (total,),
        [((27, C, C), F32), ((C, 8, C), F32), ((27, C, C), F32), ((8, C, C), F32)],
    )
    shape_out = (1, 1, number, C, VOX)
    return (
        output.reshape(shape_out),
        input_grad.reshape(shape_out),
        fine_total.transpose(1, 0, 2),
        down_total,
        coarse_total.transpose(1, 0, 2),
        up_total,
    )


def solution(mesh):
    split = P("gx", "gy", None, None, None)
    return jax.shard_map(
        on_device,
        mesh=mesh,
        in_specs=(split, P("gx", "gy", None), P("gx", "gy"), split, P(), P(), P(), P()),
        out_specs=(split, split, P(), P(), P(), P()),
        check_vma=False,
    )
```

```python
import functools
import math

import jax
import jax.numpy as jnp
from jax import lax
from jax.experimental import pallas as pl
from jax.experimental.pallas import tpu as pltpu
from jax.sharding import PartitionSpec as P

C = 48
EDGE = 8
VOX = 512
LANES = 128
F32 = jnp.float32
BF16 = jnp.bfloat16
SLACK = 8 * 1024 * 1024
SHIFTS = (0, 1, 16, 17)


def marks(rows, columns, row_key, column_key):
    across = column_key(lax.broadcasted_iota(jnp.int32, (1, columns), 1))
    down = row_key(lax.broadcasted_iota(jnp.int32, (rows, 1), 0))
    return jnp.where(down == across, 1.0, 0.0).astype(BF16)


def plain(index):
    return index


def own_source(column):
    lane, y = column % LANES, column // LANES
    x = lane % 16 - 4
    return jnp.where((x >= 0) & (x < 8), 64 * (lane // 16) + 8 * x + y, -1)


def halo_source(column):
    lane, y = column % LANES, column // LANES
    x = lane % 16
    at = 24 * (lane // 16) + y
    left = jnp.where((x >= 1) & (x < 4), at + 8 * (x - 1), -1)
    return jnp.where((x >= 12) & (x < 15), at + 8 * (x - 12) + 256, left)


def pair_source(column):
    lane, y = (column - 4) % LANES, column // LANES
    return 512 * (lane % 16 // 8) + 64 * (lane // 16) + 8 * (lane % 8) + y


def edge_source(column):
    at, side = column % 256, column // 256
    x = at % 24 // 8 + 5 * side
    return jnp.where(at < 192, 64 * (at // 24) + 8 * x + at % 8, -1)


def dot(left, right, contract=(1, 0)):
    dims = (((contract[0],), (contract[1],)), ((), ()))
    return lax.dot_general(left, right, dims, preferred_element_type=F32)


def roll(value, shift):
    return pltpu.roll(value, shift % LANES, 1)


def lane_ids(rows):
    return lax.broadcasted_iota(jnp.int32, (rows, LANES), 1)


def silu_parts(value):
    sigma = 1.0 / (1.0 + jnp.exp(-value))
    return value * sigma, sigma * (1.0 + value * (1.0 - sigma))


def depth_columns(base, masks, step):
    below = roll(base, step) * masks[0]
    above = roll(base, -step) * masks[1]
    return jnp.concatenate([below, base, above], axis=0)


def depth_masks(step, first):
    ids = (lane_ids(3 * C) - first) % LANES
    return (ids >= step).astype(BF16), (ids < LANES - step).astype(BF16)


def across_columns(tile, step):
    return jnp.concatenate([roll(tile, step), tile, roll(tile, -step)], axis=0)


def edge_masks(step):
    ids = lane_ids(C) % 8
    first, last = (ids == 4).astype(BF16), (ids == 4 - step).astype(BF16)
    return first, (ids != 4).astype(BF16), last, (ids != 4 - step).astype(BF16)


def pair_columns(tile, halo, masks, step):
    left = roll(halo, step) * masks[0] + roll(tile, step) * masks[1]
    right = roll(halo, -step) * masks[2] + roll(tile, -step) * masks[3]
    return jnp.concatenate([left, tile, right], axis=0)


def fill_columns(tiles, from_left, from_right, out, step):
    masks = edge_masks(step)

    def body(group):
        packed_left, packed_right = from_left[group], from_right[group]
        for place in range(8):
            tile = tiles[8 * group + place]
            left = roll(packed_left, -place) * masks[0] + roll(tile, step) * masks[1]
            right = roll(packed_right, 8 - step - place) * masks[2]
            right = right + roll(tile, -step) * masks[3]
            out[8 * group + place] = jnp.concatenate([left, tile, right], axis=0)

    loop(0, from_left.shape[0], body)


def pack_columns(tiles, low, high, step):
    masks = edge_masks(step)

    def body(group):
        lows, highs = [], []
        for place in range(8):
            tile = tiles[8 * group + place]
            lows.append(roll(tile * masks[0], place))
            highs.append(roll(tile * masks[2], place - 8 + step))
        for out, parts in ((low, lows), (high, highs)):
            while len(parts) > 1:
                parts = [a + b for a, b in zip(parts[::2], parts[1::2])]
            out[group] = parts[0]

    loop(0, low.shape[0], body)


def own_masks():
    own = own_lanes(C)
    return own.astype(BF16), jnp.logical_not(own).astype(BF16)


def pair_tiles(lower, upper, masks):
    turned = roll(upper, 8)
    return (
        lower * masks[0] + turned * masks[1],
        lower * masks[1] + turned * masks[0],
    )


def own_lanes(rows):
    across = lane_ids(rows) % 16
    return (across >= 4) & (across < 12)


def join_halves(lower, upper):
    return jnp.where(own_lanes(lower.shape[0]), lower, roll(upper, 8))


def gather_sub(parts):
    even = lane_ids(C) % 2 == 0
    above = jnp.where(even, parts[2 * C : 3 * C], parts[3 * C :])
    total = jnp.where(even, parts[:C], parts[C : 2 * C]) + roll(above, -16)
    return total + roll(total, -1)


def spread_sub(anchored):
    return jnp.concatenate([anchored] + [roll(anchored, step) for step in SHIFTS[1:]], axis=0)


def anchor_mask(first):
    ids = (lane_ids(C) - first) % LANES
    return (((ids // 16) % 2 == 0) & (ids % 2 == 0)).astype(F32)


def loop(low, high, body, unroll=1):
    def step(index, carry):
        body(index)
        return carry

    lax.fori_loop(low, high, step, 0, unroll=unroll)


def join_rows(first, second):
    low = lane_ids(C) < 64
    lead = roll(second[:, :LANES], 64)
    parts = [
        first[:, :LANES],
        jnp.where(low, first[:, LANES:], lead),
        jnp.where(low, lead, roll(second[:, LANES:], 64)),
    ]
    return jnp.concatenate(parts, axis=1)


def split_rows(joined):
    low = lane_ids(C) < 64
    middle = roll(joined[:, LANES : 2 * LANES], 64)
    last = roll(joined[:, 2 * LANES :], 64)
    second = jnp.concatenate([jnp.where(low, middle, last), last], axis=1)
    return joined[:, : 2 * LANES], second


def prepare_kernel(slots, count, feats, cots, flag_rows, x_low, x_high, y_low, y_high, rows_in):
    number = feats.shape[0]
    rows = lax.broadcasted_iota(jnp.int32, (16, LANES), 0)
    flags = jnp.zeros((16, LANES), F32)
    zero = jnp.zeros((C, VOX), BF16)
    first = jnp.zeros((), jnp.int32)
    last = jnp.zeros((), jnp.int32)
    for slot in range(number):
        live = slot < count[0]
        place = slots[slot]
        block = jnp.where(live, feats[slot], zero)
        rows_in[pl.ds(pl.multiple_of(place * C, 16), C), :] = block
        flags = jnp.where(rows == place, jnp.where(live, 1.0, 0.0), flags)
        first = jnp.where(place == 0, slot, first)
        last = jnp.where(place == number - 1, slot, last)
    flag_rows[...] = flags
    packed = dot(rows_in[...], marks(VOX, 512, plain, edge_source)).astype(BF16)
    spare = jnp.zeros((16, 2 * LANES), BF16)
    for out, at in ((x_low, 0), (x_high, 256)):
        for pair in range(number // 2):
            edges = [packed[C * i : C * (i + 1), at : at + 256] for i in (2 * pair, 2 * pair + 1)]
            out[C * pair : C * (pair + 1), :] = join_rows(*edges)
        out[C * number // 2 :, :LANES] = flags.astype(BF16)
        out[C * number // 2 :, LANES:] = spare
    for out, index, slot in ((y_low, 0, first), (y_high, number - 1, last)):
        live = slot < count[0]
        out[0:C, :] = rows_in[C * index : C * (index + 1), :]
        out[C : 2 * C, :] = jnp.where(live, cots[slot], zero)
        out[2 * C :, :] = (jnp.zeros((16, VOX), F32) + jnp.where(live, 1.0, 0.0)).astype(BF16)


def corner_kernel(y_left, y_right, low, high):
    rows = jnp.concatenate([y_left[0:C, :], y_right[0:C, :]], axis=0)
    packed = dot(rows, marks(VOX, 512, plain, edge_source)).astype(BF16)
    ids = lax.broadcasted_iota(jnp.int32, (16, LANES), 0)
    flags = jnp.where(ids == 0, y_left[2 * C :, :LANES], y_right[2 * C :, :LANES])
    spare = jnp.zeros((16, 2 * LANES), BF16)
    for out, at in ((low, 0), (high, 256)):
        out[0:C, :] = join_rows(packed[:C, at : at + 256], packed[C:, at : at + 256])
        out[C:, :LANES] = flags
        out[C:, LANES:] = spare


def arrange_weights(fine, down, coarse, up, fine_w, fine_b, coarse_w, coarse_b, down_w, up_w):
    for source, fore, back in ((fine, fine_w, fine_b), (coarse, coarse_w, coarse_b)):
        for along in range(3):
            rows = slice(C * along, C * (along + 1))
            turned_rows = slice(C * (2 - along), C * (3 - along))
            ahead = []
            behind = []
            for depth in range(3):
                for across in range(3):
                    ahead.append(source[9 * depth + 3 * across + along])
                    behind.append(source[9 * (2 - depth) + 3 * (2 - across) + along].T)
            fore[rows, :] = jnp.concatenate(ahead, axis=1)
            back[turned_rows, :] = jnp.concatenate(behind, axis=1)
    for index in range(4):
        pair = [down[:, 2 * index, :], down[:, 2 * index + 1, :]]
        down_w[C * index : C * (index + 1), :] = jnp.concatenate(pair, axis=1)
    for along in range(2):
        row = jnp.concatenate([up[2 * index + along] for index in range(4)], axis=1)
        up_w[C * along : C * (along + 1), :] = row


def place_kernel(
    slots, count, feats, cots, y_left, y_right, c_low, fine, down, coarse, up,
    grid, cot_grid, grad_r, fine_w, fine_b, coarse_w, coarse_b, down_w, up_w,
    rows_in, rows_cot, cot,
):
    arrange_weights(fine, down, coarse, up, fine_w, fine_b, coarse_w, coarse_b, down_w, up_w)
    number = feats.shape[0]
    last = number + 1
    zero = jnp.zeros((C, VOX), BF16)
    rows_in[0:C, :] = y_left[0:C, :]
    rows_in[last * C : (last + 1) * C, :] = y_right[0:C, :]
    for slot in range(number):
        live = slot < count[0]
        place = slots[slot]
        start = pl.multiple_of((place + 1) * C, 16)
        rows_in[pl.ds(start, C), :] = jnp.where(live, feats[slot], zero)
        cot[place] = jnp.where(live, cots[slot], zero)
    pairs = number // 2 + 2
    for group in range(pairs):
        at = group * C
        lower = y_left[C : 2 * C, :] if group == 0 else cot[group - 1]
        upper = y_right[C : 2 * C, :] if group == pairs - 1 else cot[group + number // 2 - 1]
        rows_cot[at : at + C, 0:512] = lower
        rows_cot[at : at + C, 512:1024] = upper
    for pair in range(4):
        placed_cot = dot(
            rows_cot[...], marks(1024, 256, plain, lambda j, at=256 * pair: pair_source(j + at))
        )
        placed = dot(
            rows_in[...], marks(VOX, 256, plain, lambda j, at=256 * pair: own_source(j + at))
        )
        for half in range(2):
            span = slice(LANES * half, LANES * (half + 1))
            for block in range(last + 1):
                tile = EDGE * block + 2 * pair + half
                grid[tile] = placed[block * C : (block + 1) * C, span].astype(BF16)
            for block in range(pairs):
                tile = EDGE * block + 2 * pair + half
                cot_grid[tile] = placed_cot[block * C : (block + 1) * C, span].astype(BF16)

    def rect_step(block):
        tiles = []
        for inner in range(4):
            tile = EDGE * block + 2 * inner
            tiles.append(jnp.concatenate([cot_grid[tile], cot_grid[tile + 1]], axis=0))
        parts = dot(up_w[...], jnp.concatenate(tiles, axis=1), (0, 0))
        for inner in range(4):
            grad_r[4 * block + inner] = gather_sub(parts[:, LANES * inner : LANES * (inner + 1)])

    loop(0, pairs, rect_step, 2)


def conv_steps(sums, weight, load, tiles, step, first, even, odd):
    masks = depth_masks(step, first)

    def fill(buffer, tile):
        for i in range(4):
            cols = depth_columns(load(tile + i), masks, step)
            buffer[:, LANES * i : LANES * (i + 1)] = cols

    def multiply(buffer, tile, carry):
        out = dot(weight[...], buffer[...])

        def part(along, i):
            return out[C * along : C * (along + 1), LANES * i : LANES * (i + 1)]

        sums[tile] += part(2, 0)
        sums[tile + 1] = carry + part(1, 0) + part(2, 1)
        sums[tile + 2] = part(0, 0) + part(1, 1) + part(2, 2)
        sums[tile + 3] = part(0, 1) + part(1, 2) + part(2, 3)
        sums[tile + 4] = part(0, 2) + part(1, 3)
        return part(0, 3)

    fill(even, 0)
    sums[0] = jnp.zeros((C, LANES), F32)

    def body(index, carry):
        tile = 8 * index
        fill(odd, tile + 4)
        carry = multiply(even, tile, carry)
        fill(even, jnp.minimum(tile + 8, tiles - 4))
        return multiply(odd, tile + 4, carry)

    lax.fori_loop(0, tiles // 8, body, jnp.zeros((C, LANES), F32))


def forward_kernel(
    grid_own, flags, y_left, y_right, grad_r, x_left, x_right, c_left, c_right, fine_w, down_w,
    coarse_w,
    grid, hidden, low_cols, rects, grad_c, live, pack_low, pack_high,
    rows_in, fine_p, coarse_p, hidden_all, lowered, live_all, even, odd,
):
    number = 2 * (x_left.shape[0] - 16) // C
    last = number + 1
    for at, left, right in ((0, x_left, x_right), (None, c_left, c_right)):
        for pair in range((left.shape[0] - 16) // C):
            rows = slice(C * pair, C * (pair + 1))
            lefts, rights = split_rows(left[rows, :]), split_rows(right[rows, :])
            for inner in range(2):
                block = last * inner if at is None else 2 * pair + inner + 1
                rows_in[block * C : (block + 1) * C, 0:256] = lefts[inner]
                rows_in[block * C : (block + 1) * C, 256:512] = rights[inner]
    across = lane_ids(16) % 16
    for start, middle, left, right in (
        (1, flags[...], x_left[number // 2 * C :, :LANES], x_right[number // 2 * C :, :LANES]),
        (0, y_left[2 * C :, :LANES], c_left[C:, :LANES], c_right[C:, :LANES]),
        (last, y_right[2 * C :, :LANES], c_left[C:, :LANES], c_right[C:, :LANES]),
    ):
        rows = jnp.where(across < 4, left.astype(F32), middle.astype(F32))
        rows = jnp.where(across >= 12, right.astype(F32), rows)
        if start == 1:
            live_all[1 : number + 1, :] = rows
        else:
            at = 0 if start == 0 else 1
            live_all[start : start + 1, :] = rows[at : at + 1, :]
    for pair in range(4):
        placed = dot(
            rows_in[...], marks(512, 256, plain, lambda j, at=256 * pair: halo_source(j + at))
        )
        for half in range(2):
            span = slice(LANES * half, LANES * (half + 1))
            for block in range(last + 1):
                tile = EDGE * block + 2 * pair + half
                halo = placed[block * C : (block + 1) * C, span].astype(BF16)
                grid[tile] = grid_own[tile] + halo
    live[...] = join_halves(live_all[0:16, :], live_all[8:24, :])
    tiles = grid.shape[0]
    conv_steps(fine_p, fine_w, lambda tile: across_columns(grid[tile], 1), tiles, 16, 0, even, odd)
    anchors = anchor_mask(0)

    def lower_step(block):
        alive = jnp.broadcast_to(live_all[pl.ds(block, 1), :], (C, LANES))
        keep = alive * anchors
        pairs = []
        for inner in range(4):
            actives = []
            for half in range(2):
                tile = EDGE * block + 2 * inner + half
                value = fine_p[tile + 1] * alive
                hidden_all[tile] = value
                actives.append(silu_parts(value)[0].astype(BF16))
            pairs.append(jnp.concatenate(actives, axis=0))
        parts = dot(down_w[...], jnp.concatenate(pairs, axis=1))
        for inner in range(4):
            total = gather_sub(parts[:, LANES * inner : LANES * (inner + 1)])
            lowered[4 * block + inner] = (total * keep).astype(BF16)

    loop(0, last + 1, lower_step, 2)
    pairs = hidden.shape[0] // EDGE
    shift = last - pairs + 1
    edges = edge_masks(2)
    halves = own_masks()

    def pair_step(block):
        for inner in range(EDGE):
            tile = EDGE * block + inner
            hidden[tile] = join_halves(hidden_all[tile], hidden_all[tile + EDGE * shift])
        for inner in range(4):
            tile = 4 * block + inner
            lower, upper = lowered[tile], lowered[tile + 4 * shift]
            low_cols[tile] = pair_columns(*pair_tiles(lower, upper, halves), edges, 2)

    loop(0, pairs, pair_step, 2)
    conv_steps(coarse_p, coarse_w, lambda tile: low_cols[tile], 4 * pairs, 32, 4, even, odd)
    pair_anchors = anchor_mask(4)

    def grad_step(block):
        alive = jnp.broadcast_to(live[pl.ds(block, 1), :], (C, LANES))
        keep = alive * pair_anchors
        for inner in range(4):
            coarse = 4 * block + inner
            smooth, slope = silu_parts(coarse_p[coarse + 1])
            rects[coarse] = (smooth * pair_anchors).astype(BF16)
            grad_c[coarse] = (grad_r[coarse] * slope * keep).astype(BF16)

    loop(0, pairs, grad_step, 2)
    pack_columns(grad_c, pack_low, pack_high, 2)


def to_blocks(slots, rows_out, flat, out):
    flat[...] = dot(rows_out[...], marks(1024, 1024, pair_source, plain)).astype(BF16)
    number = out.shape[0]
    for slot in range(number):
        place = slots[slot]
        upper = place >= number // 2
        start = pl.multiple_of(jnp.where(upper, place - number // 2, place) * C, 16)
        rows = flat[pl.ds(start, C), :]
        out[slot] = jnp.where(upper, rows[:, 512:], rows[:, :512])


def stacks(own, tiles):
    parts = [jnp.concatenate([own[t + 1], own[t], own[t - 1]], axis=0) for t in tiles]
    return jnp.concatenate(parts, axis=1)


def flatten_weights(total, out, at):
    turned = total[...].T.astype(BF16)
    for group in range(4):
        out[at + 3 * C * group : at + 3 * C * (group + 1), :] = turned[
            :, LANES * group : LANES * (group + 1)
        ]


def output_kernel(slots, hidden, rects, live, up_w, out, rows_out, flat):
    pairs = hidden.shape[0] // EDGE

    def block_step(block):
        alive = jnp.broadcast_to(live[pl.ds(block, 1), :], (C, LANES))
        start = pl.multiple_of((block - 1) * C, 16)
        spreads = [spread_sub(rects[4 * block + inner]) for inner in range(4)]
        upward = dot(up_w[...], jnp.concatenate(spreads, axis=1))
        for inner in range(4):
            for half in range(2):
                part = upward[half * C : (half + 1) * C, LANES * inner : LANES * (inner + 1)]
                value = hidden[EDGE * block + 2 * inner + half] + part
                at = LANES * (2 * inner + half)
                rows_out[pl.ds(start, C), at : at + LANES] = (value * alive).astype(BF16)

    loop(1, pairs - 1, block_step, 2)
    to_blocks(slots, rows_out, flat, out)


def side_kernel(rects, cot_grid, low_cols, grad_c, flat, grad_own, up_g, coarse_g):
    tiles = low_cols.shape[0]
    up_g[...] = jnp.zeros_like(up_g)
    coarse_g[...] = jnp.zeros_like(coarse_g)

    def up_step(block):
        spreads = []
        pairs = []
        for inner in range(4):
            coarse = 4 * block + inner
            spreads.append(spread_sub(rects[coarse]))
            pairs.append(
                jnp.concatenate([cot_grid[2 * coarse], cot_grid[2 * coarse + 1]], axis=0)
            )
        up_g[:, 0 : 2 * C] += dot(
            jnp.concatenate(spreads, axis=1), jnp.concatenate(pairs, axis=1), (1, 1)
        )

    loop(1, tiles // 4 - 1, up_step, 2)
    zero = jnp.zeros((C, LANES), BF16)
    for coarse in range(1, 4):
        grad_own[coarse] = zero
        grad_own[tiles - 1 - coarse] = zero

    def copy_step(coarse):
        grad_own[coarse] = grad_c[coarse]

    loop(4, tiles - 4, copy_step, 8)
    masks = depth_masks(32, 4)

    def weight_step(index):
        at = [2 + 4 * index + inner for inner in range(4)]
        rights = [depth_columns(low_cols[tile], masks, 32) for tile in at]
        coarse_g[0 : 9 * C, :] += dot(
            jnp.concatenate(rights, axis=1), stacks(grad_own, at), (1, 1)
        )

    loop(0, (tiles - 4) // 4, weight_step, 3)
    flatten_weights(coarse_g, flat, 0)
    flat[12 * C :, :] = up_g[...].astype(BF16)


def backward_kernel(
    grad_c, from_left, from_right, hidden, cot_grid, live, coarse_w, down_w,
    grad_h, grad_d, pack_low, pack_high, coarse_p, grad_x, even, odd,
):
    tiles = grad_c.shape[0]
    fill_columns(grad_c, from_left, from_right, grad_x, 2)
    conv_steps(coarse_p, coarse_w, lambda tile: grad_x[tile], tiles, 32, 4, even, odd)
    anchors = anchor_mask(4)

    def step(block):
        alive = jnp.broadcast_to(live[pl.ds(block, 1), :], (C, LANES))
        keep = alive * anchors
        spreads = []
        for inner in range(4):
            coarse = 4 * block + inner
            down = (coarse_p[coarse + 1] * keep).astype(BF16)
            grad_d[coarse] = down
            spreads.append(spread_sub(down))
        acts = dot(down_w[...], jnp.concatenate(spreads, axis=1), (0, 0))
        for inner in range(4):
            for side in range(2):
                tile = EDGE * block + 2 * inner + side
                slope = silu_parts(hidden[tile])[1]
                part = acts[side * C : (side + 1) * C, LANES * inner : LANES * (inner + 1)]
                grad = cot_grid[tile].astype(F32) + part * slope
                grad_h[tile] = (grad * alive).astype(BF16)

    loop(0, tiles // 4, step, 2)
    pack_columns(grad_h, pack_low, pack_high, 1)


def weight_kernel(grid, grad_h, grad_d, hidden, early, joined, grad_own, fine_g, down_g):
    tiles = grad_h.shape[0]
    shift = tiles - 16
    fine_g[...] = jnp.zeros_like(fine_g)
    down_g[...] = jnp.zeros_like(down_g)
    zero = jnp.zeros((C, LANES), BF16)
    for tile in range(3, 8):
        grad_own[tile] = zero
        grad_own[tiles - 1 - tile] = zero

    def copy_step(tile):
        grad_own[tile] = grad_h[tile]

    loop(8, tiles - 8, copy_step, 8)
    masks = depth_masks(16, 4)
    edges = edge_masks(1)
    halves = own_masks()

    def fine_step(index):
        at = [4 + 8 * index + inner for inner in range(8)]
        rights = []
        for tile in at:
            lower, upper = grid[tile], grid[tile + shift]
            base = pair_columns(*pair_tiles(lower, upper, halves), edges, 1)
            rights.append(depth_columns(base, masks, 16))
        fine_g[0 : 9 * C, :] += dot(
            jnp.concatenate(rights, axis=1), stacks(grad_own, at), (1, 1)
        )

    loop(0, (tiles - 8) // 8, fine_step)

    def down_step(index):
        lefts = []
        rights = []
        for inner in range(4):
            coarse = 4 + 4 * index + inner
            lefts.append(spread_sub(grad_d[coarse]))
            actives = [silu_parts(hidden[2 * coarse + side])[0].astype(BF16) for side in range(2)]
            rights.append(jnp.concatenate(actives, axis=0))
        down_g[:, 0 : 2 * C] += dot(
            jnp.concatenate(lefts, axis=1), jnp.concatenate(rights, axis=1), (1, 1)
        )

    loop(0, (tiles // 2 - 8) // 4, down_step, 2)
    flatten_weights(fine_g, joined, 0)
    joined[12 * C : 16 * C, :] = down_g[...].astype(BF16)
    joined[16 * C :, :] = early[...]


def input_kernel(
    slots, grad_h, from_left, from_right, live, fine_w, out,
    fine_p, rows_out, flat, grad_x, even, odd,
):
    tiles = grad_h.shape[0]
    fill_columns(grad_h, from_left, from_right, grad_x, 1)
    conv_steps(fine_p, fine_w, lambda tile: grad_x[tile], tiles, 16, 4, even, odd)

    def block_step(block):
        alive = jnp.broadcast_to(live[pl.ds(block, 1), :], (C, LANES))
        start = pl.multiple_of((block - 1) * C, 16)
        for inner in range(EDGE):
            value = fine_p[EDGE * block + inner + 1]
            rows_out[pl.ds(start, C), LANES * inner : LANES * (inner + 1)] = (
                value * alive
            ).astype(BF16)

    loop(1, tiles // EDGE - 1, block_step, 2)
    to_blocks(slots, rows_out, flat, out)


def finish_kernel(scale, total, fine, down, coarse, up):
    for out, at in ((fine, 0), (coarse, 16 * C)):
        for along in range(3):
            first = at + C * along
            rows = [total[first + 3 * C * g : first + 3 * C * g + C, :] for g in range(4)]
            row = jnp.concatenate(rows, axis=1).astype(F32) * scale
            for index in range(9):
                out[3 * index + along] = row[:, C * index : C * (index + 1)]
    for out, at, turn in ((down, 12 * C, False), (up, 28 * C, True)):
        for index in range(4):
            rows = total[at + C * index : at + C * (index + 1), :].astype(F32) * scale
            for along in range(2):
                part = rows[:, C * along : C * (along + 1)]
                if turn:
                    out[2 * index + along] = part.T
                else:
                    out[:, 2 * index + along, :] = part


def call(kernel, inputs, outs, scratch=(), scalars=0, flops=0, limit=None):
    vmem = pl.BlockSpec(memory_space=pltpu.VMEM)
    smem = pl.BlockSpec(memory_space=pltpu.SMEM)
    held = SLACK
    for shape, kind in [(a.shape, a.dtype) for a in inputs[scalars:]] + list(outs) + list(scratch):
        rows, lanes = -(-shape[-2] // 16) * 16, -(-shape[-1] // LANES) * LANES
        held += math.prod(shape[:-2]) * rows * lanes * jnp.dtype(kind).itemsize
    moved = sum(math.prod(s) * jnp.dtype(d).itemsize for s, d in outs)
    moved += sum(math.prod(a.shape) * a.dtype.itemsize for a in inputs)
    return pl.pallas_call(
        kernel,
        out_shape=tuple(jax.ShapeDtypeStruct(s, d) for s, d in outs),
        in_specs=[smem] * scalars + [vmem] * (len(inputs) - scalars),
        out_specs=tuple(vmem for _ in outs),
        scratch_shapes=[pltpu.VMEM(s, d) for s, d in scratch],
        compiler_params=pltpu.CompilerParams(vmem_limit_bytes=limit or held),
        cost_estimate=pl.CostEstimate(flops=flops, bytes_accessed=moved, transcendentals=0),
        name=getattr(kernel, "func", kernel).__name__,
    )(*inputs)


def send(array, step_x, step_y):
    number_x, number_y = lax.axis_size("gx"), lax.axis_size("gy")
    pairs = []
    for i in range(number_x):
        for j in range(number_y):
            to_x, to_y = i + step_x, j + step_y
            if 0 <= to_x < number_x and 0 <= to_y < number_y:
                pairs.append((i * number_y + j, to_x * number_y + to_y))
    return lax.ppermute(array, ("gx", "gy"), pairs)


def reduce_share(joined):
    devices = lax.axis_size("gx") * lax.axis_size("gy")
    rows = joined.shape[0]
    share = -(-rows // devices)
    joined = jnp.pad(joined, ((0, share * devices - rows), (0, 0)))
    mine = lax.all_to_all(joined.reshape(devices, share, LANES), ("gx", "gy"), 0, 0)
    return jnp.sum(mine.astype(F32), axis=0).astype(BF16)


def spread_share(share):
    devices = lax.axis_size("gx") * lax.axis_size("gy")
    rows = share.shape[0]
    copies = jnp.broadcast_to(share[None], (devices, rows, LANES))
    full = lax.all_to_all(copies, ("gx", "gy"), 0, 0)
    return full.reshape(devices * rows, LANES)


def on_device(
    features, block_slots, block_count, cotangent, fine_weight, down_weight, coarse_weight,
    up_weight,
):
    number = features.shape[2]
    slots = block_slots.reshape(number)
    count = block_count.reshape(1)
    feats = features.reshape(number, C, VOX)
    cots = cotangent.reshape(number, C, VOX)
    tiles = EDGE * (number + 2)
    coarse_tiles = tiles // 2
    pairs = number // 2 + 2
    groups = pairs // 2
    fine_groups = pairs

    fine_3, coarse_3 = (weight.transpose(1, 0, 2) for weight in (fine_weight, coarse_weight))
    flag_rows, x_low, x_high, y_low, y_high = call(
        prepare_kernel,
        (slots, count, feats, cots),
        [((16, LANES), F32)]
        + [((number // 2 * C + 16, 384), BF16)] * 2
        + [((2 * C + 16, VOX), BF16)] * 2,
        [((number * C, VOX), BF16)],
        scalars=2,
        limit=56 * 1024 * 1024,
    )
    x_left = send(x_high, 1, 0)
    x_right = send(x_low, -1, 0)
    y_left = send(y_high, 0, 1)
    y_right = send(y_low, 0, -1)
    corner_low, corner_high = call(
        corner_kernel,
        (y_left, y_right),
        [((C + 16, 384), BF16), ((C + 16, 384), BF16)],
    )
    c_left = send(corner_high, 1, 0)
    c_right = send(corner_low, -1, 0)
    (grid_own, cot_grid, grad_r, fine_fore, fine_back, coarse_fore, coarse_back, down_w,
     up_w) = call(
        place_kernel,
        (slots, count, feats, cots, y_left, y_right, corner_low, fine_3, down_weight, coarse_3,
         up_weight),
        [
            ((tiles, C, LANES), BF16),
            ((EDGE * pairs, C, LANES), BF16),
            ((4 * pairs, C, LANES), F32),
        ]
        + [((3 * C, 9 * C), BF16)] * 4
        + [((4 * C, 2 * C), BF16), ((2 * C, 4 * C), BF16)],
        [
            (((number + 2) * C, VOX), BF16),
            ((pairs * C, 1024), BF16),
            ((number, C, VOX), BF16),
        ],
        scalars=2,
        flops=8 * 10**9,
    )
    grid, hidden, low_cols, rects, grad_c, live, pack_low, pack_high = call(
        forward_kernel,
        (grid_own, flag_rows, y_left, y_right, grad_r, x_left, x_right, c_left, c_right,
         fine_fore, down_w, coarse_fore),
        [
            ((tiles, C, LANES), BF16),
            ((EDGE * pairs, C, LANES), F32),
            ((4 * pairs, 3 * C, LANES), BF16),
            ((4 * pairs, C, LANES), BF16),
            ((4 * pairs, C, LANES), BF16),
            ((16, LANES), F32),
            ((groups, C, LANES), BF16),
            ((groups, C, LANES), BF16),
        ],
        [
            (((number + 2) * C, VOX), BF16),
            ((tiles + 1, C, LANES), F32),
            ((4 * pairs + 1, C, LANES), F32),
            ((tiles, C, LANES), F32),
            ((coarse_tiles, C, LANES), BF16),
            ((C, LANES), F32),
        ]
        + [((9 * C, 4 * LANES), BF16)] * 2,
        flops=8 * 10**9,
    )
    grad_left = send(pack_high, 1, 0)
    grad_right = send(pack_low, -1, 0)
    (early,) = call(
        side_kernel,
        (rects, cot_grid, low_cols, grad_c),
        [((16 * C, LANES), BF16)],
        [((4 * pairs, C, LANES), BF16), ((4 * C, LANES), F32), ((VOX, 3 * C), F32)],
        flops=8 * 10**9,
    )
    grad_h, grad_d, edge_low, edge_high = call(
        backward_kernel,
        (grad_c, grad_left, grad_right, hidden, cot_grid, live, coarse_back, down_w),
        [
            ((EDGE * pairs, C, LANES), BF16),
            ((4 * pairs, C, LANES), BF16),
            ((fine_groups, C, LANES), BF16),
            ((fine_groups, C, LANES), BF16),
        ],
        [((4 * pairs + 1, C, LANES), F32), ((4 * pairs, 3 * C, LANES), BF16)]
        + [((9 * C, 4 * LANES), BF16)] * 2,
        flops=8 * 10**9,
    )
    (joined,) = call(
        weight_kernel,
        (grid, grad_h, grad_d, hidden, early),
        [((32 * C, LANES), BF16)],
        [((EDGE * pairs, C, LANES), BF16), ((VOX, 3 * C), F32), ((4 * C, LANES), F32)],
        flops=12 * 10**9,
    )
    joined, slots = lax.optimization_barrier((joined, slots))
    share = reduce_share(joined)
    (output,) = call(
        output_kernel,
        (slots, hidden, rects, live, up_w),
        [((number, C, VOX), BF16)],
        [((number // 2 * C, 1024), BF16), ((number // 2 * C, 1024), BF16)],
        scalars=1,
        flops=8 * 10**9,
    )
    output, edge_low, edge_high = lax.optimization_barrier((output, edge_low, edge_high))
    edge_left = send(edge_high, 1, 0)
    edge_right = send(edge_low, -1, 0)
    share, output, slots, edge_left, edge_right = lax.optimization_barrier(
        (share, output, slots, edge_left, edge_right)
    )
    (input_grad,) = call(
        input_kernel,
        (slots, grad_h, edge_left, edge_right, live, fine_back),
        [((number, C, VOX), BF16)],
        [
            ((EDGE * pairs + 1, C, LANES), F32),
            ((number // 2 * C, 1024), BF16),
            ((number // 2 * C, 1024), BF16),
            ((EDGE * pairs, 3 * C, LANES), BF16),
        ]
        + [((9 * C, 4 * LANES), BF16)] * 2,
        scalars=1,
        flops=8 * 10**9,
    )
    total = spread_share(share)
    scale = 1.0 / math.sqrt(number * VOX * lax.axis_size("gx") * lax.axis_size("gy"))
    fine_total, down_total, coarse_total, up_total = call(
        functools.partial(finish_kernel, scale),
        (total,),
        [((27, C, C), F32), ((C, 8, C), F32), ((27, C, C), F32), ((8, C, C), F32)],
    )
    shape_out = (1, 1, number, C, VOX)
    return (
        output.reshape(shape_out),
        input_grad.reshape(shape_out),
        fine_total.transpose(1, 0, 2),
        down_total,
        coarse_total.transpose(1, 0, 2),
        up_total,
    )


def solution(mesh):
    split = P("gx", "gy", None, None, None)
    return jax.shard_map(
        on_device,
        mesh=mesh,
        in_specs=(split, P("gx", "gy", None), P("gx", "gy"), split, P(), P(), P(), P()),
        out_specs=(split, split, P(), P(), P(), P()),
        check_vma=False,
    )
```

```python
import functools
import math

import jax
import jax.numpy as jnp
from jax import lax
from jax.experimental import pallas as pl
from jax.experimental.pallas import tpu as pltpu
from jax.sharding import PartitionSpec as P

C = 48
EDGE = 8
VOX = 512
LANES = 128
F32 = jnp.float32
BF16 = jnp.bfloat16
SLACK = 8 * 1024 * 1024
SHIFTS = (0, 1, 16, 17)


def marks(rows, columns, row_key, column_key):
    across = column_key(lax.broadcasted_iota(jnp.int32, (1, columns), 1))
    down = row_key(lax.broadcasted_iota(jnp.int32, (rows, 1), 0))
    return jnp.where(down == across, 1.0, 0.0).astype(BF16)


def plain(index):
    return index


def own_source(column):
    lane, y = column % LANES, column // LANES
    x = lane % 16 - 4
    return jnp.where((x >= 0) & (x < 8), 64 * (lane // 16) + 8 * x + y, -1)


def halo_source(column):
    lane, y = column % LANES, column // LANES
    x = lane % 16
    at = 24 * (lane // 16) + y
    left = jnp.where((x >= 1) & (x < 4), at + 8 * (x - 1), -1)
    return jnp.where((x >= 12) & (x < 15), at + 8 * (x - 12) + 256, left)


def pair_source(column):
    lane, y = (column - 4) % LANES, column // LANES
    return 512 * (lane % 16 // 8) + 64 * (lane // 16) + 8 * (lane % 8) + y


def edge_source(column):
    at, side = column % 256, column // 256
    x = at % 24 // 8 + 5 * side
    return jnp.where(at < 192, 64 * (at // 24) + 8 * x + at % 8, -1)


def dot(left, right, contract=(1, 0)):
    dims = (((contract[0],), (contract[1],)), ((), ()))
    return lax.dot_general(left, right, dims, preferred_element_type=F32)


def roll(value, shift):
    return pltpu.roll(value, shift % LANES, 1)


def lane_ids(rows):
    return lax.broadcasted_iota(jnp.int32, (rows, LANES), 1)


def silu_parts(value):
    sigma = 1.0 / (1.0 + jnp.exp(-value))
    return value * sigma, sigma * (1.0 + value * (1.0 - sigma))


def depth_columns(base, masks, step):
    below = roll(base, step) * masks[0]
    above = roll(base, -step) * masks[1]
    return jnp.concatenate([below, base, above], axis=0)


def depth_masks(step, first):
    ids = (lane_ids(3 * C) - first) % LANES
    return (ids >= step).astype(BF16), (ids < LANES - step).astype(BF16)


def across_columns(tile, step):
    return jnp.concatenate([roll(tile, step), tile, roll(tile, -step)], axis=0)


def edge_masks(step):
    ids = lane_ids(C) % 8
    first, last = (ids == 4).astype(BF16), (ids == 4 - step).astype(BF16)
    return first, (ids != 4).astype(BF16), last, (ids != 4 - step).astype(BF16)


def pair_columns(tile, halo, masks, step):
    left = roll(halo, step) * masks[0] + roll(tile, step) * masks[1]
    right = roll(halo, -step) * masks[2] + roll(tile, -step) * masks[3]
    return jnp.concatenate([left, tile, right], axis=0)


def fill_columns(tiles, from_left, from_right, out, step):
    masks = edge_masks(step)

    def body(group):
        packed_left, packed_right = from_left[group], from_right[group]
        for place in range(8):
            tile = tiles[8 * group + place]
            left = roll(packed_left, -place) * masks[0] + roll(tile, step) * masks[1]
            right = roll(packed_right, 8 - step - place) * masks[2]
            right = right + roll(tile, -step) * masks[3]
            out[8 * group + place] = jnp.concatenate([left, tile, right], axis=0)

    loop(0, from_left.shape[0], body)


def pack_columns(tiles, low, high, step):
    masks = edge_masks(step)

    def body(group):
        lows, highs = [], []
        for place in range(8):
            tile = tiles[8 * group + place]
            lows.append(roll(tile * masks[0], place))
            highs.append(roll(tile * masks[2], place - 8 + step))
        for out, parts in ((low, lows), (high, highs)):
            while len(parts) > 1:
                parts = [a + b for a, b in zip(parts[::2], parts[1::2])]
            out[group] = parts[0]

    loop(0, low.shape[0], body)


def own_masks():
    own = own_lanes(C)
    return own.astype(BF16), jnp.logical_not(own).astype(BF16)


def pair_tiles(lower, upper, masks):
    turned = roll(upper, 8)
    return (
        lower * masks[0] + turned * masks[1],
        lower * masks[1] + turned * masks[0],
    )


def own_lanes(rows):
    across = lane_ids(rows) % 16
    return (across >= 4) & (across < 12)


def join_halves(lower, upper):
    return jnp.where(own_lanes(lower.shape[0]), lower, roll(upper, 8))


def gather_sub(parts):
    even = lane_ids(C) % 2 == 0
    above = jnp.where(even, parts[2 * C : 3 * C], parts[3 * C :])
    total = jnp.where(even, parts[:C], parts[C : 2 * C]) + roll(above, -16)
    return total + roll(total, -1)


def spread_sub(anchored):
    return jnp.concatenate([anchored] + [roll(anchored, step) for step in SHIFTS[1:]], axis=0)


def anchor_mask(first):
    ids = (lane_ids(C) - first) % LANES
    return (((ids // 16) % 2 == 0) & (ids % 2 == 0)).astype(F32)


def loop(low, high, body, unroll=1):
    def step(index, carry):
        body(index)
        return carry

    lax.fori_loop(low, high, step, 0, unroll=unroll)


def join_rows(first, second):
    low = lane_ids(C) < 64
    lead = roll(second[:, :LANES], 64)
    parts = [
        first[:, :LANES],
        jnp.where(low, first[:, LANES:], lead),
        jnp.where(low, lead, roll(second[:, LANES:], 64)),
    ]
    return jnp.concatenate(parts, axis=1)


def split_rows(joined):
    low = lane_ids(C) < 64
    middle = roll(joined[:, LANES : 2 * LANES], 64)
    last = roll(joined[:, 2 * LANES :], 64)
    second = jnp.concatenate([jnp.where(low, middle, last), last], axis=1)
    return joined[:, : 2 * LANES], second


def prepare_kernel(slots, count, feats, cots, flag_rows, x_low, x_high, y_low, y_high, rows_in):
    number = feats.shape[0]
    rows = lax.broadcasted_iota(jnp.int32, (16, LANES), 0)
    flags = jnp.zeros((16, LANES), F32)
    zero = jnp.zeros((C, VOX), BF16)
    first = jnp.zeros((), jnp.int32)
    last = jnp.zeros((), jnp.int32)
    for slot in range(number):
        live = slot < count[0]
        place = slots[slot]
        block = jnp.where(live, feats[slot], zero)
        rows_in[pl.ds(pl.multiple_of(place * C, 16), C), :] = block
        flags = jnp.where(rows == place, jnp.where(live, 1.0, 0.0), flags)
        first = jnp.where(place == 0, slot, first)
        last = jnp.where(place == number - 1, slot, last)
    flag_rows[...] = flags
    packed = dot(rows_in[...], marks(VOX, 512, plain, edge_source)).astype(BF16)
    spare = jnp.zeros((16, 2 * LANES), BF16)
    for out, at in ((x_low, 0), (x_high, 256)):
        for pair in range(number // 2):
            edges = [packed[C * i : C * (i + 1), at : at + 256] for i in (2 * pair, 2 * pair + 1)]
            out[C * pair : C * (pair + 1), :] = join_rows(*edges)
        out[C * number // 2 :, :LANES] = flags.astype(BF16)
        out[C * number // 2 :, LANES:] = spare
    for out, index, slot in ((y_low, 0, first), (y_high, number - 1, last)):
        live = slot < count[0]
        out[0:C, :] = rows_in[C * index : C * (index + 1), :]
        out[C : 2 * C, :] = jnp.where(live, cots[slot], zero)
        out[2 * C :, :] = (jnp.zeros((16, VOX), F32) + jnp.where(live, 1.0, 0.0)).astype(BF16)


def corner_kernel(y_left, y_right, low, high):
    rows = jnp.concatenate([y_left[0:C, :], y_right[0:C, :]], axis=0)
    packed = dot(rows, marks(VOX, 512, plain, edge_source)).astype(BF16)
    ids = lax.broadcasted_iota(jnp.int32, (16, LANES), 0)
    flags = jnp.where(ids == 0, y_left[2 * C :, :LANES], y_right[2 * C :, :LANES])
    spare = jnp.zeros((16, 2 * LANES), BF16)
    for out, at in ((low, 0), (high, 256)):
        out[0:C, :] = join_rows(packed[:C, at : at + 256], packed[C:, at : at + 256])
        out[C:, :LANES] = flags
        out[C:, LANES:] = spare


def arrange_weights(fine, down, coarse, up, fine_w, fine_b, coarse_w, coarse_b, down_w, up_w):
    for source, fore, back in ((fine, fine_w, fine_b), (coarse, coarse_w, coarse_b)):
        for along in range(3):
            rows = slice(C * along, C * (along + 1))
            turned_rows = slice(C * (2 - along), C * (3 - along))
            ahead = []
            behind = []
            for depth in range(3):
                for across in range(3):
                    ahead.append(source[9 * depth + 3 * across + along])
                    behind.append(source[9 * (2 - depth) + 3 * (2 - across) + along].T)
            fore[rows, :] = jnp.concatenate(ahead, axis=1)
            back[turned_rows, :] = jnp.concatenate(behind, axis=1)
    for index in range(4):
        pair = [down[:, 2 * index, :], down[:, 2 * index + 1, :]]
        down_w[C * index : C * (index + 1), :] = jnp.concatenate(pair, axis=1)
    for along in range(2):
        row = jnp.concatenate([up[2 * index + along] for index in range(4)], axis=1)
        up_w[C * along : C * (along + 1), :] = row


def place_kernel(
    slots, count, feats, cots, y_left, y_right, c_low, fine, down, coarse, up,
    grid, cot_grid, grad_r, fine_w, fine_b, coarse_w, coarse_b, down_w, up_w,
    rows_in, rows_cot, cot,
):
    arrange_weights(fine, down, coarse, up, fine_w, fine_b, coarse_w, coarse_b, down_w, up_w)
    number = feats.shape[0]
    last = number + 1
    zero = jnp.zeros((C, VOX), BF16)
    rows_in[0:C, :] = y_left[0:C, :]
    rows_in[last * C : (last + 1) * C, :] = y_right[0:C, :]
    for slot in range(number):
        live = slot < count[0]
        place = slots[slot]
        start = pl.multiple_of((place + 1) * C, 16)
        rows_in[pl.ds(start, C), :] = jnp.where(live, feats[slot], zero)
        cot[place] = jnp.where(live, cots[slot], zero)
    pairs = number // 2 + 2
    for group in range(pairs):
        at = group * C
        lower = y_left[C : 2 * C, :] if group == 0 else cot[group - 1]
        upper = y_right[C : 2 * C, :] if group == pairs - 1 else cot[group + number // 2 - 1]
        rows_cot[at : at + C, 0:512] = lower
        rows_cot[at : at + C, 512:1024] = upper
    for pair in range(4):
        placed_cot = dot(
            rows_cot[...], marks(1024, 256, plain, lambda j, at=256 * pair: pair_source(j + at))
        )
        placed = dot(
            rows_in[...], marks(VOX, 256, plain, lambda j, at=256 * pair: own_source(j + at))
        )
        for half in range(2):
            span = slice(LANES * half, LANES * (half + 1))
            for block in range(last + 1):
                tile = EDGE * block + 2 * pair + half
                grid[tile] = placed[block * C : (block + 1) * C, span].astype(BF16)
            for block in range(pairs):
                tile = EDGE * block + 2 * pair + half
                cot_grid[tile] = placed_cot[block * C : (block + 1) * C, span].astype(BF16)

    def rect_step(block):
        tiles = []
        for inner in range(4):
            tile = EDGE * block + 2 * inner
            tiles.append(jnp.concatenate([cot_grid[tile], cot_grid[tile + 1]], axis=0))
        parts = dot(up_w[...], jnp.concatenate(tiles, axis=1), (0, 0))
        for inner in range(4):
            grad_r[4 * block + inner] = gather_sub(parts[:, LANES * inner : LANES * (inner + 1)])

    loop(0, pairs, rect_step, 2)


def conv_steps(sums, weight, load, tiles, step, first, even, odd):
    masks = depth_masks(step, first)

    def fill(buffer, tile):
        for i in range(4):
            cols = depth_columns(load(tile + i), masks, step)
            buffer[:, LANES * i : LANES * (i + 1)] = cols

    def multiply(buffer, tile, carry):
        out = dot(weight[...], buffer[...])

        def part(along, i):
            return out[C * along : C * (along + 1), LANES * i : LANES * (i + 1)]

        sums[tile] += part(2, 0)
        sums[tile + 1] = carry + part(1, 0) + part(2, 1)
        sums[tile + 2] = part(0, 0) + part(1, 1) + part(2, 2)
        sums[tile + 3] = part(0, 1) + part(1, 2) + part(2, 3)
        sums[tile + 4] = part(0, 2) + part(1, 3)
        return part(0, 3)

    fill(even, 0)
    sums[0] = jnp.zeros((C, LANES), F32)

    def body(index, carry):
        tile = 8 * index
        fill(odd, tile + 4)
        carry = multiply(even, tile, carry)
        fill(even, jnp.minimum(tile + 8, tiles - 4))
        return multiply(odd, tile + 4, carry)

    lax.fori_loop(0, tiles // 8, body, jnp.zeros((C, LANES), F32))


def forward_kernel(
    grid_own, flags, y_left, y_right, grad_r, x_left, x_right, c_left, c_right, fine_w, down_w,
    coarse_w,
    grid, hidden, low_cols, rects, grad_c, live, pack_low, pack_high,
    rows_in, fine_p, coarse_p, hidden_all, lowered, live_all, even, odd,
):
    number = 2 * (x_left.shape[0] - 16) // C
    last = number + 1
    for at, left, right in ((0, x_left, x_right), (None, c_left, c_right)):
        for pair in range((left.shape[0] - 16) // C):
            rows = slice(C * pair, C * (pair + 1))
            lefts, rights = split_rows(left[rows, :]), split_rows(right[rows, :])
            for inner in range(2):
                block = last * inner if at is None else 2 * pair + inner + 1
                rows_in[block * C : (block + 1) * C, 0:256] = lefts[inner]
                rows_in[block * C : (block + 1) * C, 256:512] = rights[inner]
    across = lane_ids(16) % 16
    for start, middle, left, right in (
        (1, flags[...], x_left[number // 2 * C :, :LANES], x_right[number // 2 * C :, :LANES]),
        (0, y_left[2 * C :, :LANES], c_left[C:, :LANES], c_right[C:, :LANES]),
        (last, y_right[2 * C :, :LANES], c_left[C:, :LANES], c_right[C:, :LANES]),
    ):
        rows = jnp.where(across < 4, left.astype(F32), middle.astype(F32))
        rows = jnp.where(across >= 12, right.astype(F32), rows)
        if start == 1:
            live_all[1 : number + 1, :] = rows
        else:
            at = 0 if start == 0 else 1
            live_all[start : start + 1, :] = rows[at : at + 1, :]
    for pair in range(4):
        placed = dot(
            rows_in[...], marks(512, 256, plain, lambda j, at=256 * pair: halo_source(j + at))
        )
        for half in range(2):
            span = slice(LANES * half, LANES * (half + 1))
            for block in range(last + 1):
                tile = EDGE * block + 2 * pair + half
                halo = placed[block * C : (block + 1) * C, span].astype(BF16)
                grid[tile] = grid_own[tile] + halo
    live[...] = join_halves(live_all[0:16, :], live_all[8:24, :])
    tiles = grid.shape[0]
    conv_steps(fine_p, fine_w, lambda tile: across_columns(grid[tile], 1), tiles, 16, 0, even, odd)
    anchors = anchor_mask(0)

    def lower_step(block):
        alive = jnp.broadcast_to(live_all[pl.ds(block, 1), :], (C, LANES))
        keep = alive * anchors
        pairs = []
        for inner in range(4):
            actives = []
            for half in range(2):
                tile = EDGE * block + 2 * inner + half
                value = fine_p[tile + 1] * alive
                hidden_all[tile] = value
                actives.append(silu_parts(value)[0].astype(BF16))
            pairs.append(jnp.concatenate(actives, axis=0))
        parts = dot(down_w[...], jnp.concatenate(pairs, axis=1))
        for inner in range(4):
            total = gather_sub(parts[:, LANES * inner : LANES * (inner + 1)])
            lowered[4 * block + inner] = (total * keep).astype(BF16)

    loop(0, last + 1, lower_step, 2)
    pairs = hidden.shape[0] // EDGE
    shift = last - pairs + 1
    edges = edge_masks(2)
    halves = own_masks()

    def pair_step(block):
        for inner in range(EDGE):
            tile = EDGE * block + inner
            hidden[tile] = join_halves(hidden_all[tile], hidden_all[tile + EDGE * shift])
        for inner in range(4):
            tile = 4 * block + inner
            lower, upper = lowered[tile], lowered[tile + 4 * shift]
            low_cols[tile] = pair_columns(*pair_tiles(lower, upper, halves), edges, 2)

    loop(0, pairs, pair_step, 2)
    conv_steps(coarse_p, coarse_w, lambda tile: low_cols[tile], 4 * pairs, 32, 4, even, odd)
    pair_anchors = anchor_mask(4)

    def grad_step(block):
        alive = jnp.broadcast_to(live[pl.ds(block, 1), :], (C, LANES))
        keep = alive * pair_anchors
        for inner in range(4):
            coarse = 4 * block + inner
            smooth, slope = silu_parts(coarse_p[coarse + 1])
            rects[coarse] = (smooth * pair_anchors).astype(BF16)
            grad_c[coarse] = (grad_r[coarse] * slope * keep).astype(BF16)

    loop(0, pairs, grad_step, 2)
    pack_columns(grad_c, pack_low, pack_high, 2)


def to_blocks(slots, rows_out, flat, out):
    flat[...] = dot(rows_out[...], marks(1024, 1024, pair_source, plain)).astype(BF16)
    number = out.shape[0]
    for slot in range(number):
        place = slots[slot]
        upper = place >= number // 2
        start = pl.multiple_of(jnp.where(upper, place - number // 2, place) * C, 16)
        rows = flat[pl.ds(start, C), :]
        out[slot] = jnp.where(upper, rows[:, 512:], rows[:, :512])


def stacks(own, tiles):
    parts = [jnp.concatenate([own[t + 1], own[t], own[t - 1]], axis=0) for t in tiles]
    return jnp.concatenate(parts, axis=1)


def flatten_weights(total, out, at):
    turned = total[...].T.astype(BF16)
    for group in range(4):
        out[at + 3 * C * group : at + 3 * C * (group + 1), :] = turned[
            :, LANES * group : LANES * (group + 1)
        ]


def output_kernel(slots, hidden, rects, live, up_w, out, rows_out, flat):
    pairs = hidden.shape[0] // EDGE

    def block_step(block):
        alive = jnp.broadcast_to(live[pl.ds(block, 1), :], (C, LANES))
        start = pl.multiple_of((block - 1) * C, 16)
        spreads = [spread_sub(rects[4 * block + inner]) for inner in range(4)]
        upward = dot(up_w[...], jnp.concatenate(spreads, axis=1))
        for inner in range(4):
            for half in range(2):
                part = upward[half * C : (half + 1) * C, LANES * inner : LANES * (inner + 1)]
                value = hidden[EDGE * block + 2 * inner + half] + part
                at = LANES * (2 * inner + half)
                rows_out[pl.ds(start, C), at : at + LANES] = (value * alive).astype(BF16)

    loop(1, pairs - 1, block_step, 2)
    to_blocks(slots, rows_out, flat, out)


def side_kernel(rects, cot_grid, low_cols, grad_c, flat, grad_own, up_g, coarse_g):
    tiles = low_cols.shape[0]
    up_g[...] = jnp.zeros_like(up_g)
    coarse_g[...] = jnp.zeros_like(coarse_g)

    def up_step(block):
        spreads = []
        pairs = []
        for inner in range(4):
            coarse = 4 * block + inner
            spreads.append(spread_sub(rects[coarse]))
            pairs.append(
                jnp.concatenate([cot_grid[2 * coarse], cot_grid[2 * coarse + 1]], axis=0)
            )
        up_g[:, 0 : 2 * C] += dot(
            jnp.concatenate(spreads, axis=1), jnp.concatenate(pairs, axis=1), (1, 1)
        )

    loop(1, tiles // 4 - 1, up_step, 2)
    zero = jnp.zeros((C, LANES), BF16)
    for coarse in range(1, 4):
        grad_own[coarse] = zero
        grad_own[tiles - 1 - coarse] = zero

    def copy_step(coarse):
        grad_own[coarse] = grad_c[coarse]

    loop(4, tiles - 4, copy_step, 8)
    masks = depth_masks(32, 4)

    def weight_step(index):
        at = [2 + 4 * index + inner for inner in range(4)]
        rights = [depth_columns(low_cols[tile], masks, 32) for tile in at]
        coarse_g[0 : 9 * C, :] += dot(
            jnp.concatenate(rights, axis=1), stacks(grad_own, at), (1, 1)
        )

    loop(0, (tiles - 4) // 4, weight_step, 3)
    flatten_weights(coarse_g, flat, 0)
    flat[12 * C :, :] = up_g[...].astype(BF16)


def backward_kernel(
    grad_c, from_left, from_right, hidden, cot_grid, live, coarse_w, down_w,
    grad_h, grad_d, coarse_p, grad_x, even, odd,
):
    tiles = grad_c.shape[0]
    fill_columns(grad_c, from_left, from_right, grad_x, 2)
    conv_steps(coarse_p, coarse_w, lambda tile: grad_x[tile], tiles, 32, 4, even, odd)
    anchors = anchor_mask(4)

    def step(block):
        alive = jnp.broadcast_to(live[pl.ds(block, 1), :], (C, LANES))
        keep = alive * anchors
        spreads = []
        for inner in range(4):
            coarse = 4 * block + inner
            down = (coarse_p[coarse + 1] * keep).astype(BF16)
            grad_d[coarse] = down
            spreads.append(spread_sub(down))
        acts = dot(down_w[...], jnp.concatenate(spreads, axis=1), (0, 0))
        for inner in range(4):
            for side in range(2):
                tile = EDGE * block + 2 * inner + side
                slope = silu_parts(hidden[tile])[1]
                part = acts[side * C : (side + 1) * C, LANES * inner : LANES * (inner + 1)]
                grad = cot_grid[tile].astype(F32) + part * slope
                grad_h[tile] = (grad * alive).astype(BF16)

    loop(0, tiles // 4, step, 2)


def pack_kernel(grad_h, low, high):
    pack_columns(grad_h, low, high, 1)


def weight_kernel(grid, grad_h, grad_d, hidden, early, joined, grad_own, fine_g, down_g):
    tiles = grad_h.shape[0]
    shift = tiles - 16
    fine_g[...] = jnp.zeros_like(fine_g)
    down_g[...] = jnp.zeros_like(down_g)
    zero = jnp.zeros((C, LANES), BF16)
    for tile in range(3, 8):
        grad_own[tile] = zero
        grad_own[tiles - 1 - tile] = zero

    def copy_step(tile):
        grad_own[tile] = grad_h[tile]

    loop(8, tiles - 8, copy_step, 8)
    masks = depth_masks(16, 4)
    edges = edge_masks(1)
    halves = own_masks()

    def fine_step(index):
        at = [4 + 8 * index + inner for inner in range(8)]
        rights = []
        for tile in at:
            lower, upper = grid[tile], grid[tile + shift]
            base = pair_columns(*pair_tiles(lower, upper, halves), edges, 1)
            rights.append(depth_columns(base, masks, 16))
        fine_g[0 : 9 * C, :] += dot(
            jnp.concatenate(rights, axis=1), stacks(grad_own, at), (1, 1)
        )

    loop(0, (tiles - 8) // 8, fine_step)

    def down_step(index):
        lefts = []
        rights = []
        for inner in range(4):
            coarse = 4 + 4 * index + inner
            lefts.append(spread_sub(grad_d[coarse]))
            actives = [silu_parts(hidden[2 * coarse + side])[0].astype(BF16) for side in range(2)]
            rights.append(jnp.concatenate(actives, axis=0))
        down_g[:, 0 : 2 * C] += dot(
            jnp.concatenate(lefts, axis=1), jnp.concatenate(rights, axis=1), (1, 1)
        )

    loop(0, (tiles // 2 - 8) // 4, down_step, 2)
    flatten_weights(fine_g, joined, 0)
    joined[12 * C : 16 * C, :] = down_g[...].astype(BF16)
    joined[16 * C :, :] = early[...]


def input_kernel(
    slots, grad_h, from_left, from_right, live, fine_w, out,
    fine_p, rows_out, flat, grad_x, even, odd,
):
    tiles = grad_h.shape[0]
    fill_columns(grad_h, from_left, from_right, grad_x, 1)
    conv_steps(fine_p, fine_w, lambda tile: grad_x[tile], tiles, 16, 4, even, odd)

    def block_step(block):
        alive = jnp.broadcast_to(live[pl.ds(block, 1), :], (C, LANES))
        start = pl.multiple_of((block - 1) * C, 16)
        for inner in range(EDGE):
            value = fine_p[EDGE * block + inner + 1]
            rows_out[pl.ds(start, C), LANES * inner : LANES * (inner + 1)] = (
                value * alive
            ).astype(BF16)

    loop(1, tiles // EDGE - 1, block_step, 2)
    to_blocks(slots, rows_out, flat, out)


def sum_kernel(parts, copies):
    total = jnp.sum(parts[...].astype(F32), axis=0).astype(BF16)
    copies[...] = jnp.broadcast_to(total[None], copies.shape)


def finish_kernel(scale, total, fine, down, coarse, up):
    for out, at in ((fine, 0), (coarse, 16 * C)):
        for along in range(3):
            first = at + C * along
            rows = [total[first + 3 * C * g : first + 3 * C * g + C, :] for g in range(4)]
            row = jnp.concatenate(rows, axis=1).astype(F32) * scale
            for index in range(9):
                out[3 * index + along] = row[:, C * index : C * (index + 1)]
    for out, at, turn in ((down, 12 * C, False), (up, 28 * C, True)):
        for index in range(4):
            rows = total[at + C * index : at + C * (index + 1), :].astype(F32) * scale
            for along in range(2):
                part = rows[:, C * along : C * (along + 1)]
                if turn:
                    out[2 * index + along] = part.T
                else:
                    out[:, 2 * index + along, :] = part


def call(kernel, inputs, outs, scratch=(), scalars=0, flops=0, limit=None):
    vmem = pl.BlockSpec(memory_space=pltpu.VMEM)
    smem = pl.BlockSpec(memory_space=pltpu.SMEM)
    held = SLACK
    for shape, kind in [(a.shape, a.dtype) for a in inputs[scalars:]] + list(outs) + list(scratch):
        rows, lanes = -(-shape[-2] // 16) * 16, -(-shape[-1] // LANES) * LANES
        held += math.prod(shape[:-2]) * rows * lanes * jnp.dtype(kind).itemsize
    moved = sum(math.prod(s) * jnp.dtype(d).itemsize for s, d in outs)
    moved += sum(math.prod(a.shape) * a.dtype.itemsize for a in inputs)
    return pl.pallas_call(
        kernel,
        out_shape=tuple(jax.ShapeDtypeStruct(s, d) for s, d in outs),
        in_specs=[smem] * scalars + [vmem] * (len(inputs) - scalars),
        out_specs=tuple(vmem for _ in outs),
        scratch_shapes=[pltpu.VMEM(s, d) for s, d in scratch],
        compiler_params=pltpu.CompilerParams(vmem_limit_bytes=limit or held),
        cost_estimate=pl.CostEstimate(flops=flops, bytes_accessed=moved, transcendentals=0),
        name=getattr(kernel, "func", kernel).__name__,
    )(*inputs)


def send(array, step_x, step_y):
    number_x, number_y = lax.axis_size("gx"), lax.axis_size("gy")
    pairs = []
    for i in range(number_x):
        for j in range(number_y):
            to_x, to_y = i + step_x, j + step_y
            if 0 <= to_x < number_x and 0 <= to_y < number_y:
                pairs.append((i * number_y + j, to_x * number_y + to_y))
    return lax.ppermute(array, ("gx", "gy"), pairs)


def reduce_share(joined):
    devices = lax.axis_size("gx") * lax.axis_size("gy")
    rows = joined.shape[0]
    share = -(-rows // devices)
    joined = jnp.pad(joined, ((0, share * devices - rows), (0, 0)))
    mine = lax.all_to_all(joined.reshape(devices, share, LANES), ("gx", "gy"), 0, 0)
    return mine


def spread_share(parts):
    (copies,) = call(sum_kernel, (parts,), [(parts.shape, BF16)])
    full = lax.all_to_all(copies, ("gx", "gy"), 0, 0)
    return full.reshape(-1, LANES)


def on_device(
    features, block_slots, block_count, cotangent, fine_weight, down_weight, coarse_weight,
    up_weight,
):
    number = features.shape[2]
    slots = block_slots.reshape(number)
    count = block_count.reshape(1)
    feats = features.reshape(number, C, VOX)
    cots = cotangent.reshape(number, C, VOX)
    tiles = EDGE * (number + 2)
    coarse_tiles = tiles // 2
    pairs = number // 2 + 2
    groups = pairs // 2
    fine_groups = pairs

    fine_3, coarse_3 = (weight.transpose(1, 0, 2) for weight in (fine_weight, coarse_weight))
    flag_rows, x_low, x_high, y_low, y_high = call(
        prepare_kernel,
        (slots, count, feats, cots),
        [((16, LANES), F32)]
        + [((number // 2 * C + 16, 384), BF16)] * 2
        + [((2 * C + 16, VOX), BF16)] * 2,
        [((number * C, VOX), BF16)],
        scalars=2,
        limit=56 * 1024 * 1024,
    )
    x_left = send(x_high, 1, 0)
    x_right = send(x_low, -1, 0)
    y_left = send(y_high, 0, 1)
    y_right = send(y_low, 0, -1)
    corner_low, corner_high = call(
        corner_kernel,
        (y_left, y_right),
        [((C + 16, 384), BF16), ((C + 16, 384), BF16)],
    )
    c_left = send(corner_high, 1, 0)
    c_right = send(corner_low, -1, 0)
    (grid_own, cot_grid, grad_r, fine_fore, fine_back, coarse_fore, coarse_back, down_w,
     up_w) = call(
        place_kernel,
        (slots, count, feats, cots, y_left, y_right, corner_low, fine_3, down_weight, coarse_3,
         up_weight),
        [
            ((tiles, C, LANES), BF16),
            ((EDGE * pairs, C, LANES), BF16),
            ((4 * pairs, C, LANES), F32),
        ]
        + [((3 * C, 9 * C), BF16)] * 4
        + [((4 * C, 2 * C), BF16), ((2 * C, 4 * C), BF16)],
        [
            (((number + 2) * C, VOX), BF16),
            ((pairs * C, 1024), BF16),
            ((number, C, VOX), BF16),
        ],
        scalars=2,
        flops=8 * 10**9,
    )
    grid, hidden, low_cols, rects, grad_c, live, pack_low, pack_high = call(
        forward_kernel,
        (grid_own, flag_rows, y_left, y_right, grad_r, x_left, x_right, c_left, c_right,
         fine_fore, down_w, coarse_fore),
        [
            ((tiles, C, LANES), BF16),
            ((EDGE * pairs, C, LANES), F32),
            ((4 * pairs, 3 * C, LANES), BF16),
            ((4 * pairs, C, LANES), BF16),
            ((4 * pairs, C, LANES), BF16),
            ((16, LANES), F32),
            ((groups, C, LANES), BF16),
            ((groups, C, LANES), BF16),
        ],
        [
            (((number + 2) * C, VOX), BF16),
            ((tiles + 1, C, LANES), F32),
            ((4 * pairs + 1, C, LANES), F32),
            ((tiles, C, LANES), F32),
            ((coarse_tiles, C, LANES), BF16),
            ((C, LANES), F32),
        ]
        + [((9 * C, 4 * LANES), BF16)] * 2,
        flops=8 * 10**9,
    )
    grad_left = send(pack_high, 1, 0)
    grad_right = send(pack_low, -1, 0)
    (early,) = call(
        side_kernel,
        (rects, cot_grid, low_cols, grad_c),
        [((16 * C, LANES), BF16)],
        [((4 * pairs, C, LANES), BF16), ((4 * C, LANES), F32), ((VOX, 3 * C), F32)],
        flops=8 * 10**9,
    )
    grad_h, grad_d = call(
        backward_kernel,
        (grad_c, grad_left, grad_right, hidden, cot_grid, live, coarse_back, down_w),
        [
            ((EDGE * pairs, C, LANES), BF16),
            ((4 * pairs, C, LANES), BF16),
        ],
        [((4 * pairs + 1, C, LANES), F32), ((4 * pairs, 3 * C, LANES), BF16)]
        + [((9 * C, 4 * LANES), BF16)] * 2,
        flops=8 * 10**9,
    )
    (joined,) = call(
        weight_kernel,
        (grid, grad_h, grad_d, hidden, early),
        [((32 * C, LANES), BF16)],
        [((EDGE * pairs, C, LANES), BF16), ((VOX, 3 * C), F32), ((4 * C, LANES), F32)],
        flops=12 * 10**9,
    )
    joined, slots, grad_h = lax.optimization_barrier((joined, slots, grad_h))
    edge_low, edge_high = call(
        pack_kernel, (grad_h,), [((fine_groups, C, LANES), BF16)] * 2, flops=10**9
    )
    edge_left = send(edge_high, 1, 0)
    edge_right = send(edge_low, -1, 0)
    share = reduce_share(joined)
    (output,) = call(
        output_kernel,
        (slots, hidden, rects, live, up_w),
        [((number, C, VOX), BF16)],
        [((number // 2 * C, 1024), BF16), ((number // 2 * C, 1024), BF16)],
        scalars=1,
        flops=8 * 10**9,
    )
    share, output, slots, edge_left, edge_right = lax.optimization_barrier(
        (share, output, slots, edge_left, edge_right)
    )
    (input_grad,) = call(
        input_kernel,
        (slots, grad_h, edge_left, edge_right, live, fine_back),
        [((number, C, VOX), BF16)],
        [
            ((EDGE * pairs + 1, C, LANES), F32),
            ((number // 2 * C, 1024), BF16),
            ((number // 2 * C, 1024), BF16),
            ((EDGE * pairs, 3 * C, LANES), BF16),
        ]
        + [((9 * C, 4 * LANES), BF16)] * 2,
        scalars=1,
        flops=8 * 10**9,
    )
    total = spread_share(share)
    scale = 1.0 / math.sqrt(number * VOX * lax.axis_size("gx") * lax.axis_size("gy"))
    fine_total, down_total, coarse_total, up_total = call(
        functools.partial(finish_kernel, scale),
        (total,),
        [((27, C, C), F32), ((C, 8, C), F32), ((27, C, C), F32), ((8, C, C), F32)],
    )
    shape_out = (1, 1, number, C, VOX)
    return (
        output.reshape(shape_out),
        input_grad.reshape(shape_out),
        fine_total.transpose(1, 0, 2),
        down_total,
        coarse_total.transpose(1, 0, 2),
        up_total,
    )


def solution(mesh):
    split = P("gx", "gy", None, None, None)
    return jax.shard_map(
        on_device,
        mesh=mesh,
        in_specs=(split, P("gx", "gy", None), P("gx", "gy"), split, P(), P(), P(), P()),
        out_specs=(split, split, P(), P(), P(), P()),
        check_vma=False,
    )
```

```python
import functools
import math

import jax
import jax.numpy as jnp
from jax import lax
from jax.experimental import pallas as pl
from jax.experimental.pallas import tpu as pltpu
from jax.sharding import PartitionSpec as P

C = 48
EDGE = 8
VOX = 512
LANES = 128
F32 = jnp.float32
BF16 = jnp.bfloat16
SLACK = 8 * 1024 * 1024
SHIFTS = (0, 1, 16, 17)


def marks(rows, columns, row_key, column_key):
    across = column_key(lax.broadcasted_iota(jnp.int32, (1, columns), 1))
    down = row_key(lax.broadcasted_iota(jnp.int32, (rows, 1), 0))
    return jnp.where(down == across, 1.0, 0.0).astype(BF16)


def plain(index):
    return index


def own_source(column):
    lane, y = column % LANES, column // LANES
    x = lane % 16 - 4
    return jnp.where((x >= 0) & (x < 8), 64 * (lane // 16) + 8 * x + y, -1)


def halo_source(column):
    lane, y = column % LANES, column // LANES
    x = lane % 16
    at = 24 * (lane // 16) + y
    left = jnp.where((x >= 1) & (x < 4), at + 8 * (x - 1), -1)
    return jnp.where((x >= 12) & (x < 15), at + 8 * (x - 12) + 256, left)


def pair_source(column):
    lane, y = (column - 4) % LANES, column // LANES
    return 512 * (lane % 16 // 8) + 64 * (lane // 16) + 8 * (lane % 8) + y


def edge_source(column):
    at, side = column % 256, column // 256
    x = at % 24 // 8 + 5 * side
    return jnp.where(at < 192, 64 * (at // 24) + 8 * x + at % 8, -1)


def dot(left, right, contract=(1, 0)):
    dims = (((contract[0],), (contract[1],)), ((), ()))
    return lax.dot_general(left, right, dims, preferred_element_type=F32)


def roll(value, shift):
    return pltpu.roll(value, shift % LANES, 1)


def lane_ids(rows):
    return lax.broadcasted_iota(jnp.int32, (rows, LANES), 1)


def silu_parts(value):
    sigma = 1.0 / (1.0 + jnp.exp(-value))
    return value * sigma, sigma * (1.0 + value * (1.0 - sigma))


def depth_columns(base, masks, step):
    below = roll(base, step) * masks[0]
    above = roll(base, -step) * masks[1]
    return jnp.concatenate([below, base, above], axis=0)


def depth_masks(step, first):
    ids = (lane_ids(3 * C) - first) % LANES
    return (ids >= step).astype(BF16), (ids < LANES - step).astype(BF16)


def across_columns(tile, step):
    return jnp.concatenate([roll(tile, step), tile, roll(tile, -step)], axis=0)


def edge_masks(step):
    ids = lane_ids(C) % 8
    first, last = (ids == 4).astype(BF16), (ids == 4 - step).astype(BF16)
    return first, (ids != 4).astype(BF16), last, (ids != 4 - step).astype(BF16)


def pair_columns(tile, halo, masks, step):
    left = roll(halo, step) * masks[0] + roll(tile, step) * masks[1]
    right = roll(halo, -step) * masks[2] + roll(tile, -step) * masks[3]
    return jnp.concatenate([left, tile, right], axis=0)


def fill_columns(tiles, from_left, from_right, out, step):
    masks = edge_masks(step)

    def body(group):
        packed_left, packed_right = from_left[group], from_right[group]
        for place in range(8):
            tile = tiles[8 * group + place]
            left = roll(packed_left, -place) * masks[0] + roll(tile, step) * masks[1]
            right = roll(packed_right, 8 - step - place) * masks[2]
            right = right + roll(tile, -step) * masks[3]
            out[8 * group + place] = jnp.concatenate([left, tile, right], axis=0)

    loop(0, from_left.shape[0], body)


def pack_columns(tiles, low, high, step):
    masks = edge_masks(step)

    def body(group):
        lows, highs = [], []
        for place in range(8):
            tile = tiles[8 * group + place]
            lows.append(roll(tile * masks[0], place))
            highs.append(roll(tile * masks[2], place - 8 + step))
        for out, parts in ((low, lows), (high, highs)):
            while len(parts) > 1:
                parts = [a + b for a, b in zip(parts[::2], parts[1::2])]
            out[group] = parts[0]

    loop(0, low.shape[0], body)


def own_masks():
    own = own_lanes(C)
    return own.astype(BF16), jnp.logical_not(own).astype(BF16)


def pair_tiles(lower, upper, masks):
    turned = roll(upper, 8)
    return (
        lower * masks[0] + turned * masks[1],
        lower * masks[1] + turned * masks[0],
    )


def own_lanes(rows):
    across = lane_ids(rows) % 16
    return (across >= 4) & (across < 12)


def join_halves(lower, upper):
    return jnp.where(own_lanes(lower.shape[0]), lower, roll(upper, 8))


def gather_sub(parts):
    even = lane_ids(C) % 2 == 0
    above = jnp.where(even, parts[2 * C : 3 * C], parts[3 * C :])
    total = jnp.where(even, parts[:C], parts[C : 2 * C]) + roll(above, -16)
    return total + roll(total, -1)


def spread_sub(anchored):
    return jnp.concatenate([anchored] + [roll(anchored, step) for step in SHIFTS[1:]], axis=0)


def anchor_mask(first):
    ids = (lane_ids(C) - first) % LANES
    return (((ids // 16) % 2 == 0) & (ids % 2 == 0)).astype(F32)


def loop(low, high, body, unroll=1):
    def step(index, carry):
        body(index)
        return carry

    lax.fori_loop(low, high, step, 0, unroll=unroll)


def join_rows(first, second):
    low = lane_ids(C) < 64
    lead = roll(second[:, :LANES], 64)
    parts = [
        first[:, :LANES],
        jnp.where(low, first[:, LANES:], lead),
        jnp.where(low, lead, roll(second[:, LANES:], 64)),
    ]
    return jnp.concatenate(parts, axis=1)


def split_rows(joined):
    low = lane_ids(C) < 64
    middle = roll(joined[:, LANES : 2 * LANES], 64)
    last = roll(joined[:, 2 * LANES :], 64)
    second = jnp.concatenate([jnp.where(low, middle, last), last], axis=1)
    return joined[:, : 2 * LANES], second


def prepare_kernel(slots, count, feats, cots, flag_rows, x_low, x_high, y_low, y_high, rows_in):
    number = feats.shape[0]
    rows = lax.broadcasted_iota(jnp.int32, (16, LANES), 0)
    flags = jnp.zeros((16, LANES), F32)
    zero = jnp.zeros((C, VOX), BF16)
    first = jnp.zeros((), jnp.int32)
    last = jnp.zeros((), jnp.int32)
    for slot in range(number):
        live = slot < count[0]
        place = slots[slot]
        block = jnp.where(live, feats[slot], zero)
        rows_in[pl.ds(pl.multiple_of(place * C, 16), C), :] = block
        flags = jnp.where(rows == place, jnp.where(live, 1.0, 0.0), flags)
        first = jnp.where(place == 0, slot, first)
        last = jnp.where(place == number - 1, slot, last)
    flag_rows[...] = flags
    packed = dot(rows_in[...], marks(VOX, 512, plain, edge_source)).astype(BF16)
    spare = jnp.zeros((16, 2 * LANES), BF16)
    for out, at in ((x_low, 0), (x_high, 256)):
        for pair in range(number // 2):
            edges = [packed[C * i : C * (i + 1), at : at + 256] for i in (2 * pair, 2 * pair + 1)]
            out[C * pair : C * (pair + 1), :] = join_rows(*edges)
        out[C * number // 2 :, :LANES] = flags.astype(BF16)
        out[C * number // 2 :, LANES:] = spare
    for out, index, slot in ((y_low, 0, first), (y_high, number - 1, last)):
        live = slot < count[0]
        out[0:C, :] = rows_in[C * index : C * (index + 1), :]
        out[C : 2 * C, :] = jnp.where(live, cots[slot], zero)
        out[2 * C :, :] = (jnp.zeros((16, VOX), F32) + jnp.where(live, 1.0, 0.0)).astype(BF16)


def corner_kernel(y_left, y_right, low, high):
    rows = jnp.concatenate([y_left[0:C, :], y_right[0:C, :]], axis=0)
    packed = dot(rows, marks(VOX, 512, plain, edge_source)).astype(BF16)
    ids = lax.broadcasted_iota(jnp.int32, (16, LANES), 0)
    flags = jnp.where(ids == 0, y_left[2 * C :, :LANES], y_right[2 * C :, :LANES])
    spare = jnp.zeros((16, 2 * LANES), BF16)
    for out, at in ((low, 0), (high, 256)):
        out[0:C, :] = join_rows(packed[:C, at : at + 256], packed[C:, at : at + 256])
        out[C:, :LANES] = flags
        out[C:, LANES:] = spare


def arrange_weights(fine, down, coarse, up, fine_w, fine_b, coarse_w, coarse_b, down_w, up_w):
    for source, fore, back in ((fine, fine_w, fine_b), (coarse, coarse_w, coarse_b)):
        for along in range(3):
            rows = slice(C * along, C * (along + 1))
            turned_rows = slice(C * (2 - along), C * (3 - along))
            ahead = []
            behind = []
            for depth in range(3):
                for across in range(3):
                    ahead.append(source[9 * depth + 3 * across + along])
                    behind.append(source[9 * (2 - depth) + 3 * (2 - across) + along].T)
            fore[rows, :] = jnp.concatenate(ahead, axis=1)
            back[turned_rows, :] = jnp.concatenate(behind, axis=1)
    for index in range(4):
        pair = [down[:, 2 * index, :], down[:, 2 * index + 1, :]]
        down_w[C * index : C * (index + 1), :] = jnp.concatenate(pair, axis=1)
    for along in range(2):
        row = jnp.concatenate([up[2 * index + along] for index in range(4)], axis=1)
        up_w[C * along : C * (along + 1), :] = row


def place_kernel(
    slots, count, feats, cots, y_left, y_right, c_low, fine, down, coarse, up,
    grid, cot_grid, grad_r, fine_w, fine_b, coarse_w, coarse_b, down_w, up_w,
    rows_in, rows_cot, cot,
):
    arrange_weights(fine, down, coarse, up, fine_w, fine_b, coarse_w, coarse_b, down_w, up_w)
    number = feats.shape[0]
    last = number + 1
    zero = jnp.zeros((C, VOX), BF16)
    rows_in[0:C, :] = y_left[0:C, :]
    rows_in[last * C : (last + 1) * C, :] = y_right[0:C, :]
    for slot in range(number):
        live = slot < count[0]
        place = slots[slot]
        start = pl.multiple_of((place + 1) * C, 16)
        rows_in[pl.ds(start, C), :] = jnp.where(live, feats[slot], zero)
        cot[place] = jnp.where(live, cots[slot], zero)
    pairs = number // 2 + 2
    for group in range(pairs):
        at = group * C
        lower = y_left[C : 2 * C, :] if group == 0 else cot[group - 1]
        upper = y_right[C : 2 * C, :] if group == pairs - 1 else cot[group + number // 2 - 1]
        rows_cot[at : at + C, 0:512] = lower
        rows_cot[at : at + C, 512:1024] = upper
    for pair in range(4):
        placed_cot = dot(
            rows_cot[...], marks(1024, 256, plain, lambda j, at=256 * pair: pair_source(j + at))
        )
        placed = dot(
            rows_in[...], marks(VOX, 256, plain, lambda j, at=256 * pair: own_source(j + at))
        )
        for half in range(2):
            span = slice(LANES * half, LANES * (half + 1))
            for block in range(last + 1):
                tile = EDGE * block + 2 * pair + half
                grid[tile] = placed[block * C : (block + 1) * C, span].astype(BF16)
            for block in range(pairs):
                tile = EDGE * block + 2 * pair + half
                cot_grid[tile] = placed_cot[block * C : (block + 1) * C, span].astype(BF16)

    def rect_step(block):
        tiles = []
        for inner in range(4):
            tile = EDGE * block + 2 * inner
            tiles.append(jnp.concatenate([cot_grid[tile], cot_grid[tile + 1]], axis=0))
        parts = dot(up_w[...], jnp.concatenate(tiles, axis=1), (0, 0))
        for inner in range(4):
            grad_r[4 * block + inner] = gather_sub(parts[:, LANES * inner : LANES * (inner + 1)])

    loop(0, pairs, rect_step, 2)


def conv_steps(sums, weight, load, tiles, step, first, even, odd):
    masks = depth_masks(step, first)

    def fill(buffer, tile):
        for i in range(4):
            cols = depth_columns(load(tile + i), masks, step)
            buffer[:, LANES * i : LANES * (i + 1)] = cols

    def multiply(buffer, tile, carry):
        out = dot(weight[...], buffer[...])

        def part(along, i):
            return out[C * along : C * (along + 1), LANES * i : LANES * (i + 1)]

        sums[tile] += part(2, 0)
        sums[tile + 1] = carry + part(1, 0) + part(2, 1)
        sums[tile + 2] = part(0, 0) + part(1, 1) + part(2, 2)
        sums[tile + 3] = part(0, 1) + part(1, 2) + part(2, 3)
        sums[tile + 4] = part(0, 2) + part(1, 3)
        return part(0, 3)

    fill(even, 0)
    sums[0] = jnp.zeros((C, LANES), F32)

    def body(index, carry):
        tile = 8 * index
        fill(odd, tile + 4)
        carry = multiply(even, tile, carry)
        fill(even, jnp.minimum(tile + 8, tiles - 4))
        return multiply(odd, tile + 4, carry)

    lax.fori_loop(0, tiles // 8, body, jnp.zeros((C, LANES), F32))


def forward_kernel(
    grid_own, flags, y_left, y_right, grad_r, x_left, x_right, c_left, c_right, fine_w, down_w,
    coarse_w,
    grid, hidden, low_cols, rects, grad_c, live, pack_low, pack_high,
    rows_in, fine_p, coarse_p, hidden_all, lowered, live_all, even, odd,
):
    number = 2 * (x_left.shape[0] - 16) // C
    last = number + 1
    for at, left, right in ((0, x_left, x_right), (None, c_left, c_right)):
        for pair in range((left.shape[0] - 16) // C):
            rows = slice(C * pair, C * (pair + 1))
            lefts, rights = split_rows(left[rows, :]), split_rows(right[rows, :])
            for inner in range(2):
                block = last * inner if at is None else 2 * pair + inner + 1
                rows_in[block * C : (block + 1) * C, 0:256] = lefts[inner]
                rows_in[block * C : (block + 1) * C, 256:512] = rights[inner]
    across = lane_ids(16) % 16
    for start, middle, left, right in (
        (1, flags[...], x_left[number // 2 * C :, :LANES], x_right[number // 2 * C :, :LANES]),
        (0, y_left[2 * C :, :LANES], c_left[C:, :LANES], c_right[C:, :LANES]),
        (last, y_right[2 * C :, :LANES], c_left[C:, :LANES], c_right[C:, :LANES]),
    ):
        rows = jnp.where(across < 4, left.astype(F32), middle.astype(F32))
        rows = jnp.where(across >= 12, right.astype(F32), rows)
        if start == 1:
            live_all[1 : number + 1, :] = rows
        else:
            at = 0 if start == 0 else 1
            live_all[start : start + 1, :] = rows[at : at + 1, :]
    for pair in range(4):
        placed = dot(
            rows_in[...], marks(512, 256, plain, lambda j, at=256 * pair: halo_source(j + at))
        )
        for half in range(2):
            span = slice(LANES * half, LANES * (half + 1))
            for block in range(last + 1):
                tile = EDGE * block + 2 * pair + half
                halo = placed[block * C : (block + 1) * C, span].astype(BF16)
                grid[tile] = grid_own[tile] + halo
    live[...] = join_halves(live_all[0:16, :], live_all[8:24, :])
    tiles = grid.shape[0]
    conv_steps(fine_p, fine_w, lambda tile: across_columns(grid[tile], 1), tiles, 16, 0, even, odd)
    anchors = anchor_mask(0)

    def lower_step(block):
        alive = jnp.broadcast_to(live_all[pl.ds(block, 1), :], (C, LANES))
        keep = alive * anchors
        pairs = []
        for inner in range(4):
            actives = []
            for half in range(2):
                tile = EDGE * block + 2 * inner + half
                value = fine_p[tile + 1] * alive
                hidden_all[tile] = value
                actives.append(silu_parts(value)[0].astype(BF16))
            pairs.append(jnp.concatenate(actives, axis=0))
        parts = dot(down_w[...], jnp.concatenate(pairs, axis=1))
        for inner in range(4):
            total = gather_sub(parts[:, LANES * inner : LANES * (inner + 1)])
            lowered[4 * block + inner] = (total * keep).astype(BF16)

    loop(0, last + 1, lower_step, 2)
    pairs = hidden.shape[0] // EDGE
    shift = last - pairs + 1
    edges = edge_masks(2)
    halves = own_masks()

    def pair_step(block):
        for inner in range(EDGE):
            tile = EDGE * block + inner
            hidden[tile] = join_halves(hidden_all[tile], hidden_all[tile + EDGE * shift])
        for inner in range(4):
            tile = 4 * block + inner
            lower, upper = lowered[tile], lowered[tile + 4 * shift]
            low_cols[tile] = pair_columns(*pair_tiles(lower, upper, halves), edges, 2)

    loop(0, pairs, pair_step, 2)
    conv_steps(coarse_p, coarse_w, lambda tile: low_cols[tile], 4 * pairs, 32, 4, even, odd)
    pair_anchors = anchor_mask(4)

    def grad_step(block):
        alive = jnp.broadcast_to(live[pl.ds(block, 1), :], (C, LANES))
        keep = alive * pair_anchors
        for inner in range(4):
            coarse = 4 * block + inner
            smooth, slope = silu_parts(coarse_p[coarse + 1])
            rects[coarse] = (smooth * pair_anchors).astype(BF16)
            grad_c[coarse] = (grad_r[coarse] * slope * keep).astype(BF16)

    loop(0, pairs, grad_step, 2)
    pack_columns(grad_c, pack_low, pack_high, 2)


def to_blocks(slots, rows_out, flat, out):
    flat[...] = dot(rows_out[...], marks(1024, 1024, pair_source, plain)).astype(BF16)
    number = out.shape[0]
    for slot in range(number):
        place = slots[slot]
        upper = place >= number // 2
        start = pl.multiple_of(jnp.where(upper, place - number // 2, place) * C, 16)
        rows = flat[pl.ds(start, C), :]
        out[slot] = jnp.where(upper, rows[:, 512:], rows[:, :512])


def stacks(own, tiles):
    parts = [jnp.concatenate([own[t + 1], own[t], own[t - 1]], axis=0) for t in tiles]
    return jnp.concatenate(parts, axis=1)


def squeeze_rows(full, keep):
    extra = full[keep:]
    size, part = extra.shape[0], keep // 3
    lanes = lane_ids(size)
    pieces = []
    for index in range(3):
        rows = full[part * index : part * (index + 1)]
        pieces.append(jnp.where(lanes < 96, rows[:size], roll(extra, 96 - 32 * index)))
        if size < part:
            pieces.append(rows[size:])
    return jnp.concatenate(pieces, axis=0)


def widen_rows(packed, number):
    keep = packed.shape[0]
    size, part = number - keep, keep // 3
    lanes = lane_ids(size)
    extra = jnp.zeros((size, LANES), F32)
    for index in range(3):
        moved = roll(packed[part * index : part * index + size], 32 * index - 96)
        extra = jnp.where((lanes >= 32 * index) & (lanes < 32 * index + 32), moved, extra)
    return jnp.concatenate([packed, extra], axis=0)


def flatten_weights(total, out):
    turned = total[...].T
    for group in range(3):
        part = turned[:, LANES * group : LANES * (group + 1)]
        out[3 * C * group : 3 * C * (group + 1), :] = part.astype(BF16)
    return turned[:, 3 * LANES :]


def output_kernel(slots, hidden, rects, live, up_w, out, rows_out, flat):
    pairs = hidden.shape[0] // EDGE

    def block_step(block):
        alive = jnp.broadcast_to(live[pl.ds(block, 1), :], (C, LANES))
        start = pl.multiple_of((block - 1) * C, 16)
        spreads = [spread_sub(rects[4 * block + inner]) for inner in range(4)]
        upward = dot(up_w[...], jnp.concatenate(spreads, axis=1))
        for inner in range(4):
            for half in range(2):
                part = upward[half * C : (half + 1) * C, LANES * inner : LANES * (inner + 1)]
                value = hidden[EDGE * block + 2 * inner + half] + part
                at = LANES * (2 * inner + half)
                rows_out[pl.ds(start, C), at : at + LANES] = (value * alive).astype(BF16)

    loop(1, pairs - 1, block_step, 2)
    to_blocks(slots, rows_out, flat, out)


def side_kernel(rects, cot_grid, low_cols, grad_c, flat, grad_own, up_g, coarse_g):
    tiles = low_cols.shape[0]
    up_g[...] = jnp.zeros_like(up_g)
    coarse_g[...] = jnp.zeros_like(coarse_g)

    def up_step(block):
        spreads = []
        pairs = []
        for inner in range(4):
            coarse = 4 * block + inner
            spreads.append(spread_sub(rects[coarse]))
            pairs.append(
                jnp.concatenate([cot_grid[2 * coarse], cot_grid[2 * coarse + 1]], axis=0)
            )
        up_g[:, 0 : 2 * C] += dot(
            jnp.concatenate(spreads, axis=1), jnp.concatenate(pairs, axis=1), (1, 1)
        )

    loop(1, tiles // 4 - 1, up_step, 2)
    zero = jnp.zeros((C, LANES), BF16)
    for coarse in range(1, 4):
        grad_own[coarse] = zero
        grad_own[tiles - 1 - coarse] = zero

    def copy_step(coarse):
        grad_own[coarse] = grad_c[coarse]

    loop(4, tiles - 4, copy_step, 8)
    masks = depth_masks(32, 4)

    def weight_step(index):
        at = [2 + 4 * index + inner for inner in range(4)]
        rights = [depth_columns(low_cols[tile], masks, 32) for tile in at]
        coarse_g[0 : 9 * C, :] += dot(
            jnp.concatenate(rights, axis=1), stacks(grad_own, at), (1, 1)
        )

    loop(0, (tiles - 4) // 4, weight_step, 3)
    rest = flatten_weights(coarse_g, flat)
    flat[9 * C : 12 * C, :] = squeeze_rows(up_g[...], 3 * C).astype(BF16)
    flat[12 * C :, :] = roll(rest, C).astype(BF16)


def backward_kernel(
    grad_c, from_left, from_right, hidden, cot_grid, live, coarse_w, down_w,
    grad_h, grad_d, coarse_p, grad_x, even, odd,
):
    tiles = grad_c.shape[0]
    fill_columns(grad_c, from_left, from_right, grad_x, 2)
    conv_steps(coarse_p, coarse_w, lambda tile: grad_x[tile], tiles, 32, 4, even, odd)
    anchors = anchor_mask(4)

    def step(block):
        alive = jnp.broadcast_to(live[pl.ds(block, 1), :], (C, LANES))
        keep = alive * anchors
        spreads = []
        for inner in range(4):
            coarse = 4 * block + inner
            down = (coarse_p[coarse + 1] * keep).astype(BF16)
            grad_d[coarse] = down
            spreads.append(spread_sub(down))
        acts = dot(down_w[...], jnp.concatenate(spreads, axis=1), (0, 0))
        for inner in range(4):
            for side in range(2):
                tile = EDGE * block + 2 * inner + side
                slope = silu_parts(hidden[tile])[1]
                part = acts[side * C : (side + 1) * C, LANES * inner : LANES * (inner + 1)]
                grad = cot_grid[tile].astype(F32) + part * slope
                grad_h[tile] = (grad * alive).astype(BF16)

    loop(0, tiles // 4, step, 2)


def pack_kernel(grad_h, low, high):
    pack_columns(grad_h, low, high, 1)


def weight_kernel(grid, grad_h, grad_d, hidden, early, joined, grad_own, fine_g, down_g):
    tiles = grad_h.shape[0]
    shift = tiles - 16
    fine_g[...] = jnp.zeros_like(fine_g)
    down_g[...] = jnp.zeros_like(down_g)
    zero = jnp.zeros((C, LANES), BF16)
    for tile in range(3, 8):
        grad_own[tile] = zero
        grad_own[tiles - 1 - tile] = zero

    def copy_step(tile):
        grad_own[tile] = grad_h[tile]

    loop(8, tiles - 8, copy_step, 8)
    masks = depth_masks(16, 4)
    edges = edge_masks(1)
    halves = own_masks()

    def fine_step(index):
        at = [4 + 8 * index + inner for inner in range(8)]
        rights = []
        for tile in at:
            lower, upper = grid[tile], grid[tile + shift]
            base = pair_columns(*pair_tiles(lower, upper, halves), edges, 1)
            rights.append(depth_columns(base, masks, 16))
        fine_g[0 : 9 * C, :] += dot(
            jnp.concatenate(rights, axis=1), stacks(grad_own, at), (1, 1)
        )

    loop(0, (tiles - 8) // 8, fine_step)

    def down_step(index):
        lefts = []
        rights = []
        for inner in range(4):
            coarse = 4 + 4 * index + inner
            lefts.append(spread_sub(grad_d[coarse]))
            actives = [silu_parts(hidden[2 * coarse + side])[0].astype(BF16) for side in range(2)]
            rights.append(jnp.concatenate(actives, axis=0))
        down_g[:, 0 : 2 * C] += dot(
            jnp.concatenate(lefts, axis=1), jnp.concatenate(rights, axis=1), (1, 1)
        )

    loop(0, (tiles // 2 - 8) // 4, down_step, 2)
    rest = flatten_weights(fine_g, joined) + early[12 * C :, :].astype(F32)
    joined[9 * C : 18 * C, :] = early[0 : 9 * C, :]
    joined[18 * C : 21 * C, :] = squeeze_rows(down_g[...], 3 * C).astype(BF16)
    joined[21 * C : 24 * C, :] = early[9 * C : 12 * C, :]
    squeezed = squeeze_rows(rest, 120)
    joined[24 * C :, :] = jnp.concatenate([squeezed, squeezed[:8]], axis=0).astype(BF16)


def input_kernel(
    slots, grad_h, from_left, from_right, live, fine_w, out,
    fine_p, rows_out, flat, grad_x, even, odd,
):
    tiles = grad_h.shape[0]
    fill_columns(grad_h, from_left, from_right, grad_x, 1)
    conv_steps(fine_p, fine_w, lambda tile: grad_x[tile], tiles, 16, 4, even, odd)

    def block_step(block):
        alive = jnp.broadcast_to(live[pl.ds(block, 1), :], (C, LANES))
        start = pl.multiple_of((block - 1) * C, 16)
        for inner in range(EDGE):
            value = fine_p[EDGE * block + inner + 1]
            rows_out[pl.ds(start, C), LANES * inner : LANES * (inner + 1)] = (
                value * alive
            ).astype(BF16)

    loop(1, tiles // EDGE - 1, block_step, 2)
    to_blocks(slots, rows_out, flat, out)


def sum_kernel(parts, copies):
    total = jnp.sum(parts[...].astype(F32), axis=0).astype(BF16)
    copies[...] = jnp.broadcast_to(total[None], copies.shape)


def finish_kernel(scale, total, fine, down, coarse, up):
    rest = widen_rows(total[24 * C :, :].astype(F32)[:120], 3 * C) * scale
    for out, at, moved in ((fine, 0, rest), (coarse, 9 * C, roll(rest, -C))):
        for along in range(3):
            first = at + C * along
            rows = [total[first + 3 * C * g : first + 3 * C * g + C, :] for g in range(3)]
            row = jnp.concatenate(rows, axis=1).astype(F32) * scale
            row = jnp.concatenate([row, moved[C * along : C * (along + 1)]], axis=1)
            for index in range(9):
                out[3 * index + along] = row[:, C * index : C * (index + 1)]
    for out, at, turn in ((down, 18 * C, False), (up, 21 * C, True)):
        full = widen_rows(total[at : at + 3 * C, :].astype(F32), 4 * C) * scale
        for index in range(4):
            rows = full[C * index : C * (index + 1)]
            for along in range(2):
                part = rows[:, C * along : C * (along + 1)]
                if turn:
                    out[2 * index + along] = part.T
                else:
                    out[:, 2 * index + along, :] = part


def call(kernel, inputs, outs, scratch=(), scalars=0, flops=0, limit=None):
    vmem = pl.BlockSpec(memory_space=pltpu.VMEM)
    smem = pl.BlockSpec(memory_space=pltpu.SMEM)
    held = SLACK
    for shape, kind in [(a.shape, a.dtype) for a in inputs[scalars:]] + list(outs) + list(scratch):
        rows, lanes = -(-shape[-2] // 16) * 16, -(-shape[-1] // LANES) * LANES
        held += math.prod(shape[:-2]) * rows * lanes * jnp.dtype(kind).itemsize
    moved = sum(math.prod(s) * jnp.dtype(d).itemsize for s, d in outs)
    moved += sum(math.prod(a.shape) * a.dtype.itemsize for a in inputs)
    return pl.pallas_call(
        kernel,
        out_shape=tuple(jax.ShapeDtypeStruct(s, d) for s, d in outs),
        in_specs=[smem] * scalars + [vmem] * (len(inputs) - scalars),
        out_specs=tuple(vmem for _ in outs),
        scratch_shapes=[pltpu.VMEM(s, d) for s, d in scratch],
        compiler_params=pltpu.CompilerParams(vmem_limit_bytes=limit or held),
        cost_estimate=pl.CostEstimate(flops=flops, bytes_accessed=moved, transcendentals=0),
        name=getattr(kernel, "func", kernel).__name__,
    )(*inputs)


def send(array, step_x, step_y):
    number_x, number_y = lax.axis_size("gx"), lax.axis_size("gy")
    pairs = []
    for i in range(number_x):
        for j in range(number_y):
            to_x, to_y = i + step_x, j + step_y
            if 0 <= to_x < number_x and 0 <= to_y < number_y:
                pairs.append((i * number_y + j, to_x * number_y + to_y))
    return lax.ppermute(array, ("gx", "gy"), pairs)


def reduce_share(joined):
    devices = lax.axis_size("gx") * lax.axis_size("gy")
    rows = joined.shape[0]
    share = -(-rows // devices)
    joined = jnp.pad(joined, ((0, share * devices - rows), (0, 0)))
    mine = lax.all_to_all(joined.reshape(devices, share, LANES), ("gx", "gy"), 0, 0)
    return mine


def spread_share(parts):
    (copies,) = call(sum_kernel, (parts,), [(parts.shape, BF16)])
    full = lax.all_to_all(copies, ("gx", "gy"), 0, 0)
    return full.reshape(-1, LANES)


def on_device(
    features, block_slots, block_count, cotangent, fine_weight, down_weight, coarse_weight,
    up_weight,
):
    number = features.shape[2]
    slots = block_slots.reshape(number)
    count = block_count.reshape(1)
    feats = features.reshape(number, C, VOX)
    cots = cotangent.reshape(number, C, VOX)
    tiles = EDGE * (number + 2)
    coarse_tiles = tiles // 2
    pairs = number // 2 + 2
    groups = pairs // 2
    fine_groups = pairs

    fine_3, coarse_3 = (weight.transpose(1, 0, 2) for weight in (fine_weight, coarse_weight))
    flag_rows, x_low, x_high, y_low, y_high = call(
        prepare_kernel,
        (slots, count, feats, cots),
        [((16, LANES), F32)]
        + [((number // 2 * C + 16, 384), BF16)] * 2
        + [((2 * C + 16, VOX), BF16)] * 2,
        [((number * C, VOX), BF16)],
        scalars=2,
        limit=56 * 1024 * 1024,
    )
    x_left = send(x_high, 1, 0)
    x_right = send(x_low, -1, 0)
    y_left = send(y_high, 0, 1)
    y_right = send(y_low, 0, -1)
    corner_low, corner_high = call(
        corner_kernel,
        (y_left, y_right),
        [((C + 16, 384), BF16), ((C + 16, 384), BF16)],
    )
    c_left = send(corner_high, 1, 0)
    c_right = send(corner_low, -1, 0)
    (grid_own, cot_grid, grad_r, fine_fore, fine_back, coarse_fore, coarse_back, down_w,
     up_w) = call(
        place_kernel,
        (slots, count, feats, cots, y_left, y_right, corner_low, fine_3, down_weight, coarse_3,
         up_weight),
        [
            ((tiles, C, LANES), BF16),
            ((EDGE * pairs, C, LANES), BF16),
            ((4 * pairs, C, LANES), F32),
        ]
        + [((3 * C, 9 * C), BF16)] * 4
        + [((4 * C, 2 * C), BF16), ((2 * C, 4 * C), BF16)],
        [
            (((number + 2) * C, VOX), BF16),
            ((pairs * C, 1024), BF16),
            ((number, C, VOX), BF16),
        ],
        scalars=2,
        flops=8 * 10**9,
    )
    grid, hidden, low_cols, rects, grad_c, live, pack_low, pack_high = call(
        forward_kernel,
        (grid_own, flag_rows, y_left, y_right, grad_r, x_left, x_right, c_left, c_right,
         fine_fore, down_w, coarse_fore),
        [
            ((tiles, C, LANES), BF16),
            ((EDGE * pairs, C, LANES), F32),
            ((4 * pairs, 3 * C, LANES), BF16),
            ((4 * pairs, C, LANES), BF16),
            ((4 * pairs, C, LANES), BF16),
            ((16, LANES), F32),
            ((groups, C, LANES), BF16),
            ((groups, C, LANES), BF16),
        ],
        [
            (((number + 2) * C, VOX), BF16),
            ((tiles + 1, C, LANES), F32),
            ((4 * pairs + 1, C, LANES), F32),
            ((tiles, C, LANES), F32),
            ((coarse_tiles, C, LANES), BF16),
            ((C, LANES), F32),
        ]
        + [((9 * C, 4 * LANES), BF16)] * 2,
        flops=8 * 10**9,
    )
    grad_left = send(pack_high, 1, 0)
    grad_right = send(pack_low, -1, 0)
    (early,) = call(
        side_kernel,
        (rects, cot_grid, low_cols, grad_c),
        [((15 * C, LANES), BF16)],
        [((4 * pairs, C, LANES), BF16), ((4 * C, LANES), F32), ((VOX, 3 * C), F32)],
        flops=8 * 10**9,
    )
    grad_h, grad_d = call(
        backward_kernel,
        (grad_c, grad_left, grad_right, hidden, cot_grid, live, coarse_back, down_w),
        [
            ((EDGE * pairs, C, LANES), BF16),
            ((4 * pairs, C, LANES), BF16),
        ],
        [((4 * pairs + 1, C, LANES), F32), ((4 * pairs, 3 * C, LANES), BF16)]
        + [((9 * C, 4 * LANES), BF16)] * 2,
        flops=8 * 10**9,
    )
    (joined,) = call(
        weight_kernel,
        (grid, grad_h, grad_d, hidden, early),
        [((24 * C + 128, LANES), BF16)],
        [((EDGE * pairs, C, LANES), BF16), ((VOX, 3 * C), F32), ((4 * C, LANES), F32)],
        flops=12 * 10**9,
    )
    joined, slots, grad_h = lax.optimization_barrier((joined, slots, grad_h))
    edge_low, edge_high = call(
        pack_kernel, (grad_h,), [((fine_groups, C, LANES), BF16)] * 2, flops=10**9
    )
    edge_left = send(edge_high, 1, 0)
    edge_right = send(edge_low, -1, 0)
    share = reduce_share(joined)
    (output,) = call(
        output_kernel,
        (slots, hidden, rects, live, up_w),
        [((number, C, VOX), BF16)],
        [((number // 2 * C, 1024), BF16), ((number // 2 * C, 1024), BF16)],
        scalars=1,
        flops=8 * 10**9,
    )
    share, output, slots, edge_left, edge_right = lax.optimization_barrier(
        (share, output, slots, edge_left, edge_right)
    )
    (input_grad,) = call(
        input_kernel,
        (slots, grad_h, edge_left, edge_right, live, fine_back),
        [((number, C, VOX), BF16)],
        [
            ((EDGE * pairs + 1, C, LANES), F32),
            ((number // 2 * C, 1024), BF16),
            ((number // 2 * C, 1024), BF16),
            ((EDGE * pairs, 3 * C, LANES), BF16),
        ]
        + [((9 * C, 4 * LANES), BF16)] * 2,
        scalars=1,
        flops=8 * 10**9,
    )
    total = spread_share(share)
    scale = 1.0 / math.sqrt(number * VOX * lax.axis_size("gx") * lax.axis_size("gy"))
    fine_total, down_total, coarse_total, up_total = call(
        functools.partial(finish_kernel, scale),
        (total,),
        [((27, C, C), F32), ((C, 8, C), F32), ((27, C, C), F32), ((8, C, C), F32)],
    )
    shape_out = (1, 1, number, C, VOX)
    return (
        output.reshape(shape_out),
        input_grad.reshape(shape_out),
        fine_total.transpose(1, 0, 2),
        down_total,
        coarse_total.transpose(1, 0, 2),
        up_total,
    )


def solution(mesh):
    split = P("gx", "gy", None, None, None)
    return jax.shard_map(
        on_device,
        mesh=mesh,
        in_specs=(split, P("gx", "gy", None), P("gx", "gy"), split, P(), P(), P(), P()),
        out_specs=(split, split, P(), P(), P(), P()),
        check_vma=False,
    )
```

```python
import functools
import math

import jax
import jax.numpy as jnp
from jax import lax
from jax.experimental import pallas as pl
from jax.experimental.pallas import tpu as pltpu
from jax.sharding import PartitionSpec as P

C = 48
EDGE = 8
VOX = 512
LANES = 128
F32 = jnp.float32
BF16 = jnp.bfloat16
SLACK = 8 * 1024 * 1024
SHIFTS = (0, 1, 16, 17)


def marks(rows, columns, row_key, column_key):
    across = column_key(lax.broadcasted_iota(jnp.int32, (1, columns), 1))
    down = row_key(lax.broadcasted_iota(jnp.int32, (rows, 1), 0))
    return jnp.where(down == across, 1.0, 0.0).astype(BF16)


def plain(index):
    return index


def own_source(column):
    lane, y = column % LANES, column // LANES
    x = lane % 16 - 4
    return jnp.where((x >= 0) & (x < 8), 64 * (lane // 16) + 8 * x + y, -1)


def halo_source(column):
    lane, y = column % LANES, column // LANES
    x = lane % 16
    at = 24 * (lane // 16) + y
    left = jnp.where((x >= 1) & (x < 4), at + 8 * (x - 1), -1)
    return jnp.where((x >= 12) & (x < 15), at + 8 * (x - 12) + 256, left)


def pair_source(column):
    lane, y = (column - 4) % LANES, column // LANES
    return 512 * (lane % 16 // 8) + 64 * (lane // 16) + 8 * (lane % 8) + y


def edge_source(column):
    at, side = column % 256, column // 256
    x = at % 24 // 8 + 5 * side
    return jnp.where(at < 192, 64 * (at // 24) + 8 * x + at % 8, -1)


def dot(left, right, contract=(1, 0)):
    dims = (((contract[0],), (contract[1],)), ((), ()))
    return lax.dot_general(left, right, dims, preferred_element_type=F32)


def roll(value, shift):
    return pltpu.roll(value, shift % LANES, 1)


def lane_ids(rows):
    return lax.broadcasted_iota(jnp.int32, (rows, LANES), 1)


def silu_parts(value):
    sigma = 1.0 / (1.0 + jnp.exp(-value))
    return value * sigma, sigma * (1.0 + value * (1.0 - sigma))


def depth_columns(base, masks, step):
    below = roll(base, step) * masks[0]
    above = roll(base, -step) * masks[1]
    return jnp.concatenate([below, base, above], axis=0)


def depth_masks(step, first):
    ids = (lane_ids(3 * C) - first) % LANES
    return (ids >= step).astype(BF16), (ids < LANES - step).astype(BF16)


def across_columns(tile, step):
    return jnp.concatenate([roll(tile, step), tile, roll(tile, -step)], axis=0)


def edge_masks(step):
    ids = lane_ids(C) % 8
    first, last = (ids == 4).astype(BF16), (ids == 4 - step).astype(BF16)
    return first, (ids != 4).astype(BF16), last, (ids != 4 - step).astype(BF16)


def pair_columns(tile, halo, masks, step):
    left = roll(halo, step) * masks[0] + roll(tile, step) * masks[1]
    right = roll(halo, -step) * masks[2] + roll(tile, -step) * masks[3]
    return jnp.concatenate([left, tile, right], axis=0)


def beside_halo(tiles, from_left, from_right, step):
    masks = edge_masks(step)

    def load(index, place):
        group = lax.div(index, 8)
        tile = tiles[index]
        left = roll(from_left[group], -place) * masks[0] + roll(tile, step) * masks[1]
        right = roll(from_right[group], 8 - step - place) * masks[2]
        right = right + roll(tile, -step) * masks[3]
        return jnp.concatenate([left, tile, right], axis=0)

    return load


def pack_columns(tiles, low, high, step):
    masks = edge_masks(step)

    def body(group):
        lows, highs = [], []
        for place in range(8):
            tile = tiles[8 * group + place]
            lows.append(roll(tile * masks[0], place))
            highs.append(roll(tile * masks[2], place - 8 + step))
        for out, parts in ((low, lows), (high, highs)):
            while len(parts) > 1:
                parts = [a + b for a, b in zip(parts[::2], parts[1::2])]
            out[group] = parts[0]

    loop(0, low.shape[0], body)


def own_masks():
    own = own_lanes(C)
    return own.astype(BF16), jnp.logical_not(own).astype(BF16)


def pair_tiles(lower, upper, masks):
    turned = roll(upper, 8)
    return (
        lower * masks[0] + turned * masks[1],
        lower * masks[1] + turned * masks[0],
    )


def own_lanes(rows):
    across = lane_ids(rows) % 16
    return (across >= 4) & (across < 12)


def join_halves(lower, upper):
    return jnp.where(own_lanes(lower.shape[0]), lower, roll(upper, 8))


def gather_sub(parts):
    even = lane_ids(C) % 2 == 0
    above = jnp.where(even, parts[2 * C : 3 * C], parts[3 * C :])
    total = jnp.where(even, parts[:C], parts[C : 2 * C]) + roll(above, -16)
    return total + roll(total, -1)


def spread_sub(anchored):
    return jnp.concatenate([anchored] + [roll(anchored, step) for step in SHIFTS[1:]], axis=0)


def anchor_mask(first):
    ids = (lane_ids(C) - first) % LANES
    return (((ids // 16) % 2 == 0) & (ids % 2 == 0)).astype(F32)


def loop(low, high, body, unroll=1):
    def step(index, carry):
        body(index)
        return carry

    lax.fori_loop(low, high, step, 0, unroll=unroll)


def join_rows(first, second):
    low = lane_ids(C) < 64
    lead = roll(second[:, :LANES], 64)
    parts = [
        first[:, :LANES],
        jnp.where(low, first[:, LANES:], lead),
        jnp.where(low, lead, roll(second[:, LANES:], 64)),
    ]
    return jnp.concatenate(parts, axis=1)


def split_rows(joined):
    low = lane_ids(C) < 64
    middle = roll(joined[:, LANES : 2 * LANES], 64)
    last = roll(joined[:, 2 * LANES :], 64)
    second = jnp.concatenate([jnp.where(low, middle, last), last], axis=1)
    return joined[:, : 2 * LANES], second


def prepare_kernel(slots, count, feats, cots, flag_rows, x_low, x_high, y_low, y_high, rows_in):
    number = feats.shape[0]
    rows = lax.broadcasted_iota(jnp.int32, (16, LANES), 0)
    flags = jnp.zeros((16, LANES), F32)
    zero = jnp.zeros((C, VOX), BF16)
    first = jnp.zeros((), jnp.int32)
    last = jnp.zeros((), jnp.int32)
    for slot in range(number):
        live = slot < count[0]
        place = slots[slot]
        block = jnp.where(live, feats[slot], zero)
        rows_in[pl.ds(pl.multiple_of(place * C, 16), C), :] = block
        flags = jnp.where(rows == place, jnp.where(live, 1.0, 0.0), flags)
        first = jnp.where(place == 0, slot, first)
        last = jnp.where(place == number - 1, slot, last)
    flag_rows[...] = flags
    packed = dot(rows_in[...], marks(VOX, 512, plain, edge_source)).astype(BF16)
    spare = jnp.zeros((16, 2 * LANES), BF16)
    for out, at in ((x_low, 0), (x_high, 256)):
        for pair in range(number // 2):
            edges = [packed[C * i : C * (i + 1), at : at + 256] for i in (2 * pair, 2 * pair + 1)]
            out[C * pair : C * (pair + 1), :] = join_rows(*edges)
        out[C * number // 2 :, :LANES] = flags.astype(BF16)
        out[C * number // 2 :, LANES:] = spare
    for out, index, slot in ((y_low, 0, first), (y_high, number - 1, last)):
        live = slot < count[0]
        out[0:C, :] = rows_in[C * index : C * (index + 1), :]
        out[C : 2 * C, :] = jnp.where(live, cots[slot], zero)
        out[2 * C :, :] = (jnp.zeros((16, VOX), F32) + jnp.where(live, 1.0, 0.0)).astype(BF16)


def corner_kernel(y_left, y_right, low, high):
    rows = jnp.concatenate([y_left[0:C, :], y_right[0:C, :]], axis=0)
    packed = dot(rows, marks(VOX, 512, plain, edge_source)).astype(BF16)
    ids = lax.broadcasted_iota(jnp.int32, (16, LANES), 0)
    flags = jnp.where(ids == 0, y_left[2 * C :, :LANES], y_right[2 * C :, :LANES])
    spare = jnp.zeros((16, 2 * LANES), BF16)
    for out, at in ((low, 0), (high, 256)):
        out[0:C, :] = join_rows(packed[:C, at : at + 256], packed[C:, at : at + 256])
        out[C:, :LANES] = flags
        out[C:, LANES:] = spare


def arrange_weights(fine, down, coarse, up, fine_w, fine_b, coarse_w, coarse_b, down_w, up_w):
    for source, fore, back in ((fine, fine_w, fine_b), (coarse, coarse_w, coarse_b)):
        for along in range(3):
            rows = slice(C * along, C * (along + 1))
            turned_rows = slice(C * (2 - along), C * (3 - along))
            ahead = []
            behind = []
            for depth in range(3):
                for across in range(3):
                    ahead.append(source[9 * depth + 3 * across + along])
                    behind.append(source[9 * (2 - depth) + 3 * (2 - across) + along].T)
            fore[rows, :] = jnp.concatenate(ahead, axis=1)
            back[turned_rows, :] = jnp.concatenate(behind, axis=1)
    for index in range(4):
        pair = [down[:, 2 * index, :], down[:, 2 * index + 1, :]]
        down_w[C * index : C * (index + 1), :] = jnp.concatenate(pair, axis=1)
    for along in range(2):
        row = jnp.concatenate([up[2 * index + along] for index in range(4)], axis=1)
        up_w[C * along : C * (along + 1), :] = row


def place_kernel(
    slots, count, feats, cots, y_left, y_right, c_low, fine, down, coarse, up,
    grid, cot_grid, grad_r, fine_w, fine_b, coarse_w, coarse_b, down_w, up_w,
    rows_in, rows_cot, cot,
):
    arrange_weights(fine, down, coarse, up, fine_w, fine_b, coarse_w, coarse_b, down_w, up_w)
    number = feats.shape[0]
    last = number + 1
    zero = jnp.zeros((C, VOX), BF16)
    rows_in[0:C, :] = y_left[0:C, :]
    rows_in[last * C : (last + 1) * C, :] = y_right[0:C, :]
    for slot in range(number):
        live = slot < count[0]
        place = slots[slot]
        start = pl.multiple_of((place + 1) * C, 16)
        rows_in[pl.ds(start, C), :] = jnp.where(live, feats[slot], zero)
        cot[place] = jnp.where(live, cots[slot], zero)
    pairs = number // 2 + 2
    for group in range(pairs):
        at = group * C
        lower = y_left[C : 2 * C, :] if group == 0 else cot[group - 1]
        upper = y_right[C : 2 * C, :] if group == pairs - 1 else cot[group + number // 2 - 1]
        rows_cot[at : at + C, 0:512] = lower
        rows_cot[at : at + C, 512:1024] = upper
    for pair in range(4):
        placed_cot = dot(
            rows_cot[...], marks(1024, 256, plain, lambda j, at=256 * pair: pair_source(j + at))
        )
        placed = dot(
            rows_in[...], marks(VOX, 256, plain, lambda j, at=256 * pair: own_source(j + at))
        )
        for half in range(2):
            span = slice(LANES * half, LANES * (half + 1))
            for block in range(last + 1):
                tile = EDGE * block + 2 * pair + half
                grid[tile] = placed[block * C : (block + 1) * C, span].astype(BF16)
            for block in range(pairs):
                tile = EDGE * block + 2 * pair + half
                cot_grid[tile] = placed_cot[block * C : (block + 1) * C, span].astype(BF16)

    def rect_step(block):
        tiles = []
        for inner in range(4):
            tile = EDGE * block + 2 * inner
            tiles.append(jnp.concatenate([cot_grid[tile], cot_grid[tile + 1]], axis=0))
        parts = dot(up_w[...], jnp.concatenate(tiles, axis=1), (0, 0))
        for inner in range(4):
            grad_r[4 * block + inner] = gather_sub(parts[:, LANES * inner : LANES * (inner + 1)])

    loop(0, pairs, rect_step, 2)


def conv_steps(sums, weight, load, tiles, step, first, even, odd):
    masks = depth_masks(step, first)

    def fill(buffer, tile, place):
        for i in range(4):
            cols = depth_columns(load(tile + i, place + i), masks, step)
            buffer[:, LANES * i : LANES * (i + 1)] = cols

    def multiply(buffer, tile, carry):
        out = dot(weight[...], buffer[...])

        def part(along, i):
            return out[C * along : C * (along + 1), LANES * i : LANES * (i + 1)]

        sums[tile] += part(2, 0)
        sums[tile + 1] = carry + part(1, 0) + part(2, 1)
        sums[tile + 2] = part(0, 0) + part(1, 1) + part(2, 2)
        sums[tile + 3] = part(0, 1) + part(1, 2) + part(2, 3)
        sums[tile + 4] = part(0, 2) + part(1, 3)
        return part(0, 3)

    fill(even, 0, 0)
    sums[0] = jnp.zeros((C, LANES), F32)

    def body(index, carry):
        tile = 8 * index
        fill(odd, tile + 4, 4)
        carry = multiply(even, tile, carry)
        fill(even, jnp.minimum(tile + 8, tiles - 4), 0)
        return multiply(odd, tile + 4, carry)

    lax.fori_loop(0, tiles // 8, body, jnp.zeros((C, LANES), F32))


def forward_kernel(
    grid_own, flags, y_left, y_right, grad_r, x_left, x_right, c_left, c_right, fine_w, down_w,
    coarse_w,
    grid, hidden, low_cols, rects, grad_c, live, pack_low, pack_high,
    rows_in, fine_p, coarse_p, hidden_all, lowered, live_all, even, odd,
):
    number = 2 * (x_left.shape[0] - 16) // C
    last = number + 1
    for at, left, right in ((0, x_left, x_right), (None, c_left, c_right)):
        for pair in range((left.shape[0] - 16) // C):
            rows = slice(C * pair, C * (pair + 1))
            lefts, rights = split_rows(left[rows, :]), split_rows(right[rows, :])
            for inner in range(2):
                block = last * inner if at is None else 2 * pair + inner + 1
                rows_in[block * C : (block + 1) * C, 0:256] = lefts[inner]
                rows_in[block * C : (block + 1) * C, 256:512] = rights[inner]
    across = lane_ids(16) % 16
    for start, middle, left, right in (
        (1, flags[...], x_left[number // 2 * C :, :LANES], x_right[number // 2 * C :, :LANES]),
        (0, y_left[2 * C :, :LANES], c_left[C:, :LANES], c_right[C:, :LANES]),
        (last, y_right[2 * C :, :LANES], c_left[C:, :LANES], c_right[C:, :LANES]),
    ):
        rows = jnp.where(across < 4, left.astype(F32), middle.astype(F32))
        rows = jnp.where(across >= 12, right.astype(F32), rows)
        if start == 1:
            live_all[1 : number + 1, :] = rows
        else:
            at = 0 if start == 0 else 1
            live_all[start : start + 1, :] = rows[at : at + 1, :]
    for pair in range(4):
        placed = dot(
            rows_in[...], marks(512, 256, plain, lambda j, at=256 * pair: halo_source(j + at))
        )
        for half in range(2):
            span = slice(LANES * half, LANES * (half + 1))
            for block in range(last + 1):
                tile = EDGE * block + 2 * pair + half
                halo = placed[block * C : (block + 1) * C, span].astype(BF16)
                grid[tile] = grid_own[tile] + halo
    live[...] = join_halves(live_all[0:16, :], live_all[8:24, :])
    tiles = grid.shape[0]
    conv_steps(fine_p, fine_w, lambda tile, _: across_columns(grid[tile], 1), tiles, 16, 0, even, odd)
    anchors = anchor_mask(0)

    def lower_step(block):
        alive = jnp.broadcast_to(live_all[pl.ds(block, 1), :], (C, LANES))
        keep = alive * anchors
        pairs = []
        for inner in range(4):
            actives = []
            for half in range(2):
                tile = EDGE * block + 2 * inner + half
                value = fine_p[tile + 1] * alive
                hidden_all[tile] = value
                actives.append(silu_parts(value)[0].astype(BF16))
            pairs.append(jnp.concatenate(actives, axis=0))
        parts = dot(down_w[...], jnp.concatenate(pairs, axis=1))
        for inner in range(4):
            total = gather_sub(parts[:, LANES * inner : LANES * (inner + 1)])
            lowered[4 * block + inner] = (total * keep).astype(BF16)

    loop(0, last + 1, lower_step, 2)
    pairs = hidden.shape[0] // EDGE
    shift = last - pairs + 1
    edges = edge_masks(2)
    halves = own_masks()

    def pair_step(block):
        for inner in range(EDGE):
            tile = EDGE * block + inner
            hidden[tile] = join_halves(hidden_all[tile], hidden_all[tile + EDGE * shift])
        for inner in range(4):
            tile = 4 * block + inner
            lower, upper = lowered[tile], lowered[tile + 4 * shift]
            low_cols[tile] = pair_columns(*pair_tiles(lower, upper, halves), edges, 2)

    loop(0, pairs, pair_step, 2)
    conv_steps(coarse_p, coarse_w, lambda tile, _: low_cols[tile], 4 * pairs, 32, 4, even, odd)
    pair_anchors = anchor_mask(4)

    def grad_step(block):
        alive = jnp.broadcast_to(live[pl.ds(block, 1), :], (C, LANES))
        keep = alive * pair_anchors
        for inner in range(4):
            coarse = 4 * block + inner
            smooth, slope = silu_parts(coarse_p[coarse + 1])
            rects[coarse] = (smooth * pair_anchors).astype(BF16)
            grad_c[coarse] = (grad_r[coarse] * slope * keep).astype(BF16)

    loop(0, pairs, grad_step, 2)
    pack_columns(grad_c, pack_low, pack_high, 2)


def to_blocks(slots, rows_out, back, flat, out):
    flat[...] = dot(rows_out[...], back[...]).astype(BF16)
    number = out.shape[0]
    for slot in range(number):
        place = slots[slot]
        upper = place >= number // 2
        start = pl.multiple_of(jnp.where(upper, place - number // 2, place) * C, 16)
        rows = flat[pl.ds(start, C), :]
        out[slot] = jnp.where(upper, rows[:, 512:], rows[:, :512])


def stacks(own, tiles):
    parts = [jnp.concatenate([own[t + 1], own[t], own[t - 1]], axis=0) for t in tiles]
    return jnp.concatenate(parts, axis=1)


def squeeze_rows(full, keep):
    extra = full[keep:]
    size, part = extra.shape[0], keep // 3
    lanes = lane_ids(size)
    pieces = []
    for index in range(3):
        rows = full[part * index : part * (index + 1)]
        pieces.append(jnp.where(lanes < 96, rows[:size], roll(extra, 96 - 32 * index)))
        if size < part:
            pieces.append(rows[size:])
    return jnp.concatenate(pieces, axis=0)


def widen_rows(packed, number):
    keep = packed.shape[0]
    size, part = number - keep, keep // 3
    lanes = lane_ids(size)
    extra = jnp.zeros((size, LANES), F32)
    for index in range(3):
        moved = roll(packed[part * index : part * index + size], 32 * index - 96)
        extra = jnp.where((lanes >= 32 * index) & (lanes < 32 * index + 32), moved, extra)
    return jnp.concatenate([packed, extra], axis=0)


def flatten_weights(total, out):
    turned = total[...].T
    for group in range(3):
        part = turned[:, LANES * group : LANES * (group + 1)]
        out[3 * C * group : 3 * C * (group + 1), :] = part.astype(BF16)
    return turned[:, 3 * LANES :]


def output_kernel(slots, hidden, rects, live, up_w, out, back, rows_out, flat):
    back[...] = marks(1024, 1024, pair_source, plain)
    pairs = hidden.shape[0] // EDGE

    def block_step(block):
        alive = jnp.broadcast_to(live[pl.ds(block, 1), :], (C, LANES))
        start = pl.multiple_of((block - 1) * C, 16)
        spreads = [spread_sub(rects[4 * block + inner]) for inner in range(4)]
        upward = dot(up_w[...], jnp.concatenate(spreads, axis=1))
        for inner in range(4):
            for half in range(2):
                part = upward[half * C : (half + 1) * C, LANES * inner : LANES * (inner + 1)]
                value = hidden[EDGE * block + 2 * inner + half] + part
                at = LANES * (2 * inner + half)
                rows_out[pl.ds(start, C), at : at + LANES] = (value * alive).astype(BF16)

    loop(1, pairs - 1, block_step, 2)
    to_blocks(slots, rows_out, back, flat, out)


def side_kernel(rects, cot_grid, low_cols, grad_c, flat, grad_own, up_g, coarse_g):
    tiles = low_cols.shape[0]
    up_g[...] = jnp.zeros_like(up_g)
    coarse_g[...] = jnp.zeros_like(coarse_g)

    def up_step(block):
        spreads = []
        pairs = []
        for inner in range(4):
            coarse = 4 * block + inner
            spreads.append(spread_sub(rects[coarse]))
            pairs.append(
                jnp.concatenate([cot_grid[2 * coarse], cot_grid[2 * coarse + 1]], axis=0)
            )
        up_g[:, 0 : 2 * C] += dot(
            jnp.concatenate(spreads, axis=1), jnp.concatenate(pairs, axis=1), (1, 1)
        )

    loop(1, tiles // 4 - 1, up_step, 2)
    zero = jnp.zeros((C, LANES), BF16)
    for coarse in range(1, 4):
        grad_own[coarse] = zero
        grad_own[tiles - 1 - coarse] = zero

    def copy_step(coarse):
        grad_own[coarse] = grad_c[coarse]

    loop(4, tiles - 4, copy_step, 8)
    masks = depth_masks(32, 4)

    def weight_step(index):
        at = [2 + 4 * index + inner for inner in range(4)]
        rights = [depth_columns(low_cols[tile], masks, 32) for tile in at]
        coarse_g[0 : 9 * C, :] += dot(
            jnp.concatenate(rights, axis=1), stacks(grad_own, at), (1, 1)
        )

    loop(0, (tiles - 4) // 4, weight_step, 3)
    rest = flatten_weights(coarse_g, flat)
    flat[9 * C : 12 * C, :] = squeeze_rows(up_g[...], 3 * C).astype(BF16)
    flat[12 * C :, :] = roll(rest, C).astype(BF16)


def backward_kernel(
    grad_c, from_left, from_right, hidden, cot_grid, live, coarse_w, down_w,
    grad_h, grad_d, coarse_p, even, odd,
):
    tiles = grad_c.shape[0]
    load = beside_halo(grad_c, from_left, from_right, 2)
    conv_steps(coarse_p, coarse_w, load, tiles, 32, 4, even, odd)
    anchors = anchor_mask(4)

    def step(block):
        alive = jnp.broadcast_to(live[pl.ds(block, 1), :], (C, LANES))
        keep = alive * anchors
        spreads = []
        for inner in range(4):
            coarse = 4 * block + inner
            down = (coarse_p[coarse + 1] * keep).astype(BF16)
            grad_d[coarse] = down
            spreads.append(spread_sub(down))
        acts = dot(down_w[...], jnp.concatenate(spreads, axis=1), (0, 0))
        for inner in range(4):
            for side in range(2):
                tile = EDGE * block + 2 * inner + side
                slope = silu_parts(hidden[tile])[1]
                part = acts[side * C : (side + 1) * C, LANES * inner : LANES * (inner + 1)]
                grad = cot_grid[tile].astype(F32) + part * slope
                grad_h[tile] = (grad * alive).astype(BF16)

    loop(0, tiles // 4, step, 2)


def pack_kernel(grad_h, low, high):
    pack_columns(grad_h, low, high, 1)


def weight_kernel(grid, grad_h, grad_d, hidden, early, joined, grad_own, fine_g, down_g):
    tiles = grad_h.shape[0]
    shift = tiles - 16
    fine_g[...] = jnp.zeros_like(fine_g)
    down_g[...] = jnp.zeros_like(down_g)
    zero = jnp.zeros((C, LANES), BF16)
    for tile in range(3, 8):
        grad_own[tile] = zero
        grad_own[tiles - 1 - tile] = zero

    def copy_step(tile):
        grad_own[tile] = grad_h[tile]

    loop(8, tiles - 8, copy_step, 8)
    masks = depth_masks(16, 4)
    edges = edge_masks(1)
    halves = own_masks()

    def fine_step(index):
        at = [4 + 12 * index + inner for inner in range(12)]
        rights = []
        for tile in at:
            lower, upper = grid[tile], grid[tile + shift]
            base = pair_columns(*pair_tiles(lower, upper, halves), edges, 1)
            rights.append(depth_columns(base, masks, 16))
        fine_g[0 : 9 * C, :] += dot(
            jnp.concatenate(rights, axis=1), stacks(grad_own, at), (1, 1)
        )

    loop(0, (tiles - 8) // 12, fine_step)

    def down_step(index):
        lefts = []
        rights = []
        for inner in range(4):
            coarse = 4 + 4 * index + inner
            lefts.append(spread_sub(grad_d[coarse]))
            actives = [silu_parts(hidden[2 * coarse + side])[0].astype(BF16) for side in range(2)]
            rights.append(jnp.concatenate(actives, axis=0))
        down_g[:, 0 : 2 * C] += dot(
            jnp.concatenate(lefts, axis=1), jnp.concatenate(rights, axis=1), (1, 1)
        )

    loop(0, (tiles // 2 - 8) // 4, down_step, 2)
    rest = flatten_weights(fine_g, joined) + early[12 * C :, :].astype(F32)
    joined[9 * C : 18 * C, :] = early[0 : 9 * C, :]
    joined[18 * C : 21 * C, :] = squeeze_rows(down_g[...], 3 * C).astype(BF16)
    joined[21 * C : 24 * C, :] = early[9 * C : 12 * C, :]
    squeezed = squeeze_rows(rest, 120)
    joined[24 * C :, :] = jnp.concatenate([squeezed, squeezed[:8]], axis=0).astype(BF16)


def input_kernel(
    slots, grad_h, from_left, from_right, live, fine_w, back, out,
    fine_p, rows_out, flat, even, odd,
):
    tiles = grad_h.shape[0]
    load = beside_halo(grad_h, from_left, from_right, 1)
    conv_steps(fine_p, fine_w, load, tiles, 16, 4, even, odd)

    def block_step(block):
        alive = jnp.broadcast_to(live[pl.ds(block, 1), :], (C, LANES))
        start = pl.multiple_of((block - 1) * C, 16)
        for inner in range(EDGE):
            value = fine_p[EDGE * block + inner + 1]
            rows_out[pl.ds(start, C), LANES * inner : LANES * (inner + 1)] = (
                value * alive
            ).astype(BF16)

    loop(1, tiles // EDGE - 1, block_step, 2)
    to_blocks(slots, rows_out, back, flat, out)


def sum_kernel(parts, copies):
    total = jnp.sum(parts[...].astype(F32), axis=0).astype(BF16)
    copies[...] = jnp.broadcast_to(total[None], copies.shape)


def finish_kernel(scale, total, fine, down, coarse, up):
    rest = widen_rows(total[24 * C :, :].astype(F32)[:120], 3 * C) * scale
    for out, at, moved in ((fine, 0, rest), (coarse, 9 * C, roll(rest, -C))):
        for along in range(3):
            first = at + C * along
            rows = [total[first + 3 * C * g : first + 3 * C * g + C, :] for g in range(3)]
            row = jnp.concatenate(rows, axis=1).astype(F32) * scale
            row = jnp.concatenate([row, moved[C * along : C * (along + 1)]], axis=1)
            for index in range(9):
                out[3 * index + along] = row[:, C * index : C * (index + 1)]
    for out, at, turn in ((down, 18 * C, False), (up, 21 * C, True)):
        full = widen_rows(total[at : at + 3 * C, :].astype(F32), 4 * C) * scale
        for index in range(4):
            rows = full[C * index : C * (index + 1)]
            for along in range(2):
                part = rows[:, C * along : C * (along + 1)]
                if turn:
                    out[2 * index + along] = part.T
                else:
                    out[:, 2 * index + along, :] = part


def call(kernel, inputs, outs, scratch=(), scalars=0, flops=0, limit=None):
    vmem = pl.BlockSpec(memory_space=pltpu.VMEM)
    smem = pl.BlockSpec(memory_space=pltpu.SMEM)
    held = SLACK
    for shape, kind in [(a.shape, a.dtype) for a in inputs[scalars:]] + list(outs) + list(scratch):
        rows, lanes = -(-shape[-2] // 16) * 16, -(-shape[-1] // LANES) * LANES
        held += math.prod(shape[:-2]) * rows * lanes * jnp.dtype(kind).itemsize
    moved = sum(math.prod(s) * jnp.dtype(d).itemsize for s, d in outs)
    moved += sum(math.prod(a.shape) * a.dtype.itemsize for a in inputs)
    return pl.pallas_call(
        kernel,
        out_shape=tuple(jax.ShapeDtypeStruct(s, d) for s, d in outs),
        in_specs=[smem] * scalars + [vmem] * (len(inputs) - scalars),
        out_specs=tuple(vmem for _ in outs),
        scratch_shapes=[pltpu.VMEM(s, d) for s, d in scratch],
        compiler_params=pltpu.CompilerParams(vmem_limit_bytes=limit or held),
        cost_estimate=pl.CostEstimate(flops=flops, bytes_accessed=moved, transcendentals=0),
        name=getattr(kernel, "func", kernel).__name__,
    )(*inputs)


def send(array, step_x, step_y):
    number_x, number_y = lax.axis_size("gx"), lax.axis_size("gy")
    pairs = []
    for i in range(number_x):
        for j in range(number_y):
            to_x, to_y = i + step_x, j + step_y
            if 0 <= to_x < number_x and 0 <= to_y < number_y:
                pairs.append((i * number_y + j, to_x * number_y + to_y))
    return lax.ppermute(array, ("gx", "gy"), pairs)


def reduce_share(joined):
    devices = lax.axis_size("gx") * lax.axis_size("gy")
    rows = joined.shape[0]
    share = -(-rows // devices)
    joined = jnp.pad(joined, ((0, share * devices - rows), (0, 0)))
    mine = lax.all_to_all(joined.reshape(devices, share, LANES), ("gx", "gy"), 0, 0)
    return mine


def spread_share(parts):
    (copies,) = call(sum_kernel, (parts,), [(parts.shape, BF16)])
    full = lax.all_to_all(copies, ("gx", "gy"), 0, 0)
    return full.reshape(-1, LANES)


def on_device(
    features, block_slots, block_count, cotangent, fine_weight, down_weight, coarse_weight,
    up_weight,
):
    number = features.shape[2]
    slots = block_slots.reshape(number)
    count = block_count.reshape(1)
    feats = features.reshape(number, C, VOX)
    cots = cotangent.reshape(number, C, VOX)
    tiles = EDGE * (number + 2)
    coarse_tiles = tiles // 2
    pairs = number // 2 + 2
    groups = pairs // 2
    fine_groups = pairs

    fine_3, coarse_3 = (weight.transpose(1, 0, 2) for weight in (fine_weight, coarse_weight))
    flag_rows, x_low, x_high, y_low, y_high = call(
        prepare_kernel,
        (slots, count, feats, cots),
        [((16, LANES), F32)]
        + [((number // 2 * C + 16, 384), BF16)] * 2
        + [((2 * C + 16, VOX), BF16)] * 2,
        [((number * C, VOX), BF16)],
        scalars=2,
        limit=56 * 1024 * 1024,
    )
    x_left = send(x_high, 1, 0)
    x_right = send(x_low, -1, 0)
    y_left = send(y_high, 0, 1)
    y_right = send(y_low, 0, -1)
    corner_low, corner_high = call(
        corner_kernel,
        (y_left, y_right),
        [((C + 16, 384), BF16), ((C + 16, 384), BF16)],
    )
    c_left = send(corner_high, 1, 0)
    c_right = send(corner_low, -1, 0)
    (grid_own, cot_grid, grad_r, fine_fore, fine_back, coarse_fore, coarse_back, down_w,
     up_w) = call(
        place_kernel,
        (slots, count, feats, cots, y_left, y_right, corner_low, fine_3, down_weight, coarse_3,
         up_weight),
        [
            ((tiles, C, LANES), BF16),
            ((EDGE * pairs, C, LANES), BF16),
            ((4 * pairs, C, LANES), F32),
        ]
        + [((3 * C, 9 * C), BF16)] * 4
        + [((4 * C, 2 * C), BF16), ((2 * C, 4 * C), BF16)],
        [
            (((number + 2) * C, VOX), BF16),
            ((pairs * C, 1024), BF16),
            ((number, C, VOX), BF16),
        ],
        scalars=2,
        flops=8 * 10**9,
    )
    grid, hidden, low_cols, rects, grad_c, live, pack_low, pack_high = call(
        forward_kernel,
        (grid_own, flag_rows, y_left, y_right, grad_r, x_left, x_right, c_left, c_right,
         fine_fore, down_w, coarse_fore),
        [
            ((tiles, C, LANES), BF16),
            ((EDGE * pairs, C, LANES), F32),
            ((4 * pairs, 3 * C, LANES), BF16),
            ((4 * pairs, C, LANES), BF16),
            ((4 * pairs, C, LANES), BF16),
            ((16, LANES), F32),
            ((groups, C, LANES), BF16),
            ((groups, C, LANES), BF16),
        ],
        [
            (((number + 2) * C, VOX), BF16),
            ((tiles + 1, C, LANES), F32),
            ((4 * pairs + 1, C, LANES), F32),
            ((tiles, C, LANES), F32),
            ((coarse_tiles, C, LANES), BF16),
            ((C, LANES), F32),
        ]
        + [((9 * C, 4 * LANES), BF16)] * 2,
        flops=8 * 10**9,
    )
    grad_left = send(pack_high, 1, 0)
    grad_right = send(pack_low, -1, 0)
    (early,) = call(
        side_kernel,
        (rects, cot_grid, low_cols, grad_c),
        [((15 * C, LANES), BF16)],
        [((4 * pairs, C, LANES), BF16), ((4 * C, LANES), F32), ((VOX, 3 * C), F32)],
        flops=8 * 10**9,
    )
    grad_h, grad_d = call(
        backward_kernel,
        (grad_c, grad_left, grad_right, hidden, cot_grid, live, coarse_back, down_w),
        [
            ((EDGE * pairs, C, LANES), BF16),
            ((4 * pairs, C, LANES), BF16),
        ],
        [((4 * pairs + 1, C, LANES), F32)]
        + [((9 * C, 4 * LANES), BF16)] * 2,
        flops=8 * 10**9,
    )
    (joined,) = call(
        weight_kernel,
        (grid, grad_h, grad_d, hidden, early),
        [((24 * C + 128, LANES), BF16)],
        [((EDGE * pairs, C, LANES), BF16), ((VOX, 3 * C), F32), ((4 * C, LANES), F32)],
        flops=12 * 10**9,
    )
    joined, slots, grad_h = lax.optimization_barrier((joined, slots, grad_h))
    edge_low, edge_high = call(
        pack_kernel, (grad_h,), [((fine_groups, C, LANES), BF16)] * 2, flops=10**9
    )
    edge_left = send(edge_high, 1, 0)
    edge_right = send(edge_low, -1, 0)
    share = reduce_share(joined)
    output, back = call(
        output_kernel,
        (slots, hidden, rects, live, up_w),
        [((number, C, VOX), BF16), ((1024, 1024), BF16)],
        [((number // 2 * C, 1024), BF16), ((number // 2 * C, 1024), BF16)],
        scalars=1,
        flops=8 * 10**9,
    )
    share, output, slots = lax.optimization_barrier((share, output, slots))
    (input_grad,) = call(
        input_kernel,
        (slots, grad_h, edge_left, edge_right, live, fine_back, back),
        [((number, C, VOX), BF16)],
        [
            ((EDGE * pairs + 1, C, LANES), F32),
            ((number // 2 * C, 1024), BF16),
            ((number // 2 * C, 1024), BF16),
        ]
        + [((9 * C, 4 * LANES), BF16)] * 2,
        scalars=1,
        flops=8 * 10**9,
    )
    total = spread_share(share)
    scale = 1.0 / math.sqrt(number * VOX * lax.axis_size("gx") * lax.axis_size("gy"))
    fine_total, down_total, coarse_total, up_total = call(
        functools.partial(finish_kernel, scale),
        (total,),
        [((27, C, C), F32), ((C, 8, C), F32), ((27, C, C), F32), ((8, C, C), F32)],
    )
    shape_out = (1, 1, number, C, VOX)
    return (
        output.reshape(shape_out),
        input_grad.reshape(shape_out),
        fine_total.transpose(1, 0, 2),
        down_total,
        coarse_total.transpose(1, 0, 2),
        up_total,
    )


def solution(mesh):
    split = P("gx", "gy", None, None, None)
    return jax.shard_map(
        on_device,
        mesh=mesh,
        in_specs=(split, P("gx", "gy", None), P("gx", "gy"), split, P(), P(), P(), P()),
        out_specs=(split, split, P(), P(), P(), P()),
        check_vma=False,
    )
```

```python
import functools
import math

import jax
import jax.numpy as jnp
from jax import lax
from jax.experimental import pallas as pl
from jax.experimental.pallas import tpu as pltpu
from jax.sharding import PartitionSpec as P

C = 48
EDGE = 8
VOX = 512
LANES = 128
F32 = jnp.float32
BF16 = jnp.bfloat16
SLACK = 8 * 1024 * 1024
SHIFTS = (0, 1, 16, 17)


def marks(rows, columns, row_key, column_key):
    across = column_key(lax.broadcasted_iota(jnp.int32, (1, columns), 1))
    down = row_key(lax.broadcasted_iota(jnp.int32, (rows, 1), 0))
    return jnp.where(down == across, 1.0, 0.0).astype(BF16)


def plain(index):
    return index


def own_source(column):
    lane, y = column % LANES, column // LANES
    x = lane % 16 - 4
    return jnp.where((x >= 0) & (x < 8), 64 * (lane // 16) + 8 * x + y, -1)


def halo_source(column):
    lane, y = column % LANES, column // LANES
    x = lane % 16
    at = 24 * (lane // 16) + y
    left = jnp.where((x >= 1) & (x < 4), at + 8 * (x - 1), -1)
    return jnp.where((x >= 12) & (x < 15), at + 8 * (x - 12) + 256, left)


def pair_source(column):
    lane, y = (column - 4) % LANES, column // LANES
    return 512 * (lane % 16 // 8) + 64 * (lane // 16) + 8 * (lane % 8) + y


def edge_source(column):
    at, side = column % 256, column // 256
    x = at % 24 // 8 + 5 * side
    return jnp.where(at < 192, 64 * (at // 24) + 8 * x + at % 8, -1)


def dot(left, right, contract=(1, 0)):
    dims = (((contract[0],), (contract[1],)), ((), ()))
    return lax.dot_general(left, right, dims, preferred_element_type=F32)


def roll(value, shift):
    return pltpu.roll(value, shift % LANES, 1)


def lane_ids(rows):
    return lax.broadcasted_iota(jnp.int32, (rows, LANES), 1)


def silu_parts(value):
    sigma = 1.0 / (1.0 + jnp.exp(-value))
    return value * sigma, sigma * (1.0 + value * (1.0 - sigma))


def depth_columns(base, masks, step):
    below = roll(base, step) * masks[0]
    above = roll(base, -step) * masks[1]
    return jnp.concatenate([below, base, above], axis=0)


def depth_masks(step, first):
    ids = (lane_ids(3 * C) - first) % LANES
    return (ids >= step).astype(BF16), (ids < LANES - step).astype(BF16)


def across_columns(tile, step):
    return jnp.concatenate([roll(tile, step), tile, roll(tile, -step)], axis=0)


def edge_masks(step):
    ids = lane_ids(C) % 8
    first, last = (ids == 4).astype(BF16), (ids == 4 - step).astype(BF16)
    return first, (ids != 4).astype(BF16), last, (ids != 4 - step).astype(BF16)


def pair_columns(tile, halo, masks, step):
    left = roll(halo, step) * masks[0] + roll(tile, step) * masks[1]
    right = roll(halo, -step) * masks[2] + roll(tile, -step) * masks[3]
    return jnp.concatenate([left, tile, right], axis=0)


def fill_columns(tiles, from_left, from_right, out, step):
    masks = edge_masks(step)

    def body(group):
        packed_left, packed_right = from_left[group], from_right[group]
        for place in range(8):
            tile = tiles[8 * group + place]
            left = roll(packed_left, -place) * masks[0] + roll(tile, step) * masks[1]
            right = roll(packed_right, 8 - step - place) * masks[2]
            right = right + roll(tile, -step) * masks[3]
            out[8 * group + place] = jnp.concatenate([left, tile, right], axis=0)

    loop(0, from_left.shape[0], body)


def pack_columns(tiles, low, high, step):
    masks = edge_masks(step)

    def body(group):
        lows, highs = [], []
        for place in range(8):
            tile = tiles[8 * group + place]
            lows.append(roll(tile * masks[0], place))
            highs.append(roll(tile * masks[2], place - 8 + step))
        for out, parts in ((low, lows), (high, highs)):
            while len(parts) > 1:
                parts = [a + b for a, b in zip(parts[::2], parts[1::2])]
            out[group] = parts[0]

    loop(0, low.shape[0], body)


def own_masks():
    own = own_lanes(C)
    return own.astype(BF16), jnp.logical_not(own).astype(BF16)


def pair_tiles(lower, upper, masks):
    turned = roll(upper, 8)
    return (
        lower * masks[0] + turned * masks[1],
        lower * masks[1] + turned * masks[0],
    )


def own_lanes(rows):
    across = lane_ids(rows) % 16
    return (across >= 4) & (across < 12)


def join_halves(lower, upper):
    return jnp.where(own_lanes(lower.shape[0]), lower, roll(upper, 8))


def gather_sub(parts):
    even = lane_ids(C) % 2 == 0
    above = jnp.where(even, parts[2 * C : 3 * C], parts[3 * C :])
    total = jnp.where(even, parts[:C], parts[C : 2 * C]) + roll(above, -16)
    return total + roll(total, -1)


def spread_sub(anchored):
    return jnp.concatenate([anchored] + [roll(anchored, step) for step in SHIFTS[1:]], axis=0)


def anchor_mask(first):
    ids = (lane_ids(C) - first) % LANES
    return (((ids // 16) % 2 == 0) & (ids % 2 == 0)).astype(F32)


def loop(low, high, body, unroll=1):
    def step(index, carry):
        body(index)
        return carry

    lax.fori_loop(low, high, step, 0, unroll=unroll)


def join_rows(first, second):
    low = lane_ids(C) < 64
    lead = roll(second[:, :LANES], 64)
    parts = [
        first[:, :LANES],
        jnp.where(low, first[:, LANES:], lead),
        jnp.where(low, lead, roll(second[:, LANES:], 64)),
    ]
    return jnp.concatenate(parts, axis=1)


def split_rows(joined):
    low = lane_ids(C) < 64
    middle = roll(joined[:, LANES : 2 * LANES], 64)
    last = roll(joined[:, 2 * LANES :], 64)
    second = jnp.concatenate([jnp.where(low, middle, last), last], axis=1)
    return joined[:, : 2 * LANES], second


def prepare_kernel(slots, count, feats, cots, flag_rows, x_low, x_high, y_low, y_high, rows_in):
    number = feats.shape[0]
    rows = lax.broadcasted_iota(jnp.int32, (16, LANES), 0)
    flags = jnp.zeros((16, LANES), F32)
    zero = jnp.zeros((C, VOX), BF16)
    first = jnp.zeros((), jnp.int32)
    last = jnp.zeros((), jnp.int32)
    for slot in range(number):
        live = slot < count[0]
        place = slots[slot]
        block = jnp.where(live, feats[slot], zero)
        rows_in[pl.ds(pl.multiple_of(place * C, 16), C), :] = block
        flags = jnp.where(rows == place, jnp.where(live, 1.0, 0.0), flags)
        first = jnp.where(place == 0, slot, first)
        last = jnp.where(place == number - 1, slot, last)
    flag_rows[...] = flags
    packed = dot(rows_in[...], marks(VOX, 512, plain, edge_source)).astype(BF16)
    spare = jnp.zeros((16, 2 * LANES), BF16)
    for out, at in ((x_low, 0), (x_high, 256)):
        for pair in range(number // 2):
            edges = [packed[C * i : C * (i + 1), at : at + 256] for i in (2 * pair, 2 * pair + 1)]
            out[C * pair : C * (pair + 1), :] = join_rows(*edges)
        out[C * number // 2 :, :LANES] = flags.astype(BF16)
        out[C * number // 2 :, LANES:] = spare
    for out, index, slot in ((y_low, 0, first), (y_high, number - 1, last)):
        live = slot < count[0]
        out[0:C, :] = rows_in[C * index : C * (index + 1), :]
        out[C : 2 * C, :] = jnp.where(live, cots[slot], zero)
        out[2 * C :, :] = (jnp.zeros((16, VOX), F32) + jnp.where(live, 1.0, 0.0)).astype(BF16)


def corner_kernel(y_left, y_right, low, high):
    rows = jnp.concatenate([y_left[0:C, :], y_right[0:C, :]], axis=0)
    packed = dot(rows, marks(VOX, 512, plain, edge_source)).astype(BF16)
    ids = lax.broadcasted_iota(jnp.int32, (16, LANES), 0)
    flags = jnp.where(ids == 0, y_left[2 * C :, :LANES], y_right[2 * C :, :LANES])
    spare = jnp.zeros((16, 2 * LANES), BF16)
    for out, at in ((low, 0), (high, 256)):
        out[0:C, :] = join_rows(packed[:C, at : at + 256], packed[C:, at : at + 256])
        out[C:, :LANES] = flags
        out[C:, LANES:] = spare


def arrange_weights(fine, down, coarse, up, fine_w, fine_b, coarse_w, coarse_b, down_w, up_w):
    for source, fore, back in ((fine, fine_w, fine_b), (coarse, coarse_w, coarse_b)):
        for along in range(3):
            rows = slice(C * along, C * (along + 1))
            turned_rows = slice(C * (2 - along), C * (3 - along))
            ahead = []
            behind = []
            for depth in range(3):
                for across in range(3):
                    ahead.append(source[9 * depth + 3 * across + along])
                    behind.append(source[9 * (2 - depth) + 3 * (2 - across) + along].T)
            fore[rows, :] = jnp.concatenate(ahead, axis=1)
            back[turned_rows, :] = jnp.concatenate(behind, axis=1)
    for index in range(4):
        pair = [down[:, 2 * index, :], down[:, 2 * index + 1, :]]
        down_w[C * index : C * (index + 1), :] = jnp.concatenate(pair, axis=1)
    for along in range(2):
        row = jnp.concatenate([up[2 * index + along] for index in range(4)], axis=1)
        up_w[C * along : C * (along + 1), :] = row


def place_kernel(
    slots, count, feats, cots, y_left, y_right, c_low, fine, down, coarse, up,
    grid, cot_grid, grad_r, fine_w, fine_b, coarse_w, coarse_b, down_w, up_w,
    rows_in, rows_cot, cot,
):
    arrange_weights(fine, down, coarse, up, fine_w, fine_b, coarse_w, coarse_b, down_w, up_w)
    number = feats.shape[0]
    last = number + 1
    zero = jnp.zeros((C, VOX), BF16)
    rows_in[0:C, :] = y_left[0:C, :]
    rows_in[last * C : (last + 1) * C, :] = y_right[0:C, :]
    for slot in range(number):
        live = slot < count[0]
        place = slots[slot]
        start = pl.multiple_of((place + 1) * C, 16)
        rows_in[pl.ds(start, C), :] = jnp.where(live, feats[slot], zero)
        cot[place] = jnp.where(live, cots[slot], zero)
    pairs = number // 2 + 2
    for group in range(pairs):
        at = group * C
        lower = y_left[C : 2 * C, :] if group == 0 else cot[group - 1]
        upper = y_right[C : 2 * C, :] if group == pairs - 1 else cot[group + number // 2 - 1]
        rows_cot[at : at + C, 0:512] = lower
        rows_cot[at : at + C, 512:1024] = upper
    for pair in range(4):
        placed_cot = dot(
            rows_cot[...], marks(1024, 256, plain, lambda j, at=256 * pair: pair_source(j + at))
        )
        placed = dot(
            rows_in[...], marks(VOX, 256, plain, lambda j, at=256 * pair: own_source(j + at))
        )
        for half in range(2):
            span = slice(LANES * half, LANES * (half + 1))
            for block in range(last + 1):
                tile = EDGE * block + 2 * pair + half
                grid[tile] = placed[block * C : (block + 1) * C, span].astype(BF16)
            for block in range(pairs):
                tile = EDGE * block + 2 * pair + half
                cot_grid[tile] = placed_cot[block * C : (block + 1) * C, span].astype(BF16)

    def rect_step(block):
        tiles = []
        for inner in range(4):
            tile = EDGE * block + 2 * inner
            tiles.append(jnp.concatenate([cot_grid[tile], cot_grid[tile + 1]], axis=0))
        parts = dot(up_w[...], jnp.concatenate(tiles, axis=1), (0, 0))
        for inner in range(4):
            grad_r[4 * block + inner] = gather_sub(parts[:, LANES * inner : LANES * (inner + 1)])

    loop(0, pairs, rect_step, 5)


def conv_steps(sums, weight, load, tiles, step, first, even, odd):
    masks = depth_masks(step, first)

    def fill(buffer, tile):
        for i in range(4):
            cols = depth_columns(load(tile + i), masks, step)
            buffer[:, LANES * i : LANES * (i + 1)] = cols

    def multiply(buffer, tile, carry):
        out = dot(weight[...], buffer[...])

        def part(along, i):
            return out[C * along : C * (along + 1), LANES * i : LANES * (i + 1)]

        sums[tile] += part(2, 0)
        sums[tile + 1] = carry + part(1, 0) + part(2, 1)
        sums[tile + 2] = part(0, 0) + part(1, 1) + part(2, 2)
        sums[tile + 3] = part(0, 1) + part(1, 2) + part(2, 3)
        sums[tile + 4] = part(0, 2) + part(1, 3)
        return part(0, 3)

    fill(even, 0)
    sums[0] = jnp.zeros((C, LANES), F32)

    def body(index, carry):
        tile = 8 * index
        fill(odd, tile + 4)
        carry = multiply(even, tile, carry)
        fill(even, jnp.minimum(tile + 8, tiles - 4))
        return multiply(odd, tile + 4, carry)

    lax.fori_loop(0, tiles // 8, body, jnp.zeros((C, LANES), F32))


def forward_kernel(
    grid_own, flags, y_left, y_right, grad_r, x_left, x_right, c_left, c_right, fine_w, down_w,
    coarse_w,
    grid, hidden, low_cols, rects, grad_c, live, pack_low, pack_high,
    rows_in, fine_p, coarse_p, hidden_all, lowered, live_all, even, odd,
):
    number = 2 * (x_left.shape[0] - 16) // C
    last = number + 1
    for at, left, right in ((0, x_left, x_right), (None, c_left, c_right)):
        for pair in range((left.shape[0] - 16) // C):
            rows = slice(C * pair, C * (pair + 1))
            lefts, rights = split_rows(left[rows, :]), split_rows(right[rows, :])
            for inner in range(2):
                block = last * inner if at is None else 2 * pair + inner + 1
                rows_in[block * C : (block + 1) * C, 0:256] = lefts[inner]
                rows_in[block * C : (block + 1) * C, 256:512] = rights[inner]
    across = lane_ids(16) % 16
    for start, middle, left, right in (
        (1, flags[...], x_left[number // 2 * C :, :LANES], x_right[number // 2 * C :, :LANES]),
        (0, y_left[2 * C :, :LANES], c_left[C:, :LANES], c_right[C:, :LANES]),
        (last, y_right[2 * C :, :LANES], c_left[C:, :LANES], c_right[C:, :LANES]),
    ):
        rows = jnp.where(across < 4, left.astype(F32), middle.astype(F32))
        rows = jnp.where(across >= 12, right.astype(F32), rows)
        if start == 1:
            live_all[1 : number + 1, :] = rows
        else:
            at = 0 if start == 0 else 1
            live_all[start : start + 1, :] = rows[at : at + 1, :]
    for pair in range(4):
        placed = dot(
            rows_in[...], marks(512, 256, plain, lambda j, at=256 * pair: halo_source(j + at))
        )
        for half in range(2):
            span = slice(LANES * half, LANES * (half + 1))
            for block in range(last + 1):
                tile = EDGE * block + 2 * pair + half
                halo = placed[block * C : (block + 1) * C, span].astype(BF16)
                grid[tile] = grid_own[tile] + halo
    live[...] = join_halves(live_all[0:16, :], live_all[8:24, :])
    tiles = grid.shape[0]
    conv_steps(fine_p, fine_w, lambda tile: across_columns(grid[tile], 1), tiles, 16, 0, even, odd)
    anchors = anchor_mask(0)

    def lower_step(block):
        alive = jnp.broadcast_to(live_all[pl.ds(block, 1), :], (C, LANES))
        keep = alive * anchors
        pairs = []
        for inner in range(4):
            actives = []
            for half in range(2):
                tile = EDGE * block + 2 * inner + half
                value = fine_p[tile + 1] * alive
                hidden_all[tile] = value
                actives.append(silu_parts(value)[0].astype(BF16))
            pairs.append(jnp.concatenate(actives, axis=0))
        parts = dot(down_w[...], jnp.concatenate(pairs, axis=1))
        for inner in range(4):
            total = gather_sub(parts[:, LANES * inner : LANES * (inner + 1)])
            lowered[4 * block + inner] = (total * keep).astype(BF16)

    loop(0, last + 1, lower_step, 3)
    pairs = hidden.shape[0] // EDGE
    shift = last - pairs + 1
    edges = edge_masks(2)
    halves = own_masks()

    def pair_step(block):
        for inner in range(EDGE):
            tile = EDGE * block + inner
            hidden[tile] = join_halves(hidden_all[tile], hidden_all[tile + EDGE * shift])
        for inner in range(4):
            tile = 4 * block + inner
            lower, upper = lowered[tile], lowered[tile + 4 * shift]
            low_cols[tile] = pair_columns(*pair_tiles(lower, upper, halves), edges, 2)

    loop(0, pairs, pair_step, 5)
    conv_steps(coarse_p, coarse_w, lambda tile: low_cols[tile], 4 * pairs, 32, 4, even, odd)
    pair_anchors = anchor_mask(4)

    def grad_step(block):
        alive = jnp.broadcast_to(live[pl.ds(block, 1), :], (C, LANES))
        keep = alive * pair_anchors
        for inner in range(4):
            coarse = 4 * block + inner
            smooth, slope = silu_parts(coarse_p[coarse + 1])
            rects[coarse] = (smooth * pair_anchors).astype(BF16)
            grad_c[coarse] = (grad_r[coarse] * slope * keep).astype(BF16)

    loop(0, pairs, grad_step, 5)
    pack_columns(grad_c, pack_low, pack_high, 2)


def to_blocks(slots, rows_out, flat, out):
    flat[...] = dot(rows_out[...], marks(1024, 1024, pair_source, plain)).astype(BF16)
    number = out.shape[0]
    for slot in range(number):
        place = slots[slot]
        upper = place >= number // 2
        start = pl.multiple_of(jnp.where(upper, place - number // 2, place) * C, 16)
        rows = flat[pl.ds(start, C), :]
        out[slot] = jnp.where(upper, rows[:, 512:], rows[:, :512])


def stacks(own, tiles):
    parts = [jnp.concatenate([own[t + 1], own[t], own[t - 1]], axis=0) for t in tiles]
    return jnp.concatenate(parts, axis=1)


def squeeze_rows(full, keep):
    extra = full[keep:]
    size, part = extra.shape[0], keep // 3
    lanes = lane_ids(size)
    pieces = []
    for index in range(3):
        rows = full[part * index : part * (index + 1)]
        pieces.append(jnp.where(lanes < 96, rows[:size], roll(extra, 96 - 32 * index)))
        if size < part:
            pieces.append(rows[size:])
    return jnp.concatenate(pieces, axis=0)


def widen_rows(packed, number):
    keep = packed.shape[0]
    size, part = number - keep, keep // 3
    lanes = lane_ids(size)
    extra = jnp.zeros((size, LANES), F32)
    for index in range(3):
        moved = roll(packed[part * index : part * index + size], 32 * index - 96)
        extra = jnp.where((lanes >= 32 * index) & (lanes < 32 * index + 32), moved, extra)
    return jnp.concatenate([packed, extra], axis=0)


def flatten_weights(total, out):
    turned = total[...].T
    for group in range(3):
        part = turned[:, LANES * group : LANES * (group + 1)]
        out[3 * C * group : 3 * C * (group + 1), :] = part.astype(BF16)
    return turned[:, 3 * LANES :]


def output_kernel(slots, hidden, rects, live, up_w, out, rows_out, flat):
    pairs = hidden.shape[0] // EDGE

    def block_step(block):
        alive = jnp.broadcast_to(live[pl.ds(block, 1), :], (C, LANES))
        start = pl.multiple_of((block - 1) * C, 16)
        spreads = [spread_sub(rects[4 * block + inner]) for inner in range(4)]
        upward = dot(up_w[...], jnp.concatenate(spreads, axis=1))
        for inner in range(4):
            for half in range(2):
                part = upward[half * C : (half + 1) * C, LANES * inner : LANES * (inner + 1)]
                value = hidden[EDGE * block + 2 * inner + half] + part
                at = LANES * (2 * inner + half)
                rows_out[pl.ds(start, C), at : at + LANES] = (value * alive).astype(BF16)

    loop(1, pairs - 1, block_step, 2)
    to_blocks(slots, rows_out, flat, out)


def side_kernel(rects, cot_grid, low_cols, grad_c, flat, grad_own, up_g, coarse_g):
    tiles = low_cols.shape[0]
    up_g[...] = jnp.zeros_like(up_g)
    coarse_g[...] = jnp.zeros_like(coarse_g)

    def up_step(block):
        spreads = []
        pairs = []
        for inner in range(8):
            coarse = 4 + 8 * block + inner
            spreads.append(spread_sub(rects[coarse]))
            pairs.append(
                jnp.concatenate([cot_grid[2 * coarse], cot_grid[2 * coarse + 1]], axis=0)
            )
        up_g[:, 0 : 2 * C] += dot(
            jnp.concatenate(spreads, axis=1), jnp.concatenate(pairs, axis=1), (1, 1)
        )

    loop(0, (tiles - 8) // 8, up_step, 2)
    zero = jnp.zeros((C, LANES), BF16)
    for coarse in range(1, 4):
        grad_own[coarse] = zero
        grad_own[tiles - 1 - coarse] = zero

    def copy_step(coarse):
        grad_own[coarse] = grad_c[coarse]

    loop(4, tiles - 4, copy_step, 8)
    masks = depth_masks(32, 4)

    def weight_step(index):
        at = [2 + 12 * index + inner for inner in range(12)]
        rights = [depth_columns(low_cols[tile], masks, 32) for tile in at]
        coarse_g[0 : 9 * C, :] += dot(
            jnp.concatenate(rights, axis=1), stacks(grad_own, at), (1, 1)
        )

    loop(0, (tiles - 4) // 12, weight_step)
    rest = flatten_weights(coarse_g, flat)
    flat[9 * C : 12 * C, :] = squeeze_rows(up_g[...], 3 * C).astype(BF16)
    flat[12 * C :, :] = roll(rest, C).astype(BF16)


def backward_kernel(
    grad_c, from_left, from_right, hidden, cot_grid, live, coarse_w, down_w,
    grad_h, grad_d, coarse_p, grad_x, even, odd,
):
    tiles = grad_c.shape[0]
    fill_columns(grad_c, from_left, from_right, grad_x, 2)
    conv_steps(coarse_p, coarse_w, lambda tile: grad_x[tile], tiles, 32, 4, even, odd)
    anchors = anchor_mask(4)

    def step(block):
        alive = jnp.broadcast_to(live[pl.ds(block, 1), :], (C, LANES))
        keep = alive * anchors
        spreads = []
        for inner in range(4):
            coarse = 4 * block + inner
            down = (coarse_p[coarse + 1] * keep).astype(BF16)
            grad_d[coarse] = down
            spreads.append(spread_sub(down))
        acts = dot(down_w[...], jnp.concatenate(spreads, axis=1), (0, 0))
        for inner in range(4):
            for side in range(2):
                tile = EDGE * block + 2 * inner + side
                slope = silu_parts(hidden[tile])[1]
                part = acts[side * C : (side + 1) * C, LANES * inner : LANES * (inner + 1)]
                grad = cot_grid[tile].astype(F32) + part * slope
                grad_h[tile] = (grad * alive).astype(BF16)

    loop(0, tiles // 4, step, 5)


def pack_kernel(grad_h, low, high):
    pack_columns(grad_h, low, high, 1)


def weight_kernel(grid, grad_h, grad_d, hidden, early, joined, grad_own, fine_g, down_g):
    tiles = grad_h.shape[0]
    shift = tiles - 16
    fine_g[...] = jnp.zeros_like(fine_g)
    down_g[...] = jnp.zeros_like(down_g)
    zero = jnp.zeros((C, LANES), BF16)
    for tile in range(3, 8):
        grad_own[tile] = zero
        grad_own[tiles - 1 - tile] = zero

    def copy_step(tile):
        grad_own[tile] = grad_h[tile]

    loop(8, tiles - 8, copy_step, 8)
    masks = depth_masks(16, 4)
    edges = edge_masks(1)
    halves = own_masks()

    def fine_step(index):
        at = [4 + 18 * index + inner for inner in range(18)]
        rights = []
        for tile in at:
            lower, upper = grid[tile], grid[tile + shift]
            base = pair_columns(*pair_tiles(lower, upper, halves), edges, 1)
            rights.append(depth_columns(base, masks, 16))
        fine_g[0 : 9 * C, :] += dot(
            jnp.concatenate(rights, axis=1), stacks(grad_own, at), (1, 1)
        )

    loop(0, (tiles - 8) // 18, fine_step)

    def down_step(index):
        lefts = []
        rights = []
        for inner in range(8):
            coarse = 4 + 8 * index + inner
            lefts.append(spread_sub(grad_d[coarse]))
            actives = [silu_parts(hidden[2 * coarse + side])[0].astype(BF16) for side in range(2)]
            rights.append(jnp.concatenate(actives, axis=0))
        down_g[:, 0 : 2 * C] += dot(
            jnp.concatenate(lefts, axis=1), jnp.concatenate(rights, axis=1), (1, 1)
        )

    loop(0, (tiles // 2 - 8) // 8, down_step, 2)
    rest = flatten_weights(fine_g, joined) + early[12 * C :, :].astype(F32)
    joined[9 * C : 18 * C, :] = early[0 : 9 * C, :]
    joined[18 * C : 21 * C, :] = squeeze_rows(down_g[...], 3 * C).astype(BF16)
    joined[21 * C : 24 * C, :] = early[9 * C : 12 * C, :]
    squeezed = squeeze_rows(rest, 120)
    joined[24 * C :, :] = jnp.concatenate([squeezed, squeezed[:8]], axis=0).astype(BF16)


def input_kernel(
    slots, grad_h, from_left, from_right, live, fine_w, out,
    fine_p, rows_out, flat, grad_x, even, odd,
):
    tiles = grad_h.shape[0]
    fill_columns(grad_h, from_left, from_right, grad_x, 1)
    conv_steps(fine_p, fine_w, lambda tile: grad_x[tile], tiles, 16, 4, even, odd)

    def block_step(block):
        alive = jnp.broadcast_to(live[pl.ds(block, 1), :], (C, LANES))
        start = pl.multiple_of((block - 1) * C, 16)
        for inner in range(EDGE):
            value = fine_p[EDGE * block + inner + 1]
            rows_out[pl.ds(start, C), LANES * inner : LANES * (inner + 1)] = (
                value * alive
            ).astype(BF16)

    loop(1, tiles // EDGE - 1, block_step, 2)
    to_blocks(slots, rows_out, flat, out)


def sum_kernel(parts, copies):
    total = jnp.sum(parts[...].astype(F32), axis=0).astype(BF16)
    copies[...] = jnp.broadcast_to(total[None], copies.shape)


def finish_kernel(scale, total, fine, down, coarse, up):
    rest = widen_rows(total[24 * C :, :].astype(F32)[:120], 3 * C) * scale
    for out, at, moved in ((fine, 0, rest), (coarse, 9 * C, roll(rest, -C))):
        for along in range(3):
            first = at + C * along
            rows = [total[first + 3 * C * g : first + 3 * C * g + C, :] for g in range(3)]
            row = jnp.concatenate(rows, axis=1).astype(F32) * scale
            row = jnp.concatenate([row, moved[C * along : C * (along + 1)]], axis=1)
            for index in range(9):
                out[3 * index + along] = row[:, C * index : C * (index + 1)]
    for out, at, turn in ((down, 18 * C, False), (up, 21 * C, True)):
        full = widen_rows(total[at : at + 3 * C, :].astype(F32), 4 * C) * scale
        for index in range(4):
            rows = full[C * index : C * (index + 1)]
            for along in range(2):
                part = rows[:, C * along : C * (along + 1)]
                if turn:
                    out[2 * index + along] = part.T
                else:
                    out[:, 2 * index + along, :] = part


def call(kernel, inputs, outs, scratch=(), scalars=0, flops=0, limit=None):
    vmem = pl.BlockSpec(memory_space=pltpu.VMEM)
    smem = pl.BlockSpec(memory_space=pltpu.SMEM)
    held = SLACK
    for shape, kind in [(a.shape, a.dtype) for a in inputs[scalars:]] + list(outs) + list(scratch):
        rows, lanes = -(-shape[-2] // 16) * 16, -(-shape[-1] // LANES) * LANES
        held += math.prod(shape[:-2]) * rows * lanes * jnp.dtype(kind).itemsize
    moved = sum(math.prod(s) * jnp.dtype(d).itemsize for s, d in outs)
    moved += sum(math.prod(a.shape) * a.dtype.itemsize for a in inputs)
    return pl.pallas_call(
        kernel,
        out_shape=tuple(jax.ShapeDtypeStruct(s, d) for s, d in outs),
        in_specs=[smem] * scalars + [vmem] * (len(inputs) - scalars),
        out_specs=tuple(vmem for _ in outs),
        scratch_shapes=[pltpu.VMEM(s, d) for s, d in scratch],
        compiler_params=pltpu.CompilerParams(vmem_limit_bytes=limit or held),
        cost_estimate=pl.CostEstimate(flops=flops, bytes_accessed=moved, transcendentals=0),
        name=getattr(kernel, "func", kernel).__name__,
    )(*inputs)


def send(array, step_x, step_y):
    number_x, number_y = lax.axis_size("gx"), lax.axis_size("gy")
    pairs = []
    for i in range(number_x):
        for j in range(number_y):
            to_x, to_y = i + step_x, j + step_y
            if 0 <= to_x < number_x and 0 <= to_y < number_y:
                pairs.append((i * number_y + j, to_x * number_y + to_y))
    return lax.ppermute(array, ("gx", "gy"), pairs)


def reduce_share(joined):
    devices = lax.axis_size("gx") * lax.axis_size("gy")
    rows = joined.shape[0]
    share = -(-rows // devices)
    joined = jnp.pad(joined, ((0, share * devices - rows), (0, 0)))
    mine = lax.all_to_all(joined.reshape(devices, share, LANES), ("gx", "gy"), 0, 0)
    return mine


def spread_share(parts):
    (copies,) = call(sum_kernel, (parts,), [(parts.shape, BF16)])
    full = lax.all_to_all(copies, ("gx", "gy"), 0, 0)
    return full.reshape(-1, LANES)


def on_device(
    features, block_slots, block_count, cotangent, fine_weight, down_weight, coarse_weight,
    up_weight,
):
    number = features.shape[2]
    slots = block_slots.reshape(number)
    count = block_count.reshape(1)
    feats = features.reshape(number, C, VOX)
    cots = cotangent.reshape(number, C, VOX)
    tiles = EDGE * (number + 2)
    coarse_tiles = tiles // 2
    pairs = number // 2 + 2
    groups = pairs // 2
    fine_groups = pairs

    fine_3, coarse_3 = (weight.transpose(1, 0, 2) for weight in (fine_weight, coarse_weight))
    flag_rows, x_low, x_high, y_low, y_high = call(
        prepare_kernel,
        (slots, count, feats, cots),
        [((16, LANES), F32)]
        + [((number // 2 * C + 16, 384), BF16)] * 2
        + [((2 * C + 16, VOX), BF16)] * 2,
        [((number * C, VOX), BF16)],
        scalars=2,
        limit=56 * 1024 * 1024,
    )
    x_left = send(x_high, 1, 0)
    x_right = send(x_low, -1, 0)
    y_left = send(y_high, 0, 1)
    y_right = send(y_low, 0, -1)
    corner_low, corner_high = call(
        corner_kernel,
        (y_left, y_right),
        [((C + 16, 384), BF16), ((C + 16, 384), BF16)],
    )
    c_left = send(corner_high, 1, 0)
    c_right = send(corner_low, -1, 0)
    (grid_own, cot_grid, grad_r, fine_fore, fine_back, coarse_fore, coarse_back, down_w,
     up_w) = call(
        place_kernel,
        (slots, count, feats, cots, y_left, y_right, corner_low, fine_3, down_weight, coarse_3,
         up_weight),
        [
            ((tiles, C, LANES), BF16),
            ((EDGE * pairs, C, LANES), BF16),
            ((4 * pairs, C, LANES), F32),
        ]
        + [((3 * C, 9 * C), BF16)] * 4
        + [((4 * C, 2 * C), BF16), ((2 * C, 4 * C), BF16)],
        [
            (((number + 2) * C, VOX), BF16),
            ((pairs * C, 1024), BF16),
            ((number, C, VOX), BF16),
        ],
        scalars=2,
        flops=8 * 10**9,
    )
    grid, hidden, low_cols, rects, grad_c, live, pack_low, pack_high = call(
        forward_kernel,
        (grid_own, flag_rows, y_left, y_right, grad_r, x_left, x_right, c_left, c_right,
         fine_fore, down_w, coarse_fore),
        [
            ((tiles, C, LANES), BF16),
            ((EDGE * pairs, C, LANES), F32),
            ((4 * pairs, 3 * C, LANES), BF16),
            ((4 * pairs, C, LANES), BF16),
            ((4 * pairs, C, LANES), BF16),
            ((16, LANES), F32),
            ((groups, C, LANES), BF16),
            ((groups, C, LANES), BF16),
        ],
        [
            (((number + 2) * C, VOX), BF16),
            ((tiles + 1, C, LANES), F32),
            ((4 * pairs + 1, C, LANES), F32),
            ((tiles, C, LANES), F32),
            ((coarse_tiles, C, LANES), BF16),
            ((C, LANES), F32),
        ]
        + [((9 * C, 4 * LANES), BF16)] * 2,
        flops=8 * 10**9,
    )
    grad_left = send(pack_high, 1, 0)
    grad_right = send(pack_low, -1, 0)
    (early,) = call(
        side_kernel,
        (rects, cot_grid, low_cols, grad_c),
        [((15 * C, LANES), BF16)],
        [((4 * pairs, C, LANES), BF16), ((4 * C, LANES), F32), ((VOX, 3 * C), F32)],
        flops=8 * 10**9,
    )
    grad_h, grad_d = call(
        backward_kernel,
        (grad_c, grad_left, grad_right, hidden, cot_grid, live, coarse_back, down_w),
        [
            ((EDGE * pairs, C, LANES), BF16),
            ((4 * pairs, C, LANES), BF16),
        ],
        [((4 * pairs + 1, C, LANES), F32), ((4 * pairs, 3 * C, LANES), BF16)]
        + [((9 * C, 4 * LANES), BF16)] * 2,
        flops=8 * 10**9,
    )
    (joined,) = call(
        weight_kernel,
        (grid, grad_h, grad_d, hidden, early),
        [((24 * C + 128, LANES), BF16)],
        [((EDGE * pairs, C, LANES), BF16), ((VOX, 3 * C), F32), ((4 * C, LANES), F32)],
        flops=12 * 10**9,
    )
    joined, slots, grad_h = lax.optimization_barrier((joined, slots, grad_h))
    edge_low, edge_high = call(
        pack_kernel, (grad_h,), [((fine_groups, C, LANES), BF16)] * 2, flops=10**9
    )
    edge_left = send(edge_high, 1, 0)
    edge_right = send(edge_low, -1, 0)
    share = reduce_share(joined)
    (output,) = call(
        output_kernel,
        (slots, hidden, rects, live, up_w),
        [((number, C, VOX), BF16)],
        [((number // 2 * C, 1024), BF16), ((number // 2 * C, 1024), BF16)],
        scalars=1,
        flops=8 * 10**9,
    )
    share, output, slots = lax.optimization_barrier((share, output, slots))
    (input_grad,) = call(
        input_kernel,
        (slots, grad_h, edge_left, edge_right, live, fine_back),
        [((number, C, VOX), BF16)],
        [
            ((EDGE * pairs + 1, C, LANES), F32),
            ((number // 2 * C, 1024), BF16),
            ((number // 2 * C, 1024), BF16),
            ((EDGE * pairs, 3 * C, LANES), BF16),
        ]
        + [((9 * C, 4 * LANES), BF16)] * 2,
        scalars=1,
        flops=8 * 10**9,
    )
    total = spread_share(share)
    scale = 1.0 / math.sqrt(number * VOX * lax.axis_size("gx") * lax.axis_size("gy"))
    fine_total, down_total, coarse_total, up_total = call(
        functools.partial(finish_kernel, scale),
        (total,),
        [((27, C, C), F32), ((C, 8, C), F32), ((27, C, C), F32), ((8, C, C), F32)],
    )
    shape_out = (1, 1, number, C, VOX)
    return (
        output.reshape(shape_out),
        input_grad.reshape(shape_out),
        fine_total.transpose(1, 0, 2),
        down_total,
        coarse_total.transpose(1, 0, 2),
        up_total,
    )


def solution(mesh):
    split = P("gx", "gy", None, None, None)
    return jax.shard_map(
        on_device,
        mesh=mesh,
        in_specs=(split, P("gx", "gy", None), P("gx", "gy"), split, P(), P(), P(), P()),
        out_specs=(split, split, P(), P(), P(), P()),
        check_vma=False,
    )
```

```python
import functools
import math

import jax
import jax.numpy as jnp
from jax import lax
from jax.experimental import pallas as pl
from jax.experimental.pallas import tpu as pltpu
from jax.sharding import PartitionSpec as P

C = 48
EDGE = 8
VOX = 512
LANES = 128
F32 = jnp.float32
BF16 = jnp.bfloat16
SLACK = 8 * 1024 * 1024
SHIFTS = (0, 1, 16, 17)


def marks(rows, columns, row_key, column_key):
    across = column_key(lax.broadcasted_iota(jnp.int32, (1, columns), 1))
    down = row_key(lax.broadcasted_iota(jnp.int32, (rows, 1), 0))
    return jnp.where(down == across, 1.0, 0.0).astype(BF16)


def plain(index):
    return index


def own_source(column):
    lane, y = column % LANES, column // LANES
    x = lane % 16 - 4
    return jnp.where((x >= 0) & (x < 8), 64 * (lane // 16) + 8 * x + y, -1)


def halo_source(column):
    lane, y = column % LANES, column // LANES
    x = lane % 16
    at = 24 * (lane // 16) + y
    left = jnp.where((x >= 1) & (x < 4), at + 8 * (x - 1), -1)
    return jnp.where((x >= 12) & (x < 15), at + 8 * (x - 12) + 256, left)


def pair_source(column):
    lane, y = (column - 4) % LANES, column // LANES
    return 512 * (lane % 16 // 8) + 64 * (lane // 16) + 8 * (lane % 8) + y


def edge_source(column):
    at, side = column % 256, column // 256
    x = at % 24 // 8 + 5 * side
    return jnp.where(at < 192, 64 * (at // 24) + 8 * x + at % 8, -1)


def dot(left, right, contract=(1, 0)):
    dims = (((contract[0],), (contract[1],)), ((), ()))
    return lax.dot_general(left, right, dims, preferred_element_type=F32)


def roll(value, shift):
    return pltpu.roll(value, shift % LANES, 1)


def lane_ids(rows):
    return lax.broadcasted_iota(jnp.int32, (rows, LANES), 1)


def silu_parts(value):
    sigma = 1.0 / (1.0 + jnp.exp(-value))
    return value * sigma, sigma * (1.0 + value * (1.0 - sigma))


def depth_columns(base, masks, step):
    below = roll(base, step) * masks[0]
    above = roll(base, -step) * masks[1]
    return jnp.concatenate([below, base, above], axis=0)


def depth_masks(step, first):
    ids = (lane_ids(3 * C) - first) % LANES
    return (ids >= step).astype(BF16), (ids < LANES - step).astype(BF16)


def across_columns(tile, step):
    return jnp.concatenate([roll(tile, step), tile, roll(tile, -step)], axis=0)


def edge_masks(step):
    ids = lane_ids(C) % 8
    first, last = (ids == 4).astype(BF16), (ids == 4 - step).astype(BF16)
    return first, (ids != 4).astype(BF16), last, (ids != 4 - step).astype(BF16)


def pair_columns(tile, halo, masks, step):
    left = roll(halo, step) * masks[0] + roll(tile, step) * masks[1]
    right = roll(halo, -step) * masks[2] + roll(tile, -step) * masks[3]
    return jnp.concatenate([left, tile, right], axis=0)


def fill_columns(tiles, from_left, from_right, out, step):
    masks = edge_masks(step)

    def body(group):
        packed_left, packed_right = from_left[group], from_right[group]
        for place in range(8):
            tile = tiles[8 * group + place]
            left = roll(packed_left, -place) * masks[0] + roll(tile, step) * masks[1]
            right = roll(packed_right, 8 - step - place) * masks[2]
            right = right + roll(tile, -step) * masks[3]
            out[8 * group + place] = jnp.concatenate([left, tile, right], axis=0)

    loop(0, from_left.shape[0], body)


def pack_columns(tiles, low, high, step):
    masks = edge_masks(step)

    def body(group):
        lows, highs = [], []
        for place in range(8):
            tile = tiles[8 * group + place]
            lows.append(roll(tile * masks[0], place))
            highs.append(roll(tile * masks[2], place - 8 + step))
        for out, parts in ((low, lows), (high, highs)):
            while len(parts) > 1:
                parts = [a + b for a, b in zip(parts[::2], parts[1::2])]
            out[group] = parts[0]

    loop(0, low.shape[0], body)


def own_masks():
    own = own_lanes(C)
    return own.astype(BF16), jnp.logical_not(own).astype(BF16)


def pair_tiles(lower, upper, masks):
    turned = roll(upper, 8)
    return (
        lower * masks[0] + turned * masks[1],
        lower * masks[1] + turned * masks[0],
    )


def own_lanes(rows):
    across = lane_ids(rows) % 16
    return (across >= 4) & (across < 12)


def join_halves(lower, upper):
    return jnp.where(own_lanes(lower.shape[0]), lower, roll(upper, 8))


def gather_sub(parts):
    even = lane_ids(C) % 2 == 0
    above = jnp.where(even, parts[2 * C : 3 * C], parts[3 * C :])
    total = jnp.where(even, parts[:C], parts[C : 2 * C]) + roll(above, -16)
    return total + roll(total, -1)


def spread_sub(anchored):
    return jnp.concatenate([anchored] + [roll(anchored, step) for step in SHIFTS[1:]], axis=0)


def anchor_mask(first):
    ids = (lane_ids(C) - first) % LANES
    return (((ids // 16) % 2 == 0) & (ids % 2 == 0)).astype(F32)


def loop(low, high, body, unroll=1):
    def step(index, carry):
        body(index)
        return carry

    lax.fori_loop(low, high, step, 0, unroll=unroll)


def join_rows(first, second):
    low = lane_ids(C) < 64
    lead = roll(second[:, :LANES], 64)
    parts = [
        first[:, :LANES],
        jnp.where(low, first[:, LANES:], lead),
        jnp.where(low, lead, roll(second[:, LANES:], 64)),
    ]
    return jnp.concatenate(parts, axis=1)


def split_rows(joined):
    low = lane_ids(C) < 64
    middle = roll(joined[:, LANES : 2 * LANES], 64)
    last = roll(joined[:, 2 * LANES :], 64)
    second = jnp.concatenate([jnp.where(low, middle, last), last], axis=1)
    return joined[:, : 2 * LANES], second


def prepare_kernel(slots, count, feats, cots, flag_rows, x_low, x_high, y_low, y_high, rows_in):
    number = feats.shape[0]
    rows = lax.broadcasted_iota(jnp.int32, (16, LANES), 0)
    flags = jnp.zeros((16, LANES), F32)
    zero = jnp.zeros((C, VOX), BF16)
    first = jnp.zeros((), jnp.int32)
    last = jnp.zeros((), jnp.int32)
    for slot in range(number):
        live = slot < count[0]
        place = slots[slot]
        block = jnp.where(live, feats[slot], zero)
        rows_in[pl.ds(pl.multiple_of(place * C, 16), C), :] = block
        flags = jnp.where(rows == place, jnp.where(live, 1.0, 0.0), flags)
        first = jnp.where(place == 0, slot, first)
        last = jnp.where(place == number - 1, slot, last)
    flag_rows[...] = flags
    packed = dot(rows_in[...], marks(VOX, 512, plain, edge_source)).astype(BF16)
    spare = jnp.zeros((16, 2 * LANES), BF16)
    for out, at in ((x_low, 0), (x_high, 256)):
        for pair in range(number // 2):
            edges = [packed[C * i : C * (i + 1), at : at + 256] for i in (2 * pair, 2 * pair + 1)]
            out[C * pair : C * (pair + 1), :] = join_rows(*edges)
        out[C * number // 2 :, :LANES] = flags.astype(BF16)
        out[C * number // 2 :, LANES:] = spare
    for out, index, slot in ((y_low, 0, first), (y_high, number - 1, last)):
        live = slot < count[0]
        out[0:C, :] = rows_in[C * index : C * (index + 1), :]
        out[C : 2 * C, :] = jnp.where(live, cots[slot], zero)
        out[2 * C :, :] = (jnp.zeros((16, VOX), F32) + jnp.where(live, 1.0, 0.0)).astype(BF16)


def corner_kernel(y_left, y_right, low, high):
    rows = jnp.concatenate([y_left[0:C, :], y_right[0:C, :]], axis=0)
    packed = dot(rows, marks(VOX, 512, plain, edge_source)).astype(BF16)
    ids = lax.broadcasted_iota(jnp.int32, (16, LANES), 0)
    flags = jnp.where(ids == 0, y_left[2 * C :, :LANES], y_right[2 * C :, :LANES])
    spare = jnp.zeros((16, 2 * LANES), BF16)
    for out, at in ((low, 0), (high, 256)):
        out[0:C, :] = join_rows(packed[:C, at : at + 256], packed[C:, at : at + 256])
        out[C:, :LANES] = flags
        out[C:, LANES:] = spare


def arrange_weights(fine, down, coarse, up, fine_w, fine_b, coarse_w, coarse_b, down_w, up_w):
    for source, fore, back in ((fine, fine_w, fine_b), (coarse, coarse_w, coarse_b)):
        for along in range(3):
            rows = slice(C * along, C * (along + 1))
            turned_rows = slice(C * (2 - along), C * (3 - along))
            ahead = []
            behind = []
            for depth in range(3):
                for across in range(3):
                    ahead.append(source[9 * depth + 3 * across + along])
                    behind.append(source[9 * (2 - depth) + 3 * (2 - across) + along].T)
            fore[rows, :] = jnp.concatenate(ahead, axis=1)
            back[turned_rows, :] = jnp.concatenate(behind, axis=1)
    for index in range(4):
        pair = [down[:, 2 * index, :], down[:, 2 * index + 1, :]]
        down_w[C * index : C * (index + 1), :] = jnp.concatenate(pair, axis=1)
    for along in range(2):
        row = jnp.concatenate([up[2 * index + along] for index in range(4)], axis=1)
        up_w[C * along : C * (along + 1), :] = row


def place_kernel(
    slots, count, feats, cots, y_left, y_right, c_low, fine, down, coarse, up,
    grid, cot_grid, grad_r, fine_w, fine_b, coarse_w, coarse_b, down_w, up_w,
    rows_in, rows_cot, cot,
):
    arrange_weights(fine, down, coarse, up, fine_w, fine_b, coarse_w, coarse_b, down_w, up_w)
    number = feats.shape[0]
    last = number + 1
    zero = jnp.zeros((C, VOX), BF16)
    rows_in[0:C, :] = y_left[0:C, :]
    rows_in[last * C : (last + 1) * C, :] = y_right[0:C, :]
    for slot in range(number):
        live = slot < count[0]
        place = slots[slot]
        start = pl.multiple_of((place + 1) * C, 16)
        rows_in[pl.ds(start, C), :] = jnp.where(live, feats[slot], zero)
        cot[place] = jnp.where(live, cots[slot], zero)
    pairs = number // 2 + 2
    for group in range(pairs):
        at = group * C
        lower = y_left[C : 2 * C, :] if group == 0 else cot[group - 1]
        upper = y_right[C : 2 * C, :] if group == pairs - 1 else cot[group + number // 2 - 1]
        rows_cot[at : at + C, 0:512] = lower
        rows_cot[at : at + C, 512:1024] = upper
    for pair in range(4):
        placed_cot = dot(
            rows_cot[...], marks(1024, 256, plain, lambda j, at=256 * pair: pair_source(j + at))
        )
        placed = dot(
            rows_in[...], marks(VOX, 256, plain, lambda j, at=256 * pair: own_source(j + at))
        )
        for half in range(2):
            span = slice(LANES * half, LANES * (half + 1))
            for block in range(last + 1):
                tile = EDGE * block + 2 * pair + half
                grid[tile] = placed[block * C : (block + 1) * C, span].astype(BF16)
            for block in range(pairs):
                tile = EDGE * block + 2 * pair + half
                cot_grid[tile] = placed_cot[block * C : (block + 1) * C, span].astype(BF16)

    def rect_step(block):
        tiles = []
        for inner in range(4):
            tile = EDGE * block + 2 * inner
            tiles.append(jnp.concatenate([cot_grid[tile], cot_grid[tile + 1]], axis=0))
        parts = dot(up_w[...], jnp.concatenate(tiles, axis=1), (0, 0))
        for inner in range(4):
            grad_r[4 * block + inner] = gather_sub(parts[:, LANES * inner : LANES * (inner + 1)])

    loop(0, pairs, rect_step, 5)


def conv_steps(sums, weight, load, tiles, step, first, even, odd):
    masks = depth_masks(step, first)

    def fill(buffer, tile):
        for i in range(4):
            cols = depth_columns(load(tile + i), masks, step)
            buffer[:, LANES * i : LANES * (i + 1)] = cols

    def multiply(buffer, tile, carry):
        out = dot(weight[...], buffer[...])

        def part(along, i):
            return out[C * along : C * (along + 1), LANES * i : LANES * (i + 1)]

        sums[tile] += part(2, 0)
        sums[tile + 1] = carry + part(1, 0) + part(2, 1)
        sums[tile + 2] = part(0, 0) + part(1, 1) + part(2, 2)
        sums[tile + 3] = part(0, 1) + part(1, 2) + part(2, 3)
        sums[tile + 4] = part(0, 2) + part(1, 3)
        return part(0, 3)

    fill(even, 0)
    sums[0] = jnp.zeros((C, LANES), F32)

    def body(index, carry):
        tile = 8 * index
        fill(odd, tile + 4)
        carry = multiply(even, tile, carry)
        fill(even, jnp.minimum(tile + 8, tiles - 4))
        return multiply(odd, tile + 4, carry)

    unroll = 3 if tiles % 24 == 0 else 5
    lax.fori_loop(0, tiles // 8, body, jnp.zeros((C, LANES), F32), unroll=unroll)


def forward_kernel(
    grid_own, flags, y_left, y_right, grad_r, x_left, x_right, c_left, c_right, fine_w, down_w,
    coarse_w,
    grid, hidden, low_cols, rects, grad_c, live, pack_low, pack_high,
    rows_in, fine_p, coarse_p, hidden_all, lowered, live_all, even, odd,
):
    number = 2 * (x_left.shape[0] - 16) // C
    last = number + 1
    for at, left, right in ((0, x_left, x_right), (None, c_left, c_right)):
        for pair in range((left.shape[0] - 16) // C):
            rows = slice(C * pair, C * (pair + 1))
            lefts, rights = split_rows(left[rows, :]), split_rows(right[rows, :])
            for inner in range(2):
                block = last * inner if at is None else 2 * pair + inner + 1
                rows_in[block * C : (block + 1) * C, 0:256] = lefts[inner]
                rows_in[block * C : (block + 1) * C, 256:512] = rights[inner]
    across = lane_ids(16) % 16
    for start, middle, left, right in (
        (1, flags[...], x_left[number // 2 * C :, :LANES], x_right[number // 2 * C :, :LANES]),
        (0, y_left[2 * C :, :LANES], c_left[C:, :LANES], c_right[C:, :LANES]),
        (last, y_right[2 * C :, :LANES], c_left[C:, :LANES], c_right[C:, :LANES]),
    ):
        rows = jnp.where(across < 4, left.astype(F32), middle.astype(F32))
        rows = jnp.where(across >= 12, right.astype(F32), rows)
        if start == 1:
            live_all[1 : number + 1, :] = rows
        else:
            at = 0 if start == 0 else 1
            live_all[start : start + 1, :] = rows[at : at + 1, :]
    for pair in range(4):
        placed = dot(
            rows_in[...], marks(512, 256, plain, lambda j, at=256 * pair: halo_source(j + at))
        )
        for half in range(2):
            span = slice(LANES * half, LANES * (half + 1))
            for block in range(last + 1):
                tile = EDGE * block + 2 * pair + half
                halo = placed[block * C : (block + 1) * C, span].astype(BF16)
                grid[tile] = grid_own[tile] + halo
    live[...] = join_halves(live_all[0:16, :], live_all[8:24, :])
    tiles = grid.shape[0]
    conv_steps(fine_p, fine_w, lambda tile: across_columns(grid[tile], 1), tiles, 16, 0, even, odd)
    anchors = anchor_mask(0)

    def lower_step(block):
        alive = jnp.broadcast_to(live_all[pl.ds(block, 1), :], (C, LANES))
        keep = alive * anchors
        pairs = []
        for inner in range(4):
            actives = []
            for half in range(2):
                tile = EDGE * block + 2 * inner + half
                value = fine_p[tile + 1] * alive
                hidden_all[tile] = value
                actives.append(silu_parts(value)[0].astype(BF16))
            pairs.append(jnp.concatenate(actives, axis=0))
        parts = dot(down_w[...], jnp.concatenate(pairs, axis=1))
        for inner in range(4):
            total = gather_sub(parts[:, LANES * inner : LANES * (inner + 1)])
            lowered[4 * block + inner] = (total * keep).astype(BF16)

    loop(0, last + 1, lower_step, 3)
    pairs = hidden.shape[0] // EDGE
    shift = last - pairs + 1
    edges = edge_masks(2)
    halves = own_masks()

    def pair_step(block):
        for inner in range(EDGE):
            tile = EDGE * block + inner
            hidden[tile] = join_halves(hidden_all[tile], hidden_all[tile + EDGE * shift])
        for inner in range(4):
            tile = 4 * block + inner
            lower, upper = lowered[tile], lowered[tile + 4 * shift]
            low_cols[tile] = pair_columns(*pair_tiles(lower, upper, halves), edges, 2)

    loop(0, pairs, pair_step, 5)
    conv_steps(coarse_p, coarse_w, lambda tile: low_cols[tile], 4 * pairs, 32, 4, even, odd)
    pair_anchors = anchor_mask(4)

    def grad_step(block):
        alive = jnp.broadcast_to(live[pl.ds(block, 1), :], (C, LANES))
        keep = alive * pair_anchors
        for inner in range(4):
            coarse = 4 * block + inner
            smooth, slope = silu_parts(coarse_p[coarse + 1])
            rects[coarse] = (smooth * pair_anchors).astype(BF16)
            grad_c[coarse] = (grad_r[coarse] * slope * keep).astype(BF16)

    loop(0, pairs, grad_step, 5)
    pack_columns(grad_c, pack_low, pack_high, 2)


def to_blocks(slots, rows_out, flat, out):
    flat[...] = dot(rows_out[...], marks(1024, 1024, pair_source, plain)).astype(BF16)
    number = out.shape[0]
    for slot in range(number):
        place = slots[slot]
        upper = place >= number // 2
        start = pl.multiple_of(jnp.where(upper, place - number // 2, place) * C, 16)
        rows = flat[pl.ds(start, C), :]
        out[slot] = jnp.where(upper, rows[:, 512:], rows[:, :512])


def stacks(own, tiles):
    parts = [jnp.concatenate([own[t + 1], own[t], own[t - 1]], axis=0) for t in tiles]
    return jnp.concatenate(parts, axis=1)


def squeeze_rows(full, keep):
    extra = full[keep:]
    size, part = extra.shape[0], keep // 3
    lanes = lane_ids(size)
    pieces = []
    for index in range(3):
        rows = full[part * index : part * (index + 1)]
        pieces.append(jnp.where(lanes < 96, rows[:size], roll(extra, 96 - 32 * index)))
        if size < part:
            pieces.append(rows[size:])
    return jnp.concatenate(pieces, axis=0)


def widen_rows(packed, number):
    keep = packed.shape[0]
    size, part = number - keep, keep // 3
    lanes = lane_ids(size)
    extra = jnp.zeros((size, LANES), F32)
    for index in range(3):
        moved = roll(packed[part * index : part * index + size], 32 * index - 96)
        extra = jnp.where((lanes >= 32 * index) & (lanes < 32 * index + 32), moved, extra)
    return jnp.concatenate([packed, extra], axis=0)


def flatten_weights(total, out):
    turned = total[...].T
    for group in range(3):
        part = turned[:, LANES * group : LANES * (group + 1)]
        out[3 * C * group : 3 * C * (group + 1), :] = part.astype(BF16)
    return turned[:, 3 * LANES :]


def output_kernel(slots, hidden, rects, live, up_w, out, rows_out, flat):
    pairs = hidden.shape[0] // EDGE

    def block_step(block):
        alive = jnp.broadcast_to(live[pl.ds(block, 1), :], (C, LANES))
        start = pl.multiple_of((block - 1) * C, 16)
        spreads = [spread_sub(rects[4 * block + inner]) for inner in range(4)]
        upward = dot(up_w[...], jnp.concatenate(spreads, axis=1))
        for inner in range(4):
            for half in range(2):
                part = upward[half * C : (half + 1) * C, LANES * inner : LANES * (inner + 1)]
                value = hidden[EDGE * block + 2 * inner + half] + part
                at = LANES * (2 * inner + half)
                rows_out[pl.ds(start, C), at : at + LANES] = (value * alive).astype(BF16)

    loop(1, pairs - 1, block_step, 4)
    to_blocks(slots, rows_out, flat, out)


def side_kernel(rects, cot_grid, low_cols, grad_c, flat, grad_own, up_g, coarse_g):
    tiles = low_cols.shape[0]
    up_g[...] = jnp.zeros_like(up_g)
    coarse_g[...] = jnp.zeros_like(coarse_g)

    def up_step(block):
        spreads = []
        pairs = []
        for inner in range(8):
            coarse = 4 + 8 * block + inner
            spreads.append(spread_sub(rects[coarse]))
            pairs.append(
                jnp.concatenate([cot_grid[2 * coarse], cot_grid[2 * coarse + 1]], axis=0)
            )
        up_g[:, 0 : 2 * C] += dot(
            jnp.concatenate(spreads, axis=1), jnp.concatenate(pairs, axis=1), (1, 1)
        )

    loop(0, (tiles - 8) // 8, up_step, 2)
    zero = jnp.zeros((C, LANES), BF16)
    for coarse in range(1, 4):
        grad_own[coarse] = zero
        grad_own[tiles - 1 - coarse] = zero

    def copy_step(coarse):
        grad_own[coarse] = grad_c[coarse]

    loop(4, tiles - 4, copy_step, 8)
    masks = depth_masks(32, 4)

    def weight_step(index):
        at = [2 + 18 * index + inner for inner in range(18)]
        rights = [depth_columns(low_cols[tile], masks, 32) for tile in at]
        coarse_g[0 : 9 * C, :] += dot(
            jnp.concatenate(rights, axis=1), stacks(grad_own, at), (1, 1)
        )

    loop(0, (tiles - 4) // 18, weight_step)
    rest = flatten_weights(coarse_g, flat)
    flat[9 * C : 12 * C, :] = squeeze_rows(up_g[...], 3 * C).astype(BF16)
    flat[12 * C :, :] = roll(rest, C).astype(BF16)


def backward_kernel(
    grad_c, from_left, from_right, hidden, cot_grid, live, coarse_w, down_w,
    grad_h, grad_d, coarse_p, grad_x, even, odd,
):
    tiles = grad_c.shape[0]
    fill_columns(grad_c, from_left, from_right, grad_x, 2)
    conv_steps(coarse_p, coarse_w, lambda tile: grad_x[tile], tiles, 32, 4, even, odd)
    anchors = anchor_mask(4)

    def step(block):
        alive = jnp.broadcast_to(live[pl.ds(block, 1), :], (C, LANES))
        keep = alive * anchors
        spreads = []
        for inner in range(4):
            coarse = 4 * block + inner
            down = (coarse_p[coarse + 1] * keep).astype(BF16)
            grad_d[coarse] = down
            spreads.append(spread_sub(down))
        acts = dot(down_w[...], jnp.concatenate(spreads, axis=1), (0, 0))
        for inner in range(4):
            for side in range(2):
                tile = EDGE * block + 2 * inner + side
                slope = silu_parts(hidden[tile])[1]
                part = acts[side * C : (side + 1) * C, LANES * inner : LANES * (inner + 1)]
                grad = cot_grid[tile].astype(F32) + part * slope
                grad_h[tile] = (grad * alive).astype(BF16)

    loop(0, tiles // 4, step, 5)


def pack_kernel(grad_h, low, high):
    pack_columns(grad_h, low, high, 1)


def weight_kernel(grid, grad_h, grad_d, hidden, early, joined, grad_own, fine_g, down_g):
    tiles = grad_h.shape[0]
    shift = tiles - 16
    fine_g[...] = jnp.zeros_like(fine_g)
    down_g[...] = jnp.zeros_like(down_g)
    zero = jnp.zeros((C, LANES), BF16)
    for tile in range(3, 8):
        grad_own[tile] = zero
        grad_own[tiles - 1 - tile] = zero

    def copy_step(tile):
        grad_own[tile] = grad_h[tile]

    loop(8, tiles - 8, copy_step, 8)
    masks = depth_masks(16, 4)
    edges = edge_masks(1)
    halves = own_masks()

    def fine_step(index):
        at = [4 + 36 * index + inner for inner in range(36)]
        rights = []
        for tile in at:
            lower, upper = grid[tile], grid[tile + shift]
            base = pair_columns(*pair_tiles(lower, upper, halves), edges, 1)
            rights.append(depth_columns(base, masks, 16))
        fine_g[0 : 9 * C, :] += dot(
            jnp.concatenate(rights, axis=1), stacks(grad_own, at), (1, 1)
        )

    loop(0, (tiles - 8) // 36, fine_step)

    def down_step(index):
        lefts = []
        rights = []
        for inner in range(8):
            coarse = 4 + 8 * index + inner
            lefts.append(spread_sub(grad_d[coarse]))
            actives = [silu_parts(hidden[2 * coarse + side])[0].astype(BF16) for side in range(2)]
            rights.append(jnp.concatenate(actives, axis=0))
        down_g[:, 0 : 2 * C] += dot(
            jnp.concatenate(lefts, axis=1), jnp.concatenate(rights, axis=1), (1, 1)
        )

    loop(0, (tiles // 2 - 8) // 8, down_step, 2)
    rest = flatten_weights(fine_g, joined) + early[12 * C :, :].astype(F32)
    joined[9 * C : 18 * C, :] = early[0 : 9 * C, :]
    joined[18 * C : 21 * C, :] = squeeze_rows(down_g[...], 3 * C).astype(BF16)
    joined[21 * C : 24 * C, :] = early[9 * C : 12 * C, :]
    squeezed = squeeze_rows(rest, 120)
    joined[24 * C :, :] = jnp.concatenate([squeezed, squeezed[:8]], axis=0).astype(BF16)


def input_kernel(
    slots, grad_h, from_left, from_right, live, fine_w, out,
    fine_p, rows_out, flat, grad_x, even, odd,
):
    tiles = grad_h.shape[0]
    fill_columns(grad_h, from_left, from_right, grad_x, 1)
    conv_steps(fine_p, fine_w, lambda tile: grad_x[tile], tiles, 16, 4, even, odd)

    def block_step(block):
        alive = jnp.broadcast_to(live[pl.ds(block, 1), :], (C, LANES))
        start = pl.multiple_of((block - 1) * C, 16)
        for inner in range(EDGE):
            value = fine_p[EDGE * block + inner + 1]
            rows_out[pl.ds(start, C), LANES * inner : LANES * (inner + 1)] = (
                value * alive
            ).astype(BF16)

    loop(1, tiles // EDGE - 1, block_step, 4)
    to_blocks(slots, rows_out, flat, out)


def sum_kernel(parts, copies):
    total = jnp.sum(parts[...].astype(F32), axis=0).astype(BF16)
    copies[...] = jnp.broadcast_to(total[None], copies.shape)


def finish_kernel(scale, total, fine, down, coarse, up):
    rest = widen_rows(total[24 * C :, :].astype(F32)[:120], 3 * C) * scale
    for out, at, moved in ((fine, 0, rest), (coarse, 9 * C, roll(rest, -C))):
        for along in range(3):
            first = at + C * along
            rows = [total[first + 3 * C * g : first + 3 * C * g + C, :] for g in range(3)]
            row = jnp.concatenate(rows, axis=1).astype(F32) * scale
            row = jnp.concatenate([row, moved[C * along : C * (along + 1)]], axis=1)
            for index in range(9):
                out[3 * index + along] = row[:, C * index : C * (index + 1)]
    for out, at, turn in ((down, 18 * C, False), (up, 21 * C, True)):
        full = widen_rows(total[at : at + 3 * C, :].astype(F32), 4 * C) * scale
        for index in range(4):
            rows = full[C * index : C * (index + 1)]
            for along in range(2):
                part = rows[:, C * along : C * (along + 1)]
                if turn:
                    out[2 * index + along] = part.T
                else:
                    out[:, 2 * index + along, :] = part


def call(kernel, inputs, outs, scratch=(), scalars=0, flops=0, limit=None):
    vmem = pl.BlockSpec(memory_space=pltpu.VMEM)
    smem = pl.BlockSpec(memory_space=pltpu.SMEM)
    held = SLACK
    for shape, kind in [(a.shape, a.dtype) for a in inputs[scalars:]] + list(outs) + list(scratch):
        rows, lanes = -(-shape[-2] // 16) * 16, -(-shape[-1] // LANES) * LANES
        held += math.prod(shape[:-2]) * rows * lanes * jnp.dtype(kind).itemsize
    moved = sum(math.prod(s) * jnp.dtype(d).itemsize for s, d in outs)
    moved += sum(math.prod(a.shape) * a.dtype.itemsize for a in inputs)
    return pl.pallas_call(
        kernel,
        out_shape=tuple(jax.ShapeDtypeStruct(s, d) for s, d in outs),
        in_specs=[smem] * scalars + [vmem] * (len(inputs) - scalars),
        out_specs=tuple(vmem for _ in outs),
        scratch_shapes=[pltpu.VMEM(s, d) for s, d in scratch],
        compiler_params=pltpu.CompilerParams(vmem_limit_bytes=limit or held),
        cost_estimate=pl.CostEstimate(flops=flops, bytes_accessed=moved, transcendentals=0),
        name=getattr(kernel, "func", kernel).__name__,
    )(*inputs)


def send(array, step_x, step_y):
    number_x, number_y = lax.axis_size("gx"), lax.axis_size("gy")
    pairs = []
    for i in range(number_x):
        for j in range(number_y):
            to_x, to_y = i + step_x, j + step_y
            if 0 <= to_x < number_x and 0 <= to_y < number_y:
                pairs.append((i * number_y + j, to_x * number_y + to_y))
    return lax.ppermute(array, ("gx", "gy"), pairs)


def reduce_share(joined):
    devices = lax.axis_size("gx") * lax.axis_size("gy")
    rows = joined.shape[0]
    share = -(-rows // devices)
    joined = jnp.pad(joined, ((0, share * devices - rows), (0, 0)))
    mine = lax.all_to_all(joined.reshape(devices, share, LANES), ("gx", "gy"), 0, 0)
    return mine


def spread_share(parts):
    (copies,) = call(sum_kernel, (parts,), [(parts.shape, BF16)])
    full = lax.all_to_all(copies, ("gx", "gy"), 0, 0)
    return full.reshape(-1, LANES)


def on_device(
    features, block_slots, block_count, cotangent, fine_weight, down_weight, coarse_weight,
    up_weight,
):
    number = features.shape[2]
    slots = block_slots.reshape(number)
    count = block_count.reshape(1)
    feats = features.reshape(number, C, VOX)
    cots = cotangent.reshape(number, C, VOX)
    tiles = EDGE * (number + 2)
    coarse_tiles = tiles // 2
    pairs = number // 2 + 2
    groups = pairs // 2
    fine_groups = pairs

    fine_3, coarse_3 = (weight.transpose(1, 0, 2) for weight in (fine_weight, coarse_weight))
    flag_rows, x_low, x_high, y_low, y_high = call(
        prepare_kernel,
        (slots, count, feats, cots),
        [((16, LANES), F32)]
        + [((number // 2 * C + 16, 384), BF16)] * 2
        + [((2 * C + 16, VOX), BF16)] * 2,
        [((number * C, VOX), BF16)],
        scalars=2,
        limit=56 * 1024 * 1024,
    )
    x_left = send(x_high, 1, 0)
    x_right = send(x_low, -1, 0)
    y_left = send(y_high, 0, 1)
    y_right = send(y_low, 0, -1)
    corner_low, corner_high = call(
        corner_kernel,
        (y_left, y_right),
        [((C + 16, 384), BF16), ((C + 16, 384), BF16)],
    )
    c_left = send(corner_high, 1, 0)
    c_right = send(corner_low, -1, 0)
    (grid_own, cot_grid, grad_r, fine_fore, fine_back, coarse_fore, coarse_back, down_w,
     up_w) = call(
        place_kernel,
        (slots, count, feats, cots, y_left, y_right, corner_low, fine_3, down_weight, coarse_3,
         up_weight),
        [
            ((tiles, C, LANES), BF16),
            ((EDGE * pairs, C, LANES), BF16),
            ((4 * pairs, C, LANES), F32),
        ]
        + [((3 * C, 9 * C), BF16)] * 4
        + [((4 * C, 2 * C), BF16), ((2 * C, 4 * C), BF16)],
        [
            (((number + 2) * C, VOX), BF16),
            ((pairs * C, 1024), BF16),
            ((number, C, VOX), BF16),
        ],
        scalars=2,
        flops=8 * 10**9,
    )
    grid, hidden, low_cols, rects, grad_c, live, pack_low, pack_high = call(
        forward_kernel,
        (grid_own, flag_rows, y_left, y_right, grad_r, x_left, x_right, c_left, c_right,
         fine_fore, down_w, coarse_fore),
        [
            ((tiles, C, LANES), BF16),
            ((EDGE * pairs, C, LANES), F32),
            ((4 * pairs, 3 * C, LANES), BF16),
            ((4 * pairs, C, LANES), BF16),
            ((4 * pairs, C, LANES), BF16),
            ((16, LANES), F32),
            ((groups, C, LANES), BF16),
            ((groups, C, LANES), BF16),
        ],
        [
            (((number + 2) * C, VOX), BF16),
            ((tiles + 1, C, LANES), F32),
            ((4 * pairs + 1, C, LANES), F32),
            ((tiles, C, LANES), F32),
            ((coarse_tiles, C, LANES), BF16),
            ((C, LANES), F32),
        ]
        + [((9 * C, 4 * LANES), BF16)] * 2,
        flops=8 * 10**9,
    )
    grad_left = send(pack_high, 1, 0)
    grad_right = send(pack_low, -1, 0)
    (early,) = call(
        side_kernel,
        (rects, cot_grid, low_cols, grad_c),
        [((15 * C, LANES), BF16)],
        [((4 * pairs, C, LANES), BF16), ((4 * C, LANES), F32), ((VOX, 3 * C), F32)],
        flops=8 * 10**9,
    )
    grad_h, grad_d = call(
        backward_kernel,
        (grad_c, grad_left, grad_right, hidden, cot_grid, live, coarse_back, down_w),
        [
            ((EDGE * pairs, C, LANES), BF16),
            ((4 * pairs, C, LANES), BF16),
        ],
        [((4 * pairs + 1, C, LANES), F32), ((4 * pairs, 3 * C, LANES), BF16)]
        + [((9 * C, 4 * LANES), BF16)] * 2,
        flops=8 * 10**9,
    )
    (joined,) = call(
        weight_kernel,
        (grid, grad_h, grad_d, hidden, early),
        [((24 * C + 128, LANES), BF16)],
        [((EDGE * pairs, C, LANES), BF16), ((VOX, 3 * C), F32), ((4 * C, LANES), F32)],
        flops=12 * 10**9,
    )
    joined, slots, grad_h = lax.optimization_barrier((joined, slots, grad_h))
    edge_low, edge_high = call(
        pack_kernel, (grad_h,), [((fine_groups, C, LANES), BF16)] * 2, flops=10**9
    )
    edge_left = send(edge_high, 1, 0)
    edge_right = send(edge_low, -1, 0)
    share = reduce_share(joined)
    (output,) = call(
        output_kernel,
        (slots, hidden, rects, live, up_w),
        [((number, C, VOX), BF16)],
        [((number // 2 * C, 1024), BF16), ((number // 2 * C, 1024), BF16)],
        scalars=1,
        flops=8 * 10**9,
    )
    share, output, slots = lax.optimization_barrier((share, output, slots))
    (input_grad,) = call(
        input_kernel,
        (slots, grad_h, edge_left, edge_right, live, fine_back),
        [((number, C, VOX), BF16)],
        [
            ((EDGE * pairs + 1, C, LANES), F32),
            ((number // 2 * C, 1024), BF16),
            ((number // 2 * C, 1024), BF16),
            ((EDGE * pairs, 3 * C, LANES), BF16),
        ]
        + [((9 * C, 4 * LANES), BF16)] * 2,
        scalars=1,
        flops=8 * 10**9,
    )
    total = spread_share(share)
    scale = 1.0 / math.sqrt(number * VOX * lax.axis_size("gx") * lax.axis_size("gy"))
    fine_total, down_total, coarse_total, up_total = call(
        functools.partial(finish_kernel, scale),
        (total,),
        [((27, C, C), F32), ((C, 8, C), F32), ((27, C, C), F32), ((8, C, C), F32)],
    )
    shape_out = (1, 1, number, C, VOX)
    return (
        output.reshape(shape_out),
        input_grad.reshape(shape_out),
        fine_total.transpose(1, 0, 2),
        down_total,
        coarse_total.transpose(1, 0, 2),
        up_total,
    )


def solution(mesh):
    split = P("gx", "gy", None, None, None)
    return jax.shard_map(
        on_device,
        mesh=mesh,
        in_specs=(split, P("gx", "gy", None), P("gx", "gy"), split, P(), P(), P(), P()),
        out_specs=(split, split, P(), P(), P(), P()),
        check_vma=False,
    )
```

```python
import functools
import math

import jax
import jax.numpy as jnp
from jax import lax
from jax.experimental import pallas as pl
from jax.experimental.pallas import tpu as pltpu
from jax.sharding import PartitionSpec as P

C = 48
EDGE = 8
VOX = 512
LANES = 128
F32 = jnp.float32
BF16 = jnp.bfloat16
SLACK = 8 * 1024 * 1024
SHIFTS = (0, 1, 16, 17)


def marks(rows, columns, row_key, column_key):
    across = column_key(lax.broadcasted_iota(jnp.int32, (1, columns), 1))
    down = row_key(lax.broadcasted_iota(jnp.int32, (rows, 1), 0))
    return jnp.where(down == across, 1.0, 0.0).astype(BF16)


def plain(index):
    return index


def own_source(column):
    lane, y = column % LANES, column // LANES
    x = lane % 16 - 4
    return jnp.where((x >= 0) & (x < 8), 64 * (lane // 16) + 8 * x + y, -1)


def halo_source(column):
    lane, y = column % LANES, column // LANES
    x = lane % 16
    at = 24 * (lane // 16) + y
    left = jnp.where((x >= 1) & (x < 4), at + 8 * (x - 1), -1)
    return jnp.where((x >= 12) & (x < 15), at + 8 * (x - 12) + 256, left)


def pair_source(column):
    lane, y = (column - 4) % LANES, column // LANES
    return 512 * (lane % 16 // 8) + 64 * (lane // 16) + 8 * (lane % 8) + y


def edge_source(column):
    at, side = column % 256, column // 256
    x = at % 24 // 8 + 5 * side
    return jnp.where(at < 192, 64 * (at // 24) + 8 * x + at % 8, -1)


def dot(left, right, contract=(1, 0)):
    dims = (((contract[0],), (contract[1],)), ((), ()))
    return lax.dot_general(left, right, dims, preferred_element_type=F32)


def roll(value, shift):
    return pltpu.roll(value, shift % LANES, 1)


def lane_ids(rows):
    return lax.broadcasted_iota(jnp.int32, (rows, LANES), 1)


def silu_parts(value):
    sigma = 1.0 / (1.0 + jnp.exp(-value))
    return value * sigma, sigma * (1.0 + value * (1.0 - sigma))


def depth_columns(base, masks, step):
    below = roll(base, step) * masks[0]
    above = roll(base, -step) * masks[1]
    return jnp.concatenate([below, base, above], axis=0)


def depth_masks(step, first):
    ids = (lane_ids(3 * C) - first) % LANES
    return (ids >= step).astype(BF16), (ids < LANES - step).astype(BF16)


def across_columns(tile, step):
    return jnp.concatenate([roll(tile, step), tile, roll(tile, -step)], axis=0)


def edge_masks(step):
    ids = lane_ids(C) % 8
    first, last = (ids == 4).astype(BF16), (ids == 4 - step).astype(BF16)
    return first, (ids != 4).astype(BF16), last, (ids != 4 - step).astype(BF16)


def pair_columns(tile, halo, masks, step):
    left = roll(halo, step) * masks[0] + roll(tile, step) * masks[1]
    right = roll(halo, -step) * masks[2] + roll(tile, -step) * masks[3]
    return jnp.concatenate([left, tile, right], axis=0)


def fill_columns(tiles, from_left, from_right, out, step):
    masks = edge_masks(step)

    def body(group):
        packed_left, packed_right = from_left[group], from_right[group]
        for place in range(8):
            tile = tiles[8 * group + place]
            left = roll(packed_left, -place) * masks[0] + roll(tile, step) * masks[1]
            right = roll(packed_right, 8 - step - place) * masks[2]
            right = right + roll(tile, -step) * masks[3]
            out[8 * group + place] = jnp.concatenate([left, tile, right], axis=0)

    loop(0, from_left.shape[0], body)


def pack_columns(tiles, low, high, step):
    masks = edge_masks(step)

    def body(group):
        lows, highs = [], []
        for place in range(8):
            tile = tiles[8 * group + place]
            lows.append(roll(tile * masks[0], place))
            highs.append(roll(tile * masks[2], place - 8 + step))
        for out, parts in ((low, lows), (high, highs)):
            while len(parts) > 1:
                parts = [a + b for a, b in zip(parts[::2], parts[1::2])]
            out[group] = parts[0]

    loop(0, low.shape[0], body, 5)


def own_masks():
    own = own_lanes(C)
    return own.astype(BF16), jnp.logical_not(own).astype(BF16)


def pair_tiles(lower, upper, masks):
    turned = roll(upper, 8)
    return (
        lower * masks[0] + turned * masks[1],
        lower * masks[1] + turned * masks[0],
    )


def own_lanes(rows):
    across = lane_ids(rows) % 16
    return (across >= 4) & (across < 12)


def join_halves(lower, upper):
    return jnp.where(own_lanes(lower.shape[0]), lower, roll(upper, 8))


def gather_sub(parts):
    even = lane_ids(C) % 2 == 0
    above = jnp.where(even, parts[2 * C : 3 * C], parts[3 * C :])
    total = jnp.where(even, parts[:C], parts[C : 2 * C]) + roll(above, -16)
    return total + roll(total, -1)


def spread_sub(anchored):
    return jnp.concatenate([anchored] + [roll(anchored, step) for step in SHIFTS[1:]], axis=0)


def anchor_mask(first):
    ids = (lane_ids(C) - first) % LANES
    return (((ids // 16) % 2 == 0) & (ids % 2 == 0)).astype(F32)


def loop(low, high, body, unroll=1):
    def step(index, carry):
        body(index)
        return carry

    lax.fori_loop(low, high, step, 0, unroll=unroll)


def join_rows(first, second):
    low = lane_ids(C) < 64
    lead = roll(second[:, :LANES], 64)
    parts = [
        first[:, :LANES],
        jnp.where(low, first[:, LANES:], lead),
        jnp.where(low, lead, roll(second[:, LANES:], 64)),
    ]
    return jnp.concatenate(parts, axis=1)


def split_rows(joined):
    low = lane_ids(C) < 64
    middle = roll(joined[:, LANES : 2 * LANES], 64)
    last = roll(joined[:, 2 * LANES :], 64)
    second = jnp.concatenate([jnp.where(low, middle, last), last], axis=1)
    return joined[:, : 2 * LANES], second


def prepare_kernel(slots, count, feats, cots, flag_rows, x_low, x_high, y_low, y_high, rows_in):
    number = feats.shape[0]
    rows = lax.broadcasted_iota(jnp.int32, (16, LANES), 0)
    flags = jnp.zeros((16, LANES), F32)
    zero = jnp.zeros((C, VOX), BF16)
    first = jnp.zeros((), jnp.int32)
    last = jnp.zeros((), jnp.int32)
    for slot in range(number):
        live = slot < count[0]
        place = slots[slot]
        block = jnp.where(live, feats[slot], zero)
        rows_in[pl.ds(pl.multiple_of(place * C, 16), C), :] = block
        flags = jnp.where(rows == place, jnp.where(live, 1.0, 0.0), flags)
        first = jnp.where(place == 0, slot, first)
        last = jnp.where(place == number - 1, slot, last)
    flag_rows[...] = flags
    packed = dot(rows_in[...], marks(VOX, 512, plain, edge_source)).astype(BF16)
    spare = jnp.zeros((16, 2 * LANES), BF16)
    for out, at in ((x_low, 0), (x_high, 256)):
        for pair in range(number // 2):
            edges = [packed[C * i : C * (i + 1), at : at + 256] for i in (2 * pair, 2 * pair + 1)]
            out[C * pair : C * (pair + 1), :] = join_rows(*edges)
        out[C * number // 2 :, :LANES] = flags.astype(BF16)
        out[C * number // 2 :, LANES:] = spare
    for out, index, slot in ((y_low, 0, first), (y_high, number - 1, last)):
        live = slot < count[0]
        out[0:C, :] = rows_in[C * index : C * (index + 1), :]
        out[C : 2 * C, :] = jnp.where(live, cots[slot], zero)
        out[2 * C :, :] = (jnp.zeros((16, VOX), F32) + jnp.where(live, 1.0, 0.0)).astype(BF16)


def corner_kernel(y_left, y_right, low, high):
    rows = jnp.concatenate([y_left[0:C, :], y_right[0:C, :]], axis=0)
    packed = dot(rows, marks(VOX, 512, plain, edge_source)).astype(BF16)
    ids = lax.broadcasted_iota(jnp.int32, (16, LANES), 0)
    flags = jnp.where(ids == 0, y_left[2 * C :, :LANES], y_right[2 * C :, :LANES])
    spare = jnp.zeros((16, 2 * LANES), BF16)
    for out, at in ((low, 0), (high, 256)):
        out[0:C, :] = join_rows(packed[:C, at : at + 256], packed[C:, at : at + 256])
        out[C:, :LANES] = flags
        out[C:, LANES:] = spare


def arrange_weights(fine, down, coarse, up, fine_w, fine_b, coarse_w, coarse_b, down_w, up_w):
    for source, fore, back in ((fine, fine_w, fine_b), (coarse, coarse_w, coarse_b)):
        for along in range(3):
            rows = slice(C * along, C * (along + 1))
            turned_rows = slice(C * (2 - along), C * (3 - along))
            ahead = []
            behind = []
            for depth in range(3):
                for across in range(3):
                    ahead.append(source[9 * depth + 3 * across + along])
                    behind.append(source[9 * (2 - depth) + 3 * (2 - across) + along].T)
            fore[rows, :] = jnp.concatenate(ahead, axis=1)
            back[turned_rows, :] = jnp.concatenate(behind, axis=1)
    for index in range(4):
        pair = [down[:, 2 * index, :], down[:, 2 * index + 1, :]]
        down_w[C * index : C * (index + 1), :] = jnp.concatenate(pair, axis=1)
    for along in range(2):
        row = jnp.concatenate([up[2 * index + along] for index in range(4)], axis=1)
        up_w[C * along : C * (along + 1), :] = row


def place_kernel(
    slots, count, feats, cots, y_left, y_right, c_low, fine, down, coarse, up,
    grid, cot_grid, grad_r, fine_w, fine_b, coarse_w, coarse_b, down_w, up_w,
    rows_in, rows_cot, cot,
):
    arrange_weights(fine, down, coarse, up, fine_w, fine_b, coarse_w, coarse_b, down_w, up_w)
    number = feats.shape[0]
    last = number + 1
    zero = jnp.zeros((C, VOX), BF16)
    rows_in[0:C, :] = y_left[0:C, :]
    rows_in[last * C : (last + 1) * C, :] = y_right[0:C, :]
    for slot in range(number):
        live = slot < count[0]
        place = slots[slot]
        start = pl.multiple_of((place + 1) * C, 16)
        rows_in[pl.ds(start, C), :] = jnp.where(live, feats[slot], zero)
        cot[place] = jnp.where(live, cots[slot], zero)
    pairs = number // 2 + 2
    for group in range(pairs):
        at = group * C
        lower = y_left[C : 2 * C, :] if group == 0 else cot[group - 1]
        upper = y_right[C : 2 * C, :] if group == pairs - 1 else cot[group + number // 2 - 1]
        rows_cot[at : at + C, 0:512] = lower
        rows_cot[at : at + C, 512:1024] = upper
    for pair in range(4):
        placed_cot = dot(
            rows_cot[...], marks(1024, 256, plain, lambda j, at=256 * pair: pair_source(j + at))
        )
        placed = dot(
            rows_in[...], marks(VOX, 256, plain, lambda j, at=256 * pair: own_source(j + at))
        )
        for half in range(2):
            span = slice(LANES * half, LANES * (half + 1))
            for block in range(last + 1):
                tile = EDGE * block + 2 * pair + half
                grid[tile] = placed[block * C : (block + 1) * C, span].astype(BF16)
            for block in range(pairs):
                tile = EDGE * block + 2 * pair + half
                cot_grid[tile] = placed_cot[block * C : (block + 1) * C, span].astype(BF16)

    def rect_step(block):
        tiles = []
        for inner in range(4):
            tile = EDGE * block + 2 * inner
            tiles.append(jnp.concatenate([cot_grid[tile], cot_grid[tile + 1]], axis=0))
        parts = dot(up_w[...], jnp.concatenate(tiles, axis=1), (0, 0))
        for inner in range(4):
            grad_r[4 * block + inner] = gather_sub(parts[:, LANES * inner : LANES * (inner + 1)])

    loop(0, pairs, rect_step, 5)


def conv_steps(sums, weight, load, tiles, step, first, even, odd):
    masks = depth_masks(step, first)

    def fill(buffer, tile):
        for i in range(4):
            cols = depth_columns(load(tile + i), masks, step)
            buffer[:, LANES * i : LANES * (i + 1)] = cols

    def multiply(buffer, tile, carry):
        out = dot(weight[...], buffer[...])

        def part(along, i):
            return out[C * along : C * (along + 1), LANES * i : LANES * (i + 1)]

        sums[tile] += part(2, 0)
        sums[tile + 1] = carry + part(1, 0) + part(2, 1)
        sums[tile + 2] = part(0, 0) + part(1, 1) + part(2, 2)
        sums[tile + 3] = part(0, 1) + part(1, 2) + part(2, 3)
        sums[tile + 4] = part(0, 2) + part(1, 3)
        return part(0, 3)

    fill(even, 0)
    sums[0] = jnp.zeros((C, LANES), F32)

    def body(index, carry):
        tile = 8 * index
        fill(odd, tile + 4)
        carry = multiply(even, tile, carry)
        fill(even, jnp.minimum(tile + 8, tiles - 4))
        return multiply(odd, tile + 4, carry)

    unroll = 6 if tiles % 48 == 0 else 10 if tiles % 80 == 0 else 5
    lax.fori_loop(0, tiles // 8, body, jnp.zeros((C, LANES), F32), unroll=unroll)


def forward_kernel(
    grid_own, flags, y_left, y_right, grad_r, x_left, x_right, c_left, c_right, fine_w, down_w,
    coarse_w,
    grid, hidden, low_cols, rects, grad_c, live, pack_low, pack_high,
    rows_in, fine_p, coarse_p, hidden_all, lowered, live_all, even, odd,
):
    number = 2 * (x_left.shape[0] - 16) // C
    last = number + 1
    for at, left, right in ((0, x_left, x_right), (None, c_left, c_right)):
        for pair in range((left.shape[0] - 16) // C):
            rows = slice(C * pair, C * (pair + 1))
            lefts, rights = split_rows(left[rows, :]), split_rows(right[rows, :])
            for inner in range(2):
                block = last * inner if at is None else 2 * pair + inner + 1
                rows_in[block * C : (block + 1) * C, 0:256] = lefts[inner]
                rows_in[block * C : (block + 1) * C, 256:512] = rights[inner]
    across = lane_ids(16) % 16
    for start, middle, left, right in (
        (1, flags[...], x_left[number // 2 * C :, :LANES], x_right[number // 2 * C :, :LANES]),
        (0, y_left[2 * C :, :LANES], c_left[C:, :LANES], c_right[C:, :LANES]),
        (last, y_right[2 * C :, :LANES], c_left[C:, :LANES], c_right[C:, :LANES]),
    ):
        rows = jnp.where(across < 4, left.astype(F32), middle.astype(F32))
        rows = jnp.where(across >= 12, right.astype(F32), rows)
        if start == 1:
            live_all[1 : number + 1, :] = rows
        else:
            at = 0 if start == 0 else 1
            live_all[start : start + 1, :] = rows[at : at + 1, :]
    for pair in range(4):
        placed = dot(
            rows_in[...], marks(512, 256, plain, lambda j, at=256 * pair: halo_source(j + at))
        )
        for half in range(2):
            span = slice(LANES * half, LANES * (half + 1))
            for block in range(last + 1):
                tile = EDGE * block + 2 * pair + half
                halo = placed[block * C : (block + 1) * C, span].astype(BF16)
                grid[tile] = grid_own[tile] + halo
    live[...] = join_halves(live_all[0:16, :], live_all[8:24, :])
    tiles = grid.shape[0]
    conv_steps(fine_p, fine_w, lambda tile: across_columns(grid[tile], 1), tiles, 16, 0, even, odd)
    anchors = anchor_mask(0)

    def lower_step(block):
        alive = jnp.broadcast_to(live_all[pl.ds(block, 1), :], (C, LANES))
        keep = alive * anchors
        pairs = []
        for inner in range(4):
            actives = []
            for half in range(2):
                tile = EDGE * block + 2 * inner + half
                value = fine_p[tile + 1] * alive
                hidden_all[tile] = value
                actives.append(silu_parts(value)[0].astype(BF16))
            pairs.append(jnp.concatenate(actives, axis=0))
        parts = dot(down_w[...], jnp.concatenate(pairs, axis=1))
        for inner in range(4):
            total = gather_sub(parts[:, LANES * inner : LANES * (inner + 1)])
            lowered[4 * block + inner] = (total * keep).astype(BF16)

    loop(0, last + 1, lower_step, 6)
    pairs = hidden.shape[0] // EDGE
    shift = last - pairs + 1
    edges = edge_masks(2)
    halves = own_masks()

    def pair_step(block):
        for inner in range(EDGE):
            tile = EDGE * block + inner
            hidden[tile] = join_halves(hidden_all[tile], hidden_all[tile + EDGE * shift])
        for inner in range(4):
            tile = 4 * block + inner
            lower, upper = lowered[tile], lowered[tile + 4 * shift]
            low_cols[tile] = pair_columns(*pair_tiles(lower, upper, halves), edges, 2)

    loop(0, pairs, pair_step, 5)
    conv_steps(coarse_p, coarse_w, lambda tile: low_cols[tile], 4 * pairs, 32, 4, even, odd)
    pair_anchors = anchor_mask(4)

    def grad_step(block):
        alive = jnp.broadcast_to(live[pl.ds(block, 1), :], (C, LANES))
        keep = alive * pair_anchors
        for inner in range(4):
            coarse = 4 * block + inner
            smooth, slope = silu_parts(coarse_p[coarse + 1])
            rects[coarse] = (smooth * pair_anchors).astype(BF16)
            grad_c[coarse] = (grad_r[coarse] * slope * keep).astype(BF16)

    loop(0, pairs, grad_step, 5)
    pack_columns(grad_c, pack_low, pack_high, 2)


def to_blocks(slots, rows_out, flat, out):
    flat[...] = dot(rows_out[...], marks(1024, 1024, pair_source, plain)).astype(BF16)
    number = out.shape[0]
    for slot in range(number):
        place = slots[slot]
        upper = place >= number // 2
        start = pl.multiple_of(jnp.where(upper, place - number // 2, place) * C, 16)
        rows = flat[pl.ds(start, C), :]
        out[slot] = jnp.where(upper, rows[:, 512:], rows[:, :512])


def stacks(own, tiles):
    parts = [jnp.concatenate([own[t + 1], own[t], own[t - 1]], axis=0) for t in tiles]
    return jnp.concatenate(parts, axis=1)


def squeeze_rows(full, keep):
    extra = full[keep:]
    size, part = extra.shape[0], keep // 3
    lanes = lane_ids(size)
    pieces = []
    for index in range(3):
        rows = full[part * index : part * (index + 1)]
        pieces.append(jnp.where(lanes < 96, rows[:size], roll(extra, 96 - 32 * index)))
        if size < part:
            pieces.append(rows[size:])
    return jnp.concatenate(pieces, axis=0)


def widen_rows(packed, number):
    keep = packed.shape[0]
    size, part = number - keep, keep // 3
    lanes = lane_ids(size)
    extra = jnp.zeros((size, LANES), F32)
    for index in range(3):
        moved = roll(packed[part * index : part * index + size], 32 * index - 96)
        extra = jnp.where((lanes >= 32 * index) & (lanes < 32 * index + 32), moved, extra)
    return jnp.concatenate([packed, extra], axis=0)


def flatten_weights(total, out):
    turned = total[...].T
    for group in range(3):
        part = turned[:, LANES * group : LANES * (group + 1)]
        out[3 * C * group : 3 * C * (group + 1), :] = part.astype(BF16)
    return turned[:, 3 * LANES :]


def output_kernel(slots, hidden, rects, live, up_w, out, rows_out, flat):
    pairs = hidden.shape[0] // EDGE

    def block_step(block):
        alive = jnp.broadcast_to(live[pl.ds(block, 1), :], (C, LANES))
        start = pl.multiple_of((block - 1) * C, 16)
        spreads = [spread_sub(rects[4 * block + inner]) for inner in range(4)]
        upward = dot(up_w[...], jnp.concatenate(spreads, axis=1))
        for inner in range(4):
            for half in range(2):
                part = upward[half * C : (half + 1) * C, LANES * inner : LANES * (inner + 1)]
                value = hidden[EDGE * block + 2 * inner + half] + part
                at = LANES * (2 * inner + half)
                rows_out[pl.ds(start, C), at : at + LANES] = (value * alive).astype(BF16)

    loop(1, pairs - 1, block_step, 4)
    to_blocks(slots, rows_out, flat, out)


def side_kernel(rects, cot_grid, low_cols, grad_c, flat, grad_own, up_g, coarse_g):
    tiles = low_cols.shape[0]
    up_g[...] = jnp.zeros_like(up_g)
    coarse_g[...] = jnp.zeros_like(coarse_g)

    def up_step(block):
        spreads = []
        pairs = []
        for inner in range(8):
            coarse = 4 + 8 * block + inner
            spreads.append(spread_sub(rects[coarse]))
            pairs.append(
                jnp.concatenate([cot_grid[2 * coarse], cot_grid[2 * coarse + 1]], axis=0)
            )
        up_g[:, 0 : 2 * C] += dot(
            jnp.concatenate(spreads, axis=1), jnp.concatenate(pairs, axis=1), (1, 1)
        )

    loop(0, (tiles - 8) // 8, up_step, 4)
    zero = jnp.zeros((C, LANES), BF16)
    for coarse in range(1, 4):
        grad_own[coarse] = zero
        grad_own[tiles - 1 - coarse] = zero

    def copy_step(coarse):
        grad_own[coarse] = grad_c[coarse]

    loop(4, tiles - 4, copy_step, 8)
    masks = depth_masks(32, 4)

    def weight_step(index):
        at = [2 + 18 * index + inner for inner in range(18)]
        rights = [depth_columns(low_cols[tile], masks, 32) for tile in at]
        coarse_g[0 : 9 * C, :] += dot(
            jnp.concatenate(rights, axis=1), stacks(grad_own, at), (1, 1)
        )

    loop(0, (tiles - 4) // 18, weight_step, 2)
    rest = flatten_weights(coarse_g, flat)
    flat[9 * C : 12 * C, :] = squeeze_rows(up_g[...], 3 * C).astype(BF16)
    flat[12 * C :, :] = roll(rest, C).astype(BF16)


def backward_kernel(
    grad_c, from_left, from_right, hidden, cot_grid, live, coarse_w, down_w,
    grad_h, grad_d, coarse_p, grad_x, even, odd,
):
    tiles = grad_c.shape[0]
    fill_columns(grad_c, from_left, from_right, grad_x, 2)
    conv_steps(coarse_p, coarse_w, lambda tile: grad_x[tile], tiles, 32, 4, even, odd)
    anchors = anchor_mask(4)

    def step(block):
        alive = jnp.broadcast_to(live[pl.ds(block, 1), :], (C, LANES))
        keep = alive * anchors
        spreads = []
        for inner in range(4):
            coarse = 4 * block + inner
            down = (coarse_p[coarse + 1] * keep).astype(BF16)
            grad_d[coarse] = down
            spreads.append(spread_sub(down))
        acts = dot(down_w[...], jnp.concatenate(spreads, axis=1), (0, 0))
        for inner in range(4):
            for side in range(2):
                tile = EDGE * block + 2 * inner + side
                slope = silu_parts(hidden[tile])[1]
                part = acts[side * C : (side + 1) * C, LANES * inner : LANES * (inner + 1)]
                grad = cot_grid[tile].astype(F32) + part * slope
                grad_h[tile] = (grad * alive).astype(BF16)

    loop(0, tiles // 4, step, 5)


def pack_kernel(grad_h, low, high):
    pack_columns(grad_h, low, high, 1)


def weight_kernel(grid, grad_h, grad_d, hidden, early, joined, grad_own, fine_g, down_g):
    tiles = grad_h.shape[0]
    shift = tiles - 16
    fine_g[...] = jnp.zeros_like(fine_g)
    down_g[...] = jnp.zeros_like(down_g)
    zero = jnp.zeros((C, LANES), BF16)
    for tile in range(3, 8):
        grad_own[tile] = zero
        grad_own[tiles - 1 - tile] = zero

    def copy_step(tile):
        grad_own[tile] = grad_h[tile]

    loop(8, tiles - 8, copy_step, 8)
    masks = depth_masks(16, 4)
    edges = edge_masks(1)
    halves = own_masks()

    def fine_step(index):
        at = [4 + 36 * index + inner for inner in range(36)]
        rights = []
        for tile in at:
            lower, upper = grid[tile], grid[tile + shift]
            base = pair_columns(*pair_tiles(lower, upper, halves), edges, 1)
            rights.append(depth_columns(base, masks, 16))
        fine_g[0 : 9 * C, :] += dot(
            jnp.concatenate(rights, axis=1), stacks(grad_own, at), (1, 1)
        )

    loop(0, (tiles - 8) // 36, fine_step)

    def down_step(index):
        lefts = []
        rights = []
        for inner in range(8):
            coarse = 4 + 8 * index + inner
            lefts.append(spread_sub(grad_d[coarse]))
            actives = [silu_parts(hidden[2 * coarse + side])[0].astype(BF16) for side in range(2)]
            rights.append(jnp.concatenate(actives, axis=0))
        down_g[:, 0 : 2 * C] += dot(
            jnp.concatenate(lefts, axis=1), jnp.concatenate(rights, axis=1), (1, 1)
        )

    loop(0, (tiles // 2 - 8) // 8, down_step, 4)
    rest = flatten_weights(fine_g, joined) + early[12 * C :, :].astype(F32)
    joined[9 * C : 18 * C, :] = early[0 : 9 * C, :]
    joined[18 * C : 21 * C, :] = squeeze_rows(down_g[...], 3 * C).astype(BF16)
    joined[21 * C : 24 * C, :] = early[9 * C : 12 * C, :]
    squeezed = squeeze_rows(rest, 120)
    joined[24 * C :, :] = jnp.concatenate([squeezed, squeezed[:8]], axis=0).astype(BF16)


def input_kernel(
    slots, grad_h, from_left, from_right, live, fine_w, out,
    fine_p, rows_out, flat, grad_x, even, odd,
):
    tiles = grad_h.shape[0]
    fill_columns(grad_h, from_left, from_right, grad_x, 1)
    conv_steps(fine_p, fine_w, lambda tile: grad_x[tile], tiles, 16, 4, even, odd)

    def block_step(block):
        alive = jnp.broadcast_to(live[pl.ds(block, 1), :], (C, LANES))
        start = pl.multiple_of((block - 1) * C, 16)
        for inner in range(EDGE):
            value = fine_p[EDGE * block + inner + 1]
            rows_out[pl.ds(start, C), LANES * inner : LANES * (inner + 1)] = (
                value * alive
            ).astype(BF16)

    loop(1, tiles // EDGE - 1, block_step, 4)
    to_blocks(slots, rows_out, flat, out)


def sum_kernel(parts, copies):
    total = jnp.sum(parts[...].astype(F32), axis=0).astype(BF16)
    copies[...] = jnp.broadcast_to(total[None], copies.shape)


def finish_kernel(scale, total, fine, down, coarse, up):
    rest = widen_rows(total[24 * C :, :].astype(F32)[:120], 3 * C) * scale
    for out, at, moved in ((fine, 0, rest), (coarse, 9 * C, roll(rest, -C))):
        for along in range(3):
            first = at + C * along
            rows = [total[first + 3 * C * g : first + 3 * C * g + C, :] for g in range(3)]
            row = jnp.concatenate(rows, axis=1).astype(F32) * scale
            row = jnp.concatenate([row, moved[C * along : C * (along + 1)]], axis=1)
            for index in range(9):
                out[3 * index + along] = row[:, C * index : C * (index + 1)]
    for out, at, turn in ((down, 18 * C, False), (up, 21 * C, True)):
        full = widen_rows(total[at : at + 3 * C, :].astype(F32), 4 * C) * scale
        for index in range(4):
            rows = full[C * index : C * (index + 1)]
            for along in range(2):
                part = rows[:, C * along : C * (along + 1)]
                if turn:
                    out[2 * index + along] = part.T
                else:
                    out[:, 2 * index + along, :] = part


def call(kernel, inputs, outs, scratch=(), scalars=0, flops=0, limit=None):
    vmem = pl.BlockSpec(memory_space=pltpu.VMEM)
    smem = pl.BlockSpec(memory_space=pltpu.SMEM)
    held = SLACK
    for shape, kind in [(a.shape, a.dtype) for a in inputs[scalars:]] + list(outs) + list(scratch):
        rows, lanes = -(-shape[-2] // 16) * 16, -(-shape[-1] // LANES) * LANES
        held += math.prod(shape[:-2]) * rows * lanes * jnp.dtype(kind).itemsize
    moved = sum(math.prod(s) * jnp.dtype(d).itemsize for s, d in outs)
    moved += sum(math.prod(a.shape) * a.dtype.itemsize for a in inputs)
    return pl.pallas_call(
        kernel,
        out_shape=tuple(jax.ShapeDtypeStruct(s, d) for s, d in outs),
        in_specs=[smem] * scalars + [vmem] * (len(inputs) - scalars),
        out_specs=tuple(vmem for _ in outs),
        scratch_shapes=[pltpu.VMEM(s, d) for s, d in scratch],
        compiler_params=pltpu.CompilerParams(vmem_limit_bytes=limit or held),
        cost_estimate=pl.CostEstimate(flops=flops, bytes_accessed=moved, transcendentals=0),
        name=getattr(kernel, "func", kernel).__name__,
    )(*inputs)


def send(array, step_x, step_y):
    number_x, number_y = lax.axis_size("gx"), lax.axis_size("gy")
    pairs = []
    for i in range(number_x):
        for j in range(number_y):
            to_x, to_y = i + step_x, j + step_y
            if 0 <= to_x < number_x and 0 <= to_y < number_y:
                pairs.append((i * number_y + j, to_x * number_y + to_y))
    return lax.ppermute(array, ("gx", "gy"), pairs)


def reduce_share(joined):
    devices = lax.axis_size("gx") * lax.axis_size("gy")
    rows = joined.shape[0]
    share = -(-rows // devices)
    joined = jnp.pad(joined, ((0, share * devices - rows), (0, 0)))
    mine = lax.all_to_all(joined.reshape(devices, share, LANES), ("gx", "gy"), 0, 0)
    return mine


def spread_share(parts):
    (copies,) = call(sum_kernel, (parts,), [(parts.shape, BF16)])
    full = lax.all_to_all(copies, ("gx", "gy"), 0, 0)
    return full.reshape(-1, LANES)


def on_device(
    features, block_slots, block_count, cotangent, fine_weight, down_weight, coarse_weight,
    up_weight,
):
    number = features.shape[2]
    slots = block_slots.reshape(number)
    count = block_count.reshape(1)
    feats = features.reshape(number, C, VOX)
    cots = cotangent.reshape(number, C, VOX)
    tiles = EDGE * (number + 2)
    coarse_tiles = tiles // 2
    pairs = number // 2 + 2
    groups = pairs // 2
    fine_groups = pairs

    fine_3, coarse_3 = (weight.transpose(1, 0, 2) for weight in (fine_weight, coarse_weight))
    flag_rows, x_low, x_high, y_low, y_high = call(
        prepare_kernel,
        (slots, count, feats, cots),
        [((16, LANES), F32)]
        + [((number // 2 * C + 16, 384), BF16)] * 2
        + [((2 * C + 16, VOX), BF16)] * 2,
        [((number * C, VOX), BF16)],
        scalars=2,
        limit=56 * 1024 * 1024,
    )
    x_left = send(x_high, 1, 0)
    x_right = send(x_low, -1, 0)
    y_left = send(y_high, 0, 1)
    y_right = send(y_low, 0, -1)
    corner_low, corner_high = call(
        corner_kernel,
        (y_left, y_right),
        [((C + 16, 384), BF16), ((C + 16, 384), BF16)],
    )
    c_left = send(corner_high, 1, 0)
    c_right = send(corner_low, -1, 0)
    (grid_own, cot_grid, grad_r, fine_fore, fine_back, coarse_fore, coarse_back, down_w,
     up_w) = call(
        place_kernel,
        (slots, count, feats, cots, y_left, y_right, corner_low, fine_3, down_weight, coarse_3,
         up_weight),
        [
            ((tiles, C, LANES), BF16),
            ((EDGE * pairs, C, LANES), BF16),
            ((4 * pairs, C, LANES), F32),
        ]
        + [((3 * C, 9 * C), BF16)] * 4
        + [((4 * C, 2 * C), BF16), ((2 * C, 4 * C), BF16)],
        [
            (((number + 2) * C, VOX), BF16),
            ((pairs * C, 1024), BF16),
            ((number, C, VOX), BF16),
        ],
        scalars=2,
        flops=8 * 10**9,
    )
    grid, hidden, low_cols, rects, grad_c, live, pack_low, pack_high = call(
        forward_kernel,
        (grid_own, flag_rows, y_left, y_right, grad_r, x_left, x_right, c_left, c_right,
         fine_fore, down_w, coarse_fore),
        [
            ((tiles, C, LANES), BF16),
            ((EDGE * pairs, C, LANES), F32),
            ((4 * pairs, 3 * C, LANES), BF16),
            ((4 * pairs, C, LANES), BF16),
            ((4 * pairs, C, LANES), BF16),
            ((16, LANES), F32),
            ((groups, C, LANES), BF16),
            ((groups, C, LANES), BF16),
        ],
        [
            (((number + 2) * C, VOX), BF16),
            ((tiles + 1, C, LANES), F32),
            ((4 * pairs + 1, C, LANES), F32),
            ((tiles, C, LANES), F32),
            ((coarse_tiles, C, LANES), BF16),
            ((C, LANES), F32),
        ]
        + [((9 * C, 4 * LANES), BF16)] * 2,
        flops=8 * 10**9,
    )
    grad_left = send(pack_high, 1, 0)
    grad_right = send(pack_low, -1, 0)
    (early,) = call(
        side_kernel,
        (rects, cot_grid, low_cols, grad_c),
        [((15 * C, LANES), BF16)],
        [((4 * pairs, C, LANES), BF16), ((4 * C, LANES), F32), ((VOX, 3 * C), F32)],
        flops=8 * 10**9,
    )
    grad_h, grad_d = call(
        backward_kernel,
        (grad_c, grad_left, grad_right, hidden, cot_grid, live, coarse_back, down_w),
        [
            ((EDGE * pairs, C, LANES), BF16),
            ((4 * pairs, C, LANES), BF16),
        ],
        [((4 * pairs + 1, C, LANES), F32), ((4 * pairs, 3 * C, LANES), BF16)]
        + [((9 * C, 4 * LANES), BF16)] * 2,
        flops=8 * 10**9,
    )
    (joined,) = call(
        weight_kernel,
        (grid, grad_h, grad_d, hidden, early),
        [((24 * C + 128, LANES), BF16)],
        [((EDGE * pairs, C, LANES), BF16), ((VOX, 3 * C), F32), ((4 * C, LANES), F32)],
        flops=12 * 10**9,
    )
    joined, slots, grad_h = lax.optimization_barrier((joined, slots, grad_h))
    edge_low, edge_high = call(
        pack_kernel, (grad_h,), [((fine_groups, C, LANES), BF16)] * 2, flops=10**9
    )
    edge_left = send(edge_high, 1, 0)
    edge_right = send(edge_low, -1, 0)
    share = reduce_share(joined)
    (output,) = call(
        output_kernel,
        (slots, hidden, rects, live, up_w),
        [((number, C, VOX), BF16)],
        [((number // 2 * C, 1024), BF16), ((number // 2 * C, 1024), BF16)],
        scalars=1,
        flops=8 * 10**9,
    )
    share, output, slots = lax.optimization_barrier((share, output, slots))
    (input_grad,) = call(
        input_kernel,
        (slots, grad_h, edge_left, edge_right, live, fine_back),
        [((number, C, VOX), BF16)],
        [
            ((EDGE * pairs + 1, C, LANES), F32),
            ((number // 2 * C, 1024), BF16),
            ((number // 2 * C, 1024), BF16),
            ((EDGE * pairs, 3 * C, LANES), BF16),
        ]
        + [((9 * C, 4 * LANES), BF16)] * 2,
        scalars=1,
        flops=8 * 10**9,
    )
    total = spread_share(share)
    scale = 1.0 / math.sqrt(number * VOX * lax.axis_size("gx") * lax.axis_size("gy"))
    fine_total, down_total, coarse_total, up_total = call(
        functools.partial(finish_kernel, scale),
        (total,),
        [((27, C, C), F32), ((C, 8, C), F32), ((27, C, C), F32), ((8, C, C), F32)],
    )
    shape_out = (1, 1, number, C, VOX)
    return (
        output.reshape(shape_out),
        input_grad.reshape(shape_out),
        fine_total.transpose(1, 0, 2),
        down_total,
        coarse_total.transpose(1, 0, 2),
        up_total,
    )


def solution(mesh):
    split = P("gx", "gy", None, None, None)
    return jax.shard_map(
        on_device,
        mesh=mesh,
        in_specs=(split, P("gx", "gy", None), P("gx", "gy"), split, P(), P(), P(), P()),
        out_specs=(split, split, P(), P(), P(), P()),
        check_vma=False,
    )
```

```python
import functools
import math

import jax
import jax.numpy as jnp
from jax import lax
from jax.experimental import pallas as pl
from jax.experimental.pallas import tpu as pltpu
from jax.sharding import PartitionSpec as P

C = 48
EDGE = 8
VOX = 512
LANES = 128
F32 = jnp.float32
BF16 = jnp.bfloat16
SLACK = 8 * 1024 * 1024
SHIFTS = (0, 1, 16, 17)


def marks(rows, columns, row_key, column_key):
    across = column_key(lax.broadcasted_iota(jnp.int32, (1, columns), 1))
    down = row_key(lax.broadcasted_iota(jnp.int32, (rows, 1), 0))
    return jnp.where(down == across, 1.0, 0.0).astype(BF16)


def plain(index):
    return index


def own_source(column):
    lane, y = column % LANES, column // LANES
    x = lane % 16 - 4
    return jnp.where((x >= 0) & (x < 8), 64 * (lane // 16) + 8 * x + y, -1)


def halo_source(column):
    lane, y = column % LANES, column // LANES
    x = lane % 16
    at = 24 * (lane // 16) + y
    left = jnp.where((x >= 1) & (x < 4), at + 8 * (x - 1), -1)
    return jnp.where((x >= 12) & (x < 15), at + 8 * (x - 12) + 256, left)


def pair_source(column):
    lane, y = (column - 4) % LANES, column // LANES
    return 512 * (lane % 16 // 8) + 64 * (lane // 16) + 8 * (lane % 8) + y


def edge_source(column):
    at, side = column % 256, column // 256
    x = at % 24 // 8 + 5 * side
    return jnp.where(at < 192, 64 * (at // 24) + 8 * x + at % 8, -1)


def dot(left, right, contract=(1, 0)):
    dims = (((contract[0],), (contract[1],)), ((), ()))
    return lax.dot_general(left, right, dims, preferred_element_type=F32)


def roll(value, shift):
    return pltpu.roll(value, shift % LANES, 1)


def lane_ids(rows):
    return lax.broadcasted_iota(jnp.int32, (rows, LANES), 1)


def silu_parts(value):
    sigma = 1.0 / (1.0 + jnp.exp(-value))
    return value * sigma, sigma * (1.0 + value * (1.0 - sigma))


def depth_columns(base, masks, step):
    below = roll(base, step) * masks[0]
    above = roll(base, -step) * masks[1]
    return jnp.concatenate([below, base, above], axis=0)


def depth_masks(step, first):
    ids = (lane_ids(3 * C) - first) % LANES
    return (ids >= step).astype(BF16), (ids < LANES - step).astype(BF16)


def across_columns(tile, step):
    return jnp.concatenate([roll(tile, step), tile, roll(tile, -step)], axis=0)


def edge_masks(step):
    ids = lane_ids(C) % 8
    first, last = (ids == 4).astype(BF16), (ids == 4 - step).astype(BF16)
    return first, (ids != 4).astype(BF16), last, (ids != 4 - step).astype(BF16)


def pair_columns(tile, halo, masks, step):
    left = roll(halo, step) * masks[0] + roll(tile, step) * masks[1]
    right = roll(halo, -step) * masks[2] + roll(tile, -step) * masks[3]
    return jnp.concatenate([left, tile, right], axis=0)


def fill_columns(tiles, from_left, from_right, out, step):
    masks = edge_masks(step)

    def body(group):
        packed_left, packed_right = from_left[group], from_right[group]
        for place in range(8):
            tile = tiles[8 * group + place]
            left = roll(packed_left, -place) * masks[0] + roll(tile, step) * masks[1]
            right = roll(packed_right, 8 - step - place) * masks[2]
            right = right + roll(tile, -step) * masks[3]
            out[8 * group + place] = jnp.concatenate([left, tile, right], axis=0)

    loop(0, from_left.shape[0], body)


def pack_columns(tiles, low, high, step):
    masks = edge_masks(step)

    def body(group):
        lows, highs = [], []
        for place in range(8):
            tile = tiles[8 * group + place]
            lows.append(roll(tile * masks[0], place))
            highs.append(roll(tile * masks[2], place - 8 + step))
        for out, parts in ((low, lows), (high, highs)):
            while len(parts) > 1:
                parts = [a + b for a, b in zip(parts[::2], parts[1::2])]
            out[group] = parts[0]

    loop(0, low.shape[0], body, 5)


def own_masks():
    own = own_lanes(C)
    return own.astype(BF16), jnp.logical_not(own).astype(BF16)


def pair_tiles(lower, upper, masks):
    turned = roll(upper, 8)
    return (
        lower * masks[0] + turned * masks[1],
        lower * masks[1] + turned * masks[0],
    )


def own_lanes(rows):
    across = lane_ids(rows) % 16
    return (across >= 4) & (across < 12)


def join_halves(lower, upper):
    return jnp.where(own_lanes(lower.shape[0]), lower, roll(upper, 8))


def gather_sub(parts):
    even = lane_ids(C) % 2 == 0
    above = jnp.where(even, parts[2 * C : 3 * C], parts[3 * C :])
    total = jnp.where(even, parts[:C], parts[C : 2 * C]) + roll(above, -16)
    return total + roll(total, -1)


def spread_sub(anchored):
    return jnp.concatenate([anchored] + [roll(anchored, step) for step in SHIFTS[1:]], axis=0)


def anchor_mask(first):
    ids = (lane_ids(C) - first) % LANES
    return (((ids // 16) % 2 == 0) & (ids % 2 == 0)).astype(F32)


def loop(low, high, body, unroll=1):
    def step(index, carry):
        body(index)
        return carry

    lax.fori_loop(low, high, step, 0, unroll=unroll)


def join_rows(first, second):
    low = lane_ids(C) < 64
    lead = roll(second[:, :LANES], 64)
    parts = [
        first[:, :LANES],
        jnp.where(low, first[:, LANES:], lead),
        jnp.where(low, lead, roll(second[:, LANES:], 64)),
    ]
    return jnp.concatenate(parts, axis=1)


def split_rows(joined):
    low = lane_ids(C) < 64
    middle = roll(joined[:, LANES : 2 * LANES], 64)
    last = roll(joined[:, 2 * LANES :], 64)
    second = jnp.concatenate([jnp.where(low, middle, last), last], axis=1)
    return joined[:, : 2 * LANES], second


def prepare_kernel(slots, count, feats, cots, flag_rows, x_low, x_high, y_low, y_high, rows_in):
    number = feats.shape[0]
    rows = lax.broadcasted_iota(jnp.int32, (16, LANES), 0)
    flags = jnp.zeros((16, LANES), F32)
    zero = jnp.zeros((C, VOX), BF16)
    first = jnp.zeros((), jnp.int32)
    last = jnp.zeros((), jnp.int32)
    for slot in range(number):
        live = slot < count[0]
        place = slots[slot]
        block = jnp.where(live, feats[slot], zero)
        rows_in[pl.ds(pl.multiple_of(place * C, 16), C), :] = block
        flags = jnp.where(rows == place, jnp.where(live, 1.0, 0.0), flags)
        first = jnp.where(place == 0, slot, first)
        last = jnp.where(place == number - 1, slot, last)
    flag_rows[...] = flags
    packed = dot(rows_in[...], marks(VOX, 512, plain, edge_source)).astype(BF16)
    spare = jnp.zeros((16, 2 * LANES), BF16)
    for out, at in ((x_low, 0), (x_high, 256)):
        for pair in range(number // 2):
            edges = [packed[C * i : C * (i + 1), at : at + 256] for i in (2 * pair, 2 * pair + 1)]
            out[C * pair : C * (pair + 1), :] = join_rows(*edges)
        out[C * number // 2 :, :LANES] = flags.astype(BF16)
        out[C * number // 2 :, LANES:] = spare
    for out, index, slot in ((y_low, 0, first), (y_high, number - 1, last)):
        live = slot < count[0]
        out[0:C, :] = rows_in[C * index : C * (index + 1), :]
        out[C : 2 * C, :] = jnp.where(live, cots[slot], zero)
        out[2 * C :, :] = (jnp.zeros((16, VOX), F32) + jnp.where(live, 1.0, 0.0)).astype(BF16)


def corner_kernel(y_left, y_right, low, high):
    rows = jnp.concatenate([y_left[0:C, :], y_right[0:C, :]], axis=0)
    packed = dot(rows, marks(VOX, 512, plain, edge_source)).astype(BF16)
    ids = lax.broadcasted_iota(jnp.int32, (16, LANES), 0)
    flags = jnp.where(ids == 0, y_left[2 * C :, :LANES], y_right[2 * C :, :LANES])
    spare = jnp.zeros((16, 2 * LANES), BF16)
    for out, at in ((low, 0), (high, 256)):
        out[0:C, :] = join_rows(packed[:C, at : at + 256], packed[C:, at : at + 256])
        out[C:, :LANES] = flags
        out[C:, LANES:] = spare


def arrange_weights(fine, down, coarse, up, fine_w, fine_b, coarse_w, coarse_b, down_w, up_w):
    for source, fore, back in ((fine, fine_w, fine_b), (coarse, coarse_w, coarse_b)):
        for along in range(3):
            rows = slice(C * along, C * (along + 1))
            turned_rows = slice(C * (2 - along), C * (3 - along))
            ahead = []
            behind = []
            for depth in range(3):
                for across in range(3):
                    ahead.append(source[9 * depth + 3 * across + along])
                    behind.append(source[9 * (2 - depth) + 3 * (2 - across) + along].T)
            fore[rows, :] = jnp.concatenate(ahead, axis=1)
            back[turned_rows, :] = jnp.concatenate(behind, axis=1)
    for index in range(4):
        pair = [down[:, 2 * index, :], down[:, 2 * index + 1, :]]
        down_w[C * index : C * (index + 1), :] = jnp.concatenate(pair, axis=1)
    for along in range(2):
        row = jnp.concatenate([up[2 * index + along] for index in range(4)], axis=1)
        up_w[C * along : C * (along + 1), :] = row


def place_kernel(
    slots, count, feats, cots, y_left, y_right, c_low, fine, down, coarse, up,
    grid, cot_grid, grad_r, fine_w, fine_b, coarse_w, coarse_b, down_w, up_w,
    rows_in, rows_cot, cot,
):
    arrange_weights(fine, down, coarse, up, fine_w, fine_b, coarse_w, coarse_b, down_w, up_w)
    number = feats.shape[0]
    last = number + 1
    zero = jnp.zeros((C, VOX), BF16)
    rows_in[0:C, :] = y_left[0:C, :]
    rows_in[last * C : (last + 1) * C, :] = y_right[0:C, :]
    for slot in range(number):
        live = slot < count[0]
        place = slots[slot]
        start = pl.multiple_of((place + 1) * C, 16)
        rows_in[pl.ds(start, C), :] = jnp.where(live, feats[slot], zero)
        cot[place] = jnp.where(live, cots[slot], zero)
    pairs = number // 2 + 2
    for group in range(pairs):
        at = group * C
        lower = y_left[C : 2 * C, :] if group == 0 else cot[group - 1]
        upper = y_right[C : 2 * C, :] if group == pairs - 1 else cot[group + number // 2 - 1]
        rows_cot[at : at + C, 0:512] = lower
        rows_cot[at : at + C, 512:1024] = upper
    for pair in range(4):
        placed_cot = dot(
            rows_cot[...], marks(1024, 256, plain, lambda j, at=256 * pair: pair_source(j + at))
        )
        placed = dot(
            rows_in[...], marks(VOX, 256, plain, lambda j, at=256 * pair: own_source(j + at))
        )
        for half in range(2):
            span = slice(LANES * half, LANES * (half + 1))
            for block in range(last + 1):
                tile = EDGE * block + 2 * pair + half
                grid[tile] = placed[block * C : (block + 1) * C, span].astype(BF16)
            for block in range(pairs):
                tile = EDGE * block + 2 * pair + half
                cot_grid[tile] = placed_cot[block * C : (block + 1) * C, span].astype(BF16)

    def rect_step(block):
        tiles = []
        for inner in range(4):
            tile = EDGE * block + 2 * inner
            tiles.append(jnp.concatenate([cot_grid[tile], cot_grid[tile + 1]], axis=0))
        parts = dot(up_w[...], jnp.concatenate(tiles, axis=1), (0, 0))
        for inner in range(4):
            grad_r[4 * block + inner] = gather_sub(parts[:, LANES * inner : LANES * (inner + 1)])

    loop(0, pairs, rect_step, 5)


def conv_steps(sums, weight, load, tiles, step, first, even, odd):
    masks = depth_masks(step, first)

    def fill(buffer, tile):
        for i in range(4):
            cols = depth_columns(load(tile + i), masks, step)
            buffer[:, LANES * i : LANES * (i + 1)] = cols

    def multiply(buffer, tile, carry):
        out = dot(weight[...], buffer[...])

        def part(along, i):
            return out[C * along : C * (along + 1), LANES * i : LANES * (i + 1)]

        sums[tile] += part(2, 0)
        sums[tile + 1] = carry + part(1, 0) + part(2, 1)
        sums[tile + 2] = part(0, 0) + part(1, 1) + part(2, 2)
        sums[tile + 3] = part(0, 1) + part(1, 2) + part(2, 3)
        sums[tile + 4] = part(0, 2) + part(1, 3)
        return part(0, 3)

    fill(even, 0)
    sums[0] = jnp.zeros((C, LANES), F32)

    def body(index, carry):
        tile = 8 * index
        fill(odd, tile + 4)
        carry = multiply(even, tile, carry)
        fill(even, jnp.minimum(tile + 8, tiles - 4))
        return multiply(odd, tile + 4, carry)

    unroll = 3 if tiles % 24 == 0 else 10 if tiles % 80 == 0 else 5
    lax.fori_loop(0, tiles // 8, body, jnp.zeros((C, LANES), F32), unroll=unroll)


def forward_kernel(
    grid_own, flags, y_left, y_right, grad_r, x_left, x_right, c_left, c_right, fine_w, down_w,
    coarse_w,
    grid, hidden, low_cols, rects, grad_c, live, pack_low, pack_high,
    rows_in, fine_p, coarse_p, hidden_all, lowered, live_all, even, odd,
):
    number = 2 * (x_left.shape[0] - 16) // C
    last = number + 1
    for at, left, right in ((0, x_left, x_right), (None, c_left, c_right)):
        for pair in range((left.shape[0] - 16) // C):
            rows = slice(C * pair, C * (pair + 1))
            lefts, rights = split_rows(left[rows, :]), split_rows(right[rows, :])
            for inner in range(2):
                block = last * inner if at is None else 2 * pair + inner + 1
                rows_in[block * C : (block + 1) * C, 0:256] = lefts[inner]
                rows_in[block * C : (block + 1) * C, 256:512] = rights[inner]
    across = lane_ids(16) % 16
    for start, middle, left, right in (
        (1, flags[...], x_left[number // 2 * C :, :LANES], x_right[number // 2 * C :, :LANES]),
        (0, y_left[2 * C :, :LANES], c_left[C:, :LANES], c_right[C:, :LANES]),
        (last, y_right[2 * C :, :LANES], c_left[C:, :LANES], c_right[C:, :LANES]),
    ):
        rows = jnp.where(across < 4, left.astype(F32), middle.astype(F32))
        rows = jnp.where(across >= 12, right.astype(F32), rows)
        if start == 1:
            live_all[1 : number + 1, :] = rows
        else:
            at = 0 if start == 0 else 1
            live_all[start : start + 1, :] = rows[at : at + 1, :]
    for pair in range(4):
        placed = dot(
            rows_in[...], marks(512, 256, plain, lambda j, at=256 * pair: halo_source(j + at))
        )
        for half in range(2):
            span = slice(LANES * half, LANES * (half + 1))
            for block in range(last + 1):
                tile = EDGE * block + 2 * pair + half
                halo = placed[block * C : (block + 1) * C, span].astype(BF16)
                grid[tile] = grid_own[tile] + halo
    live[...] = join_halves(live_all[0:16, :], live_all[8:24, :])
    tiles = grid.shape[0]
    conv_steps(fine_p, fine_w, lambda tile: across_columns(grid[tile], 1), tiles, 16, 0, even, odd)
    anchors = anchor_mask(0)

    def lower_step(block):
        alive = jnp.broadcast_to(live_all[pl.ds(block, 1), :], (C, LANES))
        keep = alive * anchors
        pairs = []
        for inner in range(4):
            actives = []
            for half in range(2):
                tile = EDGE * block + 2 * inner + half
                value = fine_p[tile + 1] * alive
                hidden_all[tile] = value
                actives.append(silu_parts(value)[0].astype(BF16))
            pairs.append(jnp.concatenate(actives, axis=0))
        parts = dot(down_w[...], jnp.concatenate(pairs, axis=1))
        for inner in range(4):
            total = gather_sub(parts[:, LANES * inner : LANES * (inner + 1)])
            lowered[4 * block + inner] = (total * keep).astype(BF16)

    loop(0, last + 1, lower_step, 3)
    pairs = hidden.shape[0] // EDGE
    shift = last - pairs + 1
    edges = edge_masks(2)
    halves = own_masks()

    def pair_step(block):
        for inner in range(EDGE):
            tile = EDGE * block + inner
            hidden[tile] = join_halves(hidden_all[tile], hidden_all[tile + EDGE * shift])
        for inner in range(4):
            tile = 4 * block + inner
            lower, upper = lowered[tile], lowered[tile + 4 * shift]
            low_cols[tile] = pair_columns(*pair_tiles(lower, upper, halves), edges, 2)

    loop(0, pairs, pair_step, 5)
    conv_steps(coarse_p, coarse_w, lambda tile: low_cols[tile], 4 * pairs, 32, 4, even, odd)
    pair_anchors = anchor_mask(4)

    def grad_step(block):
        alive = jnp.broadcast_to(live[pl.ds(block, 1), :], (C, LANES))
        keep = alive * pair_anchors
        for inner in range(4):
            coarse = 4 * block + inner
            smooth, slope = silu_parts(coarse_p[coarse + 1])
            rects[coarse] = (smooth * pair_anchors).astype(BF16)
            grad_c[coarse] = (grad_r[coarse] * slope * keep).astype(BF16)

    loop(0, pairs, grad_step, 5)
    pack_columns(grad_c, pack_low, pack_high, 2)


def to_blocks(slots, rows_out, flat, out):
    flat[...] = dot(rows_out[...], marks(1024, 1024, pair_source, plain)).astype(BF16)
    number = out.shape[0]
    for slot in range(number):
        place = slots[slot]
        upper = place >= number // 2
        start = pl.multiple_of(jnp.where(upper, place - number // 2, place) * C, 16)
        rows = flat[pl.ds(start, C), :]
        out[slot] = jnp.where(upper, rows[:, 512:], rows[:, :512])


def stacks(own, tiles):
    parts = [jnp.concatenate([own[t + 1], own[t], own[t - 1]], axis=0) for t in tiles]
    return jnp.concatenate(parts, axis=1)


def squeeze_rows(full, keep):
    extra = full[keep:]
    size, part = extra.shape[0], keep // 3
    lanes = lane_ids(size)
    pieces = []
    for index in range(3):
        rows = full[part * index : part * (index + 1)]
        pieces.append(jnp.where(lanes < 96, rows[:size], roll(extra, 96 - 32 * index)))
        if size < part:
            pieces.append(rows[size:])
    return jnp.concatenate(pieces, axis=0)


def widen_rows(packed, number):
    keep = packed.shape[0]
    size, part = number - keep, keep // 3
    lanes = lane_ids(size)
    extra = jnp.zeros((size, LANES), F32)
    for index in range(3):
        moved = roll(packed[part * index : part * index + size], 32 * index - 96)
        extra = jnp.where((lanes >= 32 * index) & (lanes < 32 * index + 32), moved, extra)
    return jnp.concatenate([packed, extra], axis=0)


def flatten_weights(total, out):
    turned = total[...].T
    for group in range(3):
        part = turned[:, LANES * group : LANES * (group + 1)]
        out[3 * C * group : 3 * C * (group + 1), :] = part.astype(BF16)
    return turned[:, 3 * LANES :]


def output_kernel(slots, hidden, rects, live, up_w, out, rows_out, flat):
    pairs = hidden.shape[0] // EDGE

    def block_step(block):
        alive = jnp.broadcast_to(live[pl.ds(block, 1), :], (C, LANES))
        start = pl.multiple_of((block - 1) * C, 16)
        spreads = [spread_sub(rects[4 * block + inner]) for inner in range(4)]
        upward = dot(up_w[...], jnp.concatenate(spreads, axis=1))
        for inner in range(4):
            for half in range(2):
                part = upward[half * C : (half + 1) * C, LANES * inner : LANES * (inner + 1)]
                value = hidden[EDGE * block + 2 * inner + half] + part
                at = LANES * (2 * inner + half)
                rows_out[pl.ds(start, C), at : at + LANES] = (value * alive).astype(BF16)

    loop(1, pairs - 1, block_step, 4)
    to_blocks(slots, rows_out, flat, out)


def side_kernel(rects, cot_grid, low_cols, grad_c, flat, grad_own, up_g, coarse_g):
    tiles = low_cols.shape[0]
    up_g[...] = jnp.zeros_like(up_g)
    coarse_g[...] = jnp.zeros_like(coarse_g)

    def up_step(block):
        spreads = []
        pairs = []
        for inner in range(8):
            coarse = 4 + 8 * block + inner
            spreads.append(spread_sub(rects[coarse]))
            pairs.append(
                jnp.concatenate([cot_grid[2 * coarse], cot_grid[2 * coarse + 1]], axis=0)
            )
        up_g[:, 0 : 2 * C] += dot(
            jnp.concatenate(spreads, axis=1), jnp.concatenate(pairs, axis=1), (1, 1)
        )

    loop(0, (tiles - 8) // 8, up_step, 4)
    zero = jnp.zeros((C, LANES), BF16)
    for coarse in range(1, 4):
        grad_own[coarse] = zero
        grad_own[tiles - 1 - coarse] = zero

    def copy_step(coarse):
        grad_own[coarse] = grad_c[coarse]

    loop(4, tiles - 4, copy_step, 8)
    masks = depth_masks(32, 4)

    def weight_step(index):
        at = [2 + 18 * index + inner for inner in range(18)]
        rights = [depth_columns(low_cols[tile], masks, 32) for tile in at]
        coarse_g[0 : 9 * C, :] += dot(
            jnp.concatenate(rights, axis=1), stacks(grad_own, at), (1, 1)
        )

    loop(0, (tiles - 4) // 18, weight_step, 2)
    rest = flatten_weights(coarse_g, flat)
    flat[9 * C : 12 * C, :] = squeeze_rows(up_g[...], 3 * C).astype(BF16)
    flat[12 * C :, :] = roll(rest, C).astype(BF16)


def backward_kernel(
    grad_c, from_left, from_right, hidden, cot_grid, live, coarse_w, down_w,
    grad_h, grad_d, coarse_p, grad_x, even, odd,
):
    tiles = grad_c.shape[0]
    fill_columns(grad_c, from_left, from_right, grad_x, 2)
    conv_steps(coarse_p, coarse_w, lambda tile: grad_x[tile], tiles, 32, 4, even, odd)
    anchors = anchor_mask(4)

    def step(block):
        alive = jnp.broadcast_to(live[pl.ds(block, 1), :], (C, LANES))
        keep = alive * anchors
        spreads = []
        for inner in range(4):
            coarse = 4 * block + inner
            down = (coarse_p[coarse + 1] * keep).astype(BF16)
            grad_d[coarse] = down
            spreads.append(spread_sub(down))
        acts = dot(down_w[...], jnp.concatenate(spreads, axis=1), (0, 0))
        for inner in range(4):
            for side in range(2):
                tile = EDGE * block + 2 * inner + side
                slope = silu_parts(hidden[tile])[1]
                part = acts[side * C : (side + 1) * C, LANES * inner : LANES * (inner + 1)]
                grad = cot_grid[tile].astype(F32) + part * slope
                grad_h[tile] = (grad * alive).astype(BF16)

    loop(0, tiles // 4, step, 5)


def pack_kernel(grad_h, low, high):
    pack_columns(grad_h, low, high, 1)


def weight_kernel(grid, grad_h, grad_d, hidden, early, joined, grad_own, fine_g, down_g):
    tiles = grad_h.shape[0]
    shift = tiles - 16
    fine_g[...] = jnp.zeros_like(fine_g)
    down_g[...] = jnp.zeros_like(down_g)
    zero = jnp.zeros((C, LANES), BF16)
    for tile in range(3, 8):
        grad_own[tile] = zero
        grad_own[tiles - 1 - tile] = zero

    def copy_step(tile):
        grad_own[tile] = grad_h[tile]

    loop(8, tiles - 8, copy_step, 8)
    masks = depth_masks(16, 4)
    edges = edge_masks(1)
    halves = own_masks()

    def fine_step(index):
        at = [4 + 36 * index + inner for inner in range(36)]
        rights = []
        for tile in at:
            lower, upper = grid[tile], grid[tile + shift]
            base = pair_columns(*pair_tiles(lower, upper, halves), edges, 1)
            rights.append(depth_columns(base, masks, 16))
        fine_g[0 : 9 * C, :] += dot(
            jnp.concatenate(rights, axis=1), stacks(grad_own, at), (1, 1)
        )

    loop(0, (tiles - 8) // 36, fine_step)

    def down_step(index):
        lefts = []
        rights = []
        for inner in range(8):
            coarse = 4 + 8 * index + inner
            lefts.append(spread_sub(grad_d[coarse]))
            actives = [silu_parts(hidden[2 * coarse + side])[0].astype(BF16) for side in range(2)]
            rights.append(jnp.concatenate(actives, axis=0))
        down_g[:, 0 : 2 * C] += dot(
            jnp.concatenate(lefts, axis=1), jnp.concatenate(rights, axis=1), (1, 1)
        )

    loop(0, (tiles // 2 - 8) // 8, down_step, 4)
    rest = flatten_weights(fine_g, joined) + early[12 * C :, :].astype(F32)
    joined[9 * C : 18 * C, :] = early[0 : 9 * C, :]
    joined[18 * C : 21 * C, :] = squeeze_rows(down_g[...], 3 * C).astype(BF16)
    joined[21 * C : 24 * C, :] = early[9 * C : 12 * C, :]
    squeezed = squeeze_rows(rest, 120)
    joined[24 * C :, :] = jnp.concatenate([squeezed, squeezed[:8]], axis=0).astype(BF16)


def input_kernel(
    slots, grad_h, from_left, from_right, live, fine_w, out,
    fine_p, rows_out, flat, grad_x, even, odd,
):
    tiles = grad_h.shape[0]
    fill_columns(grad_h, from_left, from_right, grad_x, 1)
    conv_steps(fine_p, fine_w, lambda tile: grad_x[tile], tiles, 16, 4, even, odd)

    def block_step(block):
        alive = jnp.broadcast_to(live[pl.ds(block, 1), :], (C, LANES))
        start = pl.multiple_of((block - 1) * C, 16)
        for inner in range(EDGE):
            value = fine_p[EDGE * block + inner + 1]
            rows_out[pl.ds(start, C), LANES * inner : LANES * (inner + 1)] = (
                value * alive
            ).astype(BF16)

    loop(1, tiles // EDGE - 1, block_step, 4)
    to_blocks(slots, rows_out, flat, out)


def sum_kernel(parts, copies):
    total = jnp.sum(parts[...].astype(F32), axis=0).astype(BF16)
    copies[...] = jnp.broadcast_to(total[None], copies.shape)


def finish_kernel(scale, total, fine, down, coarse, up):
    rest = widen_rows(total[24 * C :, :].astype(F32)[:120], 3 * C) * scale
    for out, at, moved in ((fine, 0, rest), (coarse, 9 * C, roll(rest, -C))):
        for along in range(3):
            first = at + C * along
            rows = [total[first + 3 * C * g : first + 3 * C * g + C, :] for g in range(3)]
            row = jnp.concatenate(rows, axis=1).astype(F32) * scale
            row = jnp.concatenate([row, moved[C * along : C * (along + 1)]], axis=1)
            for index in range(9):
                out[3 * index + along] = row[:, C * index : C * (index + 1)]
    for out, at, turn in ((down, 18 * C, False), (up, 21 * C, True)):
        full = widen_rows(total[at : at + 3 * C, :].astype(F32), 4 * C) * scale
        for index in range(4):
            rows = full[C * index : C * (index + 1)]
            for along in range(2):
                part = rows[:, C * along : C * (along + 1)]
                if turn:
                    out[2 * index + along] = part.T
                else:
                    out[:, 2 * index + along, :] = part


def call(kernel, inputs, outs, scratch=(), scalars=0, flops=0, limit=None):
    vmem = pl.BlockSpec(memory_space=pltpu.VMEM)
    smem = pl.BlockSpec(memory_space=pltpu.SMEM)
    held = SLACK
    for shape, kind in [(a.shape, a.dtype) for a in inputs[scalars:]] + list(outs) + list(scratch):
        rows, lanes = -(-shape[-2] // 16) * 16, -(-shape[-1] // LANES) * LANES
        held += math.prod(shape[:-2]) * rows * lanes * jnp.dtype(kind).itemsize
    moved = sum(math.prod(s) * jnp.dtype(d).itemsize for s, d in outs)
    moved += sum(math.prod(a.shape) * a.dtype.itemsize for a in inputs)
    return pl.pallas_call(
        kernel,
        out_shape=tuple(jax.ShapeDtypeStruct(s, d) for s, d in outs),
        in_specs=[smem] * scalars + [vmem] * (len(inputs) - scalars),
        out_specs=tuple(vmem for _ in outs),
        scratch_shapes=[pltpu.VMEM(s, d) for s, d in scratch],
        compiler_params=pltpu.CompilerParams(vmem_limit_bytes=limit or held),
        cost_estimate=pl.CostEstimate(flops=flops, bytes_accessed=moved, transcendentals=0),
        name=getattr(kernel, "func", kernel).__name__,
    )(*inputs)


def send(array, step_x, step_y):
    number_x, number_y = lax.axis_size("gx"), lax.axis_size("gy")
    pairs = []
    for i in range(number_x):
        for j in range(number_y):
            to_x, to_y = i + step_x, j + step_y
            if 0 <= to_x < number_x and 0 <= to_y < number_y:
                pairs.append((i * number_y + j, to_x * number_y + to_y))
    return lax.ppermute(array, ("gx", "gy"), pairs)


def reduce_share(joined):
    devices = lax.axis_size("gx") * lax.axis_size("gy")
    rows = joined.shape[0]
    share = -(-rows // devices)
    joined = jnp.pad(joined, ((0, share * devices - rows), (0, 0)))
    mine = lax.all_to_all(joined.reshape(devices, share, LANES), ("gx", "gy"), 0, 0)
    return mine


def spread_share(parts):
    (copies,) = call(sum_kernel, (parts,), [(parts.shape, BF16)])
    full = lax.all_to_all(copies, ("gx", "gy"), 0, 0)
    return full.reshape(-1, LANES)


def on_device(
    features, block_slots, block_count, cotangent, fine_weight, down_weight, coarse_weight,
    up_weight,
):
    number = features.shape[2]
    slots = block_slots.reshape(number)
    count = block_count.reshape(1)
    feats = features.reshape(number, C, VOX)
    cots = cotangent.reshape(number, C, VOX)
    tiles = EDGE * (number + 2)
    coarse_tiles = tiles // 2
    pairs = number // 2 + 2
    groups = pairs // 2
    fine_groups = pairs

    fine_3, coarse_3 = (weight.transpose(1, 0, 2) for weight in (fine_weight, coarse_weight))
    flag_rows, x_low, x_high, y_low, y_high = call(
        prepare_kernel,
        (slots, count, feats, cots),
        [((16, LANES), F32)]
        + [((number // 2 * C + 16, 384), BF16)] * 2
        + [((2 * C + 16, VOX), BF16)] * 2,
        [((number * C, VOX), BF16)],
        scalars=2,
        limit=56 * 1024 * 1024,
    )
    x_left = send(x_high, 1, 0)
    x_right = send(x_low, -1, 0)
    y_left = send(y_high, 0, 1)
    y_right = send(y_low, 0, -1)
    corner_low, corner_high = call(
        corner_kernel,
        (y_left, y_right),
        [((C + 16, 384), BF16), ((C + 16, 384), BF16)],
    )
    c_left = send(corner_high, 1, 0)
    c_right = send(corner_low, -1, 0)
    (grid_own, cot_grid, grad_r, fine_fore, fine_back, coarse_fore, coarse_back, down_w,
     up_w) = call(
        place_kernel,
        (slots, count, feats, cots, y_left, y_right, corner_low, fine_3, down_weight, coarse_3,
         up_weight),
        [
            ((tiles, C, LANES), BF16),
            ((EDGE * pairs, C, LANES), BF16),
            ((4 * pairs, C, LANES), F32),
        ]
        + [((3 * C, 9 * C), BF16)] * 4
        + [((4 * C, 2 * C), BF16), ((2 * C, 4 * C), BF16)],
        [
            (((number + 2) * C, VOX), BF16),
            ((pairs * C, 1024), BF16),
            ((number, C, VOX), BF16),
        ],
        scalars=2,
        flops=8 * 10**9,
    )
    grid, hidden, low_cols, rects, grad_c, live, pack_low, pack_high = call(
        forward_kernel,
        (grid_own, flag_rows, y_left, y_right, grad_r, x_left, x_right, c_left, c_right,
         fine_fore, down_w, coarse_fore),
        [
            ((tiles, C, LANES), BF16),
            ((EDGE * pairs, C, LANES), F32),
            ((4 * pairs, 3 * C, LANES), BF16),
            ((4 * pairs, C, LANES), BF16),
            ((4 * pairs, C, LANES), BF16),
            ((16, LANES), F32),
            ((groups, C, LANES), BF16),
            ((groups, C, LANES), BF16),
        ],
        [
            (((number + 2) * C, VOX), BF16),
            ((tiles + 1, C, LANES), F32),
            ((4 * pairs + 1, C, LANES), F32),
            ((tiles, C, LANES), F32),
            ((coarse_tiles, C, LANES), BF16),
            ((C, LANES), F32),
        ]
        + [((9 * C, 4 * LANES), BF16)] * 2,
        flops=8 * 10**9,
    )
    grad_left = send(pack_high, 1, 0)
    grad_right = send(pack_low, -1, 0)
    (early,) = call(
        side_kernel,
        (rects, cot_grid, low_cols, grad_c),
        [((15 * C, LANES), BF16)],
        [((4 * pairs, C, LANES), BF16), ((4 * C, LANES), F32), ((VOX, 3 * C), F32)],
        flops=8 * 10**9,
    )
    grad_h, grad_d = call(
        backward_kernel,
        (grad_c, grad_left, grad_right, hidden, cot_grid, live, coarse_back, down_w),
        [
            ((EDGE * pairs, C, LANES), BF16),
            ((4 * pairs, C, LANES), BF16),
        ],
        [((4 * pairs + 1, C, LANES), F32), ((4 * pairs, 3 * C, LANES), BF16)]
        + [((9 * C, 4 * LANES), BF16)] * 2,
        flops=8 * 10**9,
    )
    (joined,) = call(
        weight_kernel,
        (grid, grad_h, grad_d, hidden, early),
        [((24 * C + 128, LANES), BF16)],
        [((EDGE * pairs, C, LANES), BF16), ((VOX, 3 * C), F32), ((4 * C, LANES), F32)],
        flops=12 * 10**9,
    )
    joined, slots, grad_h = lax.optimization_barrier((joined, slots, grad_h))
    edge_low, edge_high = call(
        pack_kernel, (grad_h,), [((fine_groups, C, LANES), BF16)] * 2, flops=10**9
    )
    edge_left = send(edge_high, 1, 0)
    edge_right = send(edge_low, -1, 0)
    share = reduce_share(joined)
    (output,) = call(
        output_kernel,
        (slots, hidden, rects, live, up_w),
        [((number, C, VOX), BF16)],
        [((number // 2 * C, 1024), BF16), ((number // 2 * C, 1024), BF16)],
        scalars=1,
        flops=8 * 10**9,
    )
    share, output, slots = lax.optimization_barrier((share, output, slots))
    (input_grad,) = call(
        input_kernel,
        (slots, grad_h, edge_left, edge_right, live, fine_back),
        [((number, C, VOX), BF16)],
        [
            ((EDGE * pairs + 1, C, LANES), F32),
            ((number // 2 * C, 1024), BF16),
            ((number // 2 * C, 1024), BF16),
            ((EDGE * pairs, 3 * C, LANES), BF16),
        ]
        + [((9 * C, 4 * LANES), BF16)] * 2,
        scalars=1,
        flops=8 * 10**9,
    )
    total = spread_share(share)
    scale = 1.0 / math.sqrt(number * VOX * lax.axis_size("gx") * lax.axis_size("gy"))
    fine_total, down_total, coarse_total, up_total = call(
        functools.partial(finish_kernel, scale),
        (total,),
        [((27, C, C), F32), ((C, 8, C), F32), ((27, C, C), F32), ((8, C, C), F32)],
    )
    shape_out = (1, 1, number, C, VOX)
    return (
        output.reshape(shape_out),
        input_grad.reshape(shape_out),
        fine_total.transpose(1, 0, 2),
        down_total,
        coarse_total.transpose(1, 0, 2),
        up_total,
    )


def solution(mesh):
    split = P("gx", "gy", None, None, None)
    return jax.shard_map(
        on_device,
        mesh=mesh,
        in_specs=(split, P("gx", "gy", None), P("gx", "gy"), split, P(), P(), P(), P()),
        out_specs=(split, split, P(), P(), P(), P()),
        check_vma=False,
    )
```
